32 devices in a mesh: fsdp: 2 (over x), ctx: 4 (over y, core), tp: 4 (over z).
Axes of the slice: x: 2, y: 2, z: 4, core: 2. Of those that a mesh axis runs over, the one named last changes fastest.
Arguments:
- tokens: bfloat16 [2, 1024, 2048], P('fsdp', 'ctx'), may hold values from -6 to 6
- gain_attn: bfloat16 [2048], P(('fsdp', 'ctx')), may hold values from 0.5 to 1.5
- gain_mlp: bfloat16 [2048], P(('fsdp', 'ctx')), may hold values from 0.5 to 1.5
- w_kv: bfloat16 [2048, 2, 2048], P(('fsdp', 'ctx'), None, 'tp'), may hold values from -0.125 to 0.125
- w_query: bfloat16 [2048, 4, 2048], P(('fsdp', 'ctx'), None, 'tp'), may hold values from -0.125 to 0.125
- w_out_attn: bfloat16 [2048, 4, 2048], P(('fsdp', 'ctx'), None, 'tp'), may hold values from -1 to 1
- w_in: bfloat16 [2048, 4, 2, 5632], P(('fsdp', 'ctx'), None, None, 'tp'), may hold values from -0.125 to 0.125
- w_down: bfloat16 [2048, 4, 5632], P(('fsdp', 'ctx'), None, 'tp'), may hold values from -0.15625 to 0.15625
- segments: int32 [2, 1024], P('fsdp'), may hold values from 0 to 255, as said below
- attn_routes: int32 [2, 1024, 2], P('fsdp', 'ctx'), may hold values from 0 to 3, all different within a row; in each aligned block of 256 rows (0 to 255, 256 to 511, ..., all dimensions but the last counted through in order) at most 144 rows name the same one
- attn_gates: float32 [2, 1024, 2], P('fsdp', 'ctx'), may hold values from 0.2 to 0.8
- mlp_routes: int32 [2, 1024, 2], P('fsdp', 'ctx'), may hold values from 0 to 3, all different within a row; in each aligned block of 256 rows (0 to 255, 256 to 511, ..., all dimensions but the last counted through in order) at most 144 rows name the same one
- mlp_gates: float32 [2, 1024, 2], P('fsdp', 'ctx'), may hold values from 0.2 to 0.8
- cotangent: bfloat16 [2, 1024, 2048], P('fsdp', 'ctx'), may hold values from -6 to 6
Outputs:
- output: bfloat16 [2, 1024, 2048], P('fsdp', 'ctx')
- grad_tokens: bfloat16 [2, 1024, 2048], P('fsdp', 'ctx')
- grad_gain_attn: float32 [2048], P(('fsdp', 'ctx'))
- grad_gain_mlp: float32 [2048], P(('fsdp', 'ctx'))
- grad_w_kv: float32 [2048, 2, 2048], P(('fsdp', 'ctx'), None, 'tp')
- grad_w_query: float32 [2048, 4, 2048], P(('fsdp', 'ctx'), None, 'tp')
- grad_w_out_attn: float32 [2048, 4, 2048], P(('fsdp', 'ctx'), None, 'tp')
- grad_w_in: float32 [2048, 4, 2, 5632], P(('fsdp', 'ctx'), None, None, 'tp')
- grad_w_down: float32 [2048, 4, 5632], P(('fsdp', 'ctx'), None, 'tp')
The draws below stay inside these ranges and needn't reach their ends.
Inputs may be any that keep to these rules, and one draw needn't show every extreme that they name: `segments`: along each sequence the segment numbers start at 0, never fall and end at 255; positions 255 to 768 of every sequence lie in one segment. `attn_routes`: among the 256 tokens of one context index of a sequence, no attention expert is named by more than 144 tokens, a bound that some block reaches in some such block. `mlp_routes`: among the 256 tokens of one context index of a sequence, no feed-forward expert is named by more than 144 tokens, a bound that some block reaches in some such block.
All inputs are finite; a program needn't handle non-finite values.
Results may differ from the reference program's by a relative error of at most 0.024.
Values may be sent and summed in bfloat16 or wider, within the bound.
A program may use at most 576 MiB of HBM per device.

```python
import math
import jax
import jax.numpy as jnp
import numpy as np
from jax import lax

D = 2048
HEADS = 16
HD = 128
FF = 5632
EXPERTS = 4
EXPERTS_ATT = 4
LEN = 1024
ROWS = 256
CAP = 144
SEQS = 2


def one_sequence(key):
    place_idx = jnp.arange(LEN, dtype=jnp.int32)
    border = (place_idx > 0) & (place_idx < ROWS - 1) | (place_idx > LEN - ROWS)
    ranks = jax.random.permutation(key, LEN).astype(jnp.int32)
    keyed = jnp.where(border, ranks, ranks + LEN)
    order = jnp.argsort(keyed, stable=True)
    chosen = order[:ROWS - 1]
    starts = jnp.zeros((LEN,), jnp.int32).at[chosen].set(1)
    return jnp.cumsum(starts).astype(jnp.int32)


def draw_segments(key, part):
    key = jax.random.fold_in(key, 17)
    keys = jax.random.split(key, SEQS)
    return jax.vmap(one_sequence)(keys).astype(jnp.int32)


def block_scale(key, shape, cuts, smallest, largest):
    level, own = 1.0, jax.random.fold_in(key, 6)
    for axis_at, shards_of in cuts:
        draws = jnp.exp(jax.random.uniform(jax.random.fold_in(own, axis_at), (shards_of,), jnp.float32, smallest / len(cuts), largest / len(cuts)))
        level = level * jnp.repeat(draws, shape[axis_at] // shards_of).reshape([-1 if axis == axis_at else 1 for axis in range(len(shape))])
    return level


def shared_out(rng, own, number, rows, amount, top, bound, slope):
    sequence = jax.random.permutation(rng, amount)
    crowded, usual = portions_of(amount, rows * top, bound, slope, True), portions_of(amount, rows * top, bound, slope, False)
    places = jnp.arange(amount)

    def named(lengths, rotation):
        used = int((lengths > 0).sum())
        fixed = max(1, used // 4)
        shifted = fixed + (places - fixed + rotation * (used - fixed)) % max(1, amount - fixed)
        return jnp.zeros((amount,), jnp.int32).at[sequence[jnp.where(places < fixed, places, shifted)]].set(jnp.asarray(lengths, jnp.int32))

    lengths = jnp.where(number % 4 == 0, named(crowded, number // 4), named(usual, number - number // 4 - 1))
    mixed = jax.random.permutation(jax.random.fold_in(own, 3), amount)
    source_of, receiver = mixed[0:amount // 2 * 2:2], mixed[1:amount // 2 * 2:2]
    slack = jnp.minimum(lengths[source_of] - 1, bound - lengths[receiver]) // 2
    slack = jnp.where((source_of == sequence[0]) | (receiver == sequence[0]) | (lengths[receiver] == 0), 0, jnp.maximum(slack, 0))
    shifted = jax.random.randint(jax.random.fold_in(own, 4), (amount // 2,), 0, 1 << 20) % (slack + 1)
    lengths = lengths.at[source_of].add(-shifted).at[receiver].add(shifted)
    labels = jnp.searchsorted(jnp.cumsum(lengths), jnp.arange(rows * top), side="right").astype(jnp.int32)
    listing = labels.reshape(top, rows).T
    listing = listing[jax.random.permutation(jax.random.fold_in(own, 1), rows)]
    rotation = jax.random.randint(jax.random.fold_in(own, 2), (rows, 1), 0, top)
    return jnp.take_along_axis(listing, (jnp.arange(top)[None, :] + rotation) % top, axis=1)


def portions_of(count, total, most, lean, full):
    loads = [(1 << 20) // math.isqrt(grade ** lean) + 1 for grade in range(1, count + 1)]
    largest = most if full else min(most, max(-(-total // count), total * loads[0] // sum(loads)))
    least = 1 if total - largest >= count - 1 else 0
    counts, spare = [largest] + [least] * (count - 1), total - largest - least * (count - 1)
    while spare > 0:
        movable = [i for i in range(1, count) if counts[i] < largest] or [i for i in range(1, count) if counts[i] < most]
        whole, left = sum([loads[i] for i in movable]), spare
        for i in movable:
            extra = min(most - counts[i], max(1, left * loads[i] // whole), spare)
            counts[i] = counts[i] + extra
            spare = spare - extra
    return np.array(counts)


def noise(key, shape, deviation, limit, cuts=(), kind=jnp.bfloat16):
    values = jax.random.normal(key, shape, jnp.float32) * deviation
    if len(cuts) > 0:
        values = block_scale(key, shape, cuts, -0.22, 0.18) * values
    return jnp.clip(values, min=-limit, max=limit).astype(kind)


def setup_inputs(seed: int = 0) -> dict:
    key_list = jax.random.split(jax.random.key(seed), 15)
    tokens = noise(key_list[0], (SEQS, LEN, D), 1.0, 6.0, ((0, 2), (1, 4)))
    gain_attn = jnp.clip(1.0 + 0.1 * jax.random.normal(key_list[1], (D,), jnp.float32), 0.5, 1.5).astype(jnp.bfloat16)
    gain_mlp = jnp.clip(1.0 + 0.1 * jax.random.normal(key_list[2], (D,), jnp.float32), 0.5, 1.5).astype(jnp.bfloat16)
    w_kv = noise(key_list[3], (D, 2, HEADS * HD), D ** -0.5, 0.125, ((0, 8), (2, 4)))
    w_query = noise(key_list[4], (D, EXPERTS_ATT, HEADS * HD), D ** -0.5, 0.125, ((0, 8), (2, 4)))
    w_out_attn = noise(key_list[5], (D, EXPERTS_ATT, HEADS * HD), (HEADS * HD // 64) ** -0.5, 1.0, ((0, 8), (2, 4)))
    w_in = noise(key_list[6], (D, EXPERTS, 2, FF), D ** -0.5, 0.125, ((0, 8), (3, 4)))
    w_down = noise(key_list[7], (D, EXPERTS, FF), (FF // 4) ** -0.5, 0.15625, ((0, 8), (2, 4)))
    segments = draw_segments(jax.random.fold_in(key_list[14], 71), 0)
    attn_routes_keys = jax.random.split(jax.random.fold_in(key_list[9], 1), SEQS * LEN // ROWS)
    attn_routes_turns = jax.random.permutation(jax.random.fold_in(key_list[9], 3), SEQS * LEN // ROWS)
    attn_routes = jax.vmap(lambda own, number: shared_out(jax.random.fold_in(key_list[9], 2), own, number, ROWS, EXPERTS_ATT, 2, CAP, 1))(attn_routes_keys, attn_routes_turns).reshape((SEQS, LEN, 2))
    attn_gates = jnp.clip(0.2 + 0.6 * jax.random.uniform(key_list[10], (SEQS, LEN, 2), jnp.float32) ** block_scale(key_list[10], (SEQS, LEN, 2), ((0, 2), (1, 4)), -0.2, 0.2), 0.2, 0.8)
    mlp_routes_keys = jax.random.split(jax.random.fold_in(key_list[11], 1), SEQS * LEN // ROWS)
    mlp_routes_turns = jax.random.permutation(jax.random.fold_in(key_list[11], 3), SEQS * LEN // ROWS)
    mlp_routes = jax.vmap(lambda own, number: shared_out(jax.random.fold_in(key_list[11], 2), own, number, ROWS, EXPERTS, 2, CAP, 1))(mlp_routes_keys, mlp_routes_turns).reshape((SEQS, LEN, 2))
    mlp_gates = jnp.clip(0.2 + 0.6 * jax.random.uniform(key_list[12], (SEQS, LEN, 2), jnp.float32) ** block_scale(key_list[12], (SEQS, LEN, 2), ((0, 2), (1, 4)), -0.2, 0.2), 0.2, 0.8)
    cotangent = noise(key_list[13], (SEQS, LEN, D), 1.0, 6.0, ((0, 2), (1, 4)))
    return {"tokens": tokens, "gain_attn": gain_attn, "gain_mlp": gain_mlp, "w_kv": w_kv, "w_query": w_query, "w_out_attn": w_out_attn, "w_in": w_in, "w_down": w_down, "segments": segments, "attn_routes": attn_routes, "attn_gates": attn_gates, "mlp_routes": mlp_routes, "mlp_gates": mlp_gates, "cotangent": cotangent}


@jax.custom_vjp
def low(v):
    return lax.optimization_barrier(v.astype(jnp.bfloat16)).astype(jnp.float32)

@jax.custom_vjp
def low_back(v):
    return v

def low_keep(v):
    return (low(v), None)

def low_pass(kept, grad):
    return (grad,)

def back_keep(v):
    return (v, None)

def back_low(kept, grad):
    return (low(grad),)
low.defvjp(low_keep, low_pass)
low_back.defvjp(back_keep, back_low)
EPSILON = 1e-06
ROPE_BASE = 10000.0
MASKED = -1e+30

def positions(seg_row):
    place_idx = jnp.arange(seg_row.shape[0], dtype=jnp.int32)
    before = jnp.concatenate([seg_row[:1] - 1, seg_row[:-1]])
    doc_start = lax.cummax(jnp.where(seg_row != before, place_idx, 0), axis=0)
    return (place_idx - doc_start).astype(jnp.float32)

def rotary(pos_rows, size):
    frequency = ROPE_BASE ** (-(jnp.arange(size // 2, dtype=jnp.float32) * 2.0) / size)
    angles = pos_rows[:, None] * frequency[None, :]
    return (jnp.cos(angles), jnp.sin(angles))

def rotate(tensor, cos_table, sin_table, size):
    dims_all = tensor.shape
    per_head = tensor.reshape(dims_all[:-1] + (dims_all[-1] // size, size))
    ones_pad = (1,) * (per_head.ndim - 2)
    cos_wide = cos_table.reshape((cos_table.shape[0],) + ones_pad + (size // 2,))
    sin_wide = sin_table.reshape((sin_table.shape[0],) + ones_pad + (size // 2,))
    front_half = per_head[..., :size // 2]
    back_half = per_head[..., size // 2:]
    turned = jnp.concatenate([front_half * cos_wide - back_half * sin_wide, back_half * cos_wide + front_half * sin_wide], axis=-1)
    return turned.reshape(dims_all)

def rms_norm(tensor, gain_vec):
    return tensor * lax.rsqrt(lax.optimization_barrier(jnp.mean(tensor * tensor, axis=-1, keepdims=True)) + EPSILON) * gain_vec

def attention(queries, keys_in, values_in, seg_row):
    length = queries.shape[0]
    slot_count = queries.shape[1]
    head_count = keys_in.shape[1] // HD
    query_total = length * slot_count
    block_rows = math.gcd(query_total, 2048)
    block_count = query_total // block_rows
    query_h = queries.reshape(length, slot_count, head_count, HD).transpose(2, 0, 1, 3).reshape(head_count, block_count, block_rows, HD)
    key_h = keys_in.reshape(length, head_count, HD).transpose(1, 0, 2)
    value_h = values_in.reshape(length, head_count, HD).transpose(1, 0, 2)
    place_idx = jnp.arange(length, dtype=jnp.int32)
    query_seg = jnp.repeat(seg_row, slot_count).reshape(block_count, block_rows)
    query_idx = jnp.repeat(place_idx, slot_count).reshape(block_count, block_rows)

    def one_head(operands):
        query_blocks, key_rows, value_rows = operands

        def one_block(block_ops):
            query_rows, seg_block, idx_block = block_ops
            allowed = (seg_block[:, None] == seg_row[None, :]) & (place_idx[None, :] <= idx_block[:, None])
            scores = low_back(jnp.einsum('qd,kd->qk', query_rows, key_rows, precision=lax.Precision.HIGHEST) * HD ** (-0.5))
            scores = jnp.where(allowed, scores, MASKED)
            top_score = lax.optimization_barrier(jnp.max(scores, axis=-1, keepdims=True))
            exp_scores = jnp.where(allowed, jnp.exp(scores - top_score), 0.0)
            total = lax.optimization_barrier(jnp.sum(exp_scores, axis=-1, keepdims=True))
            return jnp.einsum('qk,kd->qd', low(exp_scores), value_rows, precision=lax.Precision.HIGHEST) / total
        return lax.map(jax.checkpoint(one_block), (query_blocks, query_seg, query_idx))
    result = lax.map(jax.checkpoint(one_head), (query_h, key_h, value_h))
    return result.reshape(head_count, length, slot_count, HD).transpose(1, 2, 0, 3).reshape(length, slot_count, head_count * HD)

def forward(inputs, gain_one, gain_two, kv_weight, query_weight, outw_weight, in_weight, down_weight, seg_row, attn_route, attn_gate, mlp_route, mlp_gate):
    cos_table, sin_table = rotary(positions(seg_row), HD)
    hidden_one = low(rms_norm(inputs, gain_one))
    kv_raw = low_back(jnp.einsum('td,dck->tck', hidden_one, kv_weight, precision=lax.Precision.HIGHEST))
    keys_all = low(rotate(kv_raw[:, 0], cos_table, sin_table, HD))
    values_all = low(kv_raw[:, 1])
    attn_mask = (attn_route[:, :, None] == jnp.arange(query_weight.shape[1], dtype=jnp.int32)[None, None, :]).astype(jnp.float32)
    query_all = low_back(jnp.einsum('td,deq->teq', hidden_one, query_weight, precision=lax.Precision.HIGHEST))
    query_sel = jnp.einsum('tje,teq->tjq', attn_mask, query_all, precision=lax.Precision.HIGHEST)
    queries = low(rotate(query_sel, cos_table, sin_table, HD))
    attn_rows = low_back(attention(queries, keys_all, values_all, seg_row))
    mixed = low(jnp.einsum('tje,tj,tjq->teq', attn_mask, attn_gate, attn_rows, precision=lax.Precision.HIGHEST))
    branch = low_back(jnp.einsum('teq,deq->td', mixed, outw_weight, precision=lax.Precision.HIGHEST))
    resid = inputs + branch
    hidden_two = low(rms_norm(resid, gain_two))
    gate_up = low_back(jnp.einsum('td,dkcf->tkcf', hidden_two, in_weight, precision=lax.Precision.HIGHEST))
    mlp_mask = (mlp_route[:, :, None] == jnp.arange(in_weight.shape[1], dtype=jnp.int32)[None, None, :]).astype(jnp.float32)
    expert_weight = jnp.einsum('tjk,tj->tk', mlp_mask, mlp_gate, precision=lax.Precision.HIGHEST)
    active = low(jax.nn.silu(gate_up[:, :, 0]) * gate_up[:, :, 1] * expert_weight[:, :, None])
    experts_out = jnp.einsum('tkf,dkf->td', active, down_weight, precision=lax.Precision.HIGHEST)
    return resid + experts_out

def reference(tokens, gain_attn, gain_mlp, w_kv, w_query, w_out_attn, w_in, w_down, segments, attn_routes, attn_gates, mlp_routes, mlp_gates, cotangent):
    weights = (gain_attn.astype(jnp.float32), gain_mlp.astype(jnp.float32), w_kv.astype(jnp.float32), w_query.astype(jnp.float32), w_out_attn.astype(jnp.float32), w_in.astype(jnp.float32), w_down.astype(jnp.float32))
    totals_init = tuple((jnp.zeros_like(weight_one) for weight_one in weights))

    def per_sequence(totals, item):
        inputs, seg_row, attn_route, attn_gate, mlp_route, mlp_gate, grad_out = item

        def layer(inputs_in, gain_one, gain_two, kv_weight, query_weight, outw_weight, in_weight, down_weight):
            return forward(inputs_in, gain_one, gain_two, kv_weight, query_weight, outw_weight, in_weight, down_weight, seg_row, attn_route, attn_gate, mlp_route, mlp_gate)
        result, pullback = jax.vjp(layer, inputs, *weights)
        grads = pullback(grad_out)
        totals = tuple((total + grad_one for total, grad_one in zip(totals, grads[1:])))
        return (totals, (result.astype(jnp.bfloat16), grads[0].astype(jnp.bfloat16)))
    sequences = (tokens.astype(jnp.float32), segments, attn_routes, attn_gates.astype(jnp.float32), mlp_routes, mlp_gates.astype(jnp.float32), cotangent.astype(jnp.float32))
    totals, (output, grad_tokens) = lax.scan(per_sequence, totals_init, sequences)
    return (output, grad_tokens, totals[0], totals[1], totals[2], totals[3], totals[4], totals[5], totals[6])
```

```python
import functools

import jax
import jax.numpy as jnp
from jax import lax
from jax.experimental import pallas as pl
from jax.experimental.pallas import tpu as pltpu
from jax.sharding import PartitionSpec as P

HD = 128
EPSILON = 1e-06
ROPE_BASE = 10000.0
MASKED = -1e30
GROUP = ("fsdp", "ctx")
BF = jnp.bfloat16
F32 = jnp.float32
VMEM_LIMIT = 56 * 1024 * 1024


def normalize(tensor, gain_vec):
    inverse = lax.rsqrt(jnp.mean(tensor * tensor, axis=-1, keepdims=True) + EPSILON)
    normed = tensor * inverse
    return (normed, inverse, normed * gain_vec)


def norm_back(grad_in, normed, inverse, gain_vec):
    scaled = grad_in * gain_vec
    inner_mean = jnp.mean(scaled * normed, axis=-1, keepdims=True)
    return (inverse * (scaled - normed * inner_mean), jnp.sum(grad_in * normed, axis=0))


def dot(a, b, ca, cb):
    return lax.dot_general(a, b, (((ca,), (cb,)), ((), ())), preferred_element_type=F32)


def turn(x, cos, sin):
    return x * cos + pltpu.roll(x, HD // 2, 1) * sin


def swap(x, mask, axes, count):
    return lax.ppermute(x, axes, [(i, i ^ mask) for i in range(count)])


def bits_of(count):
    return count.bit_length() - 1


def project_kernel(h_ref, w_ref, cos_ref, sin_ref, out_ref):
    y = jnp.dot(h_ref[...], w_ref[0], preferred_element_type=F32)
    for head in range(y.shape[1] // HD):
        cols = slice(head * HD, (head + 1) * HD)
        out_ref[:, cols] = turn(y[:, cols], cos_ref[0], sin_ref[0]).astype(BF)


def project(hidden, planes, cos, sin, plain):
    rows, width = hidden.shape
    count, _, cols = planes.shape
    tables = [
        jnp.stack([cos, jnp.ones_like(cos)]),
        jnp.stack([sin, jnp.zeros_like(sin)]),
    ]
    table_spec = pl.BlockSpec((1, rows, HD), lambda p: (p // plain, 0, 0))
    return pl.pallas_call(
        project_kernel,
        out_shape=jax.ShapeDtypeStruct((rows, count * cols), BF),
        grid=(count,),
        in_specs=[
            pl.BlockSpec((rows, width), lambda p: (0, 0)),
            pl.BlockSpec((1, width, cols), lambda p: (p, 0, 0)),
            table_spec,
            table_spec,
        ],
        out_specs=pl.BlockSpec((rows, cols), lambda p: (0, p)),
        compiler_params=pltpu.CompilerParams(vmem_limit_bytes=VMEM_LIMIT),
        name="project",
    )(hidden, planes, *tables)


def scores_of(d_ref, q_ref, k_ref, segq_ref, idxq_ref, segk_ref, idxk_ref):
    slots = dot(d_ref[0], q_ref[...], 1, 0).astype(BF)
    scores = dot(slots, k_ref[...], 1, 1) * (HD**-0.5)
    allowed = (segq_ref[0] == segk_ref[...]) & (idxk_ref[...] <= idxq_ref[0])
    scores = jnp.where(allowed, scores, MASKED)
    top = jnp.max(scores, axis=-1, keepdims=True)
    exps = jnp.exp(scores - top)
    total = jnp.sum(exps, axis=-1, keepdims=True)
    return slots, exps, 1.0 / total


def attend_kernel(
    q_ref, k_ref, v_ref, d_ref, segq_ref, idxq_ref, gate_ref, segk_ref, idxk_ref, out_ref
):
    _, exps, inv = scores_of(d_ref, q_ref, k_ref, segq_ref, idxq_ref, segk_ref, idxk_ref)
    attn = dot(exps.astype(BF), v_ref[...], 1, 0) * inv
    mixed = (attn * gate_ref[0]).astype(BF)
    out_ref[...] = dot(d_ref[0], mixed, 0, 0).astype(BF)


def attend_back_kernel(
    heads,
    experts,
    q_ref,
    k_ref,
    v_ref,
    d_ref,
    segq_ref,
    idxq_ref,
    segk_ref,
    idxk_ref,
    da_ref,
    cosq_ref,
    sinq_ref,
    cosk_ref,
    sink_ref,
    dq_ref,
    dk_ref,
    dv_ref,
    dk_acc,
    dv_acc,
):
    expert = pl.program_id(1)

    @pl.when(expert == 0)
    def _():
        dk_acc[...] = jnp.zeros_like(dk_acc)
        dv_acc[...] = jnp.zeros_like(dv_acc)

    slots, exps, inv = scores_of(d_ref, q_ref, k_ref, segq_ref, idxq_ref, segk_ref, idxk_ref)
    attn = dot(exps.astype(BF), v_ref[...], 1, 0) * inv
    probs = exps * inv
    grad = dot(d_ref[0], da_ref[...], 1, 0)
    delta = jnp.sum(grad * attn, axis=-1, keepdims=True)
    grad = grad.astype(BF)
    dv_acc[...] += dot(probs.astype(BF), grad, 0, 0)
    grad_probs = dot(grad, v_ref[...], 1, 1)
    grad_scores = (probs * (grad_probs - delta)).astype(BF)
    dq = dot(grad_scores, k_ref[...], 1, 0) * (HD**-0.5)
    dk_acc[...] += dot(grad_scores, slots, 0, 0) * (HD**-0.5)
    high = dq.astype(BF)
    low = (dq - high.astype(F32)).astype(BF)
    rows = dot(d_ref[0], high, 0, 0) + dot(d_ref[0], low, 0, 0)
    dq_ref[...] = turn(rows, cosq_ref[...], -sinq_ref[...]).astype(BF)

    @pl.when(expert == experts - 1)
    def _():
        dk_ref[...] = turn(dk_acc[...], cosk_ref[...], -sink_ref[...]).astype(BF)
        dv_ref[...] = dv_acc[...].astype(BF)


def attend_specs(rows, keys, heads, experts, cap):
    q_spec = pl.BlockSpec((rows, HD), lambda h, e: (0, e * heads + h))
    k_spec = pl.BlockSpec((keys, HD), lambda h, e: (0, h))
    v_spec = pl.BlockSpec((keys, HD), lambda h, e: (0, heads + h))
    d_spec = pl.BlockSpec((1, cap, rows), lambda h, e: (e, 0, 0))
    s_spec = pl.BlockSpec((1, cap, 1), lambda h, e: (e, 0, 0))
    t_spec = pl.BlockSpec((1, keys), lambda h, e: (0, 0))
    return q_spec, k_spec, v_spec, d_spec, s_spec, t_spec


def attend(qkv, kv, place, slot_seg, slot_idx, slot_gate, key_seg, key_idx):
    experts, cap, rows = place.shape
    keys = kv.shape[0]
    heads = kv.shape[1] // (2 * HD)
    q_spec, k_spec, v_spec, d_spec, s_spec, t_spec = attend_specs(rows, keys, heads, experts, cap)
    return pl.pallas_call(
        attend_kernel,
        out_shape=jax.ShapeDtypeStruct((rows, experts * heads * HD), BF),
        grid=(heads, experts),
        in_specs=[q_spec, k_spec, v_spec, d_spec, s_spec, s_spec, s_spec, t_spec, t_spec],
        out_specs=q_spec,
        compiler_params=pltpu.CompilerParams(vmem_limit_bytes=VMEM_LIMIT),
        name="attend",
    )(qkv, kv, kv, place, slot_seg, slot_idx, slot_gate, key_seg, key_idx)


def attend_back(qkv, kv, place, slot_seg, slot_idx, key_seg, key_idx, grad, tables):
    experts, cap, rows = place.shape
    keys = kv.shape[0]
    heads = kv.shape[1] // (2 * HD)
    q_spec, k_spec, v_spec, d_spec, s_spec, t_spec = attend_specs(rows, keys, heads, experts, cap)
    cos, sin = tables
    cq_spec = pl.BlockSpec((rows, HD), lambda h, e: (0, 0))
    ck_spec = pl.BlockSpec((keys, HD), lambda h, e: (0, 0))
    return pl.pallas_call(
        functools.partial(attend_back_kernel, heads, experts),
        out_shape=(
            jax.ShapeDtypeStruct((rows, experts * heads * HD), BF),
            jax.ShapeDtypeStruct((keys, heads * HD), BF),
            jax.ShapeDtypeStruct((keys, heads * HD), BF),
        ),
        grid=(heads, experts),
        in_specs=[q_spec, k_spec, v_spec, d_spec, s_spec, s_spec, t_spec, t_spec]
        + [q_spec, cq_spec, cq_spec, ck_spec, ck_spec],
        out_specs=(q_spec, k_spec, k_spec),
        scratch_shapes=[pltpu.VMEM((keys, HD), F32)] * 2,
        compiler_params=pltpu.CompilerParams(vmem_limit_bytes=VMEM_LIMIT),
        name="attend_back",
    )(qkv, kv, kv, place, slot_seg, slot_idx, key_seg, key_idx, grad, cos, sin, cos, sin)


def places(routes, gates, experts, cap, room):
    rows = routes.shape[0]
    named = routes[:, :, None] == jnp.arange(experts, dtype=jnp.int32)[None, None, :]
    member = jnp.any(named, axis=1)
    gate = jnp.sum(jnp.where(named, gates[:, :, None], 0.0), axis=1)
    token = jnp.arange(rows, dtype=jnp.int32)
    earlier = (token[None, :] < token[:, None]).astype(BF)
    rank = dot(earlier, member.astype(BF), 1, 0).astype(jnp.int32)
    slot = jnp.where(member, rank, -1).T
    taken = slot[:, None, :] == jnp.arange(room, dtype=jnp.int32)[None, :, None]
    return taken, gate


def slot_sum(taken, values):
    return jnp.sum(jnp.where(taken, values, 0), axis=-1, keepdims=True)


def layer(
    counts,
    tokens,
    gain_attn,
    gain_mlp,
    w_kv,
    w_query,
    w_out_attn,
    w_in,
    w_down,
    segments,
    attn_routes,
    attn_gates,
    mlp_routes,
    mlp_gates,
    cotangent,
):
    fsdp_count, ctx_count = counts
    group = fsdp_count * ctx_count
    me = lax.axis_index(GROUP)
    ctx_me = lax.axis_index("ctx")
    inputs = tokens[0].astype(F32)
    rows, width = inputs.shape
    cap = 9 * rows // 16
    room = -(-cap // 16) * 16
    part = width // group
    attn_experts = w_query.shape[1]
    experts = w_in.shape[1]
    share = group // experts
    expert_me = me // share
    hidden_units = w_down.shape[2]
    head_width = w_kv.shape[2]

    def piece(x, index, size=part, axis=1):
        return lax.dynamic_slice_in_dim(x, index * size, size, axis)

    def relative(x, order):
        return jnp.concatenate([piece(x, me ^ j) for j in order], axis=1)

    def exchange(x, mask):
        return swap(x, mask, GROUP, group)

    qkv_own = jnp.concatenate([w_query, w_kv], axis=1).transpose(1, 0, 2)
    qkv_full = lax.all_gather(qkv_own, GROUP, axis=1, tiled=True)
    outw_full = lax.all_gather(w_out_attn.transpose(1, 0, 2), GROUP, axis=1, tiled=True)
    gains = lax.all_gather(jnp.stack([gain_attn, gain_mlp]), GROUP, axis=1, tiled=True).astype(F32)
    gain_one, gain_two = gains[0], gains[1]

    seg_row = segments[0]
    seq_total = seg_row.shape[0]
    ctx_bits = list(range(bits_of(ctx_count)))[::-1]
    key_order = [0]
    for bit in ctx_bits:
        key_order = key_order + [j | (1 << bit) for j in key_order]
    key_seg = jnp.concatenate([piece(seg_row, ctx_me ^ j, rows, 0) for j in key_order])
    key_idx = jnp.concatenate(
        [(ctx_me ^ j) * rows + jnp.arange(rows, dtype=jnp.int32) for j in key_order]
    )
    place_idx = jnp.arange(seq_total, dtype=jnp.int32)
    pos = jnp.sum(
        (seg_row[None, :] == key_seg[:, None]) & (place_idx[None, :] < key_idx[:, None]),
        axis=1,
        dtype=jnp.int32,
    ).astype(F32)
    frequency = ROPE_BASE ** (-(jnp.arange(HD // 2, dtype=F32) * 2.0) / HD)
    angles = pos[:, None] * frequency[None, :]
    cos_half, sin_half = jnp.cos(angles), jnp.sin(angles)
    cos = jnp.concatenate([cos_half, cos_half], axis=1)
    sin = jnp.concatenate([-sin_half, sin_half], axis=1)
    taken_attn, gate_attn = places(attn_routes[0], attn_gates[0], attn_experts, cap, room)
    place_attn = taken_attn.astype(BF)
    own_seg, own_idx = key_seg[:rows], key_idx[:rows]
    filled = jnp.any(taken_attn, axis=-1, keepdims=True)
    slot_seg = jnp.where(filled, slot_sum(taken_attn, own_seg), own_seg[0])
    slot_idx = jnp.where(filled, slot_sum(taken_attn, own_idx), own_idx[0])
    slot_gate = slot_sum(taken_attn, gate_attn.T[:, None, :])
    taken_mlp, gate_mlp = places(mlp_routes[0], mlp_gates[0], experts, cap, room)
    mine_first = [expert_me ^ k for k in range(experts)]
    place_mlp = jnp.concatenate([piece(taken_mlp, e, 1, 0) for e in mine_first]).astype(BF)
    weight_slots = slot_sum(taken_mlp, gate_mlp.T[:, None, :])

    normed_one, inverse_one, pre_one = normalize(inputs, gain_one)
    hidden_one = pre_one.astype(BF)
    qkv = project(hidden_one, qkv_full, cos[:rows], sin[:rows], attn_experts + 1)
    kv = qkv[:, attn_experts * head_width :]
    for bit in ctx_bits:
        kv = jnp.concatenate([kv, swap(kv, 1 << bit, "ctx", ctx_count)], axis=0)
    key_row = (key_seg[None, :], key_idx[None, :])
    mixed = attend(qkv, kv, place_attn, slot_seg, slot_idx, slot_gate, *key_row)

    def planes(x):
        return x.reshape(rows, x.shape[1] // head_width, head_width)

    branch = jnp.einsum("tpc,pdc->td", planes(mixed), outw_full, preferred_element_type=F32)
    resid = inputs + lax.psum(branch.astype(BF), "tp").astype(F32)
    normed_two, inverse_two, pre_two = normalize(resid, gain_two)
    hidden_two = pre_two.astype(BF)

    w_in_late, w_down_late, _ = lax.optimization_barrier((w_in, w_down, outw_full))

    def expert_rows(k):
        in_rows = piece(w_in_late, expert_me ^ k, 1, 1).reshape(part, 2 * hidden_units)
        down_rows = piece(w_down_late, expert_me ^ k, 1, 1).reshape(part, hidden_units)
        return jnp.concatenate([in_rows, down_rows], axis=1)

    by_source = [expert_rows(0)] + [
        exchange(expert_rows(k), k * share) for k in range(1, experts)
    ]
    blocks = []
    for block in by_source:
        blocks += [block] + [exchange(block, t) for t in range(1, share)]
    in_full = jnp.concatenate([b[:, : 2 * hidden_units] for b in blocks], axis=0)
    down_full = jnp.concatenate([b[:, 2 * hidden_units :] for b in blocks], axis=0)

    def turned(x, k):
        wide = share * part
        return jnp.concatenate(
            [x[:, (i ^ k) * wide : ((i ^ k) + 1) * wide] for i in range(experts)], axis=1
        )

    def send_out(x):
        slots = jnp.einsum("kct,td->kcd", place_mlp, x, preferred_element_type=F32).astype(BF)
        got = [slots[0]]
        for k in range(1, experts):
            got.append(exchange(turned(slots[k], k), k * share))
        return jnp.concatenate(got, axis=0)

    def send_back(x):
        slots = x.reshape(experts, room, width)
        got = [slots[0]]
        for k in range(1, experts):
            got.append(turned(exchange(slots[k], k * share), k))
        rows_rel = jnp.einsum(
            "kct,kcd->td", place_mlp, jnp.stack(got), preferred_element_type=F32
        ).astype(BF)
        return relative(rows_rel, range(group))

    every = range(group)
    weight_own = [piece(weight_slots, expert_me ^ k, 1, 0)[0] for k in range(experts)]
    slot_weight = jnp.concatenate(
        [weight_own[0]] + [exchange(weight_own[k], k * share) for k in range(1, experts)]
    )
    grad_out = cotangent[0]
    grad_slots = send_out(relative(grad_out, every))
    two_slots = send_out(relative(hidden_two, every))
    gate_up = dot(two_slots, in_full, 1, 0)
    gate_part, up_part = gate_up[:, :hidden_units], gate_up[:, hidden_units:]
    sigmoid_gate = jax.nn.sigmoid(gate_part)
    silu_gate = gate_part * sigmoid_gate
    active = (silu_gate * up_part * slot_weight).astype(BF)
    mlp_slots = dot(active, down_full, 1, 1).astype(BF)
    grad_active = dot(grad_slots, down_full, 1, 0)
    scaled = grad_active * slot_weight
    grad_gate = scaled * up_part * sigmoid_gate * (1.0 + gate_part * (1.0 - sigmoid_gate))
    grad_up = scaled * silu_gate
    grad_gu = jnp.concatenate([grad_gate, grad_up], axis=1).astype(BF)
    back_two_slots = dot(grad_gu, in_full, 1, 1).astype(BF)
    back_two = lax.psum(send_back(back_two_slots), "tp").astype(F32)
    mlp_total = lax.psum(send_back(mlp_slots), "tp").astype(F32)
    output = (resid + mlp_total).astype(BF)

    def for_share(x, t):
        return jnp.concatenate(
            [x[:, (k * share + t) * part : (k * share + t + 1) * part] for k in range(experts)],
            axis=1,
        )

    def every_share(x, cut):
        got = [for_share(x, 0) if cut else x]
        for t in range(1, share):
            got.append(exchange(for_share(x, t) if cut else x, t))
        return jnp.concatenate(got, axis=0)

    grad_in_w = dot(every_share(two_slots, True), every_share(grad_gu, False), 0, 0).astype(BF)
    grad_down_w = dot(every_share(grad_slots, True), every_share(active, False), 0, 0).astype(BF)
    expert_grads = []
    for k in range(experts):
        cut = slice(k * part, (k + 1) * part)
        block = jnp.concatenate([grad_in_w[cut], grad_down_w[cut]], axis=1)
        expert_grads.append(exchange(block, k * share) if k else block)
    expert_grads = jnp.stack(expert_grads)
    expert_grads = jnp.stack(
        [piece(expert_grads, expert_me ^ e, 1, 0)[0] for e in range(experts)], axis=1
    ).astype(F32)
    grad_in_out = expert_grads[:, :, : 2 * hidden_units].reshape(w_in.shape)
    grad_down_out = expert_grads[:, :, 2 * hidden_units :]

    grad_resid_norm, gain_two_grad = norm_back(back_two, normed_two, inverse_two, gain_two)
    grad_resid = grad_out.astype(F32) + grad_resid_norm
    grad_branch = grad_resid.astype(BF)
    grad_mixed = jnp.einsum("td,pdc->tpc", grad_branch, outw_full, preferred_element_type=F32)
    grad_attn = (grad_mixed * gate_attn[:, :, None]).astype(BF).reshape(mixed.shape)
    grad_query, grad_key, grad_value = attend_back(
        qkv, kv, place_attn, slot_seg, slot_idx, *key_row, grad_attn, (cos, sin)
    )
    grad_kv = jnp.concatenate([grad_key, grad_value], axis=1)
    for bit in ctx_bits[::-1]:
        half = grad_kv.shape[0] // 2
        got = swap(grad_kv[half:], 1 << bit, "ctx", ctx_count)
        grad_kv = (grad_kv[:half].astype(F32) + got.astype(F32)).astype(BF)
    grad_qkv = jnp.concatenate([grad_query, grad_kv], axis=1)
    back_one_part = jnp.einsum(
        "tpc,pdc->td", planes(grad_qkv), qkv_full, preferred_element_type=F32
    )
    back_one = lax.psum(back_one_part.astype(BF), "tp").astype(F32)
    grad_input_norm, gain_one_grad = norm_back(back_one, normed_one, inverse_one, gain_one)
    grad_tokens = (grad_resid + grad_input_norm).astype(BF)

    ours = [j for j in every if j % 2 == 0]
    theirs = [j for j in every if j % 2 == 1]

    def both(x):
        return jnp.concatenate([x, exchange(x, 1)], axis=0)

    def both_cut(x):
        return jnp.concatenate([relative(x, ours), exchange(relative(x, theirs), 1)], axis=0)

    def reduced(x, bits):
        x = x.astype(BF).reshape((2,) * (bits_of(group) - 1) + (part, x.shape[1]))
        axes = list(range(1, bits_of(group)))[::-1]
        for bit in bits:
            at = axes.index(bit)
            keep = lax.index_in_dim(x, 0, at, False).astype(F32)
            got = exchange(lax.index_in_dim(x, 1, at, False), 1 << bit).astype(F32)
            axes.remove(bit)
            x = keep + got
            if axes:
                x = x.astype(BF)
        return x

    def reduced_both(x):
        bits = list(range(1, bits_of(group)))
        half = x.shape[1] // 2
        return jnp.concatenate([reduced(x[:, :half], bits), reduced(x[:, half:], bits[::-1])], axis=1)

    grad_outw = reduced_both(dot(both_cut(grad_branch), both(mixed), 0, 0))
    grad_qkvw = reduced_both(dot(both_cut(hidden_one), both(grad_qkv), 0, 0))
    grad_outw = grad_outw.reshape(w_out_attn.shape)
    grad_qkvw = grad_qkvw.reshape(part, attn_experts + 2, head_width)
    gain_grads = lax.psum(jnp.stack([gain_one_grad, gain_two_grad]), GROUP)
    gain_grads = piece(gain_grads, me)
    return (
        output[None],
        grad_tokens[None],
        gain_grads[0],
        gain_grads[1],
        grad_qkvw[:, attn_experts:],
        grad_qkvw[:, :attn_experts],
        grad_outw,
        grad_in_out,
        grad_down_out,
    )


def solution(mesh):
    rows = P("fsdp", "ctx", None)
    weight = P(GROUP, None, "tp")
    weight_in = P(GROUP, None, None, "tp")
    return jax.shard_map(
        functools.partial(layer, (mesh.shape["fsdp"], mesh.shape["ctx"])),
        mesh=mesh,
        in_specs=(
            rows,
            P(GROUP),
            P(GROUP),
            weight,
            weight,
            weight,
            weight_in,
            weight,
            P("fsdp", None),
            rows,
            rows,
            rows,
            rows,
            rows,
        ),
        out_specs=(rows, rows, P(GROUP), P(GROUP), weight, weight, weight, weight_in, weight),
        check_vma=False,
    )
```

```python
import functools

import jax
import jax.numpy as jnp
from jax import lax
from jax.experimental import pallas as pl
from jax.experimental.pallas import tpu as pltpu
from jax.sharding import PartitionSpec as P

HD = 128
EPSILON = 1e-06
ROPE_BASE = 10000.0
MASKED = -1e30
GROUP = ("fsdp", "ctx")
BF = jnp.bfloat16
F32 = jnp.float32
VMEM_LIMIT = 56 * 1024 * 1024


def normalize(tensor, gain_vec):
    inverse = lax.rsqrt(jnp.mean(tensor * tensor, axis=-1, keepdims=True) + EPSILON)
    normed = tensor * inverse
    return (normed, inverse, normed * gain_vec)


def norm_back(grad_in, normed, inverse, gain_vec):
    scaled = grad_in * gain_vec
    inner_mean = jnp.mean(scaled * normed, axis=-1, keepdims=True)
    return (inverse * (scaled - normed * inner_mean), jnp.sum(grad_in * normed, axis=0))


def dot(a, b, ca, cb):
    return lax.dot_general(a, b, (((ca,), (cb,)), ((), ())), preferred_element_type=F32)


def turn(x, cos, sin):
    return x * cos + pltpu.roll(x, HD // 2, 1) * sin


def swap(x, mask, axes, count):
    return lax.ppermute(x, axes, [(i, i ^ mask) for i in range(count)])


def bits_of(count):
    return count.bit_length() - 1


def flip(value, mask):
    step = 1
    while step <= mask:
        if mask & step:
            value = value + step - 2 * step * ((value // step) % 2)
        step *= 2
    return value


def peer(ctx_count, mask):
    return {
        "fsdp": flip(lax.axis_index("fsdp"), mask // ctx_count),
        "ctx": flip(lax.axis_index("ctx"), mask % ctx_count),
    }


def greet(ctx_count, masks):
    barrier = pltpu.get_barrier_semaphore()
    for mask in masks:
        pl.semaphore_signal(
            barrier, inc=1, device_id=peer(ctx_count, mask), device_id_type=pl.DeviceIdType.MESH
        )
    pl.semaphore_wait(barrier, len(masks))


def window(ref, rows, cols):
    if cols is None:
        return ref.at[pl.ds(rows[0], rows[1])]
    return ref.at[pl.ds(rows[0], rows[1]), pl.ds(cols[0], cols[1])]


class Moves:
    def __init__(self, ctx_count, moves, arrays, send, recv, bounces=()):
        self.moves = moves
        self.onward = {}
        bounces = list(bounces)
        self.copies = []
        self.place = {m[1]: i for i, m in enumerate(moves)}
        self.started, self.came = set(), set()
        for i, (source, target, mask, _) in enumerate(moves):
            src = window(arrays[source[0]], *source[1:])
            dst = window(arrays[target[0]], *target[1:])
            if mask:
                copy = pltpu.make_async_remote_copy(
                    src_ref=src,
                    dst_ref=dst,
                    send_sem=send.at[i],
                    recv_sem=recv.at[i],
                    device_id=peer(ctx_count, mask),
                    device_id_type=pl.DeviceIdType.MESH,
                )
            else:
                bounce = bounces.pop(0)
                copy = pltpu.make_async_copy(src, bounce, recv.at[i])
                self.onward[i] = pltpu.make_async_copy(bounce, dst, send.at[i])
            self.copies.append(copy)

    def start(self, i):
        if i not in self.started:
            self.started.add(i)
            self.copies[i].start()

    def begin(self, count=None):
        for i, move in enumerate(self.moves[:count]):
            if not move[3]:
                self.start(i)

    def await_one(self, i):
        if i not in self.came:
            self.came.add(i)
            if i in self.onward:
                self.copies[i].wait()
                self.onward[i].start()
            else:
                self.copies[i].wait_recv()

    def settle(self, count):
        for i in range(count):
            if i in self.onward:
                self.await_one(i)
        for i in range(count):
            for target in self.moves[i][3]:
                self.await_one(self.place[target])
            self.start(i)
        for i in range(count):
            self.await_one(i)

    def finish(self):
        self.settle(len(self.moves))
        for i in range(len(self.moves)):
            if i in self.onward:
                self.onward[i].wait()
            else:
                self.copies[i].wait_send()


def masks_of(moves):
    return sorted({move[2] for move in moves if move[2]})


def move_kernel(ctx_count, moves, names_in, names_out, *refs):
    count = len(names_in) + len(names_out)
    refs, (send, recv, *bounces) = refs[:count], refs[count:]
    arrays = dict(zip(names_in, refs))
    arrays.update(zip(names_out, refs[len(names_in) :]))
    greet(ctx_count, masks_of(moves))
    run = Moves(ctx_count, moves, arrays, send, recv, bounces)
    run.begin()
    run.finish()


def move(name, number, ctx_count, moves, given, made):
    names_in = [n for n in given if n not in made] + [n for n in given if n in made]
    plain = [n for n in names_in if n not in made]
    names_out = list(made)
    any_spec = pl.BlockSpec(memory_space=pl.ANY)
    bounces = [
        pltpu.VMEM((source[1][1], (source[2] or (0, given[source[0]].shape[1]))[1]), BF)
        for source, _, mask, _ in moves
        if not mask
    ]
    return dict(
        zip(
            names_out,
            pl.pallas_call(
                functools.partial(
                    move_kernel,
                    ctx_count,
                    moves,
                    plain + ["old_" + n for n in names_in[len(plain) :]],
                    names_out,
                ),
                out_shape=[jax.ShapeDtypeStruct(shape, BF) for shape in made.values()],
                in_specs=[any_spec] * len(names_in),
                out_specs=[any_spec] * len(names_out),
                input_output_aliases={
                    names_in.index(n): names_out.index(n) for n in names_out if n in given
                },
                scratch_shapes=[pltpu.SemaphoreType.DMA((len(moves),))] * 2 + bounces,
                compiler_params=pltpu.CompilerParams(
                    collective_id=number, has_side_effects=True, vmem_limit_bytes=VMEM_LIMIT
                ),
                name=name,
            )(*[given[n] for n in names_in]),
        )
    )


def reduce_kernel(ctx_count, bits, part, pieces, grad_ref, out_ref, sums, got, send, recv):
    count, wide = grad_ref.shape[0] // part, grad_ref.shape[1]
    greet(ctx_count, sorted(1 << b for b in bits))
    half = wide // 2
    size = half // pieces
    number = [0]

    def copy(source, mask, block, cols):
        i = number[0]
        number[0] += 1
        rows = pl.ds(block * part, part)
        return pltpu.make_async_remote_copy(
            src_ref=source.at[rows, cols],
            dst_ref=got.at[rows, cols],
            send_sem=send.at[i],
            recv_sem=recv.at[i],
            device_id=peer(ctx_count, mask),
            device_id_type=pl.DeviceIdType.MESH,
        )

    lanes = []
    for piece in range(pieces):
        for side in range(2):
            order = bits if side == 0 else bits[::-1]
            cols = pl.ds(side * half + piece * size, size)
            lanes.append((order, cols))
    sent = []
    flying = []
    for order, cols in lanes:
        at = bits.index(order[0])
        copies = {j: copy(grad_ref, 1 << order[0], j, cols) for j in range(count) if j >> at & 1}
        for c in copies.values():
            c.start()
        flying.append(copies)
        sent += list(copies.values())
    left = [list(range(count)) for _ in lanes]
    for step in range(len(bits)):
        last = step == len(bits) - 1
        for n, (order, cols) in enumerate(lanes):
            at = bits.index(order[step])
            left[n] = [j for j in left[n] if not j >> at & 1]
            for j in left[n]:
                flying[n][j | 1 << at].wait_recv()
                rows = pl.ds(j * part, part)
                mine = grad_ref if step == 0 else sums
                total = mine[rows, cols].astype(F32) + got[
                    pl.ds((j | 1 << at) * part, part), cols
                ].astype(F32)
                if last:
                    out_ref[:, cols] = total
                else:
                    sums[rows, cols] = total.astype(BF)
            if not last:
                following = bits.index(order[step + 1])
                copies = {
                    j: copy(sums, 1 << order[step + 1], j, cols)
                    for j in left[n]
                    if j >> following & 1
                }
                for c in copies.values():
                    c.start()
                flying[n] = copies
                sent += list(copies.values())
    for c in sent:
        c.wait_send()


def reduce_grads(number, ctx_count, bits, part, grad):
    pieces = 4
    copies = 2 * pieces * (grad.shape[0] // part)
    full = pl.BlockSpec(memory_space=pltpu.VMEM)
    return pl.pallas_call(
        functools.partial(reduce_kernel, ctx_count, bits, part, pieces),
        out_shape=jax.ShapeDtypeStruct((part, grad.shape[1]), F32),
        in_specs=[full],
        out_specs=full,
        scratch_shapes=[pltpu.VMEM(grad.shape, BF)] * 2
        + [pltpu.SemaphoreType.DMA((copies,))] * 2,
        compiler_params=pltpu.CompilerParams(
            collective_id=number, has_side_effects=True, vmem_limit_bytes=VMEM_LIMIT
        ),
        name="reduce_grads",
    )(grad)


def project_kernel(h_ref, w_ref, cos_ref, sin_ref, out_ref):
    y = jnp.dot(h_ref[...], w_ref[...], preferred_element_type=F32)
    for head in range(y.shape[1] // HD):
        cols = slice(head * HD, (head + 1) * HD)
        out_ref[:, cols] = turn(y[:, cols], cos_ref[0], sin_ref[0]).astype(BF)


def project(hidden, weight, cos, sin, plain, cols, count):
    rows, width = hidden.shape
    tables = [
        jnp.stack([cos, jnp.ones_like(cos)]),
        jnp.stack([sin, jnp.zeros_like(sin)]),
    ]
    table_spec = pl.BlockSpec((1, rows, HD), lambda p: (p // plain, 0, 0))
    return pl.pallas_call(
        project_kernel,
        out_shape=jax.ShapeDtypeStruct((rows, count * cols), BF),
        grid=(count,),
        in_specs=[
            pl.BlockSpec((rows, width), lambda p: (0, 0)),
            pl.BlockSpec((width, cols), lambda p: (0, p)),
            table_spec,
            table_spec,
        ],
        out_specs=pl.BlockSpec((rows, cols), lambda p: (0, p)),
        compiler_params=pltpu.CompilerParams(vmem_limit_bytes=VMEM_LIMIT),
        name="project",
    )(hidden, weight, *tables)


def head_cols(index):
    return pl.ds(pl.multiple_of(index * HD, HD), HD)


def scores_of(place, queries, keys, segq, idxq, segk, idxk):
    slots = dot(place, queries, 1, 0).astype(BF)
    scores = dot(slots, keys, 1, 1) * (HD**-0.5)
    allowed = (segq == segk) & (idxk <= idxq)
    scores = jnp.where(allowed, scores, MASKED)
    top = jnp.max(scores, axis=-1, keepdims=True)
    exps = jnp.exp(scores - top)
    total = jnp.sum(exps, axis=-1, keepdims=True)
    return slots, exps, 1.0 / total


def attend_kernel(
    ctx_count,
    moves,
    first_moves,
    names_in,
    names_out,
    heads,
    qkv_ref,
    place_ref,
    segq_ref,
    idxq_ref,
    gate_ref,
    segk_ref,
    idxk_ref,
    *refs,
):
    experts, _, rows = place_ref.shape
    given, refs = refs[: len(names_in)], refs[len(names_in) :]
    mixed_ref, kv_ref = refs[:2]
    made, (send, recv) = refs[2:-2], refs[-2:]
    arrays = {"qkv": qkv_ref, "kv": kv_ref, **dict(zip(names_in, given)), **dict(zip(names_out, made))}
    greet(ctx_count, masks_of(moves))
    run = Moves(ctx_count, moves, arrays, send, recv)
    run.begin(first_moves)
    kv_ref[:rows] = qkv_ref[:, experts * heads * HD :]
    run.settle(first_moves)
    run.begin()

    def step(i, carry):
        h, e = i // experts, i % experts
        cols = head_cols(e * heads + h)
        place = place_ref[e]
        _, exps, inv = scores_of(
            place,
            qkv_ref[:, cols],
            kv_ref[:, head_cols(h)],
            segq_ref[e],
            idxq_ref[e],
            segk_ref[...],
            idxk_ref[...],
        )
        attn = dot(exps.astype(BF), kv_ref[:, head_cols(heads + h)], 1, 0) * inv
        mixed = (attn * gate_ref[e]).astype(BF)
        mixed_ref[:, cols] = dot(place, mixed, 0, 0).astype(BF)
        return carry

    lax.fori_loop(0, heads * experts, step, 0)
    run.finish()


def attend(number, ctx_count, heads, moves, given, made, qkv, place, *slots_and_keys):
    experts, _, rows = place.shape
    wide = heads * HD
    kv_moves = []
    order = [0]
    bits = range(bits_of(ctx_count))[::-1]
    for bit in bits:
        for at in range(len(order)):
            target = ("kv", ((at + len(order)) * rows, rows), None)
            if at:
                source = ("kv", (at * rows, rows), None)
                kv_moves.append((source, target, 1 << bit, (source,)))
            else:
                source = ("qkv", (0, rows), (experts * wide, 2 * wide))
                kv_moves.append((source, target, 1 << bit, ()))
        order = order + order
    names_in = [n for n in given if n not in made] + [n for n in given if n in made]
    names_out = list(made)
    any_spec = pl.BlockSpec(memory_space=pl.ANY)
    full = pl.BlockSpec(memory_space=pltpu.VMEM)
    moves = kv_moves + moves
    before = 2 + len(slots_and_keys)
    mixed, kv, *rest = pl.pallas_call(
        functools.partial(
            attend_kernel,
            ctx_count,
            moves,
            len(kv_moves),
            [n if n not in made else "old_" + n for n in names_in],
            names_out,
            heads,
        ),
        out_shape=[
            jax.ShapeDtypeStruct((rows, experts * wide), BF),
            jax.ShapeDtypeStruct((ctx_count * rows, 2 * wide), BF),
        ]
        + [jax.ShapeDtypeStruct(shape, BF) for shape in made.values()],
        in_specs=[full] * before + [any_spec] * len(names_in),
        out_specs=[full] * 2 + [any_spec] * len(names_out),
        input_output_aliases={
            before + names_in.index(n): 2 + names_out.index(n) for n in names_out if n in given
        },
        scratch_shapes=[pltpu.SemaphoreType.DMA((len(moves),))] * 2,
        compiler_params=pltpu.CompilerParams(
            collective_id=number, has_side_effects=True, vmem_limit_bytes=VMEM_LIMIT
        ),
        name="attend",
    )(qkv, place, *slots_and_keys, *[given[n] for n in names_in])
    return mixed, kv, dict(zip(names_out, rest))


def attend_back_kernel(
    ctx_count,
    moves,
    names_in,
    names_out,
    heads,
    qkv_ref,
    kv_ref,
    place_ref,
    segq_ref,
    idxq_ref,
    segk_ref,
    idxk_ref,
    grad_ref,
    cos_ref,
    sin_ref,
    *refs,
):
    experts, _, rows = place_ref.shape
    keys = kv_ref.shape[0]
    given, refs = refs[: len(names_in)], refs[len(names_in) :]
    out_ref = refs[0]
    made, (dk_acc, dv_acc, total, got, send, recv, pass_send, pass_recv) = refs[1:-8], refs[-8:]
    arrays = {**dict(zip(names_in, given)), **dict(zip(names_out, made))}
    bits = range(bits_of(ctx_count))
    greet(ctx_count, sorted({*masks_of(moves), *[1 << b for b in bits]}))
    run = Moves(ctx_count, moves, arrays, send, recv)
    run.begin()

    def head_copy(h, bit):
        size = keys >> (bit + 1)
        i = h * len(bits) + bit
        return pltpu.make_async_remote_copy(
            src_ref=total.at[h, pl.ds(size, size)],
            dst_ref=got.at[h, pl.ds(size, size)],
            send_sem=pass_send.at[i],
            recv_sem=pass_recv.at[i],
            device_id=peer(ctx_count, 1 << bit),
            device_id_type=pl.DeviceIdType.MESH,
        )

    def head_sum(h, bit):
        size = keys >> (bit + 1)
        head_copy(h, bit).wait_recv()
        mine = total[h, :size].astype(F32) + got[h, size : 2 * size].astype(F32)
        mine = mine.astype(BF)
        if bit + 1 < len(bits):
            total[h, :size] = mine
            head_copy(h, bit + 1).start()
        else:
            at = experts * heads * HD
            out_ref[:, at + h * HD : at + (h + 1) * HD] = mine[:, :HD]
            at += heads * HD
            out_ref[:, at + h * HD : at + (h + 1) * HD] = mine[:, HD:]

    for h in range(heads):
        dk_acc[...] = jnp.zeros_like(dk_acc)
        dv_acc[...] = jnp.zeros_like(dv_acc)

        def step(e, carry, h=h):
            cols = head_cols(e * heads + h)
            place = place_ref[e]
            k, v = kv_ref[:, h * HD : (h + 1) * HD], kv_ref[:, (heads + h) * HD : (heads + h + 1) * HD]
            slots, exps, inv = scores_of(
                place, qkv_ref[:, cols], k, segq_ref[e], idxq_ref[e], segk_ref[...], idxk_ref[...]
            )
            attn = dot(exps.astype(BF), v, 1, 0) * inv
            probs = exps * inv
            grad = dot(place, grad_ref[:, cols], 1, 0)
            delta = jnp.sum(grad * attn, axis=-1, keepdims=True)
            grad = grad.astype(BF)
            dv_acc[...] += dot(probs.astype(BF), grad, 0, 0)
            grad_probs = dot(grad, v, 1, 1)
            grad_scores = (probs * (grad_probs - delta)).astype(BF)
            dq = dot(grad_scores, k, 1, 0) * (HD**-0.5)
            dk_acc[...] += dot(grad_scores, slots, 0, 0) * (HD**-0.5)
            top = dq.astype(BF)
            low = (dq - top.astype(F32)).astype(BF)
            back = dot(place, top, 0, 0) + dot(place, low, 0, 0)
            out_ref[:, cols] = turn(back, cos_ref[:rows], -sin_ref[:rows]).astype(BF)
            return carry

        lax.fori_loop(0, experts, step, 0)
        total[h, :, :HD] = turn(dk_acc[...], cos_ref[...], -sin_ref[...]).astype(BF)
        total[h, :, HD:] = dv_acc[...].astype(BF)
        head_copy(h, 0).start()
        for bit in bits:
            if h - 1 - bit >= 0:
                head_sum(h - 1 - bit, bit)
    for h in range(heads, heads + len(bits)):
        for bit in bits:
            if 0 <= h - 1 - bit < heads:
                head_sum(h - 1 - bit, bit)
    for h in range(heads):
        for bit in bits:
            head_copy(h, bit).wait_send()
    run.finish()


def attend_back(number, ctx_count, heads, moves, given, made, qkv, kv, place, *others):
    rows, keys = qkv.shape[0], kv.shape[0]
    any_spec = pl.BlockSpec(memory_space=pl.ANY)
    full = pl.BlockSpec(memory_space=pltpu.VMEM)
    passes = heads * bits_of(ctx_count)
    out, *rest = pl.pallas_call(
        functools.partial(attend_back_kernel, ctx_count, moves, list(given), list(made), heads),
        out_shape=[jax.ShapeDtypeStruct(qkv.shape, BF)]
        + [jax.ShapeDtypeStruct(shape, BF) for shape in made.values()],
        in_specs=[full] * (3 + len(others)) + [any_spec] * len(given),
        out_specs=[full] + [any_spec] * len(made),
        scratch_shapes=[pltpu.VMEM((keys, HD), F32)] * 2
        + [pltpu.VMEM((heads, keys, 2 * HD), BF)] * 2
        + [pltpu.SemaphoreType.DMA((max(1, len(moves)),))] * 2
        + [pltpu.SemaphoreType.DMA((passes,))] * 2,
        compiler_params=pltpu.CompilerParams(
            collective_id=number, has_side_effects=True, vmem_limit_bytes=VMEM_LIMIT
        ),
        name="attend_back",
    )(qkv, kv, place, *others, *given.values())
    return out, dict(zip(made, rest))


def spread_kernel(experts, me_ref, *refs):
    blocks, (in_ref, down_ref) = refs[:experts], refs[experts:]
    units = down_ref.shape[2]
    for m in range(experts):

        @pl.when(me_ref[0] == m)
        def _():
            for e in range(experts):
                block = blocks[e ^ m]
                for c in range(2):
                    in_ref[:, e, c, :] = block[:, c * units : (c + 1) * units].astype(F32)
                down_ref[:, e, :] = block[:, 2 * units :].astype(F32)


def spread_grads(blocks, me, in_shape, down_shape):
    experts = len(blocks)
    step = min(32, in_shape[0])
    return pl.pallas_call(
        functools.partial(spread_kernel, experts),
        grid_spec=pltpu.PrefetchScalarGridSpec(
            num_scalar_prefetch=1,
            grid=(in_shape[0] // step,),
            in_specs=[pl.BlockSpec((step, blocks[0].shape[1]), lambda i, m: (i, 0))] * experts,
            out_specs=[
                pl.BlockSpec((step, *in_shape[1:]), lambda i, m: (i, 0, 0, 0)),
                pl.BlockSpec((step, *down_shape[1:]), lambda i, m: (i, 0, 0)),
            ],
        ),
        out_shape=[
            jax.ShapeDtypeStruct(in_shape, F32),
            jax.ShapeDtypeStruct(down_shape, F32),
        ],
        compiler_params=pltpu.CompilerParams(vmem_limit_bytes=VMEM_LIMIT),
        name="spread_grads",
    )(me.astype(jnp.int32).reshape(1), *blocks)


def places(routes, gates, experts, cap, room):
    rows = routes.shape[0]
    named = routes[:, :, None] == jnp.arange(experts, dtype=jnp.int32)[None, None, :]
    member = jnp.any(named, axis=1)
    gate = jnp.sum(jnp.where(named, gates[:, :, None], 0.0), axis=1)
    token = jnp.arange(rows, dtype=jnp.int32)
    earlier = (token[None, :] < token[:, None]).astype(BF)
    rank = dot(earlier, member.astype(BF), 1, 0).astype(jnp.int32)
    slot = jnp.where(member, rank, -1).T
    taken = slot[:, None, :] == jnp.arange(room, dtype=jnp.int32)[None, :, None]
    return taken, gate


def slot_sum(taken, values):
    return jnp.sum(jnp.where(taken, values, 0), axis=-1, keepdims=True)


def layer(
    counts,
    tokens,
    gain_attn,
    gain_mlp,
    w_kv,
    w_query,
    w_out_attn,
    w_in,
    w_down,
    segments,
    attn_routes,
    attn_gates,
    mlp_routes,
    mlp_gates,
    cotangent,
):
    fsdp_count, ctx_count, tp_count = counts
    group = fsdp_count * ctx_count
    me = lax.axis_index(GROUP)
    ctx_me = lax.axis_index("ctx")
    rows, width = tokens.shape[1:]
    cap = 9 * rows // 16
    room = -(-cap // 16) * 16
    part = width // group
    attn_experts = w_query.shape[1]
    experts = w_in.shape[1]
    share = group // experts
    expert_me = me // share
    hidden_units = w_down.shape[2]
    head_width = w_kv.shape[2]

    def piece(x, index, size=part, axis=1):
        return lax.dynamic_slice_in_dim(x, index * size, size, axis)

    def exchange(x, mask):
        return swap(x, mask, GROUP, group)

    def after(x, *events):
        return lax.optimization_barrier((x, *events))[0]

    def relative(x):
        return jnp.concatenate([piece(x, me ^ j) for j in range(group)], axis=1)

    high, second = group // 2, group // 4

    qkv_wide = (attn_experts + 2) * head_width
    attn_own = jnp.concatenate(
        [w_query.reshape(part, -1), w_kv.reshape(part, -1), w_out_attn.reshape(part, -1)], axis=1
    )
    attn_wide = attn_own.shape[1]
    gain_own = jnp.pad(
        jnp.concatenate([gain_attn, gain_mlp])[None, :], ((0, 15), (0, 0))
    )
    far_x, far_y = exchange(attn_own, high), exchange(attn_own, second)

    seg_row = segments[0]
    seq_total = seg_row.shape[0]
    ctx_bits = list(range(bits_of(ctx_count)))[::-1]
    key_order = [0]
    for bit in ctx_bits:
        key_order = key_order + [j | (1 << bit) for j in key_order]
    key_seg = jnp.concatenate([piece(seg_row, ctx_me ^ j, rows, 0) for j in key_order])
    key_idx = jnp.concatenate(
        [(ctx_me ^ j) * rows + jnp.arange(rows, dtype=jnp.int32) for j in key_order]
    )
    place_idx = jnp.arange(seq_total, dtype=jnp.int32)
    pos = jnp.sum(
        (seg_row[None, :] == key_seg[:, None]) & (place_idx[None, :] < key_idx[:, None]),
        axis=1,
        dtype=jnp.int32,
    ).astype(F32)
    frequency = ROPE_BASE ** (-(jnp.arange(HD // 2, dtype=F32) * 2.0) / HD)
    angles = pos[:, None] * frequency[None, :]
    cos_half, sin_half = jnp.cos(angles), jnp.sin(angles)
    cos = jnp.concatenate([cos_half, cos_half], axis=1)
    sin = jnp.concatenate([-sin_half, sin_half], axis=1)
    taken_attn, gate_attn = places(attn_routes[0], attn_gates[0], attn_experts, cap, room)
    place_attn = taken_attn.astype(BF)
    own_seg, own_idx = key_seg[:rows], key_idx[:rows]
    filled = jnp.any(taken_attn, axis=-1, keepdims=True)
    slot_seg = jnp.where(filled, slot_sum(taken_attn, own_seg), own_seg[0])
    slot_idx = jnp.where(filled, slot_sum(taken_attn, own_idx), own_idx[0])
    slot_gate = slot_sum(taken_attn, gate_attn.T[:, None, :])
    taken_mlp, gate_mlp = places(mlp_routes[0], mlp_gates[0], experts, cap, room)
    mine_first = [expert_me ^ k for k in range(experts)]
    place_mlp = jnp.concatenate([piece(taken_mlp, e, 1, 0) for e in mine_first]).astype(BF)
    inputs = relative(tokens[0]).astype(F32)
    grad_out = relative(cotangent[0])

    def expert_rows(k):
        in_rows = piece(w_in, expert_me ^ k, 1, 1).reshape(part, 2 * hidden_units)
        down_rows = piece(w_down, expert_me ^ k, 1, 1).reshape(part, hidden_units)
        return jnp.concatenate([in_rows, down_rows], axis=1)

    to_send = [expert_rows(k) for k in range(experts)]
    in_cols, down_cols = (0, 2 * hidden_units), (2 * hidden_units, hidden_units)
    weight_shapes = {"in": (width, 2 * hidden_units), "down": (width, hidden_units)}

    def weight_moves(k, first, size):
        moves = []
        for name, cols in (("in", in_cols), ("down", down_cols)):
            base = k * share * part + first
            source = (f"send{k}", (first, size), cols)
            landed = (name, (base, size), None)
            moves.append((source, landed, k * share, ()))
            for t in range(1, share):
                target = (name, (base + t * part, size), None)
                if k:
                    moves.append((landed, target, t, (landed,)))
                else:
                    moves.append((source, target, t, ()))
        return moves

    def many_weight_moves(cuts):
        return [m for cut in cuts for m in weight_moves(*cut)]

    near = [k for k in range(1, experts) if k & (k - 1) == 0]
    far = [k for k in range(1, experts) if k & (k - 1)]
    half_part = part // 2

    (attn_own, far_x, far_y, gain_own), to_send, tables = lax.optimization_barrier(
        (
            (attn_own, far_x, far_y, gain_own),
            to_send,
            (cos, sin, place_attn, slot_seg, slot_idx, slot_gate, place_mlp),
        )
    )
    cos, sin, place_attn, slot_seg, slot_idx, slot_gate, place_mlp = tables
    quarter = part // 4
    moves = []
    held = {0: [("own", 0, part, ())], high: [("far_x", 0, part, ())], second: [("far_y", 0, part, ())]}
    held[high | second] = []
    for i in (0, 2, 1, 3):
        source, mask = (("far_x", second), ("far_y", high))[i // 2]
        target = ("full", ((high | second) * part + i * quarter, quarter), None)
        moves.append(((source, (i * quarter, quarter), None), target, mask, ()))
        held[high | second].append(("full", i * quarter, quarter, (target,)))
    for j in (0, high, second):
        name = held[j][0][0]
        moves.append(((name, (0, part), None), ("full", (j * part, part), None), 0, ()))
    for j in range(group):
        moves.append((("gain_own", (0, 16), None), ("gains", (j * 16, 16), None), j, ()))
    moves += weight_moves(0, 0, part)
    for bit in range(bits_of(group) - 2)[::-1]:
        for j in list(held):
            there = []
            for name, at, size, needs in held[j]:
                source = (name, (at + j * part if name == "full" else at, size), None)
                target = ("full", ((j | 1 << bit) * part + at, size), None)
                moves.append((source, target, 1 << bit, needs))
                there.append(("full", at, size, (target,)))
            held[j | 1 << bit] = there
    made = move(
        "gather",
        1,
        ctx_count,
        moves,
        {"own": attn_own, "far_x": far_x, "far_y": far_y, "gain_own": gain_own, "send0": to_send[0]},
        {"full": (width, attn_wide), "gains": (16 * group, 2 * part), **weight_shapes},
    )
    attn_full, weights = made["full"], {n: made[n] for n in weight_shapes}
    gains = made["gains"].reshape(group, 16, 2 * part)[:, 0].astype(F32)
    gain_one, gain_two = gains[:, :part].reshape(1, width), gains[:, part:].reshape(1, width)
    qkv_full, out_full = attn_full[:, :qkv_wide], attn_full[:, qkv_wide:]
    normed_one, inverse_one, pre_one = normalize(inputs, gain_one)
    hidden_one = pre_one.astype(BF)
    qkv = project(hidden_one, attn_full, cos[:rows], sin[:rows], attn_experts + 1, head_width, attn_experts + 2)
    key_row = (key_seg[None, :], key_idx[None, :])
    heads = head_width // HD
    cuts = [(k, 0, half_part) for k in near]
    mixed, kv, weights = attend(
        2,
        ctx_count,
        heads,
        many_weight_moves(cuts),
        {**{f"send{k}": to_send[k] for k in near}, **weights},
        weight_shapes,
        qkv,
        place_attn,
        slot_seg,
        slot_idx,
        slot_gate,
        *key_row,
    )

    def turned(x, k):
        wide = share * part
        return jnp.concatenate(
            [x[:, (i ^ k) * wide : ((i ^ k) + 1) * wide] for i in range(experts)], axis=1
        )

    def pick(k, x):
        return dot(place_mlp[k], x, 1, 0).astype(BF)

    run = width // tp_count
    tp_me = lax.axis_index("tp")
    gate_high = gate_mlp.astype(BF)
    gate_low = (gate_mlp - gate_high.astype(F32)).astype(BF)
    gate_ride = jnp.pad(
        jnp.concatenate([gate_high, gate_low], axis=1), ((0, 0), (0, HD - 2 * experts))
    )
    grad_got = []
    for k in range(experts):
        sent = jnp.concatenate([piece(grad_out, tp_me ^ k, run), gate_ride], axis=1)
        slots = pick(k, sent)
        grad_got.append(exchange(slots, k * share) if k else slots)
    grad_got = jnp.concatenate(grad_got, axis=0)
    own_gate = jnp.tile(jnp.arange(experts) == expert_me, 2)
    slot_weight = jnp.sum(
        jnp.where(own_gate[None, :], grad_got[:, run : run + 2 * experts].astype(F32), 0.0),
        axis=1,
        keepdims=True,
    )
    grad_slots = lax.all_gather(grad_got[:, :run], "tp", axis=1, tiled=True)

    def send_weights(name, number, cuts, weights, slots=None):
        moves, given, made_shapes = [], {f"send{k}": to_send[k] for k, _, _ in cuts}, dict(weight_shapes)
        if slots is not None:
            made_shapes["slots"] = (experts * room, width)
            for k, x in enumerate(slots):
                given[f"slots{k}"] = x
                target = ("slots", (k * room, room), None)
                moves.append(((f"slots{k}", (0, room), None), target, k * share, ()))
        moves += many_weight_moves(cuts)
        made = move(name, number, ctx_count, moves, {**given, **weights}, made_shapes)
        return {n: made[n] for n in weight_shapes}, made.get("slots")

    branch = dot(mixed, out_full, 1, 1).astype(BF)
    branch_sum = lax.psum(branch, "tp")
    cuts = [(k, half_part, part - half_part) for k in near] + [(k, 0, half_part) for k in far]
    to_send, weights, _ = lax.optimization_barrier((to_send, weights, branch))
    weights, _ = send_weights("weights_two", 3, cuts, weights)
    resid = inputs + branch_sum.astype(F32)
    normed_two, inverse_two, pre_two = normalize(resid, gain_two)
    hidden_two = pre_two.astype(BF)
    slots = [pick(0, hidden_two)] + [turned(pick(k, hidden_two), k) for k in range(1, experts)]
    cuts = [(k, half_part, part - half_part) for k in far]
    weights, two_slots = send_weights("dispatch", 4, cuts, weights, slots)
    in_full, down_full = weights["in"], weights["down"]

    def send_back(x):
        slots = x.reshape(experts, room, width)
        return [slots[0]] + [exchange(slots[k], k * share) for k in range(1, experts)]

    def gathered_rows(got):
        got = [got[0]] + [turned(got[k], k) for k in range(1, experts)]
        return jnp.einsum(
            "kct,kcd->td", place_mlp, jnp.stack(got), preferred_element_type=F32
        ).astype(BF)

    gate_up = dot(two_slots, in_full, 1, 0)
    gate_part, up_part = gate_up[:, :hidden_units], gate_up[:, hidden_units:]
    sigmoid_gate = jax.nn.sigmoid(gate_part)
    silu_gate = gate_part * sigmoid_gate
    active = (silu_gate * up_part * slot_weight).astype(BF)
    mlp_slots = dot(active, down_full, 1, 1).astype(BF)
    mlp_back = send_back(mlp_slots)
    grad_active = dot(after(grad_slots, mlp_slots), down_full, 1, 0)
    scaled = grad_active * slot_weight
    grad_gate = scaled * up_part * sigmoid_gate * (1.0 + gate_part * (1.0 - sigmoid_gate))
    grad_up = scaled * silu_gate
    grad_gu = jnp.concatenate([grad_gate, grad_up], axis=1).astype(BF)
    back_two_slots = dot(grad_gu, in_full, 1, 1).astype(BF)
    two_back = send_back(after(back_two_slots, *mlp_back))

    def for_share(x, t):
        return jnp.concatenate(
            [x[:, (k * share + t) * part : (k * share + t + 1) * part] for k in range(experts)],
            axis=1,
        )

    def every_share(x, cut):
        got = [for_share(x, 0) if cut else x]
        for t in range(1, share):
            got.append(exchange(for_share(x, t) if cut else x, t))
        return jnp.concatenate(got, axis=0)

    grad_gu_late = after(grad_gu, back_two_slots)
    grad_in_w = dot(every_share(two_slots, True), every_share(grad_gu_late, False), 0, 0)
    grad_down_w = dot(every_share(grad_slots, True), every_share(active, False), 0, 0)
    expert_grads = jnp.concatenate([grad_in_w.astype(BF), grad_down_w.astype(BF)], axis=1)
    two_back = after(two_back, expert_grads)
    back_two = lax.psum(gathered_rows(two_back), "tp").astype(F32)
    grads_got = {0: expert_grads[:part]}

    def grad_moves(ks):
        return [
            (("grads", (k * part, part), None), (f"got{k}", (0, part), None), k * share, ())
            for k in ks
        ], {f"got{k}": (part, expert_grads.shape[1]) for k in ks}

    moves, made_shapes = grad_moves(near)
    made = move("grads_near", 5, ctx_count, moves, {"grads": expert_grads}, made_shapes)
    grads_got.update({k: made[f"got{k}"] for k in near})
    grads_near = [grads_got[k] for k in near]

    grad_resid_norm, gain_two_grad = norm_back(back_two, normed_two, inverse_two, gain_two)
    grad_resid = grad_out.astype(F32) + grad_resid_norm
    grad_branch = grad_resid.astype(BF)
    grad_mixed = dot(after(grad_branch, *grads_near), out_full, 1, 0)
    gate_wide = jnp.repeat(gate_attn, head_width, axis=1)
    grad_attn = (grad_mixed * gate_wide).astype(BF)
    moves, made_shapes = grad_moves(far)
    grad_qkv, made = attend_back(
        6,
        ctx_count,
        heads,
        moves,
        {"grads": expert_grads},
        made_shapes,
        qkv,
        kv,
        place_attn,
        slot_seg,
        slot_idx,
        *key_row,
        grad_attn,
        cos,
        sin,
    )
    grads_got.update({k: made[f"got{k}"] for k in far})
    mlp_total = lax.psum(gathered_rows(after(mlp_back, grad_attn)), "tp").astype(F32)
    back_one_part = dot(grad_qkv, qkv_full, 1, 1)
    back_one = lax.psum(back_one_part.astype(BF), "tp").astype(F32)
    grad_input_norm, gain_one_grad = norm_back(back_one, normed_one, inverse_one, gain_one)
    grad_tokens = relative((grad_resid + grad_input_norm).astype(BF))

    output = relative((resid + mlp_total).astype(BF))

    def both(x):
        return jnp.concatenate([x, exchange(x, 1)], axis=0)

    def both_cut(x):
        sides = [
            jnp.concatenate([x[:, j * part : (j + 1) * part] for j in range(side, group, 2)], axis=1)
            for side in range(2)
        ]
        return jnp.concatenate([sides[0], exchange(sides[1], 1)], axis=0)

    def reduced(x, bits, kind=BF):
        axes = sorted(bits)[::-1]
        x = x.reshape((2,) * len(bits) + (-1, x.shape[1]))
        for bit in bits:
            at = axes.index(bit)
            keep = lax.index_in_dim(x, 0, at, False).astype(F32)
            got = exchange(lax.index_in_dim(x, 1, at, False), 1 << bit).astype(F32)
            axes.remove(bit)
            x = keep + got
            if axes:
                x = x.astype(kind)
        return x

    upper = list(range(1, bits_of(group)))

    grad_outw = dot(both_cut(grad_branch), both(mixed), 0, 0).astype(BF)
    grad_qkvw = dot(both_cut(hidden_one), both(grad_qkv), 0, 0).astype(BF)
    grad_attnw = jnp.concatenate([grad_qkvw, grad_outw], axis=1)
    grad_attnw = reduce_grads(7, ctx_count, upper, part, grad_attnw)

    def planes(first, count):
        cut = grad_attnw[:, first * head_width : (first + count) * head_width]
        return cut.reshape(part, count, head_width)

    def gain_sum(x):
        return reduced(x.reshape(width, 1), [0] + upper, F32).reshape(part)

    return (
        output[None],
        grad_tokens[None],
        gain_sum(gain_one_grad),
        gain_sum(gain_two_grad),
        planes(attn_experts, 2),
        planes(0, attn_experts),
        planes(attn_experts + 2, attn_experts),
        *spread_grads([grads_got[k] for k in range(experts)], expert_me, w_in.shape, w_down.shape),
    )


def solution(mesh):
    rows = P("fsdp", "ctx", None)
    weight = P(GROUP, None, "tp")
    weight_in = P(GROUP, None, None, "tp")
    return jax.shard_map(
        functools.partial(layer, tuple(mesh.shape[a] for a in ("fsdp", "ctx", "tp"))),
        mesh=mesh,
        in_specs=(
            rows,
            P(GROUP),
            P(GROUP),
            weight,
            weight,
            weight,
            weight_in,
            weight,
            P("fsdp", None),
            rows,
            rows,
            rows,
            rows,
            rows,
        ),
        out_specs=(rows, rows, P(GROUP), P(GROUP), weight, weight, weight, weight_in, weight),
        check_vma=False,
    )
```

```python
import functools

import jax
import jax.numpy as jnp
from jax import lax
from jax.experimental import pallas as pl
from jax.experimental.pallas import tpu as pltpu
from jax.sharding import PartitionSpec as P

HD = 128
EPSILON = 1e-06
ROPE_BASE = 10000.0
MASKED = -1e30
GROUP = ("fsdp", "ctx")
BF = jnp.bfloat16
F32 = jnp.float32
VMEM_LIMIT = 56 * 1024 * 1024


def normalize(tensor):
    inverse = lax.rsqrt(jnp.mean(tensor * tensor, axis=-1, keepdims=True) + EPSILON)
    return (tensor * inverse, inverse)


def norm_back(grad_in, normed, inverse, gain_vec):
    scaled = grad_in * gain_vec
    inner_mean = jnp.mean(scaled * normed, axis=-1, keepdims=True)
    return (inverse * (scaled - normed * inner_mean), jnp.sum(grad_in * normed, axis=0))


def dot(a, b, ca, cb):
    return lax.dot_general(a, b, (((ca,), (cb,)), ((), ())), preferred_element_type=F32)


def turn(x, cos, sin):
    return x * cos + pltpu.roll(x, HD // 2, 1) * sin


def swap(x, mask, axes, count):
    return lax.ppermute(x, axes, [(i, i ^ mask) for i in range(count)])


def bits_of(count):
    return count.bit_length() - 1


def flip(value, mask):
    step = 1
    while step <= mask:
        if mask & step:
            value = value + step - 2 * step * ((value // step) % 2)
        step *= 2
    return value


def peer(ctx_count, mask):
    return {
        "fsdp": flip(lax.axis_index("fsdp"), mask // ctx_count),
        "ctx": flip(lax.axis_index("ctx"), mask % ctx_count),
    }


def greet(ctx_count, masks):
    barrier = pltpu.get_barrier_semaphore()
    for mask in masks:
        pl.semaphore_signal(
            barrier, inc=1, device_id=peer(ctx_count, mask), device_id_type=pl.DeviceIdType.MESH
        )
    pl.semaphore_wait(barrier, len(masks))


def window(ref, rows, cols):
    if cols is None:
        return ref.at[pl.ds(rows[0], rows[1])]
    return ref.at[pl.ds(rows[0], rows[1]), pl.ds(cols[0], cols[1])]


class Moves:
    def __init__(self, ctx_count, moves, arrays, send, recv, bounces=()):
        self.moves = moves
        self.onward = {}
        bounces = list(bounces)
        self.copies = []
        self.place = {m[1]: i for i, m in enumerate(moves)}
        self.started, self.came = set(), set()
        for i, (source, target, mask, _) in enumerate(moves):
            src = window(arrays[source[0]], *source[1:])
            dst = window(arrays[target[0]], *target[1:])
            if mask:
                copy = pltpu.make_async_remote_copy(
                    src_ref=src,
                    dst_ref=dst,
                    send_sem=send.at[i],
                    recv_sem=recv.at[i],
                    device_id=peer(ctx_count, mask),
                    device_id_type=pl.DeviceIdType.MESH,
                )
            elif mask is None:
                copy = pltpu.make_async_copy(src, dst, recv.at[i])
            else:
                bounce = bounces.pop(0)
                copy = pltpu.make_async_copy(src, bounce, recv.at[i])
                self.onward[i] = pltpu.make_async_copy(bounce, dst, send.at[i])
            self.copies.append(copy)

    def start(self, i):
        if i not in self.started:
            self.started.add(i)
            self.copies[i].start()

    def begin(self, count=None):
        for i, move in enumerate(self.moves[:count]):
            if not move[3]:
                self.start(i)

    def await_one(self, i):
        if i not in self.came:
            self.came.add(i)
            if i in self.onward:
                self.copies[i].wait()
                self.onward[i].start()
            elif self.moves[i][2] is None:
                self.copies[i].wait()
            else:
                self.copies[i].wait_recv()

    def settle(self, count, first=0):
        for i in range(first, count):
            if i in self.onward:
                self.await_one(i)
        for i in range(first, count):
            for target in self.moves[i][3]:
                self.await_one(self.place[target])
            self.start(i)
        for i in range(first, count):
            self.await_one(i)

    def finish(self):
        self.settle(len(self.moves))
        for i in range(len(self.moves)):
            if i in self.onward:
                self.onward[i].wait()
            elif self.moves[i][2] is not None:
                self.copies[i].wait_send()


def masks_of(moves):
    return sorted({move[2] for move in moves if move[2]})


def move_kernel(ctx_count, moves, names_in, names_out, *refs):
    count = len(names_in) + len(names_out)
    refs, (send, recv, *bounces) = refs[:count], refs[count:]
    arrays = dict(zip(names_in, refs))
    arrays.update(zip(names_out, refs[len(names_in) :]))
    greet(ctx_count, masks_of(moves))
    run = Moves(ctx_count, moves, arrays, send, recv, bounces)
    run.begin()
    run.finish()


def move(name, number, ctx_count, moves, given, made):
    names_in = [n for n in given if n not in made] + [n for n in given if n in made]
    plain = [n for n in names_in if n not in made]
    names_out = list(made)
    any_spec = pl.BlockSpec(memory_space=pl.ANY)
    bounces = [
        pltpu.VMEM((source[1][1], (source[2] or (0, given[source[0]].shape[1]))[1]), BF)
        for source, _, mask, _ in moves
        if not mask
    ]
    return dict(
        zip(
            names_out,
            pl.pallas_call(
                functools.partial(
                    move_kernel,
                    ctx_count,
                    moves,
                    plain + ["old_" + n for n in names_in[len(plain) :]],
                    names_out,
                ),
                out_shape=[jax.ShapeDtypeStruct(shape, BF) for shape in made.values()],
                in_specs=[any_spec] * len(names_in),
                out_specs=[any_spec] * len(names_out),
                input_output_aliases={
                    names_in.index(n): names_out.index(n) for n in names_out if n in given
                },
                scratch_shapes=[pltpu.SemaphoreType.DMA((len(moves),))] * 2 + bounces,
                compiler_params=pltpu.CompilerParams(
                    collective_id=number, has_side_effects=True, vmem_limit_bytes=VMEM_LIMIT
                ),
                name=name,
            )(*[given[n] for n in names_in]),
        )
    )


def attn_grads_kernel(
    ctx_count,
    bits,
    part,
    cols,
    hidden_ref,
    branch_ref,
    qkv_ref,
    mixed_ref,
    out_ref,
    hidden,
    branch,
    hidden_odd,
    branch_odd,
    right,
    grads,
    got,
    send,
    recv,
    pass_send,
    pass_recv,
):
    rows, width = hidden_ref.shape
    count = width // part // 2
    planes = right.shape[1] // cols
    first = qkv_ref.shape[1]
    greet(ctx_count, [1, *[1 << b for b in bits]])
    arrays = {
        "hidden_odd": hidden_odd,
        "branch_odd": branch_odd,
        "qkv_in": qkv_ref,
        "mixed_in": mixed_ref,
        "hidden": hidden,
        "branch": branch,
        "right": right,
    }
    theirs = (rows, rows)
    moves = [
        (("mixed_in", (0, rows), None), ("right", theirs, (first, mixed_ref.shape[1])), 1, ()),
        (("branch_odd", (0, rows), None), ("branch", theirs, None), 1, ()),
        (("qkv_in", (0, rows), None), ("right", theirs, (0, first)), 1, ()),
        (("hidden_odd", (0, rows), None), ("hidden", theirs, None), 1, ()),
    ]
    run = Moves(ctx_count, moves, arrays, pass_send, pass_recv)
    for given, even_side, odd_side in (
        (branch_ref, branch, branch_odd),
        (hidden_ref, hidden, hidden_odd),
    ):
        for j in range(count):
            block = slice(j * part, (j + 1) * part)
            even_side[:rows, block] = given[:, 2 * j * part : (2 * j + 1) * part]
            odd_side[:, block] = given[:, (2 * j + 1) * part : (2 * j + 2) * part]
    run.begin()
    right[:rows, :first] = qkv_ref[...]
    right[:rows, first:] = mixed_ref[...]
    number = [0]

    def copy(mask, block, plane):
        i = number[0]
        number[0] += 1
        window_of = (pl.ds(block * part, part), pl.ds(plane * cols, cols))
        return pltpu.make_async_remote_copy(
            src_ref=grads.at[window_of],
            dst_ref=got.at[window_of],
            send_sem=send.at[i],
            recv_sem=recv.at[i],
            device_id=peer(ctx_count, mask),
            device_id_type=pl.DeviceIdType.MESH,
        )

    sent, flying, left = [], {}, {}

    def send_half(plane, order, step):
        at = bits.index(order[step])
        flying[plane] = {
            j: copy(1 << order[step], j, plane) for j in left[plane] if j >> at & 1
        }
        for c in flying[plane].values():
            c.start()
        sent.extend(flying[plane].values())

    lanes = []
    late = first // cols
    for n, plane in enumerate([*range(late, planes), *range(late)]):
        lanes.append((plane, bits if n % 2 else bits[::-1]))
    for plane, order in lanes:
        run.settle(2 if plane >= late else 4)
        at = pl.ds(plane * cols, cols)
        left_side = hidden if plane < late else branch
        grads[:, at] = dot(left_side[...], right[:, at], 0, 0).astype(BF)
        left[plane] = list(range(count))
        send_half(plane, order, 0)
    for step in range(len(bits)):
        for plane, order in lanes:
            at = bits.index(order[step])
            left[plane] = [j for j in left[plane] if not j >> at & 1]
            across = pl.ds(plane * cols, cols)
            for j in left[plane]:
                flying[plane][j | 1 << at].wait_recv()
                down, other = pl.ds(j * part, part), pl.ds((j | 1 << at) * part, part)
                total = grads[down, across].astype(F32) + got[other, across].astype(F32)
                if step == len(bits) - 1:
                    out_ref[:, across] = total
                else:
                    grads[down, across] = total.astype(BF)
            if step < len(bits) - 1:
                send_half(plane, order, step + 1)
    run.finish()
    for c in sent:
        c.wait_send()


def attn_grads(number, ctx_count, bits, part, cols, hidden, branch, qkv, mixed):
    rows, width = hidden.shape
    wide = qkv.shape[1] + mixed.shape[1]
    copies = (wide // cols) * (width // part // 2)
    full = pl.BlockSpec(memory_space=pltpu.VMEM)
    return pl.pallas_call(
        functools.partial(attn_grads_kernel, ctx_count, bits, part, cols),
        out_shape=jax.ShapeDtypeStruct((part, wide), F32),
        in_specs=[full] * 4,
        out_specs=full,
        scratch_shapes=[pltpu.VMEM((2 * rows, width // 2), BF)] * 2
        + [pltpu.VMEM((rows, width // 2), BF)] * 2
        + [pltpu.VMEM((2 * rows, wide), BF)]
        + [pltpu.VMEM((width // 2, wide), BF)] * 2
        + [pltpu.SemaphoreType.DMA((copies,))] * 2
        + [pltpu.SemaphoreType.DMA((4,))] * 2,
        compiler_params=pltpu.CompilerParams(
            collective_id=number, has_side_effects=True, vmem_limit_bytes=VMEM_LIMIT
        ),
        name="attn_grads",
    )(hidden, branch, qkv, mixed)


def lay_kernel(grad_ref, *out_refs):
    at = 0
    for ref in out_refs:
        for p in range(ref.shape[1]):
            ref[:, p, :] = grad_ref[:, at : at + ref.shape[2]]
            at += ref.shape[2]


def lay_out(grad, shapes):
    step = min(64, grad.shape[0])
    return pl.pallas_call(
        lay_kernel,
        grid=(grad.shape[0] // step,),
        in_specs=[pl.BlockSpec((step, grad.shape[1]), lambda i: (i, 0))],
        out_specs=[pl.BlockSpec((step, *shape[1:]), lambda i: (i, 0, 0)) for shape in shapes],
        out_shape=[jax.ShapeDtypeStruct(shape, F32) for shape in shapes],
        compiler_params=pltpu.CompilerParams(vmem_limit_bytes=VMEM_LIMIT),
        name="lay_out",
    )(grad)


def gain_kernel(ctx_count, group, gain_ref, out_ref, got, send, recv):
    greet(ctx_count, range(1, group))
    copies = []
    for j in range(1, group):
        rows = pl.ds(j * 8, 8)
        copies.append(
            pltpu.make_async_remote_copy(
                src_ref=gain_ref.at[rows],
                dst_ref=got.at[rows],
                send_sem=send.at[j],
                recv_sem=recv.at[j],
                device_id=peer(ctx_count, j),
                device_id_type=pl.DeviceIdType.MESH,
            )
        )
        copies[-1].start()
    total = gain_ref[:8]
    for j, copy in enumerate(copies):
        copy.wait_recv()
        total = total + got[(j + 1) * 8 : (j + 2) * 8]
    out_ref[...] = total
    for copy in copies:
        copy.wait_send()


def gain_sums(number, ctx_count, group, gains):
    count, part = len(gains), gains[0].shape[0] // group
    laid = jnp.stack([g.reshape(group, part) for g in gains], axis=1)
    laid = jnp.pad(laid, ((0, 0), (0, 8 - count), (0, 0))).reshape(group * 8, part)
    full = pl.BlockSpec(memory_space=pltpu.VMEM)
    total = pl.pallas_call(
        functools.partial(gain_kernel, ctx_count, group),
        out_shape=jax.ShapeDtypeStruct((8, part), F32),
        in_specs=[full],
        out_specs=full,
        scratch_shapes=[pltpu.VMEM((group * 8, part), F32)]
        + [pltpu.SemaphoreType.DMA((group,))] * 2,
        compiler_params=pltpu.CompilerParams(collective_id=number, has_side_effects=True),
        name="gain_sums",
    )(laid)
    return [total[i] for i in range(count)]


def expert_grads_kernel(
    ctx_count,
    experts,
    share,
    part,
    moves,
    two_ref,
    down_ref,
    gu_ref,
    active_ref,
    back_ref,
    place_ref,
    grads_ref,
    out_ref,
    back_got,
    two_out,
    down_out,
    two_got,
    down_got,
    gu_got,
    active_got,
    send,
    recv,
):
    slots, width = two_ref.shape
    units = active_ref.shape[1]
    room = slots // experts
    run = Moves(
        ctx_count,
        moves,
        {
            "two": two_out,
            "down": down_out,
            "gu": gu_ref,
            "active": active_ref,
            "back": back_ref,
            "back_got": back_got,
            "two_got": two_got,
            "down_got": down_got,
            "gu_got": gu_got,
            "active_got": active_got,
        },
        send,
        recv,
    )
    greet(ctx_count, masks_of(moves))
    for t in range(1, share):
        rows = slice((t - 1) * slots, t * slots)
        for k in range(experts):
            at = (k * share + t) * part
            two_out[rows, k * part : (k + 1) * part] = two_ref[:, at : at + part]
            down_out[rows, k * part : (k + 1) * part] = down_ref[:, at : at + part]
    run.begin()
    for i in range(experts - 1, len(moves)):
        run.await_one(i)
    for k in range(experts):
        rows = pl.ds(k * part, part)
        own, other = slice(k * share * part, (k * share + 1) * part), slice(k * part, (k + 1) * part)
        for cols, left, left_got, right, right_got in (
            (pl.ds(0, 2 * units), two_ref, two_got, gu_ref, gu_got),
            (pl.ds(2 * units, units), down_ref, down_got, active_ref, active_got),
        ):
            total = dot(left[:, own], right[...], 0, 0)
            if share > 1:
                total = total + dot(left_got[:, other], right_got[...], 0, 0)
            grads_ref[rows, cols] = total.astype(BF)
    run.finish()
    run_of = width // experts
    for i in range(experts):
        total = dot(place_ref[0], back_ref[:room, i * run_of : (i + 1) * run_of], 0, 0)
        for k in range(1, experts):
            at = (i ^ k) * run_of
            total = total + dot(
                place_ref[k], back_got[k * room : (k + 1) * room, at : at + run_of], 0, 0
            )
        out_ref[:, i * run_of : (i + 1) * run_of] = total.astype(BF)


def expert_grads_of(number, ctx_count, experts, share, part, two, down, gu, active, back, place):
    slots, width = two.shape
    room, units = slots // experts, active.shape[1]
    moves = []
    for k in range(1, experts):
        moves.append(
            (("back", (k * room, room), None), ("back_got", (k * room, room), None), k * share, ())
        )
    for t in range(1, share):
        rows = ((t - 1) * slots, slots)
        for name in ("gu", "active"):
            moves.append(((name, (0, slots), None), (name + "_got", rows, None), t, ()))
        for name in ("two", "down"):
            moves.append(((name, rows, None), (name + "_got", rows, None), t, ()))
    others = max(1, share - 1) * slots
    full = pl.BlockSpec(memory_space=pltpu.VMEM)
    return pl.pallas_call(
        functools.partial(
            expert_grads_kernel, ctx_count, experts, share, part, moves
        ),
        out_shape=[
            jax.ShapeDtypeStruct((experts * part, 3 * units), BF),
            jax.ShapeDtypeStruct((place.shape[2], width), BF),
        ],
        in_specs=[full] * 6,
        out_specs=[full] * 2,
        scratch_shapes=[
            pltpu.VMEM((slots, width), BF),
            *[pltpu.VMEM((others, experts * part), BF)] * 4,
            pltpu.VMEM((others, 2 * units), BF),
            pltpu.VMEM((others, units), BF),
        ]
        + [pltpu.SemaphoreType.DMA((len(moves),))] * 2,
        compiler_params=pltpu.CompilerParams(
            collective_id=number, has_side_effects=True, vmem_limit_bytes=VMEM_LIMIT
        ),
        name="expert_grads",
    )(two, down, gu, active, back, place)


def head_cols(index):
    return pl.ds(pl.multiple_of(index * HD, HD), HD)


def scores_of(place, queries, keys, segq, idxq, segk, idxk):
    slots = dot(place, queries, 1, 0).astype(BF)
    scores = dot(slots, keys, 1, 1) * (HD**-0.5)
    allowed = (segq == segk) & (idxk <= idxq)
    scores = jnp.where(allowed, scores, MASKED)
    top = jnp.max(scores, axis=-1, keepdims=True)
    exps = jnp.exp(scores - top)
    total = jnp.sum(exps, axis=-1, keepdims=True)
    return slots, exps, 1.0 / total


def front_kernel(
    ctx_count,
    moves,
    marks,
    names_in,
    names_out,
    heads,
    part,
    normed_ref,
    gain_ref,
    cos_ref,
    sin_ref,
    place_ref,
    segq_ref,
    idxq_ref,
    gate_ref,
    segk_ref,
    idxk_ref,
    *refs,
):
    experts, _, rows = place_ref.shape
    width = normed_ref.shape[1]
    wide = heads * HD
    group = width // part
    given, refs = refs[: len(names_in)], refs[len(names_in) :]
    gains_ref, hidden_ref, qkv_ref, kv_ref, mixed_ref, branch_ref = refs[:6]
    refs = refs[6:]
    made, (full, send, recv, *bounces) = refs[: len(names_out)], refs[len(names_out) :]
    arrays = {
        "gain_own": gain_ref,
        "gains": gains_ref,
        "full": full,
        "qkv": qkv_ref,
        "kv": kv_ref,
        **dict(zip(names_in, given)),
        **dict(zip(names_out, made)),
    }
    greet(ctx_count, masks_of(moves))
    run = Moves(ctx_count, moves, arrays, send, recv, bounces)
    gains_done, first_done, rest_done, keys_done = marks
    run.begin(rest_done)
    gains_ref[:16] = gain_ref[...]
    run.settle(gains_done)
    for j in range(group):
        cols = slice(j * part, (j + 1) * part)
        gain = gains_ref[j * 16 : (j + 1) * 16].astype(F32)[:1, :part]
        hidden_ref[:, cols] = (normed_ref[:, cols] * gain).astype(BF)
    run.settle(first_done, gains_done)
    cos, sin = cos_ref[...], sin_ref[...]

    def project(plane):
        y = dot(hidden_ref[...], full[:, plane * wide : (plane + 1) * wide], 1, 0)
        for head in range(heads):
            cols = slice(head * HD, (head + 1) * HD)
            at = slice(plane * wide + head * HD, plane * wide + (head + 1) * HD)
            z = y[:, cols]
            qkv_ref[:, at] = (turn(z, cos, sin) if plane <= experts else z).astype(BF)

    project(experts)
    project(experts + 1)
    run.begin(keys_done)
    kv_ref[:rows] = qkv_ref[:, experts * wide :]
    run.begin()
    for plane in range(experts):
        project(plane)
    run.settle(keys_done, rest_done)

    def step(i, carry):
        h, e = i // experts, i % experts
        cols = head_cols(e * heads + h)
        place = place_ref[e]
        _, exps, inv = scores_of(
            place,
            qkv_ref[:, cols],
            kv_ref[:, head_cols(h)],
            segq_ref[e],
            idxq_ref[e],
            segk_ref[...],
            idxk_ref[...],
        )
        attn = dot(exps.astype(BF), kv_ref[:, head_cols(heads + h)], 1, 0) * inv
        mixed = (attn * gate_ref[e]).astype(BF)
        mixed_ref[:, cols] = dot(place, mixed, 0, 0).astype(BF)
        return carry

    lax.fori_loop(0, heads * experts, step, 0)
    run.settle(rest_done, first_done)
    for j in range(group):
        rows_at = slice(j * part, (j + 1) * part)
        branch_ref[:, rows_at] = dot(mixed_ref[...], full[rows_at, (experts + 2) * wide :], 1, 1).astype(BF)
    run.finish()


def front(number, ctx_count, heads, part, moves, later, given, made, small):
    normed, gain_own, place = small[0], small[1], small[4]
    experts, _, rows = place.shape
    width = normed.shape[1]
    wide = heads * HD
    group = width // part
    full_wide = 2 * (experts + 1) * wide
    kv_moves = []
    order = [0]
    for bit in range(bits_of(ctx_count))[::-1]:
        for at in range(len(order)):
            target = ("kv", ((at + len(order)) * rows, rows), None)
            if at:
                source = ("kv", (at * rows, rows), None)
                kv_moves.append((source, target, 1 << bit, (source,)))
            else:
                source = ("qkv", (0, rows), (experts * wide, 2 * wide))
                kv_moves.append((source, target, 1 << bit, ()))
        order = order + order
    gains_moves, first_moves, rest_moves = moves
    marks = [len(gains_moves)]
    for more in (first_moves, rest_moves, kv_moves):
        marks.append(marks[-1] + len(more))
    whole = ("full", (0, width), None)
    landed = tuple(m[1] for m in first_moves + rest_moves if m[1][0] == "full")
    keep = [(whole, ("kept", (0, width), None), None, landed)]
    moves = gains_moves + first_moves + rest_moves + kv_moves + later + keep
    names_in, names_out = list(given), [*made, "kept"]
    shapes_out = [*made.values(), (width, full_wide)]
    any_spec = pl.BlockSpec(memory_space=pl.ANY)
    full = pl.BlockSpec(memory_space=pltpu.VMEM)
    small_out = [
        ((16 * group, gain_own.shape[1]), BF),
        ((rows, width), BF),
        ((rows, (experts + 2) * wide), BF),
        ((ctx_count * rows, 2 * wide), BF),
        ((rows, experts * wide), BF),
        ((rows, width), BF),
    ]
    bounces = [
        pltpu.VMEM((source[1][1], (source[2] or (0, given[source[0]].shape[1]))[1]), BF)
        for source, _, mask, _ in moves
        if mask == 0
    ]
    out = pl.pallas_call(
        functools.partial(
            front_kernel, ctx_count, moves, marks, names_in, names_out, heads, part
        ),
        out_shape=[jax.ShapeDtypeStruct(*x) for x in small_out]
        + [jax.ShapeDtypeStruct(shape, BF) for shape in shapes_out],
        in_specs=[full] * len(small) + [any_spec] * len(names_in),
        out_specs=[full] * len(small_out) + [any_spec] * len(names_out),
        scratch_shapes=[pltpu.VMEM((width, full_wide), BF)]
        + [pltpu.SemaphoreType.DMA((len(moves),))] * 2
        + bounces,
        compiler_params=pltpu.CompilerParams(
            collective_id=number, has_side_effects=True, vmem_limit_bytes=VMEM_LIMIT
        ),
        name="front",
    )(*small, *given.values())
    return out[: len(small_out)], dict(zip(names_out, out[len(small_out) :]))


def attend_back_kernel(
    ctx_count,
    moves,
    names_in,
    names_out,
    heads,
    qkv_ref,
    kv_ref,
    place_ref,
    segq_ref,
    idxq_ref,
    segk_ref,
    idxk_ref,
    grad_ref,
    cos_ref,
    sin_ref,
    *refs,
):
    experts, _, rows = place_ref.shape
    keys = kv_ref.shape[0]
    given, refs = refs[: len(names_in)], refs[len(names_in) :]
    out_ref = refs[0]
    made, (dk_acc, dv_acc, total, got, send, recv, pass_send, pass_recv) = refs[1:-8], refs[-8:]
    arrays = {**dict(zip(names_in, given)), **dict(zip(names_out, made))}
    bits = range(bits_of(ctx_count))
    greet(ctx_count, sorted({*masks_of(moves), *[1 << b for b in bits]}))
    run = Moves(ctx_count, moves, arrays, send, recv)
    run.begin()

    def head_copy(h, bit):
        size = keys >> (bit + 1)
        i = h * len(bits) + bit
        return pltpu.make_async_remote_copy(
            src_ref=total.at[h, pl.ds(size, size)],
            dst_ref=got.at[h, pl.ds(size, size)],
            send_sem=pass_send.at[i],
            recv_sem=pass_recv.at[i],
            device_id=peer(ctx_count, 1 << bit),
            device_id_type=pl.DeviceIdType.MESH,
        )

    def head_sum(h, bit):
        size = keys >> (bit + 1)
        head_copy(h, bit).wait_recv()
        mine = total[h, :size].astype(F32) + got[h, size : 2 * size].astype(F32)
        mine = mine.astype(BF)
        if bit + 1 < len(bits):
            total[h, :size] = mine
            head_copy(h, bit + 1).start()
        else:
            at = experts * heads * HD
            out_ref[:, at + h * HD : at + (h + 1) * HD] = mine[:, :HD]
            at += heads * HD
            out_ref[:, at + h * HD : at + (h + 1) * HD] = mine[:, HD:]

    for h in range(heads):
        dk_acc[...] = jnp.zeros_like(dk_acc)
        dv_acc[...] = jnp.zeros_like(dv_acc)

        def step(e, carry, h=h):
            cols = head_cols(e * heads + h)
            place = place_ref[e]
            k, v = kv_ref[:, h * HD : (h + 1) * HD], kv_ref[:, (heads + h) * HD : (heads + h + 1) * HD]
            slots, exps, inv = scores_of(
                place, qkv_ref[:, cols], k, segq_ref[e], idxq_ref[e], segk_ref[...], idxk_ref[...]
            )
            attn = dot(exps.astype(BF), v, 1, 0) * inv
            probs = exps * inv
            grad = dot(place, grad_ref[:, cols], 1, 0)
            delta = jnp.sum(grad * attn, axis=-1, keepdims=True)
            grad = grad.astype(BF)
            dv_acc[...] += dot(probs.astype(BF), grad, 0, 0)
            grad_probs = dot(grad, v, 1, 1)
            grad_scores = (probs * (grad_probs - delta)).astype(BF)
            dq = dot(grad_scores, k, 1, 0) * (HD**-0.5)
            dk_acc[...] += dot(grad_scores, slots, 0, 0) * (HD**-0.5)
            top = dq.astype(BF)
            low = (dq - top.astype(F32)).astype(BF)
            back = dot(place, top, 0, 0) + dot(place, low, 0, 0)
            out_ref[:, cols] = turn(back, cos_ref[:rows], -sin_ref[:rows]).astype(BF)
            return carry

        lax.fori_loop(0, experts, step, 0)
        total[h, :, :HD] = turn(dk_acc[...], cos_ref[...], -sin_ref[...]).astype(BF)
        total[h, :, HD:] = dv_acc[...].astype(BF)
        head_copy(h, 0).start()
        for bit in bits:
            if h - 1 - bit >= 0:
                head_sum(h - 1 - bit, bit)
    for h in range(heads, heads + len(bits)):
        for bit in bits:
            if 0 <= h - 1 - bit < heads:
                head_sum(h - 1 - bit, bit)
    for h in range(heads):
        for bit in bits:
            head_copy(h, bit).wait_send()
    run.finish()


def attend_back(number, ctx_count, heads, moves, given, made, qkv, kv, place, *others):
    rows, keys = qkv.shape[0], kv.shape[0]
    any_spec = pl.BlockSpec(memory_space=pl.ANY)
    full = pl.BlockSpec(memory_space=pltpu.VMEM)
    passes = heads * bits_of(ctx_count)
    out, *rest = pl.pallas_call(
        functools.partial(attend_back_kernel, ctx_count, moves, list(given), list(made), heads),
        out_shape=[jax.ShapeDtypeStruct(qkv.shape, BF)]
        + [jax.ShapeDtypeStruct(shape, BF) for shape in made.values()],
        in_specs=[full] * (3 + len(others)) + [any_spec] * len(given),
        out_specs=[full] + [any_spec] * len(made),
        scratch_shapes=[pltpu.VMEM((keys, HD), F32)] * 2
        + [pltpu.VMEM((heads, keys, 2 * HD), BF)] * 2
        + [pltpu.SemaphoreType.DMA((max(1, len(moves)),))] * 2
        + [pltpu.SemaphoreType.DMA((passes,))] * 2,
        compiler_params=pltpu.CompilerParams(
            collective_id=number, has_side_effects=True, vmem_limit_bytes=VMEM_LIMIT
        ),
        name="attend_back",
    )(qkv, kv, place, *others, *given.values())
    return out, dict(zip(made, rest))


def spread_kernel(experts, me_ref, *refs):
    blocks, (in_ref, down_ref) = refs[:experts], refs[experts:]
    units = down_ref.shape[2]
    for m in range(experts):

        @pl.when(me_ref[0] == m)
        def _():
            for e in range(experts):
                block = blocks[e ^ m]
                for c in range(2):
                    in_ref[:, e, c, :] = block[:, c * units : (c + 1) * units].astype(F32)
                down_ref[:, e, :] = block[:, 2 * units :].astype(F32)


def spread_grads(blocks, me, in_shape, down_shape):
    experts = len(blocks)
    step = min(32, in_shape[0])
    return pl.pallas_call(
        functools.partial(spread_kernel, experts),
        grid_spec=pltpu.PrefetchScalarGridSpec(
            num_scalar_prefetch=1,
            grid=(in_shape[0] // step,),
            in_specs=[pl.BlockSpec((step, blocks[0].shape[1]), lambda i, m: (i, 0))] * experts,
            out_specs=[
                pl.BlockSpec((step, *in_shape[1:]), lambda i, m: (i, 0, 0, 0)),
                pl.BlockSpec((step, *down_shape[1:]), lambda i, m: (i, 0, 0)),
            ],
        ),
        out_shape=[
            jax.ShapeDtypeStruct(in_shape, F32),
            jax.ShapeDtypeStruct(down_shape, F32),
        ],
        compiler_params=pltpu.CompilerParams(vmem_limit_bytes=VMEM_LIMIT),
        name="spread_grads",
    )(me.astype(jnp.int32).reshape(1), *blocks)


def places(routes, gates, experts, cap, room):
    rows = routes.shape[0]
    named = routes[:, :, None] == jnp.arange(experts, dtype=jnp.int32)[None, None, :]
    member = jnp.any(named, axis=1)
    gate = jnp.sum(jnp.where(named, gates[:, :, None], 0.0), axis=1)
    token = jnp.arange(rows, dtype=jnp.int32)
    earlier = (token[None, :] < token[:, None]).astype(BF)
    rank = dot(earlier, member.astype(BF), 1, 0).astype(jnp.int32)
    slot = jnp.where(member, rank, -1).T
    taken = slot[:, None, :] == jnp.arange(room, dtype=jnp.int32)[None, :, None]
    return taken, gate


def slot_sum(taken, values):
    return jnp.sum(jnp.where(taken, values, 0), axis=-1, keepdims=True)


def layer(
    counts,
    tokens,
    gain_attn,
    gain_mlp,
    w_kv,
    w_query,
    w_out_attn,
    w_in,
    w_down,
    segments,
    attn_routes,
    attn_gates,
    mlp_routes,
    mlp_gates,
    cotangent,
):
    fsdp_count, ctx_count, tp_count = counts
    group = fsdp_count * ctx_count
    me = lax.axis_index(GROUP)
    ctx_me = lax.axis_index("ctx")
    rows, width = tokens.shape[1:]
    cap = 9 * rows // 16
    room = -(-cap // 16) * 16
    part = width // group
    attn_experts = w_query.shape[1]
    experts = w_in.shape[1]
    share = group // experts
    expert_me = me // share
    hidden_units = w_down.shape[2]
    head_width = w_kv.shape[2]

    def piece(x, index, size=part, axis=1):
        return lax.dynamic_slice_in_dim(x, index * size, size, axis)

    def exchange(x, mask):
        return swap(x, mask, GROUP, group)

    def after(x, *events):
        return lax.optimization_barrier((x, *events))[0]

    def relative(x):
        return jnp.concatenate([piece(x, me ^ j) for j in range(group)], axis=1)

    high, second = group // 2, group // 4

    qkv_wide = (attn_experts + 2) * head_width
    attn_own = jnp.concatenate(
        [w_query.reshape(part, -1), w_kv.reshape(part, -1), w_out_attn.reshape(part, -1)], axis=1
    )
    attn_wide = attn_own.shape[1]
    gain_own = jnp.pad(
        jnp.concatenate([gain_attn, gain_mlp])[None, :], ((0, 15), (0, 0))
    )
    far_x, far_y = exchange(attn_own, high), exchange(attn_own, second)

    seg_row = segments[0]
    seq_total = seg_row.shape[0]
    ctx_bits = list(range(bits_of(ctx_count)))[::-1]
    key_order = [0]
    for bit in ctx_bits:
        key_order = key_order + [j | (1 << bit) for j in key_order]
    key_seg = jnp.concatenate([piece(seg_row, ctx_me ^ j, rows, 0) for j in key_order])
    key_idx = jnp.concatenate(
        [(ctx_me ^ j) * rows + jnp.arange(rows, dtype=jnp.int32) for j in key_order]
    )
    place_idx = jnp.arange(seq_total, dtype=jnp.int32)
    pos = jnp.sum(
        (seg_row[None, :] == key_seg[:, None]) & (place_idx[None, :] < key_idx[:, None]),
        axis=1,
        dtype=jnp.int32,
    ).astype(F32)
    frequency = ROPE_BASE ** (-(jnp.arange(HD // 2, dtype=F32) * 2.0) / HD)
    angles = pos[:, None] * frequency[None, :]
    cos_half, sin_half = jnp.cos(angles), jnp.sin(angles)
    cos = jnp.concatenate([cos_half, cos_half], axis=1)
    sin = jnp.concatenate([-sin_half, sin_half], axis=1)
    taken_attn, gate_attn = places(attn_routes[0], attn_gates[0], attn_experts, cap, room)
    place_attn = taken_attn.astype(BF)
    own_seg, own_idx = key_seg[:rows], key_idx[:rows]
    filled = jnp.any(taken_attn, axis=-1, keepdims=True)
    slot_seg = jnp.where(filled, slot_sum(taken_attn, own_seg), own_seg[0])
    slot_idx = jnp.where(filled, slot_sum(taken_attn, own_idx), own_idx[0])
    slot_gate = slot_sum(taken_attn, gate_attn.T[:, None, :])
    taken_mlp, gate_mlp = places(mlp_routes[0], mlp_gates[0], experts, cap, room)
    mine_first = [expert_me ^ k for k in range(experts)]
    place_mlp = jnp.concatenate([piece(taken_mlp, e, 1, 0) for e in mine_first]).astype(BF)
    inputs = relative(tokens[0]).astype(F32)
    grad_out = relative(cotangent[0])

    def expert_rows(k):
        in_rows = piece(w_in, expert_me ^ k, 1, 1).reshape(part, 2 * hidden_units)
        down_rows = piece(w_down, expert_me ^ k, 1, 1).reshape(part, hidden_units)
        return jnp.concatenate([in_rows, down_rows], axis=1)

    to_send = [expert_rows(k) for k in range(experts)]
    in_cols, down_cols = (0, 2 * hidden_units), (2 * hidden_units, hidden_units)
    weight_shapes = {"in": (width, 2 * hidden_units), "down": (width, hidden_units)}

    def weight_moves(k, first, size):
        moves = []
        for name, cols in (("in", in_cols), ("down", down_cols)):
            base = k * share * part + first
            source = (f"send{k}", (first, size), cols)
            landed = (name, (base, size), None)
            moves.append((source, landed, k * share, ()))
            for t in range(1, share):
                target = (name, (base + t * part, size), None)
                if k:
                    moves.append((landed, target, t, (landed,)))
                else:
                    moves.append((source, target, t, ()))
        return moves

    def many_weight_moves(cuts):
        return [m for cut in cuts for m in weight_moves(*cut)]

    near = [k for k in range(1, experts) if k & (k - 1) == 0]
    far = [k for k in range(1, experts) if k & (k - 1)]
    half_part = part // 2

    normed_one, inverse_one = normalize(inputs)
    (attn_own, far_x, far_y, gain_own), to_send, tables = lax.optimization_barrier(
        (
            (attn_own, far_x, far_y, gain_own),
            to_send,
            (normed_one, cos, sin, place_attn, slot_seg, slot_idx, slot_gate, place_mlp),
        )
    )
    normed_one, cos, sin, place_attn, slot_seg, slot_idx, slot_gate, place_mlp = tables
    quarter = part // 4
    gather_moves = []
    for cols in ((0, qkv_wide), (qkv_wide, attn_wide - qkv_wide)):
        moves = []
        held = {0: [("own", 0, part, ())], high: [("far_x", 0, part, ())], second: [("far_y", 0, part, ())]}
        held[high | second] = []
        for i in (0, 2, 1, 3):
            source, mask = (("far_x", second), ("far_y", high))[i // 2]
            target = ("full", ((high | second) * part + i * quarter, quarter), cols)
            moves.append(((source, (i * quarter, quarter), cols), target, mask, ()))
            held[high | second].append(("full", i * quarter, quarter, (target,)))
        for j in (0, high, second):
            name = held[j][0][0]
            moves.append(((name, (0, part), cols), ("full", (j * part, part), cols), None, ()))
        for bit in range(bits_of(group) - 2)[::-1]:
            for j in list(held):
                there = []
                for name, at, size, needs in held[j]:
                    source = (name, (at + j * part if name == "full" else at, size), cols)
                    target = ("full", ((j | 1 << bit) * part + at, size), cols)
                    moves.append((source, target, 1 << bit, needs))
                    there.append(("full", at, size, (target,)))
                held[j | 1 << bit] = there
        gather_moves.append(moves)
    gain_moves = [
        (("gain_own", (0, 16), None), ("gains", (j * 16, 16), None), j, ())
        for j in range(1, group)
    ]
    key_row = (key_seg[None, :], key_idx[None, :])
    heads = head_width // HD
    later = weight_moves(0, 0, part) + many_weight_moves([(k, 0, half_part) for k in near])
    (gains, hidden_one, qkv, kv, mixed, branch), made = front(
        1,
        ctx_count,
        heads,
        part,
        (gain_moves, *gather_moves),
        later,
        {
            "own": attn_own,
            "far_x": far_x,
            "far_y": far_y,
            **{f"send{k}": to_send[k] for k in [0, *near]},
        },
        weight_shapes,
        (
            normed_one,
            gain_own,
            cos[:rows],
            sin[:rows],
            place_attn,
            slot_seg,
            slot_idx,
            slot_gate,
            *key_row,
        ),
    )
    attn_full, weights = made["kept"], {n: made[n] for n in weight_shapes}
    gains = gains.reshape(group, 16, 2 * part)[:, 0].astype(F32)
    gain_one, gain_two = gains[:, :part].reshape(1, width), gains[:, part:].reshape(1, width)
    qkv_full, out_full = attn_full[:, :qkv_wide], attn_full[:, qkv_wide:]

    def turned(x, k):
        wide = share * part
        return jnp.concatenate(
            [x[:, (i ^ k) * wide : ((i ^ k) + 1) * wide] for i in range(experts)], axis=1
        )

    def pick(k, x):
        return dot(place_mlp[k], x, 1, 0).astype(BF)

    run = width // tp_count
    tp_me = lax.axis_index("tp")
    gate_high = gate_mlp.astype(BF)
    gate_low = (gate_mlp - gate_high.astype(F32)).astype(BF)
    gate_ride = jnp.pad(
        jnp.concatenate([gate_high, gate_low], axis=1), ((0, 0), (0, HD - 2 * experts))
    )
    grad_got = []
    for k in range(experts):
        sent = jnp.concatenate([piece(grad_out, tp_me ^ k, run), gate_ride], axis=1)
        slots = pick(k, sent)
        grad_got.append(exchange(slots, k * share) if k else slots)
    grad_got = jnp.concatenate(grad_got, axis=0)
    own_gate = jnp.tile(jnp.arange(experts) == expert_me, 2)
    slot_weight = jnp.sum(
        jnp.where(own_gate[None, :], grad_got[:, run : run + 2 * experts].astype(F32), 0.0),
        axis=1,
        keepdims=True,
    )
    grad_slots = lax.all_gather(grad_got[:, :run], "tp", axis=1, tiled=True)

    def send_weights(name, number, cuts, weights, slots=None):
        moves, given, made_shapes = [], {f"send{k}": to_send[k] for k, _, _ in cuts}, dict(weight_shapes)
        if slots is not None:
            made_shapes["slots"] = (experts * room, width)
            for k, x in enumerate(slots):
                given[f"slots{k}"] = x
                target = ("slots", (k * room, room), None)
                moves.append(((f"slots{k}", (0, room), None), target, k * share, ()))
        moves += many_weight_moves(cuts)
        made = move(name, number, ctx_count, moves, {**given, **weights}, made_shapes)
        return {n: made[n] for n in weight_shapes}, made.get("slots")

    branch_sum = lax.psum(branch, "tp")
    cuts = [(k, half_part, part - half_part) for k in near] + [(k, 0, half_part) for k in far]
    to_send, weights, _ = lax.optimization_barrier((to_send, weights, branch))
    weights, _ = send_weights("weights_two", 3, cuts, weights)
    resid = inputs + branch_sum.astype(F32)
    normed_two, inverse_two = normalize(resid)
    hidden_two = (normed_two * gain_two).astype(BF)
    slots = [pick(0, hidden_two)] + [turned(pick(k, hidden_two), k) for k in range(1, experts)]
    cuts = [(k, half_part, part - half_part) for k in far]
    weights, two_slots = send_weights("dispatch", 4, cuts, weights, slots)
    in_full, down_full = weights["in"], weights["down"]

    def send_back(x):
        slots = x.reshape(experts, room, width)
        return [slots[0]] + [exchange(slots[k], k * share) for k in range(1, experts)]

    def gathered_rows(got):
        got = [got[0]] + [turned(got[k], k) for k in range(1, experts)]
        return jnp.einsum(
            "kct,kcd->td", place_mlp, jnp.stack(got), preferred_element_type=F32
        ).astype(BF)

    gate_up = dot(two_slots, in_full, 1, 0)
    gate_part, up_part = gate_up[:, :hidden_units], gate_up[:, hidden_units:]
    sigmoid_gate = jax.nn.sigmoid(gate_part)
    silu_gate = gate_part * sigmoid_gate
    active = (silu_gate * up_part * slot_weight).astype(BF)
    mlp_slots = dot(active, down_full, 1, 1).astype(BF)
    mlp_back = send_back(mlp_slots)
    grad_active = dot(after(grad_slots, mlp_slots), down_full, 1, 0)
    scaled = grad_active * slot_weight
    grad_gate = scaled * up_part * sigmoid_gate * (1.0 + gate_part * (1.0 - sigmoid_gate))
    grad_up = scaled * silu_gate
    grad_gu = jnp.concatenate([grad_gate, grad_up], axis=1).astype(BF)
    back_two_slots = dot(grad_gu, in_full, 1, 1).astype(BF)
    expert_grads, back_two_part = expert_grads_of(
        8,
        ctx_count,
        experts,
        share,
        part,
        two_slots,
        grad_slots,
        grad_gu,
        active,
        after(back_two_slots, *mlp_back),
        place_mlp,
    )
    back_two = lax.psum(back_two_part, "tp").astype(F32)
    grads_got = {0: expert_grads[:part]}

    def grad_moves(ks):
        return [
            (("grads", (k * part, part), None), (f"got{k}", (0, part), None), k * share, ())
            for k in ks
        ], {f"got{k}": (part, expert_grads.shape[1]) for k in ks}

    moves, made_shapes = grad_moves(near)
    made = move("grads_near", 5, ctx_count, moves, {"grads": expert_grads}, made_shapes)
    grads_got.update({k: made[f"got{k}"] for k in near})
    grads_near = [grads_got[k] for k in near]

    grad_resid_norm, gain_two_grad = norm_back(back_two, normed_two, inverse_two, gain_two)
    grad_resid = grad_out.astype(F32) + grad_resid_norm
    grad_branch = grad_resid.astype(BF)
    grad_mixed = dot(after(grad_branch, *grads_near), out_full, 1, 0)
    gate_wide = jnp.repeat(gate_attn, head_width, axis=1)
    grad_attn = (grad_mixed * gate_wide).astype(BF)
    moves, made_shapes = grad_moves(far)
    grad_qkv, made = attend_back(
        6,
        ctx_count,
        heads,
        moves,
        {"grads": expert_grads},
        made_shapes,
        qkv,
        kv,
        place_attn,
        slot_seg,
        slot_idx,
        *key_row,
        grad_attn,
        cos,
        sin,
    )
    grads_got.update({k: made[f"got{k}"] for k in far})
    mlp_total = lax.psum(gathered_rows(after(mlp_back, grad_attn)), "tp").astype(F32)
    back_one_part = dot(grad_qkv, qkv_full, 1, 1)
    back_one = lax.psum(back_one_part.astype(BF), "tp").astype(F32)
    grad_input_norm, gain_one_grad = norm_back(back_one, normed_one, inverse_one, gain_one)
    grad_tokens = relative((grad_resid + grad_input_norm).astype(BF))

    output = relative((resid + mlp_total).astype(BF))

    upper = list(range(1, bits_of(group)))
    grad_attnw = attn_grads(
        7, ctx_count, upper, part, head_width, hidden_one, grad_branch, grad_qkv, mixed
    )
    grad_query_w, grad_kv_w, grad_out_w = lay_out(
        grad_attnw, (w_query.shape, w_kv.shape, w_out_attn.shape)
    )
    gain_grads = gain_sums(9, ctx_count, group, [gain_one_grad, gain_two_grad])

    return (
        output[None],
        grad_tokens[None],
        *gain_grads,
        grad_kv_w,
        grad_query_w,
        grad_out_w,
        *spread_grads([grads_got[k] for k in range(experts)], expert_me, w_in.shape, w_down.shape),
    )


def solution(mesh):
    rows = P("fsdp", "ctx", None)
    weight = P(GROUP, None, "tp")
    weight_in = P(GROUP, None, None, "tp")
    return jax.shard_map(
        functools.partial(layer, tuple(mesh.shape[a] for a in ("fsdp", "ctx", "tp"))),
        mesh=mesh,
        in_specs=(
            rows,
            P(GROUP),
            P(GROUP),
            weight,
            weight,
            weight,
            weight_in,
            weight,
            P("fsdp", None),
            rows,
            rows,
            rows,
            rows,
            rows,
        ),
        out_specs=(rows, rows, P(GROUP), P(GROUP), weight, weight, weight, weight_in, weight),
        check_vma=False,
    )
```

```python
import functools

import jax
import jax.numpy as jnp
from jax import lax
from jax.experimental import pallas as pl
from jax.experimental.pallas import tpu as pltpu
from jax.sharding import PartitionSpec as P

HD = 128
EPSILON = 1e-06
ROPE_BASE = 10000.0
MASKED = -1e30
GROUP = ("fsdp", "ctx")
BF = jnp.bfloat16
F32 = jnp.float32
VMEM_LIMIT = 56 * 1024 * 1024


def normalize(tensor):
    inverse = lax.rsqrt(jnp.mean(tensor * tensor, axis=-1, keepdims=True) + EPSILON)
    return (tensor * inverse, inverse)


def norm_back(grad_in, normed, inverse, gain_vec):
    scaled = grad_in * gain_vec
    inner_mean = jnp.mean(scaled * normed, axis=-1, keepdims=True)
    return (inverse * (scaled - normed * inner_mean), jnp.sum(grad_in * normed, axis=0))


def dot(a, b, ca, cb):
    return lax.dot_general(a, b, (((ca,), (cb,)), ((), ())), preferred_element_type=F32)


def turn(x, cos, sin):
    return x * cos + pltpu.roll(x, HD // 2, 1) * sin


def swap(x, mask, axes, count):
    return lax.ppermute(x, axes, [(i, i ^ mask) for i in range(count)])


def bits_of(count):
    return count.bit_length() - 1


def flip(value, mask):
    step = 1
    while step <= mask:
        if mask & step:
            value = value + step - 2 * step * ((value // step) % 2)
        step *= 2
    return value


def peer(ctx_count, mask):
    if mask < 0:
        return {"tp": flip(lax.axis_index("tp"), -mask)}
    return {
        "fsdp": flip(lax.axis_index("fsdp"), mask // ctx_count),
        "ctx": flip(lax.axis_index("ctx"), mask % ctx_count),
    }


def greet(ctx_count, masks):
    barrier = pltpu.get_barrier_semaphore()
    for mask in masks:
        pl.semaphore_signal(
            barrier, inc=1, device_id=peer(ctx_count, mask), device_id_type=pl.DeviceIdType.MESH
        )
    pl.semaphore_wait(barrier, len(masks))


def run_cols(size, flips=0):
    return pl.ds(pl.multiple_of(flip(lax.axis_index("tp"), flips) * size, size), size)


def window(ref, rows, cols):
    if cols is None:
        return ref.at[pl.ds(rows[0], rows[1])]
    if cols[0] == "tp":
        return ref.at[pl.ds(rows[0], rows[1]), run_cols(cols[1])]
    return ref.at[pl.ds(rows[0], rows[1]), pl.ds(cols[0], cols[1])]


class Moves:
    def __init__(self, ctx_count, moves, arrays, send, recv, bounces=(), base=0):
        self.moves = moves
        self.onward = {}
        bounces = list(bounces)
        self.copies = []
        self.place = {m[1]: i for i, m in enumerate(moves)}
        self.started, self.came = set(), set()
        for at, (source, target, mask, _) in enumerate(moves):
            i = base + at
            src = window(arrays[source[0]], *source[1:])
            dst = window(arrays[target[0]], *target[1:])
            if mask:
                copy = pltpu.make_async_remote_copy(
                    src_ref=src,
                    dst_ref=dst,
                    send_sem=send.at[i],
                    recv_sem=recv.at[i],
                    device_id=peer(ctx_count, mask),
                    device_id_type=pl.DeviceIdType.MESH,
                )
            elif mask is None:
                copy = pltpu.make_async_copy(src, dst, recv.at[i])
            else:
                bounce = bounces.pop(0)
                copy = pltpu.make_async_copy(src, bounce, recv.at[i])
                self.onward[at] = pltpu.make_async_copy(bounce, dst, send.at[i])
            self.copies.append(copy)

    def start(self, i):
        if i not in self.started:
            self.started.add(i)
            self.copies[i].start()

    def begin(self, count=None):
        for i, move in enumerate(self.moves[:count]):
            if not move[3]:
                self.start(i)

    def await_one(self, i):
        if i not in self.came:
            self.came.add(i)
            if i in self.onward:
                self.copies[i].wait()
                self.onward[i].start()
            elif self.moves[i][2] is None:
                self.copies[i].wait()
            else:
                self.copies[i].wait_recv()

    def settle(self, count=None, first=0):
        count = len(self.moves) if count is None else count
        for i in range(first, count):
            if i in self.onward:
                self.await_one(i)
        for i in range(first, count):
            for target in self.moves[i][3]:
                self.await_one(self.place[target])
            self.start(i)
        for i in range(first, count):
            self.await_one(i)

    def finish(self):
        self.settle()
        for i in range(len(self.moves)):
            if i in self.onward:
                self.onward[i].wait()
            elif self.moves[i][2] is not None:
                self.copies[i].wait_send()


def masks_of(moves):
    return sorted({move[2] for move in moves if move[2]})


def move_kernel(ctx_count, moves, names_in, names_out, *refs):
    count = len(names_in) + len(names_out)
    refs, (send, recv, *bounces) = refs[:count], refs[count:]
    arrays = dict(zip(names_in, refs))
    arrays.update(zip(names_out, refs[len(names_in) :]))
    greet(ctx_count, masks_of(moves))
    run = Moves(ctx_count, moves, arrays, send, recv, bounces)
    run.begin()
    run.finish()


def move(name, number, ctx_count, moves, given, made):
    names_in = [n for n in given if n not in made] + [n for n in given if n in made]
    plain = [n for n in names_in if n not in made]
    names_out = list(made)
    any_spec = pl.BlockSpec(memory_space=pl.ANY)
    bounces = [
        pltpu.VMEM((source[1][1], (source[2] or (0, given[source[0]].shape[1]))[1]), BF)
        for source, _, mask, _ in moves
        if not mask
    ]
    return dict(
        zip(
            names_out,
            pl.pallas_call(
                functools.partial(
                    move_kernel,
                    ctx_count,
                    moves,
                    plain + ["old_" + n for n in names_in[len(plain) :]],
                    names_out,
                ),
                out_shape=[jax.ShapeDtypeStruct(shape, BF) for shape in made.values()],
                in_specs=[any_spec] * len(names_in),
                out_specs=[any_spec] * len(names_out),
                input_output_aliases={
                    names_in.index(n): names_out.index(n) for n in names_out if n in given
                },
                scratch_shapes=[pltpu.SemaphoreType.DMA((len(moves),))] * 2 + bounces,
                compiler_params=pltpu.CompilerParams(
                    collective_id=number, has_side_effects=True, vmem_limit_bytes=VMEM_LIMIT
                ),
                name=name,
            )(*[given[n] for n in names_in]),
        )
    )


def attn_grads_kernel(
    ctx_count,
    bits,
    part,
    cols,
    hidden_ref,
    branch_ref,
    qkv_ref,
    mixed_ref,
    out_ref,
    hidden,
    branch,
    hidden_odd,
    branch_odd,
    right,
    grads,
    got,
    send,
    recv,
    pass_send,
    pass_recv,
):
    rows, width = hidden_ref.shape
    count = width // part // 2
    planes = right.shape[1] // cols
    first = qkv_ref.shape[1]
    greet(ctx_count, [1, *[1 << b for b in bits]])
    arrays = {
        "hidden_odd": hidden_odd,
        "branch_odd": branch_odd,
        "qkv_in": qkv_ref,
        "mixed_in": mixed_ref,
        "hidden": hidden,
        "branch": branch,
        "right": right,
    }
    theirs = (rows, rows)
    moves = [
        (("mixed_in", (0, rows), None), ("right", theirs, (first, mixed_ref.shape[1])), 1, ()),
        (("branch_odd", (0, rows), None), ("branch", theirs, None), 1, ()),
        (("qkv_in", (0, rows), None), ("right", theirs, (0, first)), 1, ()),
        (("hidden_odd", (0, rows), None), ("hidden", theirs, None), 1, ()),
    ]
    run = Moves(ctx_count, moves, arrays, pass_send, pass_recv)
    for given, even_side, odd_side in (
        (branch_ref, branch, branch_odd),
        (hidden_ref, hidden, hidden_odd),
    ):
        for j in range(count):
            block = slice(j * part, (j + 1) * part)
            even_side[:rows, block] = given[:, 2 * j * part : (2 * j + 1) * part]
            odd_side[:, block] = given[:, (2 * j + 1) * part : (2 * j + 2) * part]
    run.begin()
    right[:rows, :first] = qkv_ref[...]
    right[:rows, first:] = mixed_ref[...]
    number = [0]

    def copy(mask, block, plane):
        i = number[0]
        number[0] += 1
        window_of = (pl.ds(block * part, part), pl.ds(plane * cols, cols))
        return pltpu.make_async_remote_copy(
            src_ref=grads.at[window_of],
            dst_ref=got.at[window_of],
            send_sem=send.at[i],
            recv_sem=recv.at[i],
            device_id=peer(ctx_count, mask),
            device_id_type=pl.DeviceIdType.MESH,
        )

    sent, flying, left = [], {}, {}

    def send_half(plane, order, step):
        at = bits.index(order[step])
        flying[plane] = {
            j: copy(1 << order[step], j, plane) for j in left[plane] if j >> at & 1
        }
        for c in flying[plane].values():
            c.start()
        sent.extend(flying[plane].values())

    lanes = []
    late = first // cols
    for n, plane in enumerate([*range(late, planes), *range(late)]):
        lanes.append((plane, bits if n % 2 else bits[::-1]))
    for plane, order in lanes:
        run.settle(2 if plane >= late else 4)
        at = pl.ds(plane * cols, cols)
        left_side = hidden if plane < late else branch
        grads[:, at] = dot(left_side[...], right[:, at], 0, 0).astype(BF)
        left[plane] = list(range(count))
        send_half(plane, order, 0)
    for step in range(len(bits)):
        for plane, order in lanes:
            at = bits.index(order[step])
            left[plane] = [j for j in left[plane] if not j >> at & 1]
            across = pl.ds(plane * cols, cols)
            for j in left[plane]:
                flying[plane][j | 1 << at].wait_recv()
                down, other = pl.ds(j * part, part), pl.ds((j | 1 << at) * part, part)
                total = grads[down, across].astype(F32) + got[other, across].astype(F32)
                if step == len(bits) - 1:
                    out_ref[:, across] = total
                else:
                    grads[down, across] = total.astype(BF)
            if step < len(bits) - 1:
                send_half(plane, order, step + 1)
    run.finish()
    for c in sent:
        c.wait_send()


def attn_grads(number, ctx_count, bits, part, cols, hidden, branch, qkv, mixed):
    rows, width = hidden.shape
    wide = qkv.shape[1] + mixed.shape[1]
    copies = (wide // cols) * (width // part // 2)
    full = pl.BlockSpec(memory_space=pltpu.VMEM)
    return pl.pallas_call(
        functools.partial(attn_grads_kernel, ctx_count, bits, part, cols),
        out_shape=jax.ShapeDtypeStruct((part, wide), F32),
        in_specs=[full] * 4,
        out_specs=full,
        scratch_shapes=[pltpu.VMEM((2 * rows, width // 2), BF)] * 2
        + [pltpu.VMEM((rows, width // 2), BF)] * 2
        + [pltpu.VMEM((2 * rows, wide), BF)]
        + [pltpu.VMEM((width // 2, wide), BF)] * 2
        + [pltpu.SemaphoreType.DMA((copies,))] * 2
        + [pltpu.SemaphoreType.DMA((4,))] * 2,
        compiler_params=pltpu.CompilerParams(
            collective_id=number, has_side_effects=True, vmem_limit_bytes=VMEM_LIMIT
        ),
        name="attn_grads",
    )(hidden, branch, qkv, mixed)


def turn_kernel(me_ref, *refs):
    half = len(refs) // 2
    for given, made in zip(refs[:half], refs[half:]):
        made[...] = given[...]


def in_order(me, arrays, group):
    rows, width = arrays[0].shape
    part = width // group
    if part % HD:
        return [
            jnp.concatenate(
                [lax.dynamic_slice_in_dim(x, (me ^ j) * part, part, 1) for j in range(group)], axis=1
            )
            for x in arrays
        ]
    return pl.pallas_call(
        turn_kernel,
        grid_spec=pltpu.PrefetchScalarGridSpec(
            num_scalar_prefetch=1,
            grid=(group,),
            in_specs=[pl.BlockSpec((rows, part), lambda j, m: (0, m[0] ^ j))] * len(arrays),
            out_specs=[pl.BlockSpec((rows, part), lambda j, m: (0, j))] * len(arrays),
        ),
        out_shape=[jax.ShapeDtypeStruct((rows, width), x.dtype) for x in arrays],
        name="in_order",
    )(me.astype(jnp.int32).reshape(1), *arrays)


def lay_kernel(grad_ref, *out_refs):
    at = 0
    for ref in out_refs:
        for p in range(ref.shape[1]):
            ref[:, p, :] = grad_ref[:, at : at + ref.shape[2]]
            at += ref.shape[2]


def lay_out(grad, shapes):
    step = min(64, grad.shape[0])
    return pl.pallas_call(
        lay_kernel,
        grid=(grad.shape[0] // step,),
        in_specs=[pl.BlockSpec((step, grad.shape[1]), lambda i: (i, 0))],
        out_specs=[pl.BlockSpec((step, *shape[1:]), lambda i: (i, 0, 0)) for shape in shapes],
        out_shape=[jax.ShapeDtypeStruct(shape, F32) for shape in shapes],
        compiler_params=pltpu.CompilerParams(vmem_limit_bytes=VMEM_LIMIT),
        name="lay_out",
    )(grad)


def gain_kernel(ctx_count, group, gain_ref, out_ref, got, send, recv):
    greet(ctx_count, range(1, group))
    copies = []
    for j in range(1, group):
        rows = pl.ds(j * 8, 8)
        copies.append(
            pltpu.make_async_remote_copy(
                src_ref=gain_ref.at[rows],
                dst_ref=got.at[rows],
                send_sem=send.at[j],
                recv_sem=recv.at[j],
                device_id=peer(ctx_count, j),
                device_id_type=pl.DeviceIdType.MESH,
            )
        )
        copies[-1].start()
    total = gain_ref[:8]
    for j, copy in enumerate(copies):
        copy.wait_recv()
        total = total + got[(j + 1) * 8 : (j + 2) * 8]
    out_ref[...] = total
    for copy in copies:
        copy.wait_send()


def gain_sums(number, ctx_count, group, gains):
    count, part = len(gains), gains[0].shape[0] // group
    laid = jnp.stack([g.reshape(group, part) for g in gains], axis=1)
    laid = jnp.pad(laid, ((0, 0), (0, 8 - count), (0, 0))).reshape(group * 8, part)
    full = pl.BlockSpec(memory_space=pltpu.VMEM)
    total = pl.pallas_call(
        functools.partial(gain_kernel, ctx_count, group),
        out_shape=jax.ShapeDtypeStruct((8, part), F32),
        in_specs=[full],
        out_specs=full,
        scratch_shapes=[pltpu.VMEM((group * 8, part), F32)]
        + [pltpu.SemaphoreType.DMA((group,))] * 2,
        compiler_params=pltpu.CompilerParams(collective_id=number, has_side_effects=True),
        name="gain_sums",
    )(laid)
    return [total[i] for i in range(count)]


def chunks(total, size):
    return [(at, min(size, total - at)) for at in range(0, total, size)]


def experts_kernel(
    ctx_count,
    experts,
    share,
    part,
    groups,
    far_names,
    tokens_ref,
    branch_ref,
    gain_ref,
    place_ref,
    dy_run_ref,
    weight_ref,
    in_ref,
    down_ref,
    *refs,
):
    far_refs, refs = refs[: len(far_names)], refs[len(far_names) :]
    grads_in, grads_down, mlp_part, two_part = refs[:4]
    (
        win,
        wdown,
        two,
        slots_out,
        mlp_got,
        back_out,
        back_got,
        gate,
        up,
        active,
        gu,
        two_out,
        dy_out,
        two_got,
        dy_got,
        gu_got,
        active_got,
        dy_ref,
        send,
        recv,
    ) = refs[4:]
    slots, width = two.shape
    units = active.shape[1]
    room, run = slots // experts, width // experts
    arrays = dict(
        zip(far_names, far_refs),
        grads_in=grads_in,
        grads_down=grads_down,
        win=win,
        wdown=wdown,
        dy_run=dy_run_ref,
        dy=dy_ref,
        two=two,
        slots_out=slots_out,
        mlp_got=mlp_got,
        back_out=back_out,
        back_got=back_got,
        active=active,
        gu=gu,
        two_out=two_out,
        dy_out=dy_out,
        two_got=two_got,
        dy_got=dy_got,
        gu_got=gu_got,
        active_got=active_got,
        **{"in": in_ref, "down": down_ref},
    )
    runs, base = {}, 0
    for name, moves in groups.items():
        runs[name] = Moves(ctx_count, moves, arrays, send, recv, (), base)
        base += len(moves)
    greet(ctx_count, masks_of([m for moves in groups.values() for m in moves]))
    runs["load_in"].begin()
    runs["load_down"].begin()
    runs["far_in"].begin()
    runs["dy"].begin()
    dy_ref[:, run_cols(run)] = dy_run_ref[...]
    x = tokens_ref[...].astype(F32) + branch_ref[...].astype(F32)
    inverse = lax.rsqrt(jnp.mean(x * x, axis=-1, keepdims=True) + EPSILON)
    hidden = (x * inverse * gain_ref[...]).astype(BF)
    for k in range(experts)[::-1]:
        rows = slice(k * room, (k + 1) * room)
        picked = dot(place_ref[k], hidden, 1, 0).astype(BF)
        if k == 0:
            two[rows] = picked
            continue
        for i in range(experts):
            slots_out[rows, i * run : (i + 1) * run] = picked[:, (i ^ k) * run : ((i ^ k) + 1) * run]
        runs["slots"].start(k - 1)
    runs["far_down"].begin()
    runs["slots"].settle()
    for t in range(1, share):
        rows = slice((t - 1) * slots, t * slots)
        for k in range(experts):
            at = (k * share + t) * part
            two_out[rows, k * part : (k + 1) * part] = two[:, at : at + part]
    runs["share_two"].begin()
    runs["load_in"].settle()
    runs["far_in"].settle()
    weight = weight_ref[...]
    for at, size in chunks(units, 256):
        cols = slice(at, at + size)
        g = dot(two[...], win[:, cols], 1, 0)
        u = dot(two[...], win[:, units + at : units + at + size], 1, 0)
        silu = g * (1.0 / (1.0 + jnp.exp(-g)))
        active[:, cols] = (silu * u * weight).astype(BF)
        gate[:, cols] = g.astype(BF)
        up[:, cols] = u.astype(BF)
    runs["share_active"].begin()
    runs["load_down"].settle()
    runs["far_down"].settle()
    runs["slots"].finish()
    runs["dy"].settle()
    for t in range(1, share):
        rows = slice((t - 1) * slots, t * slots)
        for k in range(experts):
            at = (k * share + t) * part
            dy_out[rows, k * part : (k + 1) * part] = dy_ref[:, at : at + part]
    runs["share_dy"].begin()
    for i in range(experts):
        cols = slice(i * run, (i + 1) * run)
        slots_out[:, cols] = dot(active[...], wdown[cols], 1, 1).astype(BF)
        for k in range(1, experts):
            runs["mlp"].start(i * (experts - 1) + k - 1)
    for at, size in chunks(units, 256):
        cols = slice(at, at + size)
        grad = dot(dy_ref[...], wdown[:, cols], 1, 0) * weight
        g, u = gate[:, cols].astype(F32), up[:, cols].astype(F32)
        sigmoid = 1.0 / (1.0 + jnp.exp(-g))
        gu[:, cols] = (grad * u * sigmoid * (1.0 + g * (1.0 - sigmoid))).astype(BF)
        gu[:, units + at : units + at + size] = (grad * g * sigmoid).astype(BF)
    runs["share_gu"].begin()
    for i in range(experts):
        cols = slice(i * run, (i + 1) * run)
        back_out[:, cols] = dot(gu[...], win[cols], 1, 1).astype(BF)
        for k in range(1, experts):
            runs["back"].start(i * (experts - 1) + k - 1)
    for name in ("dy", "far_in", "far_down", "share_two", "share_dy", "share_active", "share_gu"):
        runs[name].finish()
    for k in range(experts):
        rows = slice(k * part, (k + 1) * part)
        own = slice(k * share * part, (k * share + 1) * part)
        for out, left, left_got, right, right_got in (
            (win, two, two_got, gu, gu_got),
            (wdown, dy_ref, dy_got, active, active_got),
        ):
            for at, size in chunks(right.shape[1], 512):
                cols = slice(at, at + size)
                total = dot(left[:, own], right[:, cols], 0, 0)
                if share > 1:
                    total = total + dot(left_got[:, rows], right_got[:, cols], 0, 0)
                out[rows, cols] = total.astype(BF)
        runs["out"].start(2 * k)
        runs["out"].start(2 * k + 1)
    for name, own, got, part_ref in (
        ("mlp", slots_out, mlp_got, mlp_part),
        ("back", back_out, back_got, two_part),
    ):
        runs[name].settle()
        for i in range(experts):
            total = dot(place_ref[0], own[:room, i * run : (i + 1) * run], 0, 0)
            for k in range(1, experts):
                at = (i ^ k) * run
                total = total + dot(
                    place_ref[k], got[k * room : (k + 1) * room, at : at + run], 0, 0
                )
            part_ref[:, i * run : (i + 1) * run] = total.astype(BF)
        runs[name].finish()
    runs["out"].finish()


def run_experts(
    number, ctx_count, tp_count, experts, share, part, fetched, far_moves, far, weights, tokens, *small
):
    place = small[2]
    room, rows = place.shape[1:]
    slots, width = experts * room, tokens.shape[1]
    units = weights["down"].shape[1]
    run = width // experts
    others = max(1, share - 1) * slots
    groups = {
        "dy": [
            (("dy_run", (0, slots), None), ("dy", (0, slots), ("tp", run)), -r, ())
            for r in range(1, tp_count)
        ],
        "slots": [
            (("slots_out", (k * room, room), None), ("two", (k * room, room), None), k * share, ())
            for k in range(1, experts)
        ],
        "load_in": [(("in", r, None), ("win", r, None), None, ()) for r in fetched],
        "load_down": [(("down", r, None), ("wdown", r, None), None, ()) for r in fetched],
        "far_in": [m for m in far_moves if m[1][0] == "win"],
        "far_down": [m for m in far_moves if m[1][0] == "wdown"],
    }
    for name in ("two", "dy", "active", "gu"):
        groups["share_" + name] = []
        for t in range(1, share):
            rows_at = ((t - 1) * slots, slots)
            if name in ("two", "dy"):
                source = (name + "_out", rows_at, None)
            else:
                source = (name, (0, slots), None)
            groups["share_" + name].append((source, (name + "_got", rows_at, None), t, ()))
    for name, source in (("mlp", "slots_out"), ("back", "back_out")):
        groups[name] = []
        for i in range(experts):
            for k in range(1, experts):
                at = ((k * room, room), (i * run, run))
                groups[name].append(((source, *at), (name + "_got", *at), k * share, ()))
    groups["out"] = []
    for k in range(experts):
        r = (k * part, part)
        groups["out"].append((("win", r, None), ("grads_in", r, None), None, ()))
        groups["out"].append((("wdown", r, None), ("grads_down", r, None), None, ()))
    total = sum(len(moves) for moves in groups.values())
    full = pl.BlockSpec(memory_space=pltpu.VMEM)
    any_spec = pl.BlockSpec(memory_space=pl.ANY)
    return pl.pallas_call(
        functools.partial(experts_kernel, ctx_count, experts, share, part, groups, list(far)),
        out_shape=[
            jax.ShapeDtypeStruct((experts * part, 2 * units), BF),
            jax.ShapeDtypeStruct((experts * part, units), BF),
            jax.ShapeDtypeStruct((rows, width), BF),
            jax.ShapeDtypeStruct((rows, width), BF),
        ],
        in_specs=[full] * 6 + [any_spec] * (2 + len(far)),
        out_specs=[any_spec] * 2 + [full] * 2,
        scratch_shapes=[
            pltpu.VMEM((width, 2 * units), BF),
            pltpu.VMEM((width, units), BF),
            *[pltpu.VMEM((slots, width), BF)] * 5,
            *[pltpu.VMEM((slots, units), BF)] * 3,
            pltpu.VMEM((slots, 2 * units), BF),
            *[pltpu.VMEM((others, experts * part), BF)] * 4,
            pltpu.VMEM((others, 2 * units), BF),
            pltpu.VMEM((others, units), BF),
            pltpu.VMEM((slots, width), BF),
        ]
        + [pltpu.SemaphoreType.DMA((total,))] * 2,
        compiler_params=pltpu.CompilerParams(
            collective_id=number, has_side_effects=True, vmem_limit_bytes=VMEM_LIMIT
        ),
        name="experts",
    )(tokens, *small, weights["in"], weights["down"], *far.values())


def head_cols(index):
    return pl.ds(pl.multiple_of(index * HD, HD), HD)


def scores_of(place, queries, keys, segq, idxq, segk, idxk):
    slots = dot(place, queries, 1, 0).astype(BF)
    scores = dot(slots, keys, 1, 1) * (HD**-0.5)
    allowed = (segq == segk) & (idxk <= idxq)
    scores = jnp.where(allowed, scores, MASKED)
    top = jnp.max(scores, axis=-1, keepdims=True)
    exps = jnp.exp(scores - top)
    total = jnp.sum(exps, axis=-1, keepdims=True)
    return slots, exps, 1.0 / total


def front_kernel(
    ctx_count,
    moves,
    marks,
    names_in,
    names_out,
    heads,
    part,
    normed_ref,
    gain_ref,
    cos_ref,
    sin_ref,
    place_ref,
    segq_ref,
    idxq_ref,
    gate_ref,
    segk_ref,
    idxk_ref,
    dy_ref,
    ride_ref,
    place_mlp_ref,
    *refs,
):
    experts, room, rows = place_ref.shape
    width = normed_ref.shape[1]
    wide = heads * HD
    group = width // part
    given, refs = refs[: len(names_in)], refs[len(names_in) :]
    gains_ref, hidden_ref, qkv_ref, kv_ref, mixed_ref, branch_ref, slots_ref = refs[:7]
    refs = refs[7:]
    made, (full, picked, send, recv, *bounces) = refs[: len(names_out)], refs[len(names_out) :]
    arrays = {
        "gain_own": gain_ref,
        "gains": gains_ref,
        "full": full,
        "picked": picked,
        "slots": slots_ref,
        "qkv": qkv_ref,
        "kv": kv_ref,
        **dict(zip(names_in, given)),
        **dict(zip(names_out, made)),
    }
    greet(ctx_count, masks_of(moves))
    run = Moves(ctx_count, moves, arrays, send, recv, bounces)
    gains_done, first_done, rest_done, keys_done, dy_done = marks
    run_of = dy_ref.shape[1] // experts
    for k in range(experts):
        rows_at = slice(k * room, (k + 1) * room)
        side = slots_ref if k == 0 else picked
        cols = run_cols(run_of, k)
        side[rows_at, :run_of] = dot(place_mlp_ref[k], dy_ref[:, cols], 1, 0).astype(BF)
        side[rows_at, run_of:] = dot(place_mlp_ref[k], ride_ref[...], 1, 0).astype(BF)
    run.begin(rest_done)
    gains_ref[:16] = gain_ref[...]
    run.settle(gains_done)
    for j in range(group):
        cols = slice(j * part, (j + 1) * part)
        gain = gains_ref[j * 16 : (j + 1) * 16].astype(F32)[:1, :part]
        hidden_ref[:, cols] = (normed_ref[:, cols] * gain).astype(BF)
    run.settle(first_done, gains_done)
    cos, sin = cos_ref[...], sin_ref[...]

    def project(plane):
        y = dot(hidden_ref[...], full[:, plane * wide : (plane + 1) * wide], 1, 0)
        for head in range(heads):
            cols = slice(head * HD, (head + 1) * HD)
            at = slice(plane * wide + head * HD, plane * wide + (head + 1) * HD)
            z = y[:, cols]
            qkv_ref[:, at] = (turn(z, cos, sin) if plane <= experts else z).astype(BF)

    project(experts)
    project(experts + 1)
    run.begin(keys_done)
    kv_ref[:rows] = qkv_ref[:, experts * wide :]
    run.begin()
    for plane in range(experts):
        project(plane)
    run.settle(rest_done, first_done)
    run.start(len(moves) - 1)
    run.settle(keys_done, rest_done)

    def step(i, carry):
        h, e = i // experts, i % experts
        cols = head_cols(e * heads + h)
        place = place_ref[e]
        _, exps, inv = scores_of(
            place,
            qkv_ref[:, cols],
            kv_ref[:, head_cols(h)],
            segq_ref[e],
            idxq_ref[e],
            segk_ref[...],
            idxk_ref[...],
        )
        attn = dot(exps.astype(BF), kv_ref[:, head_cols(heads + h)], 1, 0) * inv
        mixed = (attn * gate_ref[e]).astype(BF)
        mixed_ref[:, cols] = dot(place, mixed, 0, 0).astype(BF)
        return carry

    lax.fori_loop(0, heads * experts, step, 0)
    for j in range(group):
        rows_at = slice(j * part, (j + 1) * part)
        branch_ref[:, rows_at] = dot(mixed_ref[...], full[rows_at, (experts + 2) * wide :], 1, 1).astype(BF)
    run.finish()


def front(number, ctx_count, heads, part, moves, later, given, made, small):
    normed, gain_own, place = small[0], small[1], small[4]
    experts, _, rows = place.shape
    width = normed.shape[1]
    wide = heads * HD
    group = width // part
    full_wide = 2 * (experts + 1) * wide
    kv_moves = []
    order = [0]
    for bit in range(bits_of(ctx_count))[::-1]:
        for at in range(len(order)):
            target = ("kv", ((at + len(order)) * rows, rows), None)
            if at:
                source = ("kv", (at * rows, rows), None)
                kv_moves.append((source, target, 1 << bit, (source,)))
            else:
                source = ("qkv", (0, rows), (experts * wide, 2 * wide))
                kv_moves.append((source, target, 1 << bit, ()))
        order = order + order
    gains_moves, first_moves, rest_moves, dy_moves = moves
    marks = [len(gains_moves)]
    for more in (first_moves, rest_moves, kv_moves, dy_moves):
        marks.append(marks[-1] + len(more))
    whole = ("full", (0, width), None)
    landed = tuple(m[1] for m in first_moves + rest_moves if m[1][0] == "full")
    keep = [(whole, ("kept", (0, width), None), None, landed)]
    moves = gains_moves + first_moves + rest_moves + kv_moves + dy_moves + later + keep
    slots_shape = (experts * place.shape[1], width // experts + HD)
    names_in, names_out = list(given), [*made, "kept"]
    shapes_out = [*made.values(), (width, full_wide)]
    any_spec = pl.BlockSpec(memory_space=pl.ANY)
    full = pl.BlockSpec(memory_space=pltpu.VMEM)
    small_out = [
        ((16 * group, gain_own.shape[1]), BF),
        ((rows, width), BF),
        ((rows, (experts + 2) * wide), BF),
        ((ctx_count * rows, 2 * wide), BF),
        ((rows, experts * wide), BF),
        ((rows, width), BF),
        (slots_shape, BF),
    ]
    bounces = [
        pltpu.VMEM((source[1][1], (source[2] or (0, given[source[0]].shape[1]))[1]), BF)
        for source, _, mask, _ in moves
        if mask == 0
    ]
    out = pl.pallas_call(
        functools.partial(
            front_kernel, ctx_count, moves, marks, names_in, names_out, heads, part
        ),
        out_shape=[jax.ShapeDtypeStruct(*x) for x in small_out]
        + [jax.ShapeDtypeStruct(shape, BF) for shape in shapes_out],
        in_specs=[full] * len(small) + [any_spec] * len(names_in),
        out_specs=[full] * len(small_out) + [any_spec] * len(names_out),
        scratch_shapes=[pltpu.VMEM((width, full_wide), BF), pltpu.VMEM(slots_shape, BF)]
        + [pltpu.SemaphoreType.DMA((len(moves),))] * 2
        + bounces,
        compiler_params=pltpu.CompilerParams(
            collective_id=number, has_side_effects=True, vmem_limit_bytes=VMEM_LIMIT
        ),
        name="front",
    )(*small, *given.values())
    return out[: len(small_out)], dict(zip(names_out, out[len(small_out) :]))


def attend_back_kernel(
    ctx_count,
    moves,
    names_in,
    names_out,
    heads,
    part,
    tokens_ref,
    branch_ref,
    gain_ref,
    back_ref,
    dy_ref,
    gate_ref,
    qkv_ref,
    kv_ref,
    place_ref,
    segq_ref,
    idxq_ref,
    segk_ref,
    idxk_ref,
    cos_ref,
    sin_ref,
    weight_ref,
    *refs,
):
    experts, _, rows = place_ref.shape
    keys = kv_ref.shape[0]
    wide = heads * HD
    width = tokens_ref.shape[1]
    given, refs = refs[: len(names_in)], refs[len(names_in) :]
    out_ref, resid_ref, grad_branch_ref, gain_out_ref, back_one_ref = refs[:5]
    made, refs = refs[5 : 5 + len(names_out)], refs[5 + len(names_out) :]
    full, grad_ref, back_acc, dk_acc, dv_acc, total, got, send, recv, pass_send, pass_recv, load = refs
    arrays = {**dict(zip(names_in, given)), **dict(zip(names_out, made))}
    bits = range(bits_of(ctx_count))
    greet(ctx_count, sorted({*masks_of(moves), *[1 << b for b in bits]}))
    run = Moves(ctx_count, moves, arrays, send, recv)
    run.begin()
    edge = (experts + 2) * wide
    loads = []
    for i, cols in enumerate((pl.ds(edge, experts * wide), pl.ds(0, edge))):
        loads.append(pltpu.make_async_copy(weight_ref.at[:, cols], full.at[:, cols], load.at[i]))
        loads[-1].start()

    x = tokens_ref[...].astype(F32) + branch_ref[...].astype(F32)
    inverse = lax.rsqrt(jnp.mean(x * x, axis=-1, keepdims=True) + EPSILON)
    normed = x * inverse
    back = back_ref[...].astype(F32)
    gain_out_ref[...] = jnp.sum(back * normed, axis=0, keepdims=True)
    scaled = back * gain_ref[...]
    inner = jnp.mean(scaled * normed, axis=-1, keepdims=True)
    resid = dy_ref[...].astype(F32) + inverse * (scaled - normed * inner)
    resid_ref[...] = resid
    grad_branch_ref[...] = resid.astype(BF)
    loads[0].wait()
    for e in range(experts):
        cols = slice(edge + e * wide, edge + (e + 1) * wide)
        mixed = dot(grad_branch_ref[...], full[:, cols], 1, 0)
        grad_ref[:, e * wide : (e + 1) * wide] = (mixed * gate_ref[:, e : e + 1]).astype(BF)

    def head_copy(h, bit):
        size = keys >> (bit + 1)
        i = h * len(bits) + bit
        return pltpu.make_async_remote_copy(
            src_ref=total.at[h, pl.ds(size, size)],
            dst_ref=got.at[h, pl.ds(size, size)],
            send_sem=pass_send.at[i],
            recv_sem=pass_recv.at[i],
            device_id=peer(ctx_count, 1 << bit),
            device_id_type=pl.DeviceIdType.MESH,
        )

    def head_sum(h, bit):
        size = keys >> (bit + 1)
        head_copy(h, bit).wait_recv()
        mine = total[h, :size].astype(F32) + got[h, size : 2 * size].astype(F32)
        mine = mine.astype(BF)
        if bit + 1 < len(bits):
            total[h, :size] = mine
            head_copy(h, bit + 1).start()
        else:
            at = experts * wide
            out_ref[:, at + h * HD : at + (h + 1) * HD] = mine[:, :HD]
            at += wide
            out_ref[:, at + h * HD : at + (h + 1) * HD] = mine[:, HD:]

    for h in range(heads):
        dk_acc[...] = jnp.zeros_like(dk_acc)
        dv_acc[...] = jnp.zeros_like(dv_acc)

        def step(e, carry, h=h):
            cols = head_cols(e * heads + h)
            place = place_ref[e]
            k, v = kv_ref[:, h * HD : (h + 1) * HD], kv_ref[:, (heads + h) * HD : (heads + h + 1) * HD]
            slots, exps, inv = scores_of(
                place, qkv_ref[:, cols], k, segq_ref[e], idxq_ref[e], segk_ref[...], idxk_ref[...]
            )
            attn = dot(exps.astype(BF), v, 1, 0) * inv
            probs = exps * inv
            grad = dot(place, grad_ref[:, cols], 1, 0)
            delta = jnp.sum(grad * attn, axis=-1, keepdims=True)
            grad = grad.astype(BF)
            dv_acc[...] += dot(probs.astype(BF), grad, 0, 0)
            grad_probs = dot(grad, v, 1, 1)
            grad_scores = (probs * (grad_probs - delta)).astype(BF)
            dq = dot(grad_scores, k, 1, 0) * (HD**-0.5)
            dk_acc[...] += dot(grad_scores, slots, 0, 0) * (HD**-0.5)
            top = dq.astype(BF)
            low = (dq - top.astype(F32)).astype(BF)
            back_q = dot(place, top, 0, 0) + dot(place, low, 0, 0)
            out_ref[:, cols] = turn(back_q, cos_ref[:rows], -sin_ref[:rows]).astype(BF)
            return carry

        lax.fori_loop(0, experts, step, 0)
        total[h, :, :HD] = turn(dk_acc[...], cos_ref[...], -sin_ref[...]).astype(BF)
        total[h, :, HD:] = dv_acc[...].astype(BF)
        head_copy(h, 0).start()
        if h:
            head_sum(h - 1, 0)
    head_sum(heads - 1, 0)
    loads[1].wait()
    queries = experts * wide
    for j in range(width // part):
        rows_at = slice(j * part, (j + 1) * part)
        back_acc[:, rows_at] = dot(out_ref[:, :queries], full[rows_at, :queries], 1, 1)
    for bit in bits[1:]:
        for h in range(heads):
            head_sum(h, bit)
    for j in range(width // part):
        rows_at = slice(j * part, (j + 1) * part)
        keyed = dot(out_ref[:, queries:], full[rows_at, queries:edge], 1, 1)
        back_one_ref[:, rows_at] = (back_acc[:, rows_at] + keyed).astype(BF)
    for h in range(heads):
        for bit in bits:
            head_copy(h, bit).wait_send()
    run.finish()


def attend_back(number, ctx_count, heads, part, moves, given, made, weight, *small):
    tokens, qkv, kv = small[0], small[6], small[7]
    rows, width = tokens.shape
    keys = kv.shape[0]
    any_spec = pl.BlockSpec(memory_space=pl.ANY)
    full = pl.BlockSpec(memory_space=pltpu.VMEM)
    passes = heads * bits_of(ctx_count)
    small_out = [
        (qkv.shape, BF),
        ((rows, width), F32),
        ((rows, width), BF),
        ((1, width), F32),
        ((rows, width), BF),
    ]
    out = pl.pallas_call(
        functools.partial(
            attend_back_kernel, ctx_count, moves, list(given), list(made), heads, part
        ),
        out_shape=[jax.ShapeDtypeStruct(*x) for x in small_out]
        + [jax.ShapeDtypeStruct(shape, BF) for shape in made.values()],
        in_specs=[full] * len(small) + [any_spec] * (1 + len(given)),
        out_specs=[full] * len(small_out) + [any_spec] * len(made),
        scratch_shapes=[
            pltpu.VMEM(weight.shape, BF),
            pltpu.VMEM((rows, weight.shape[1] - qkv.shape[1]), BF),
            pltpu.VMEM((rows, width), F32),
        ]
        + [pltpu.VMEM((keys, HD), F32)] * 2
        + [pltpu.VMEM((heads, keys, 2 * HD), BF)] * 2
        + [pltpu.SemaphoreType.DMA((max(1, len(moves)),))] * 2
        + [pltpu.SemaphoreType.DMA((passes,))] * 2
        + [pltpu.SemaphoreType.DMA((2,))],
        compiler_params=pltpu.CompilerParams(
            collective_id=number, has_side_effects=True, vmem_limit_bytes=VMEM_LIMIT
        ),
        name="attend_back",
    )(*small, weight, *given.values())
    return out[: len(small_out)], dict(zip(made, out[len(small_out) :]))


def spread_kernel(experts, me_ref, *refs):
    blocks, (in_ref, down_ref) = refs[:experts], refs[experts:]
    units = down_ref.shape[2]
    for m in range(experts):

        @pl.when(me_ref[0] == m)
        def _():
            for e in range(experts):
                block = blocks[e ^ m]
                for c in range(2):
                    in_ref[:, e, c, :] = block[:, c * units : (c + 1) * units].astype(F32)
                down_ref[:, e, :] = block[:, 2 * units :].astype(F32)


def spread_grads(blocks, me, in_shape, down_shape):
    experts = len(blocks)
    step = min(32, in_shape[0])
    return pl.pallas_call(
        functools.partial(spread_kernel, experts),
        grid_spec=pltpu.PrefetchScalarGridSpec(
            num_scalar_prefetch=1,
            grid=(in_shape[0] // step,),
            in_specs=[pl.BlockSpec((step, blocks[0].shape[1]), lambda i, m: (i, 0))] * experts,
            out_specs=[
                pl.BlockSpec((step, *in_shape[1:]), lambda i, m: (i, 0, 0, 0)),
                pl.BlockSpec((step, *down_shape[1:]), lambda i, m: (i, 0, 0)),
            ],
        ),
        out_shape=[
            jax.ShapeDtypeStruct(in_shape, F32),
            jax.ShapeDtypeStruct(down_shape, F32),
        ],
        compiler_params=pltpu.CompilerParams(vmem_limit_bytes=VMEM_LIMIT),
        name="spread_grads",
    )(me.astype(jnp.int32).reshape(1), *blocks)


def places(routes, gates, experts, cap, room):
    rows = routes.shape[0]
    named = routes[:, :, None] == jnp.arange(experts, dtype=jnp.int32)[None, None, :]
    member = jnp.any(named, axis=1)
    gate = jnp.sum(jnp.where(named, gates[:, :, None], 0.0), axis=1)
    token = jnp.arange(rows, dtype=jnp.int32)
    earlier = (token[None, :] < token[:, None]).astype(BF)
    rank = dot(earlier, member.astype(BF), 1, 0).astype(jnp.int32)
    slot = jnp.where(member, rank, -1).T
    taken = slot[:, None, :] == jnp.arange(room, dtype=jnp.int32)[None, :, None]
    return taken, gate


def slot_sum(taken, values):
    return jnp.sum(jnp.where(taken, values, 0), axis=-1, keepdims=True)


def layer(
    counts,
    tokens,
    gain_attn,
    gain_mlp,
    w_kv,
    w_query,
    w_out_attn,
    w_in,
    w_down,
    segments,
    attn_routes,
    attn_gates,
    mlp_routes,
    mlp_gates,
    cotangent,
):
    fsdp_count, ctx_count, tp_count = counts
    group = fsdp_count * ctx_count
    me = lax.axis_index(GROUP)
    ctx_me = lax.axis_index("ctx")
    rows, width = tokens.shape[1:]
    cap = 9 * rows // 16
    room = -(-cap // 16) * 16
    part = width // group
    attn_experts = w_query.shape[1]
    experts = w_in.shape[1]
    share = group // experts
    expert_me = me // share
    hidden_units = w_down.shape[2]
    head_width = w_kv.shape[2]

    def piece(x, index, size=part, axis=1):
        return lax.dynamic_slice_in_dim(x, index * size, size, axis)

    def exchange(x, mask):
        return swap(x, mask, GROUP, group)

    def after(x, *events):
        return lax.optimization_barrier((x, *events))[0]

    high, second = group // 2, group // 4

    qkv_wide = (attn_experts + 2) * head_width
    attn_own = jnp.concatenate(
        [w_query.reshape(part, -1), w_kv.reshape(part, -1), w_out_attn.reshape(part, -1)], axis=1
    )
    attn_wide = attn_own.shape[1]
    gain_own = jnp.pad(
        jnp.concatenate([gain_attn, gain_mlp])[None, :], ((0, 15), (0, 0))
    )
    far_x, far_y = exchange(attn_own, high), exchange(attn_own, second)

    seg_row = segments[0]
    seq_total = seg_row.shape[0]
    ctx_bits = list(range(bits_of(ctx_count)))[::-1]
    key_order = [0]
    for bit in ctx_bits:
        key_order = key_order + [j | (1 << bit) for j in key_order]
    key_seg = jnp.concatenate([piece(seg_row, ctx_me ^ j, rows, 0) for j in key_order])
    key_idx = jnp.concatenate(
        [(ctx_me ^ j) * rows + jnp.arange(rows, dtype=jnp.int32) for j in key_order]
    )
    place_idx = jnp.arange(seq_total, dtype=jnp.int32)
    pos = jnp.sum(
        (seg_row[None, :] == key_seg[:, None]) & (place_idx[None, :] < key_idx[:, None]),
        axis=1,
        dtype=jnp.int32,
    ).astype(F32)
    frequency = ROPE_BASE ** (-(jnp.arange(HD // 2, dtype=F32) * 2.0) / HD)
    angles = pos[:, None] * frequency[None, :]
    cos_half, sin_half = jnp.cos(angles), jnp.sin(angles)
    cos = jnp.concatenate([cos_half, cos_half], axis=1)
    sin = jnp.concatenate([-sin_half, sin_half], axis=1)
    taken_attn, gate_attn = places(attn_routes[0], attn_gates[0], attn_experts, cap, room)
    place_attn = taken_attn.astype(BF)
    own_seg, own_idx = key_seg[:rows], key_idx[:rows]
    filled = jnp.any(taken_attn, axis=-1, keepdims=True)
    slot_seg = jnp.where(filled, slot_sum(taken_attn, own_seg), own_seg[0])
    slot_idx = jnp.where(filled, slot_sum(taken_attn, own_idx), own_idx[0])
    slot_gate = slot_sum(taken_attn, gate_attn.T[:, None, :])
    taken_mlp, gate_mlp = places(mlp_routes[0], mlp_gates[0], experts, cap, room)
    mine_first = [expert_me ^ k for k in range(experts)]
    place_mlp = jnp.concatenate([piece(taken_mlp, e, 1, 0) for e in mine_first]).astype(BF)
    tokens_rel, grad_out = in_order(me, [tokens[0], cotangent[0]], group)
    inputs = tokens_rel.astype(F32)

    def expert_rows(k):
        in_rows = piece(w_in, expert_me ^ k, 1, 1)
        down_rows = piece(w_down, expert_me ^ k, 1, 1)
        return [in_rows[:, 0, 0], in_rows[:, 0, 1], down_rows[:, 0]]

    to_send = [expert_rows(k) for k in range(experts)]

    def given_sends(ks):
        return {f"send{k}{c}": x for k in ks for c, x in enumerate(to_send[k])}

    in_cols, down_cols = (0, 2 * hidden_units), (2 * hidden_units, hidden_units)
    weight_shapes = {"in": (width, 2 * hidden_units), "down": (width, hidden_units)}

    def weight_moves(k, first, size, prefix=""):
        moves = []
        sides = (("in", (0, hidden_units)), ("in", (hidden_units, hidden_units)), ("down", None))
        for c, (name, cols) in enumerate(sides):
            base = k * share * part + first
            source = (f"send{k}{c}", (first, size), None)
            landed = (prefix + name, (base, size), cols)
            moves.append((source, landed, k * share, ()))
            for t in range(1, share):
                target = (prefix + name, (base + t * part, size), cols)
                if k:
                    moves.append((landed, target, t, (landed,)))
                else:
                    moves.append((source, target, t, ()))
        return moves

    def many_weight_moves(cuts):
        return [m for cut in cuts for m in weight_moves(*cut)]

    near = [k for k in range(1, experts) if k & (k - 1) == 0]
    far = [k for k in range(1, experts) if k & (k - 1)]
    half_part = part // 2

    normed_one, inverse_one = normalize(inputs)
    (attn_own, far_x, far_y, gain_own), to_send, tables = lax.optimization_barrier(
        (
            (attn_own, far_x, far_y, gain_own),
            to_send,
            (normed_one, cos, sin, place_attn, slot_seg, slot_idx, slot_gate, place_mlp),
        )
    )
    normed_one, cos, sin, place_attn, slot_seg, slot_idx, slot_gate, place_mlp = tables
    quarter = part // 4
    gather_moves = []
    for cols in ((0, qkv_wide), (qkv_wide, attn_wide - qkv_wide)):
        moves = []
        held = {0: [("own", 0, part, ())], high: [("far_x", 0, part, ())], second: [("far_y", 0, part, ())]}
        held[high | second] = []
        for i in (0, 2, 1, 3):
            source, mask = (("far_x", second), ("far_y", high))[i // 2]
            target = ("full", ((high | second) * part + i * quarter, quarter), cols)
            moves.append(((source, (i * quarter, quarter), cols), target, mask, ()))
            held[high | second].append(("full", i * quarter, quarter, (target,)))
        for j in (0, high, second):
            name = held[j][0][0]
            moves.append(((name, (0, part), cols), ("full", (j * part, part), cols), None, ()))
        for bit in range(bits_of(group) - 2)[::-1]:
            for j in list(held):
                there = []
                for name, at, size, needs in held[j]:
                    source = (name, (at + j * part if name == "full" else at, size), cols)
                    target = ("full", ((j | 1 << bit) * part + at, size), cols)
                    moves.append((source, target, 1 << bit, needs))
                    there.append(("full", at, size, (target,)))
                held[j | 1 << bit] = there
        gather_moves.append(moves)
    gain_moves = [
        (("gain_own", (0, 16), None), ("gains", (j * 16, 16), None), j, ())
        for j in range(1, group)
    ]
    key_row = (key_seg[None, :], key_idx[None, :])
    heads = head_width // HD
    later = weight_moves(0, 0, part) + many_weight_moves([(k, 0, half_part) for k in near])
    gate_high = gate_mlp.astype(BF)
    gate_low = (gate_mlp - gate_high.astype(F32)).astype(BF)
    gate_ride = jnp.pad(
        jnp.concatenate([gate_high, gate_low], axis=1), ((0, 0), (0, HD - 2 * experts))
    )
    dy_moves = [
        (("picked", (k * room, room), None), ("slots", (k * room, room), None), k * share, ())
        for k in range(1, experts)
    ]
    (gains, hidden_one, qkv, kv, mixed, branch, dy_got), made = front(
        1,
        ctx_count,
        heads,
        part,
        (gain_moves, *gather_moves, dy_moves),
        later,
        {
            "own": attn_own,
            "far_x": far_x,
            "far_y": far_y,
            **given_sends([0, *near]),
        },
        weight_shapes,
        (
            normed_one,
            gain_own,
            cos[:rows],
            sin[:rows],
            place_attn,
            slot_seg,
            slot_idx,
            slot_gate,
            *key_row,
            grad_out,
            gate_ride,
            place_mlp,
        ),
    )
    attn_full, weights = made["kept"], {n: made[n] for n in weight_shapes}
    gains = gains.reshape(group, 16, 2 * part)[:, 0].astype(F32)
    gain_one, gain_two = gains[:, :part].reshape(1, width), gains[:, part:].reshape(1, width)

    run = width // experts
    own_gate = jnp.tile(jnp.arange(experts) == expert_me, 2)
    slot_weight = jnp.sum(
        jnp.where(own_gate[None, :], dy_got[:, run : run + 2 * experts].astype(F32), 0.0),
        axis=1,
        keepdims=True,
    )
    grad_slots = dy_got[:, :run]

    branch_sum = lax.psum(branch, "tp")
    cuts = [(k, half_part, part - half_part) for k in near] + [(k, 0, half_part) for k in far]
    to_send, weights, _ = lax.optimization_barrier((to_send, weights, branch))
    given = {**given_sends([*near, *far]), **weights}
    weights = move("weights_two", 3, ctx_count, many_weight_moves(cuts), given, weight_shapes)
    fetched, far_moves = [], []
    for j in range(group):
        size = half_part if j // share in far else part
        if fetched and sum(fetched[-1]) == j * part:
            fetched[-1] = (fetched[-1][0], fetched[-1][1] + size)
        else:
            fetched.append((j * part, size))
    for k in far:
        far_moves += weight_moves(k, half_part, part - half_part, "w")
    grads_in, grads_down, mlp_part, back_two_part = run_experts(
        4,
        ctx_count,
        tp_count,
        experts,
        share,
        part,
        fetched,
        far_moves,
        given_sends(far),
        weights,
        tokens_rel,
        branch_sum,
        gain_two,
        place_mlp,
        grad_slots,
        slot_weight,
    )
    back_two = lax.psum(back_two_part, "tp")
    grads_got = {0: jnp.concatenate([grads_in[:part], grads_down[:part]], axis=1)}

    def grad_moves(ks):
        moves = []
        for k in ks:
            rows_at = (k * part, part)
            for name, cols in (("grads_in", in_cols), ("grads_down", down_cols)):
                target = (f"got{k}", (0, part), cols)
                moves.append(((name, rows_at, None), target, k * share, ()))
        return moves, {f"got{k}": (part, 3 * hidden_units) for k in ks}

    moves, made_shapes = grad_moves(near)
    grads_in, grads_down, _ = lax.optimization_barrier((grads_in, grads_down, back_two_part))
    given = {"grads_in": grads_in, "grads_down": grads_down}
    made = move("grads_near", 5, ctx_count, moves, given, made_shapes)
    grads_got.update({k: made[f"got{k}"] for k in near})
    grads_near = [grads_got[k] for k in near]

    moves, made_shapes = grad_moves(far)
    back_two, given, _ = lax.optimization_barrier((back_two, given, grads_near))
    (grad_qkv, grad_resid, grad_branch, gain_two_grad, back_one_part), made = attend_back(
        6,
        ctx_count,
        heads,
        part,
        moves,
        given,
        made_shapes,
        attn_full,
        tokens_rel,
        branch_sum,
        gain_two,
        back_two,
        grad_out,
        gate_attn,
        qkv,
        kv,
        place_attn,
        slot_seg,
        slot_idx,
        *key_row,
        cos,
        sin,
    )
    grads_got.update({k: made[f"got{k}"] for k in far})
    mlp_total = lax.psum(mlp_part, "tp").astype(F32)
    back_one = lax.psum(back_one_part, "tp").astype(F32)
    grad_input_norm, gain_one_grad = norm_back(back_one, normed_one, inverse_one, gain_one)
    grad_tokens = (grad_resid + grad_input_norm).astype(BF)

    resid = inputs + branch_sum.astype(F32)
    output, grad_tokens = in_order(me, [(resid + mlp_total).astype(BF), grad_tokens], group)

    upper = list(range(1, bits_of(group)))
    grad_attnw = attn_grads(
        7, ctx_count, upper, part, head_width, hidden_one, grad_branch, grad_qkv, mixed
    )
    grad_query_w, grad_kv_w, grad_out_w = lay_out(
        grad_attnw, (w_query.shape, w_kv.shape, w_out_attn.shape)
    )
    gain_grads = gain_sums(9, ctx_count, group, [gain_one_grad, gain_two_grad[0]])

    return (
        output[None],
        grad_tokens[None],
        *gain_grads,
        grad_kv_w,
        grad_query_w,
        grad_out_w,
        *spread_grads([grads_got[k] for k in range(experts)], expert_me, w_in.shape, w_down.shape),
    )


def solution(mesh):
    rows = P("fsdp", "ctx", None)
    weight = P(GROUP, None, "tp")
    weight_in = P(GROUP, None, None, "tp")
    return jax.shard_map(
        functools.partial(layer, tuple(mesh.shape[a] for a in ("fsdp", "ctx", "tp"))),
        mesh=mesh,
        in_specs=(
            rows,
            P(GROUP),
            P(GROUP),
            weight,
            weight,
            weight,
            weight_in,
            weight,
            P("fsdp", None),
            rows,
            rows,
            rows,
            rows,
            rows,
        ),
        out_specs=(rows, rows, P(GROUP), P(GROUP), weight, weight, weight, weight_in, weight),
        check_vma=False,
    )
```

```python
import functools

import jax
import jax.numpy as jnp
from jax import lax
from jax.experimental import pallas as pl
from jax.experimental.pallas import tpu as pltpu
from jax.sharding import PartitionSpec as P

HD = 128
EPSILON = 1e-06
ROPE_BASE = 10000.0
MASKED = -1e30
FSDP, CTX, TP = "fsdp", "ctx", "tp"
GROUP = (FSDP, CTX)
FULL = "full"
BF = jnp.bfloat16
F32 = jnp.float32
VMEM_LIMIT = 56 * 1024 * 1024


def normalize(tensor):
    inverse = lax.rsqrt(jnp.mean(tensor * tensor, axis=-1, keepdims=True) + EPSILON)
    return (tensor * inverse, inverse)


def norm_back(grad_in, normed, inverse, gain_vec):
    scaled = grad_in * gain_vec
    inner_mean = jnp.mean(scaled * normed, axis=-1, keepdims=True)
    return (inverse * (scaled - normed * inner_mean), jnp.sum(grad_in * normed, axis=0))


def dot(a, b, ca, cb):
    return lax.dot_general(a, b, (((ca,), (cb,)), ((), ())), preferred_element_type=F32)


def turn(x, cos, sin):
    return x * cos + pltpu.roll(x, HD // 2, 1) * sin


def swap(x, mask, axes, count):
    return lax.ppermute(x, axes, [(i, i ^ mask) for i in range(count)])


def bits_of(count):
    return count.bit_length() - 1


def flip(value, mask):
    step = 1
    while step <= mask:
        if mask & step:
            value = value + step - 2 * step * ((value // step) % 2)
        step *= 2
    return value


def peer(ctx_count, mask):
    if mask < 0:
        return {TP: flip(lax.axis_index(TP), -mask)}
    return {
        FSDP: flip(lax.axis_index(FSDP), mask // ctx_count),
        CTX: flip(lax.axis_index(CTX), mask % ctx_count),
    }


def greet(ctx_count, masks):
    barrier = pltpu.get_barrier_semaphore()
    for mask in masks:
        pl.semaphore_signal(
            barrier, inc=1, device_id=peer(ctx_count, mask), device_id_type=pl.DeviceIdType.MESH
        )
    pl.semaphore_wait(barrier, len(masks))


def run_cols(size, flips=0):
    return pl.ds(pl.multiple_of(flip(lax.axis_index(TP), flips) * size, size), size)


def window(ref, rows, cols):
    if rows[0] == TP:
        return ref.at[run_cols(rows[1], rows[2])]
    if cols is None:
        return ref.at[pl.ds(rows[0], rows[1])]
    if cols[0] == TP:
        return ref.at[pl.ds(rows[0], rows[1]), run_cols(*cols[1:3])]
    return ref.at[pl.ds(rows[0], rows[1]), pl.ds(cols[0], cols[1])]


def gain_of(gains_ref, which, part):
    rows = gains_ref[...].astype(F32)
    cols = slice(which * part, (which + 1) * part)
    return jnp.concatenate([rows[at : at + 1, cols] for at in range(0, rows.shape[0], 16)], axis=1)


class Moves:
    def __init__(self, ctx_count, moves, arrays, send, recv, bounces=(), base=0):
        self.moves = moves
        self.onward = {}
        bounces = list(bounces)
        self.copies = []
        self.place = {m[1]: i for i, m in enumerate(moves)}
        self.started, self.came, self.sent = set(), set(), set()
        for at, (source, target, mask, _) in enumerate(moves):
            i = base + at
            src = window(arrays[source[0]], *source[1:])
            dst = window(arrays[target[0]], *target[1:])
            if mask:
                copy = pltpu.make_async_remote_copy(
                    src_ref=src,
                    dst_ref=dst,
                    send_sem=send.at[i],
                    recv_sem=recv.at[i],
                    device_id=peer(ctx_count, mask),
                    device_id_type=pl.DeviceIdType.MESH,
                )
            elif mask is None:
                copy = pltpu.make_async_copy(src, dst, recv.at[i])
            else:
                bounce = bounces.pop(0)
                copy = pltpu.make_async_copy(src, bounce, recv.at[i])
                self.onward[at] = pltpu.make_async_copy(bounce, dst, send.at[i])
            self.copies.append(copy)

    def start(self, i):
        if i not in self.started:
            self.started.add(i)
            self.copies[i].start()

    def begin(self, count=None):
        for i, move in enumerate(self.moves[:count]):
            if not move[3]:
                self.start(i)

    def await_one(self, i):
        if i not in self.came:
            self.came.add(i)
            if i in self.onward:
                self.copies[i].wait()
                self.onward[i].start()
            elif self.moves[i][2] is None:
                self.copies[i].wait()
            else:
                self.copies[i].wait_recv()

    def await_sent(self, i):
        if i not in self.sent:
            self.sent.add(i)
            self.copies[i].wait_send()

    def settle(self, count=None, first=0):
        count = len(self.moves) if count is None else count
        for i in range(first, count):
            if i in self.onward:
                self.await_one(i)
        for i in range(first, count):
            for target in self.moves[i][3]:
                self.await_one(self.place[target])
            self.start(i)
        for i in range(first, count):
            self.await_one(i)

    def finish(self):
        self.settle()
        for i in range(len(self.moves)):
            if i in self.onward:
                self.onward[i].wait()
            elif self.moves[i][2] is not None:
                self.await_sent(i)


def masks_of(moves):
    return sorted({move[2] for move in moves if move[2]})


def move_kernel(ctx_count, moves, names_in, names_out, *refs):
    count = len(names_in) + len(names_out)
    refs, (send, recv, *bounces) = refs[:count], refs[count:]
    arrays = dict(zip(names_in, refs))
    arrays.update(zip(names_out, refs[len(names_in) :]))
    greet(ctx_count, masks_of(moves))
    run = Moves(ctx_count, moves, arrays, send, recv, bounces)
    run.begin()
    run.finish()


def move(name, number, ctx_count, moves, given, made):
    names_in = [n for n in given if n not in made] + [n for n in given if n in made]
    plain = [n for n in names_in if n not in made]
    names_out = list(made)
    any_spec = pl.BlockSpec(memory_space=pl.ANY)
    bounces = [
        pltpu.VMEM((source[1][1], (source[2] or (0, given[source[0]].shape[1]))[1]), BF)
        for source, _, mask, _ in moves
        if not mask
    ]
    return dict(
        zip(
            names_out,
            pl.pallas_call(
                functools.partial(
                    move_kernel,
                    ctx_count,
                    moves,
                    plain + ["old_" + n for n in names_in[len(plain) :]],
                    names_out,
                ),
                out_shape=[jax.ShapeDtypeStruct(shape, BF) for shape in made.values()],
                in_specs=[any_spec] * len(names_in),
                out_specs=[any_spec] * len(names_out),
                input_output_aliases={
                    names_in.index(n): names_out.index(n) for n in names_out if n in given
                },
                scratch_shapes=[pltpu.SemaphoreType.DMA((len(moves),))] * 2 + bounces,
                compiler_params=pltpu.CompilerParams(
                    collective_id=number, has_side_effects=True, vmem_limit_bytes=VMEM_LIMIT
                ),
                name=name,
            )(*[given[n] for n in names_in]),
        )
    )


def attn_grads_kernel(
    ctx_count,
    groups,
    bits,
    part,
    cols,
    hidden_ref,
    branch_ref,
    qkv_ref,
    mixed_ref,
    back_ref,
    tokens_ref,
    gain_ref,
    resid_ref,
    gain_two_ref,
    mlp_ref,
    place_ref,
    out_ref,
    grad_tokens_ref,
    gain_out_ref,
    mlp_sum_ref,
    mlp_got,
    back_got,
    back_sum,
    gain_send,
    gain_got,
    hidden,
    branch,
    hidden_odd,
    branch_odd,
    right,
    grads,
    got,
    send,
    recv,
    pass_send,
    pass_recv,
):
    rows, width = hidden_ref.shape
    count = width // part // 2
    planes = right.shape[1] // cols
    first = qkv_ref.shape[1]
    group = width // part
    run_rows = groups["spread"][0][0][1][1]
    greet(ctx_count, masks_of([m for moves in groups.values() for m in moves]))
    arrays = dict(
        back=back_ref,
        back_got=back_got,
        back_sum=back_sum,
        mlp=mlp_ref,
        mlp_got=mlp_got,
        mlp_sum=mlp_sum_ref,
        gain_send=gain_send,
        gain_got=gain_got,
        hidden_odd=hidden_odd,
        branch_odd=branch_odd,
        qkv_in=qkv_ref,
        mixed_in=mixed_ref,
        hidden=hidden,
        branch=branch,
        right=right,
    )
    runs, base = {}, 0
    for name, moves in groups.items():
        if name != "sums":
            runs[name] = Moves(ctx_count, moves, arrays, pass_send, pass_recv, (), base)
        base += len(moves)
    run = runs["share"]
    runs["reduce"].begin()
    runs["mlp"].begin()
    for given, even_side, odd_side in (
        (branch_ref, branch, branch_odd),
        (hidden_ref, hidden, hidden_odd),
    ):
        for j in range(count):
            block = slice(j * part, (j + 1) * part)
            even_side[:rows, block] = given[:, 2 * j * part : (2 * j + 1) * part]
            odd_side[:, block] = given[:, (2 * j + 1) * part : (2 * j + 2) * part]
    run.begin()
    right[:rows, :first] = qkv_ref[...]
    right[:rows, first:] = mixed_ref[...]
    number = [0]

    def copy(mask, block, plane):
        i = number[0]
        number[0] += 1
        window_of = (pl.ds(block * part, part), pl.ds(plane * cols, cols))
        return pltpu.make_async_remote_copy(
            src_ref=grads.at[window_of],
            dst_ref=got.at[window_of],
            send_sem=send.at[i],
            recv_sem=recv.at[i],
            device_id=peer(ctx_count, mask),
            device_id_type=pl.DeviceIdType.MESH,
        )

    sent, flying, left = [], {}, {}

    def send_half(plane, order, step):
        at = bits.index(order[step])
        flying[plane] = {
            j: copy(1 << order[step], j, plane) for j in left[plane] if j >> at & 1
        }
        for c in flying[plane].values():
            c.start()
        sent.extend(flying[plane].values())

    lanes = []
    late = first // cols
    for n, plane in enumerate([*range(late, planes), *range(late)]):
        lanes.append((plane, bits if n % 2 else bits[::-1]))
    for plane, order in lanes:
        run.settle(2 if plane >= late else 4)
        at = pl.ds(plane * cols, cols)
        left_side = hidden if plane < late else branch
        grads[:, at] = dot(left_side[...], right[:, at], 0, 0).astype(BF)
        left[plane] = list(range(count))
        send_half(plane, order, 0)
    def sum_back():
        runs["reduce"].settle()
        own = run_cols(run_rows)
        total = back_ref[own].astype(F32)
        for r in range(len(groups["reduce"])):
            total = total + back_got[r * run_rows : (r + 1) * run_rows].astype(F32)
        back_sum[own] = total.astype(BF)
        runs["spread"].begin()

    def sum_mlp():
        runs["mlp"].settle()
        room = mlp_ref.shape[0] // place_ref.shape[0]
        total = dot(place_ref[0], mlp_ref[:room], 0, 0)
        for k in range(1, place_ref.shape[0]):
            total = total + dot(place_ref[k], mlp_got[k * room : (k + 1) * room], 0, 0)
        mlp_sum_ref[:, run_cols(mlp_ref.shape[1])] = total.astype(BF)
        runs["mlp_spread"].begin()

    def norm_back():
        runs["spread"].settle()
        x = tokens_ref[...].astype(F32)
        inverse = lax.rsqrt(jnp.mean(x * x, axis=-1, keepdims=True) + EPSILON)
        normed = x * inverse
        back = back_sum[...].astype(F32)
        gain_grad = jnp.sum(back * normed, axis=0, keepdims=True)
        scaled = back * gain_of(gain_ref, 0, part)
        inner = jnp.mean(scaled * normed, axis=-1, keepdims=True)
        grad_tokens_ref[...] = (resid_ref[...] + inverse * (scaled - normed * inner)).astype(BF)
        gain_send[...] = jnp.zeros_like(gain_send)
        for j in range(group):
            block = slice(j * part, (j + 1) * part)
            gain_send[j * 8 : j * 8 + 1] = gain_grad[:, block]
            gain_send[j * 8 + 1 : j * 8 + 2] = gain_two_ref[:, block]
        runs["gains"].begin()

    for step in range(len(bits)):
        for n, (plane, order) in enumerate(lanes):
            if step == 0 and n == len(lanes) // 2:
                sum_mlp()
                sum_back()
            if step == 0 and n == len(lanes) - 1:
                norm_back()
            at = bits.index(order[step])
            left[plane] = [j for j in left[plane] if not j >> at & 1]
            across = pl.ds(plane * cols, cols)
            for j in left[plane]:
                flying[plane][j | 1 << at].wait_recv()
                down, other = pl.ds(j * part, part), pl.ds((j | 1 << at) * part, part)
                total = grads[down, across].astype(F32) + got[other, across].astype(F32)
                if step == len(bits) - 1:
                    out_ref[:, across] = total
                else:
                    grads[down, across] = total.astype(BF)
            if step < len(bits) - 1:
                send_half(plane, order, step + 1)
    runs["gains"].settle()
    gains = gain_send[:8]
    for j in range(1, group):
        gains = gains + gain_got[j * 8 : (j + 1) * 8]
    gain_out_ref[...] = gains
    for moves in runs.values():
        moves.finish()
    for c in sent:
        c.wait_send()


def attn_grads(number, ctx_count, tp_count, bits, part, cols, hidden, branch, qkv, mixed, *others):
    rows, width = hidden.shape
    group = width // part
    first = qkv.shape[1]
    theirs = (rows, rows)
    run_rows = rows // tp_count
    mlp, place = others[-2:]
    experts, room = place.shape[:2]
    run = mlp.shape[1]
    groups = {
        "mlp": [
            (("mlp", (k * room, room), None), ("mlp_got", (k * room, room), None), k * group // experts, ())
            for k in range(1, experts)
        ],
        "mlp_spread": [
            (("mlp_sum", (0, rows), (TP, run)), ("mlp_sum", (0, rows), (TP, run, 0, r)), -r, ())
            for r in range(1, tp_count)
        ],
        "reduce": [
            (("back", (TP, run_rows, r), None), ("back_got", ((r - 1) * run_rows, run_rows), None), -r, ())
            for r in range(1, tp_count)
        ],
        "spread": [
            (("back_sum", (TP, run_rows, 0), None), ("back_sum", (TP, run_rows, 0), r), -r, ())
            for r in range(1, tp_count)
        ],
        "gains": [
            (("gain_send", (j * 8, 8), None), ("gain_got", (j * 8, 8), None), j, ())
            for j in range(1, group)
        ],
        "share": [
            (("mixed_in", (0, rows), None), ("right", theirs, (first, mixed.shape[1])), 1, ()),
            (("branch_odd", (0, rows), None), ("branch", theirs, None), 1, ()),
            (("qkv_in", (0, rows), None), ("right", theirs, (0, first)), 1, ()),
            (("hidden_odd", (0, rows), None), ("hidden", theirs, None), 1, ()),
        ],
        "sums": [((), (), 1 << b, ()) for b in bits],
    }
    wide = qkv.shape[1] + mixed.shape[1]
    copies = (wide // cols) * (width // part // 2)
    passes = sum(len(moves) for moves in groups.values())
    full = pl.BlockSpec(memory_space=pltpu.VMEM)
    return pl.pallas_call(
        functools.partial(attn_grads_kernel, ctx_count, groups, bits, part, cols),
        out_shape=[
            jax.ShapeDtypeStruct((part, wide), F32),
            jax.ShapeDtypeStruct((rows, width), BF),
            jax.ShapeDtypeStruct((8, part), F32),
            jax.ShapeDtypeStruct((rows, width), BF),
        ],
        in_specs=[full] * (4 + len(others)),
        out_specs=[full] * 4,
        scratch_shapes=[
            pltpu.VMEM(mlp.shape, BF),
            pltpu.VMEM(((tp_count - 1) * run_rows, width), BF),
            pltpu.VMEM((rows, width), BF),
            *[pltpu.VMEM((group * 8, part), F32)] * 2,
        ]
        + [pltpu.VMEM((2 * rows, width // 2), BF)] * 2
        + [pltpu.VMEM((rows, width // 2), BF)] * 2
        + [pltpu.VMEM((2 * rows, wide), BF)]
        + [pltpu.VMEM((width // 2, wide), BF)] * 2
        + [pltpu.SemaphoreType.DMA((copies,))] * 2
        + [pltpu.SemaphoreType.DMA((passes,))] * 2,
        compiler_params=pltpu.CompilerParams(
            collective_id=number, has_side_effects=True, vmem_limit_bytes=VMEM_LIMIT
        ),
        name="attn_grads",
    )(hidden, branch, qkv, mixed, *others)


def turn_kernel(me_ref, *refs):
    half = len(refs) // 2
    for given, made in zip(refs[:half], refs[half:]):
        made[...] = given[...]


def in_order(me, arrays, group):
    rows, width = arrays[0].shape
    part = width // group
    if part % HD:
        return [
            jnp.concatenate(
                [lax.dynamic_slice_in_dim(x, (me ^ j) * part, part, 1) for j in range(group)], axis=1
            )
            for x in arrays
        ]
    return pl.pallas_call(
        turn_kernel,
        grid_spec=pltpu.PrefetchScalarGridSpec(
            num_scalar_prefetch=1,
            grid=(group,),
            in_specs=[pl.BlockSpec((rows, part), lambda j, m: (0, m[0] ^ j))] * len(arrays),
            out_specs=[pl.BlockSpec((rows, part), lambda j, m: (0, j))] * len(arrays),
        ),
        out_shape=[jax.ShapeDtypeStruct((rows, width), x.dtype) for x in arrays],
        name="in_order",
    )(me.astype(jnp.int32).reshape(1), *arrays)


def last_kernel(group, me_ref, *refs):
    tokens, branch, mlp, grad, out_ref, grad_out_ref = refs
    width = tokens.shape[1]
    part = width // group
    total = (tokens[...].astype(F32) + branch[...].astype(F32) + mlp[...].astype(F32)).astype(BF)
    for j in range(group):
        cols = slice(j * part, (j + 1) * part)
        at = pl.ds(pl.multiple_of((me_ref[0] ^ j) * part, part), part)
        out_ref[:, at] = total[:, cols]
        grad_out_ref[:, at] = grad[:, cols]


def last(me, group, tokens, branch, mlp, grad):
    rows, width = tokens.shape
    if width // group % HD:
        total = tokens.astype(F32) + branch.astype(F32) + mlp.astype(F32)
        return in_order(me, [total.astype(BF), grad], group)
    whole = pl.BlockSpec((rows, width), lambda i, m: (0, 0))
    return pl.pallas_call(
        functools.partial(last_kernel, group),
        grid_spec=pltpu.PrefetchScalarGridSpec(
            num_scalar_prefetch=1, grid=(1,), in_specs=[whole] * 4, out_specs=[whole] * 2
        ),
        out_shape=[jax.ShapeDtypeStruct((rows, width), BF)] * 2,
        compiler_params=pltpu.CompilerParams(vmem_limit_bytes=VMEM_LIMIT),
        name="last",
    )(me.astype(jnp.int32).reshape(1), tokens, branch, mlp, grad)


def lay_kernel(grad_ref, *out_refs):
    at = 0
    for ref in out_refs:
        for p in range(ref.shape[1]):
            ref[:, p, :] = grad_ref[:, at : at + ref.shape[2]]
            at += ref.shape[2]


def lay_out(grad, shapes):
    step = min(64, grad.shape[0])
    return pl.pallas_call(
        lay_kernel,
        grid=(grad.shape[0] // step,),
        in_specs=[pl.BlockSpec((step, grad.shape[1]), lambda i: (i, 0))],
        out_specs=[pl.BlockSpec((step, *shape[1:]), lambda i: (i, 0, 0)) for shape in shapes],
        out_shape=[jax.ShapeDtypeStruct(shape, F32) for shape in shapes],
        compiler_params=pltpu.CompilerParams(vmem_limit_bytes=VMEM_LIMIT),
        name="lay_out",
    )(grad)


def chunks(total, size):
    return [(at, min(size, total - at)) for at in range(0, total, size)]


def experts_kernel(
    ctx_count,
    experts,
    share,
    part,
    groups,
    far_names,
    tokens_ref,
    branch_ref,
    gain_ref,
    place_ref,
    dy_run_ref,
    rides_ref,
    in_ref,
    down_ref,
    *refs,
):
    far_refs, refs = refs[: len(far_names)], refs[len(far_names) :]
    grads_in, grads_down, mlp_ref, two_part = refs[:4]
    (
        win,
        wdown,
        two,
        slots_out,
        back_out,
        back_got,
        active,
        gu,
        two_out,
        dy_out,
        two_got,
        dy_got,
        gu_got,
        active_got,
        dy_ref,
        send,
        recv,
    ) = refs[4:]
    slots, width = two.shape
    units = active.shape[1]
    room, run = slots // experts, width // experts
    arrays = dict(
        zip(far_names, far_refs),
        gin=grads_in,
        gdown=grads_down,
        win=win,
        wdown=wdown,
        dy_run=dy_run_ref,
        dy=dy_ref,
        two=two,
        slots_out=slots_out,
        back_out=back_out,
        back_got=back_got,
        active=active,
        gu=gu,
        two_out=two_out,
        dy_out=dy_out,
        two_got=two_got,
        dy_got=dy_got,
        gu_got=gu_got,
        active_got=active_got,
        down=down_ref,
        **{"in": in_ref},
    )
    runs, base = {}, 0
    for name, moves in groups.items():
        runs[name] = Moves(ctx_count, moves, arrays, send, recv, (), base)
        base += len(moves)
    greet(ctx_count, masks_of([m for moves in groups.values() for m in moves]))
    stages = list_stages(experts)
    runs["load", "in"].begin()
    runs["load", "down"].begin()
    runs["far", "in"].begin()
    runs["far", "down"].begin()
    for stage in range(len(stages)):
        runs["dy", stage].begin()
    dy_ref[:, run_cols(run)] = dy_run_ref[...]
    x = tokens_ref[...].astype(F32) + branch_ref[...].astype(F32)
    inverse = lax.rsqrt(jnp.mean(x * x, axis=-1, keepdims=True) + EPSILON)
    hidden = (x * inverse * gain_of(gain_ref, 1, part)).astype(BF)
    mine = flip(lax.axis_index(FSDP), 0) * ctx_count + lax.axis_index(CTX)
    lane = lax.broadcasted_iota(jnp.int32, (1, HD), 1)
    chosen = (lane % experts == mine // share) & (lane < 2 * experts)
    weights = jnp.sum(jnp.where(chosen, rides_ref[...].astype(F32), 0.0), axis=1, keepdims=True)
    for k in [*range(1, experts), 0]:
        rows = slice(k * room, (k + 1) * room)
        picked = dot(place_ref[k], hidden, 1, 0).astype(BF)
        if k == 0:
            two[rows] = picked
            continue
        for i in range(experts):
            slots_out[rows, i * run : (i + 1) * run] = picked[:, (i ^ k) * run : ((i ^ k) + 1) * run]
        runs["slots"].start(k - 1)
    for move in ("load", "far"):
        for name in ("in", "down"):
            runs[move, name].settle()
    for stage, ks in enumerate(stages):
        rows = slice(ks[0] * room, (ks[-1] + 1) * room)
        for k in ks:
            if k:
                runs["slots"].await_one(k - 1)
        runs["dy", stage].settle()
        for t in range(1, share):
            out_rows = slice((t - 1) * slots + rows.start, (t - 1) * slots + rows.stop)
            for k in range(experts):
                block = slice(k * part, (k + 1) * part)
                at = slice((k * share + t) * part, (k * share + t + 1) * part)
                two_out[out_rows, block] = two[rows, at]
                dy_out[out_rows, block] = dy_ref[rows, at]
        runs["two", stage, 0].begin()
        runs["dy", stage, 0].begin()
        two_rows, grad_rows = two[rows], dy_ref[rows]
        weight = weights[rows]
        for at, size in chunks(units, 256):
            cols = slice(at, at + size)
            g = dot(two_rows, win[:, cols], 1, 0)
            u = dot(two_rows, win[:, units + at : units + at + size], 1, 0)
            sigmoid = 1.0 / (1.0 + jnp.exp(-g))
            silu = g * sigmoid
            active[rows, cols] = (silu * u * weight).astype(BF)
            grad = dot(grad_rows, wdown[:, cols], 1, 0) * weight
            gu[rows, cols] = (grad * u * (sigmoid * (1.0 + g * (1.0 - sigmoid)))).astype(BF)
            gu[rows, units + at : units + at + size] = (grad * silu).astype(BF)
        runs["active", stage, 0].begin()
        runs["gu", stage, 0].begin()
        for i in range(experts):
            cols = slice(i * run, (i + 1) * run)
            back_out[rows, cols] = dot(gu[rows], win[cols], 1, 1).astype(BF)
        for k in ks:
            if k:
                runs["back"].start(k - 1)
        for i in range(experts):
            cols = slice(i * run, (i + 1) * run)
            out = dot(active[rows], wdown[cols], 1, 1).astype(BF)
            for k in ks:
                at = slice(k * room - rows.start, (k + 1) * room - rows.start)
                turned = slice((i ^ k) * run, ((i ^ k) + 1) * run)
                mlp_ref[k * room : (k + 1) * room, turned] = out[at]
    for name in groups:
        if isinstance(name, tuple) and name[0] != "load":
            runs[name].finish()
    for k in range(experts):
        rows = slice(k * part, (k + 1) * part)
        own = slice(k * share * part, (k * share + 1) * part)
        for out, left, left_got, right, right_got in (
            (win, two, two_got, gu, gu_got),
            (wdown, dy_ref, dy_got, active, active_got),
        ):
            for at, size in chunks(right.shape[1], 512):
                cols = slice(at, at + size)
                total = dot(left[:, own], right[:, cols], 0, 0)
                if share > 1:
                    total = total + dot(left_got[:, rows], right_got[:, cols], 0, 0)
                out[rows, cols] = total.astype(BF)
        runs["out"].start(2 * k)
        runs["out"].start(2 * k + 1)
    runs["back"].settle()
    for i in range(experts):
        cols = slice(i * run, (i + 1) * run)
        total = dot(place_ref[0], back_out[:room, cols], 0, 0)
        for k in range(1, experts):
            at = slice((i ^ k) * run, ((i ^ k) + 1) * run)
            total = total + dot(place_ref[k], back_got[k * room : (k + 1) * room, at], 0, 0)
        two_part[:, cols] = total.astype(BF)
    runs["back"].finish()
    runs["out"].finish()
    runs["slots"].finish()


def list_stages(experts):
    return [[0], list(range(1, experts - 1)), [experts - 1]]


def run_experts(
    number, ctx_count, tp_count, experts, share, part, fetched, far_moves, far, weights, tokens, *small
):
    place = small[2]
    room, rows = place.shape[1:]
    slots, width = experts * room, tokens.shape[1]
    units = weights["down"].shape[1]
    run = width // experts
    others = max(1, share - 1) * slots
    groups = {
        "slots": [
            (("slots_out", (k * room, room), None), ("two", (k * room, room), None), k * share, ())
            for k in range(1, experts)
        ],
        ("load", "in"): [(("in", r, None), ("win", r, None), None, ()) for r in fetched],
        ("load", "down"): [(("down", r, None), ("wdown", r, None), None, ()) for r in fetched],
        ("far", "in"): [m for m in far_moves if m[1][0] == "win"],
        ("far", "down"): [m for m in far_moves if m[1][0] == "wdown"],
    }
    for stage, ks in enumerate(list_stages(experts)):
        mine = (ks[0] * room, len(ks) * room)
        groups["dy", stage] = [
            (("dy_run", mine, None), ("dy", mine, (TP, run)), -r, ()) for r in range(1, tp_count)
        ]
        for name in ("two", "dy", "active", "gu"):
            groups[name, stage, 0] = []
            for t in range(1, share):
                rows_at = ((t - 1) * slots + mine[0], mine[1])
                source = (name + "_out", rows_at, None) if name in ("two", "dy") else (name, mine, None)
                target = (name + "_got", rows_at, None)
                groups[name, stage, 0].append((source, target, t, ()))
    groups["back"] = [
        (("back_out", (k * room, room), None), ("back_got", (k * room, room), None), k * share, ())
        for k in range(1, experts)
    ]
    groups["out"] = []
    for k in range(experts):
        r = (k * part, part)
        groups["out"].append((("win", r, None), ("gin", r, None), None, ()))
        groups["out"].append((("wdown", r, None), ("gdown", r, None), None, ()))
    total = sum(len(moves) for moves in groups.values())
    full = pl.BlockSpec(memory_space=pltpu.VMEM)
    any_spec = pl.BlockSpec(memory_space=pl.ANY)
    return pl.pallas_call(
        functools.partial(experts_kernel, ctx_count, experts, share, part, groups, list(far)),
        out_shape=[
            jax.ShapeDtypeStruct((experts * part, 2 * units), BF),
            jax.ShapeDtypeStruct((experts * part, units), BF),
            jax.ShapeDtypeStruct((slots, width), BF),
            jax.ShapeDtypeStruct((rows, width), BF),
        ],
        in_specs=[full] * 6 + [any_spec] * (2 + len(far)),
        out_specs=[any_spec] * 2 + [full] * 2,
        scratch_shapes=[
            pltpu.VMEM((width, 2 * units), BF),
            pltpu.VMEM((width, units), BF),
            *[pltpu.VMEM((slots, width), BF)] * 4,
            pltpu.VMEM((slots, units), BF),
            pltpu.VMEM((slots, 2 * units), BF),
            *[pltpu.VMEM((others, experts * part), BF)] * 4,
            pltpu.VMEM((others, 2 * units), BF),
            pltpu.VMEM((others, units), BF),
            pltpu.VMEM((slots, width), BF),
        ]
        + [pltpu.SemaphoreType.DMA((total,))] * 2,
        compiler_params=pltpu.CompilerParams(
            collective_id=number, has_side_effects=True, vmem_limit_bytes=VMEM_LIMIT
        ),
        name="experts",
    )(tokens, *small, weights["in"], weights["down"], *far.values())


def head_cols(index):
    return pl.ds(pl.multiple_of(index * HD, HD), HD)


def slot_table(place_ref, about_ref, out):
    experts = place_ref.shape[0]
    for e in range(experts):
        found = dot(place_ref[e], about_ref[...], 1, 0)
        filled = jnp.sum(place_ref[e].astype(F32), axis=1, keepdims=True)
        found = jnp.where(filled > 0, found, about_ref[:1].astype(F32))
        out[e, :, 0:1] = found[:, 0:1]
        out[e, :, 1:2] = found[:, 1:2] * 32.0 + found[:, 2:3]
        gate = found[:, 3 + e : 4 + e] + found[:, 3 + experts + e : 4 + experts + e]
        out[e, :, 2:3] = gate * filled


def scores_of(place, queries, keys, info, segk, idxk):
    segq, idxq = info[:, 0:1], info[:, 1:2]
    slots = dot(place, queries, 1, 0).astype(BF)
    scores = dot(slots, keys, 1, 1) * (HD**-0.5)
    allowed = (segq == segk) & (idxk <= idxq)
    scores = jnp.where(allowed, scores, MASKED)
    top = jnp.max(scores, axis=-1, keepdims=True)
    exps = jnp.exp(scores - top)
    total = jnp.sum(exps, axis=-1, keepdims=True)
    return slots, exps, 1.0 / total


def front_kernel(
    ctx_count,
    moves,
    marks,
    names_in,
    names_out,
    heads,
    part,
    tokens_ref,
    gain_ref,
    cos_ref,
    sin_ref,
    place_ref,
    about_ref,
    segk_ref,
    idxk_ref,
    dy_ref,
    ride_ref,
    place_mlp_ref,
    *refs,
):
    experts, room, rows = place_ref.shape
    width = tokens_ref.shape[1]
    wide = heads * HD
    group = width // part
    given, refs = refs[: len(names_in)], refs[len(names_in) :]
    gains_ref, hidden_ref, qkv_ref, kv_ref, mixed_ref, branch_ref, slots_ref, rides_ref = refs[:8]
    refs = refs[8:]
    made, (full, picked, picked_ride, slot_info, send, recv, *bounces) = refs[: len(names_out)], refs[len(names_out) :]
    arrays = dict(
        gain_own=gain_ref,
        gains=gains_ref,
        picked=picked,
        slots=slots_ref,
        picked_ride=picked_ride,
        rides=rides_ref,
        qkv=qkv_ref,
        kv=kv_ref,
        full=full,
    )
    arrays.update(zip(names_in, given))
    arrays.update(zip(names_out, made))
    greet(ctx_count, masks_of(moves))
    run = Moves(ctx_count, moves, arrays, send, recv, bounces)
    gains_done, first_done, second_done, rest_done, keys_done, dy_done = marks
    run_of = dy_ref.shape[1] // experts
    for k in range(experts):
        rows_at = slice(k * room, (k + 1) * room)
        cols = run_cols(run_of, k)
        slots = dot(place_mlp_ref[k], dy_ref[:, cols], 1, 0).astype(BF)
        rides = dot(place_mlp_ref[k], ride_ref[...], 1, 0).astype(BF)
        if k:
            picked[rows_at], picked_ride[rows_at] = slots, rides
        else:
            slots_ref[rows_at], rides_ref[rows_at] = slots, rides
    run.begin(second_done)
    gains_ref[:16] = gain_ref[...]
    slot_table(place_ref, about_ref, slot_info)
    x = tokens_ref[...].astype(F32)
    normed = x * lax.rsqrt(jnp.mean(x * x, axis=-1, keepdims=True) + EPSILON)
    run.settle(gains_done)
    hidden_ref[...] = (normed * gain_of(gains_ref, 0, part)).astype(BF)
    run.settle(first_done, gains_done)
    cos, sin = cos_ref[:rows], sin_ref[:rows]

    def project(plane):
        y = dot(hidden_ref[...], full[:, plane * wide : (plane + 1) * wide], 1, 0)
        for head in range(heads):
            cols = slice(head * HD, (head + 1) * HD)
            at = slice(plane * wide + head * HD, plane * wide + (head + 1) * HD)
            z = y[:, cols]
            qkv_ref[:, at] = (turn(z, cos, sin) if plane <= experts else z).astype(BF)

    project(experts)
    project(experts + 1)
    for i in range(rest_done, keys_done):
        if not moves[i][3]:
            run.start(i)
    kv_ref[:rows] = qkv_ref[:, experts * wide :]
    run.begin()
    run.settle(second_done, first_done)
    for plane in range(experts):
        project(plane)
    run.settle(keys_done, rest_done)
    run.settle(rest_done, second_done)
    run.start(len(moves) - 1)

    def step(i, carry):
        h, e = i // experts, i % experts
        cols = head_cols(e * heads + h)
        place = place_ref[e]
        _, exps, inv = scores_of(
            place,
            qkv_ref[:, cols],
            kv_ref[:, head_cols(h)],
            slot_info[e],
            segk_ref[...],
            idxk_ref[...],
        )
        attn = dot(exps.astype(BF), kv_ref[:, head_cols(heads + h)], 1, 0) * inv
        mixed = (attn * slot_info[e][:, 2:3]).astype(BF)
        mixed_ref[:, cols] = dot(place, mixed, 0, 0).astype(BF)
        return carry

    lax.fori_loop(0, heads * experts, step, 0)
    for j in range(group):
        rows_at = slice(j * part, (j + 1) * part)
        branch_ref[:, rows_at] = dot(mixed_ref[...], full[rows_at, (experts + 2) * wide :], 1, 1).astype(BF)
    run.finish()


def front(number, ctx_count, heads, part, moves, later, given, made, small):
    tokens, gain_own, place = small[0], small[1], small[4]
    experts, room, rows = place.shape
    width = tokens.shape[1]
    wide = heads * HD
    group = width // part
    full_wide = 2 * (experts + 1) * wide
    kv_moves = []
    order = [0]
    for bit in range(bits_of(ctx_count))[::-1]:
        for at in range(len(order)):
            target = ("kv", ((at + len(order)) * rows, rows), None)
            if at:
                source = ("kv", (at * rows, rows), None)
                kv_moves.append((source, target, 1 << bit, (source,)))
            else:
                source = ("qkv", (0, rows), (experts * wide, 2 * wide))
                kv_moves.append((source, target, 1 << bit, ()))
        order = order + order
    gains_moves, first_moves, second_moves, rest_moves, dy_moves = moves
    marks = [len(gains_moves)]
    for more in (first_moves, second_moves, rest_moves, kv_moves, dy_moves):
        marks.append(marks[-1] + len(more))
    whole = (FULL, (0, width), None)
    gathered = first_moves + second_moves + rest_moves
    landed = tuple(m[1] for m in gathered)
    keep = [(whole, ("kept", (0, width), None), None, landed)]
    moves = gains_moves + gathered + kv_moves + dy_moves + later + keep
    slots_shape = (experts * place.shape[1], width // experts)
    rides_shape = (experts * place.shape[1], HD)
    names_in, names_out = list(given), [*made, "kept"]
    shapes_out = [*made.values(), (width, full_wide)]
    any_spec = pl.BlockSpec(memory_space=pl.ANY)
    full = pl.BlockSpec(memory_space=pltpu.VMEM)
    small_out = [
        ((16 * group, gain_own.shape[1]), BF),
        ((rows, width), BF),
        ((rows, (experts + 2) * wide), BF),
        ((ctx_count * rows, 2 * wide), BF),
        ((rows, experts * wide), BF),
        ((rows, width), BF),
        (slots_shape, BF),
        (rides_shape, BF),
    ]
    bounces = [
        pltpu.VMEM((source[1][1], (source[2] or (0, given[source[0]].shape[1]))[1]), BF)
        for source, _, mask, _ in moves
        if mask == 0
    ]
    out = pl.pallas_call(
        functools.partial(
            front_kernel, ctx_count, moves, marks, names_in, names_out, heads, part
        ),
        out_shape=[jax.ShapeDtypeStruct(*x) for x in small_out]
        + [jax.ShapeDtypeStruct(shape, BF) for shape in shapes_out],
        in_specs=[full] * len(small) + [any_spec] * len(names_in),
        out_specs=[full] * len(small_out) + [any_spec] * len(names_out),
        scratch_shapes=[
            pltpu.VMEM((width, full_wide), BF),
            pltpu.VMEM(slots_shape, BF),
            pltpu.VMEM(rides_shape, BF),
            pltpu.VMEM((experts, room, HD), F32),
        ]
        + [pltpu.SemaphoreType.DMA((len(moves),))] * 2
        + bounces,
        compiler_params=pltpu.CompilerParams(
            collective_id=number, has_side_effects=True, vmem_limit_bytes=VMEM_LIMIT
        ),
        name="front",
    )(*small, *given.values())
    return out[: len(small_out)], dict(zip(names_out, out[len(small_out) :]))


def attend_back_kernel(
    ctx_count,
    moves,
    names_in,
    names_out,
    heads,
    part,
    tokens_ref,
    branch_ref,
    gain_ref,
    back_ref,
    dy_ref,
    gate_ref,
    qkv_ref,
    kv_ref,
    place_ref,
    about_ref,
    segk_ref,
    idxk_ref,
    cos_ref,
    sin_ref,
    weight_ref,
    *refs,
):
    experts, _, rows = place_ref.shape
    keys = kv_ref.shape[0]
    wide = heads * HD
    width = tokens_ref.shape[1]
    given, refs = refs[: len(names_in)], refs[len(names_in) :]
    out_ref, resid_ref, grad_branch_ref, gain_out_ref, back_one_ref, mlp_out_ref = refs[:6]
    made, refs = refs[6 : 6 + len(names_out)], refs[6 + len(names_out) :]
    (
        full,
        grad_ref,
        back_acc,
        dk_acc,
        dv_acc,
        total,
        got,
        mlp_mine,
        mlp_got,
        slot_info,
        send,
        recv,
        pass_send,
        pass_recv,
        load,
    ) = refs
    arrays = {**dict(zip(names_in, given)), **dict(zip(names_out, made))}
    arrays.update(mlp_mine=mlp_mine, mlp_got=mlp_got)
    bits = range(bits_of(ctx_count))
    greet(ctx_count, sorted({*masks_of(moves), *[1 << b for b in bits]}))
    run = Moves(ctx_count, moves, arrays, send, recv)
    run.begin()
    slot_table(place_ref, about_ref, slot_info)
    edge = (experts + 2) * wide
    loads = []
    for i, cols in enumerate((pl.ds(edge, experts * wide), pl.ds(0, edge))):
        loads.append(pltpu.make_async_copy(weight_ref.at[:, cols], full.at[:, cols], load.at[i]))
        loads[-1].start()

    x = tokens_ref[...].astype(F32) + branch_ref[...].astype(F32)
    inverse = lax.rsqrt(jnp.mean(x * x, axis=-1, keepdims=True) + EPSILON)
    normed = x * inverse
    back = back_ref[...].astype(F32)
    gain_out_ref[...] = jnp.sum(back * normed, axis=0, keepdims=True)
    scaled = back * gain_of(gain_ref, 1, part)
    inner = jnp.mean(scaled * normed, axis=-1, keepdims=True)
    resid = dy_ref[...].astype(F32) + inverse * (scaled - normed * inner)
    resid_ref[...] = resid
    grad_branch_ref[...] = resid.astype(BF)
    loads[0].wait()
    for e in range(experts):
        cols = slice(edge + e * wide, edge + (e + 1) * wide)
        mixed = dot(grad_branch_ref[...], full[:, cols], 1, 0)
        grad_ref[:, e * wide : (e + 1) * wide] = (mixed * gate_ref[:, e : e + 1]).astype(BF)

    def head_copy(h, bit):
        size = keys >> (bit + 1)
        i = h * len(bits) + bit
        return pltpu.make_async_remote_copy(
            src_ref=total.at[h, pl.ds(size, size)],
            dst_ref=got.at[h, pl.ds(size, size)],
            send_sem=pass_send.at[i],
            recv_sem=pass_recv.at[i],
            device_id=peer(ctx_count, 1 << bit),
            device_id_type=pl.DeviceIdType.MESH,
        )

    def head_sum(h, bit):
        size = keys >> (bit + 1)
        head_copy(h, bit).wait_recv()
        mine = total[h, :size].astype(F32) + got[h, size : 2 * size].astype(F32)
        mine = mine.astype(BF)
        if bit + 1 < len(bits):
            total[h, :size] = mine
            head_copy(h, bit + 1).start()
        else:
            at = experts * wide
            out_ref[:, at + h * HD : at + (h + 1) * HD] = mine[:, :HD]
            at += wide
            out_ref[:, at + h * HD : at + (h + 1) * HD] = mine[:, HD:]

    for h in range(heads):
        dk_acc[...] = jnp.zeros_like(dk_acc)
        dv_acc[...] = jnp.zeros_like(dv_acc)

        def step(e, carry, h=h):
            cols = head_cols(e * heads + h)
            place = place_ref[e]
            k, v = kv_ref[:, h * HD : (h + 1) * HD], kv_ref[:, (heads + h) * HD : (heads + h + 1) * HD]
            slots, exps, inv = scores_of(
                place, qkv_ref[:, cols], k, slot_info[e], segk_ref[...], idxk_ref[...]
            )
            attn = dot(exps.astype(BF), v, 1, 0) * inv
            probs = exps * inv
            grad = dot(place, grad_ref[:, cols], 1, 0)
            delta = jnp.sum(grad * attn, axis=-1, keepdims=True)
            grad = grad.astype(BF)
            dv_acc[...] += dot(probs.astype(BF), grad, 0, 0)
            grad_probs = dot(grad, v, 1, 1)
            grad_scores = (probs * (grad_probs - delta)).astype(BF)
            dq = dot(grad_scores, k, 1, 0) * (HD**-0.5)
            dk_acc[...] += dot(grad_scores, slots, 0, 0) * (HD**-0.5)
            top = dq.astype(BF)
            low = (dq - top.astype(F32)).astype(BF)
            back_q = dot(place, top, 0, 0) + dot(place, low, 0, 0)
            out_ref[:, cols] = turn(back_q, cos_ref[:rows], -sin_ref[:rows]).astype(BF)
            return carry

        lax.fori_loop(0, experts, step, 0)
        total[h, :, :HD] = turn(dk_acc[...], cos_ref[...], -sin_ref[...]).astype(BF)
        total[h, :, HD:] = dv_acc[...].astype(BF)
        head_copy(h, 0).start()
        if h:
            head_sum(h - 1, 0)
    head_sum(heads - 1, 0)
    loads[1].wait()
    queries = experts * wide
    for j in range(width // part):
        rows_at = slice(j * part, (j + 1) * part)
        back_acc[:, rows_at] = dot(out_ref[:, :queries], full[rows_at, :queries], 1, 1)
    for bit in bits[1:]:
        for h in range(heads):
            head_sum(h, bit)
    for j in range(width // part):
        rows_at = slice(j * part, (j + 1) * part)
        keyed = dot(out_ref[:, queries:], full[rows_at, queries:edge], 1, 1)
        back_one_ref[:, rows_at] = (back_acc[:, rows_at] + keyed).astype(BF)
    runs_mlp = [i for i, m in enumerate(moves) if m[0][0] == "mlp"]
    for i in runs_mlp:
        run.await_one(i)
    mlp_total = mlp_mine[...].astype(F32)
    for r in range(len(runs_mlp) - 1):
        mlp_total = mlp_total + mlp_got[r * mlp_mine.shape[0] : (r + 1) * mlp_mine.shape[0]].astype(F32)
    mlp_out_ref[...] = mlp_total.astype(BF)
    for h in range(heads):
        for bit in bits:
            head_copy(h, bit).wait_send()
    run.finish()


def attend_back(number, ctx_count, tp_count, heads, part, moves, given, made, weight, *small):
    tokens, qkv, kv = small[0], small[6], small[7]
    rows, width = tokens.shape
    keys = kv.shape[0]
    any_spec = pl.BlockSpec(memory_space=pl.ANY)
    full = pl.BlockSpec(memory_space=pltpu.VMEM)
    passes = heads * bits_of(ctx_count)
    slots, run = given["mlp"].shape[0], width // tp_count
    every = (0, slots)
    mlp_moves = [(("mlp", every, (TP, run)), ("mlp_mine", every, None), None, ())]
    for r in range(1, tp_count):
        target = ("mlp_got", ((r - 1) * slots, slots), None)
        mlp_moves.append((("mlp", every, (TP, run, r)), target, -r, ()))
    moves = mlp_moves + moves
    small_out = [
        (qkv.shape, BF),
        ((rows, width), F32),
        ((rows, width), BF),
        ((1, width), F32),
        ((rows, width), BF),
        ((slots, run), BF),
    ]
    out = pl.pallas_call(
        functools.partial(
            attend_back_kernel, ctx_count, moves, list(given), list(made), heads, part
        ),
        out_shape=[jax.ShapeDtypeStruct(*x) for x in small_out]
        + [jax.ShapeDtypeStruct(shape, BF) for shape in made.values()],
        in_specs=[full] * len(small) + [any_spec] * (1 + len(given)),
        out_specs=[full] * len(small_out) + [any_spec] * len(made),
        input_output_aliases={
            len(small) + 1 + list(given).index(n): len(small_out) + i for i, n in enumerate(made)
        },
        scratch_shapes=[
            pltpu.VMEM(weight.shape, BF),
            pltpu.VMEM((rows, weight.shape[1] - qkv.shape[1]), BF),
            pltpu.VMEM((rows, width), F32),
        ]
        + [pltpu.VMEM((keys, HD), F32)] * 2
        + [pltpu.VMEM((heads, keys, 2 * HD), BF)] * 2
        + [pltpu.VMEM((slots, run), BF), pltpu.VMEM(((tp_count - 1) * slots, run), BF)]
        + [pltpu.VMEM((*small[8].shape[:2], HD), F32)]
        + [pltpu.SemaphoreType.DMA((len(moves),))] * 2
        + [pltpu.SemaphoreType.DMA((passes,))] * 2
        + [pltpu.SemaphoreType.DMA((2,))],
        compiler_params=pltpu.CompilerParams(
            collective_id=number, has_side_effects=True, vmem_limit_bytes=VMEM_LIMIT
        ),
        name="attend_back",
    )(*small, weight, *given.values())
    return out[: len(small_out)], dict(zip(made, out[len(small_out) :]))


def spread_kernel(experts, me_ref, *refs):
    from_in, from_down = refs[:experts], refs[experts : 2 * experts]
    in_ref, down_ref = refs[2 * experts :]
    units = down_ref.shape[2]
    for m in range(experts):

        @pl.when(me_ref[0] == m)
        def _():
            for e in range(experts):
                for c in range(2):
                    in_ref[:, e, c, :] = from_in[e ^ m][:, c * units : (c + 1) * units].astype(F32)
                down_ref[:, e, :] = from_down[e ^ m][...].astype(F32)


def spread_grads(from_in, from_down, me, in_shape, down_shape):
    experts = len(from_in)
    step = min(64, in_shape[0])

    def rows_of(width):
        return pl.BlockSpec((step, width), lambda i, m: (i, 0))

    return pl.pallas_call(
        functools.partial(spread_kernel, experts),
        grid_spec=pltpu.PrefetchScalarGridSpec(
            num_scalar_prefetch=1,
            grid=(in_shape[0] // step,),
            in_specs=[rows_of(from_in[0].shape[1])] * experts
            + [rows_of(from_down[0].shape[1])] * experts,
            out_specs=[
                pl.BlockSpec((step, *in_shape[1:]), lambda i, m: (i, 0, 0, 0)),
                pl.BlockSpec((step, *down_shape[1:]), lambda i, m: (i, 0, 0)),
            ],
        ),
        out_shape=[
            jax.ShapeDtypeStruct(in_shape, F32),
            jax.ShapeDtypeStruct(down_shape, F32),
        ],
        compiler_params=pltpu.CompilerParams(vmem_limit_bytes=VMEM_LIMIT),
        name="spread_grads",
    )(me.astype(jnp.int32).reshape(1), *from_in, *from_down)


def places(routes, gates, experts, cap, room):
    rows = routes.shape[0]
    named = routes[:, :, None] == jnp.arange(experts, dtype=jnp.int32)[None, None, :]
    member = jnp.any(named, axis=1)
    gate = jnp.sum(jnp.where(named, gates[:, :, None], 0.0), axis=1)
    token = jnp.arange(rows, dtype=jnp.int32)
    earlier = (token[None, :] < token[:, None]).astype(BF)
    rank = dot(earlier, member.astype(BF), 1, 0).astype(jnp.int32)
    slot = jnp.where(member, rank, -1).T
    taken = slot[:, None, :] == jnp.arange(room, dtype=jnp.int32)[None, :, None]
    return taken, gate


def split(x):
    high = x.astype(BF)
    return high, (x - high.astype(F32)).astype(BF)


def layer(
    counts,
    tokens,
    gain_attn,
    gain_mlp,
    w_kv,
    w_query,
    w_out_attn,
    w_in,
    w_down,
    segments,
    attn_routes,
    attn_gates,
    mlp_routes,
    mlp_gates,
    cotangent,
):
    fsdp_count, ctx_count, tp_count = counts
    group = fsdp_count * ctx_count
    me = lax.axis_index(GROUP)
    ctx_me = lax.axis_index(CTX)
    rows, width = tokens.shape[1:]
    cap = 9 * rows // 16
    room = -(-cap // 16) * 16
    part = width // group
    attn_experts = w_query.shape[1]
    experts = w_in.shape[1]
    share = group // experts
    expert_me = me // share
    hidden_units = w_down.shape[2]
    head_width = w_kv.shape[2]

    def piece(x, index, size=part, axis=1):
        return lax.dynamic_slice_in_dim(x, index * size, size, axis)

    def exchange(x, mask):
        return swap(x, mask, GROUP, group)

    def after(x, *events):
        return lax.optimization_barrier((x, *events))[0]

    high, second = group // 2, group // 4

    gain_own = jnp.pad(jnp.concatenate([gain_attn, gain_mlp])[None, :], ((0, 15), (0, 0)))
    kv_out_own = jnp.concatenate([w_kv.reshape(part, -1), w_out_attn.reshape(part, -1)], axis=1)
    attn_own = [w_query.reshape(part, -1), kv_out_own]
    far_x, far_y = [], []
    for own in attn_own:
        far_x.append(exchange(own, high))
        far_y.append(exchange(own, second))

    seg_row = segments[0]
    seq_total = seg_row.shape[0]
    ctx_bits = list(range(bits_of(ctx_count)))[::-1]
    key_order = [0]
    for bit in ctx_bits:
        key_order = key_order + [j | (1 << bit) for j in key_order]
    key_seg = jnp.concatenate([piece(seg_row, ctx_me ^ j, rows, 0) for j in key_order])
    key_idx = jnp.concatenate(
        [(ctx_me ^ j) * rows + jnp.arange(rows, dtype=jnp.int32) for j in key_order]
    )
    place_idx = jnp.arange(seq_total, dtype=jnp.int32)
    pos = jnp.sum(
        (seg_row[None, :] == key_seg[:, None]) & (place_idx[None, :] < key_idx[:, None]),
        axis=1,
        dtype=jnp.int32,
    ).astype(F32)
    frequency = ROPE_BASE ** (-(jnp.arange(HD // 2, dtype=F32) * 2.0) / HD)
    angles = pos[:, None] * frequency[None, :]
    cos_half, sin_half = jnp.cos(angles), jnp.sin(angles)
    cos = jnp.concatenate([cos_half, cos_half], axis=1)
    sin = jnp.concatenate([-sin_half, sin_half], axis=1)
    taken_attn, gate_attn = places(attn_routes[0], attn_gates[0], attn_experts, cap, room)
    place_attn = taken_attn.astype(BF)
    own_seg, own_idx = key_seg[:rows], key_idx[:rows]
    gate_high, gate_low = split(gate_attn)
    about = [own_seg[:, None], (own_idx // 32)[:, None], (own_idx % 32)[:, None], gate_high, gate_low]
    about = jnp.concatenate([x.astype(BF) for x in about], axis=1)
    about = jnp.pad(about, ((0, 0), (0, HD - about.shape[1])))
    key_row = (key_seg.astype(F32)[None, :], key_idx.astype(F32)[None, :])
    taken_mlp, gate_mlp = places(mlp_routes[0], mlp_gates[0], experts, cap, room)
    mine_first = [expert_me ^ k for k in range(experts)]
    place_mlp = jnp.concatenate([piece(taken_mlp, e, 1, 0) for e in mine_first]).astype(BF)
    tokens_rel, grad_out = in_order(me, [tokens[0], cotangent[0]], group)

    def expert_rows(k):
        in_rows = piece(w_in, expert_me ^ k, 1, 1)
        down_rows = piece(w_down, expert_me ^ k, 1, 1)
        return [in_rows[:, 0, 0], in_rows[:, 0, 1], down_rows[:, 0]]

    to_send = [expert_rows(k) for k in range(experts)]

    def given_sends(ks):
        return {("send", k, c): x for k in ks for c, x in enumerate(to_send[k])}

    in_cols, down_cols = (0, 2 * hidden_units), (2 * hidden_units, hidden_units)
    weight_shapes = {"in": (width, 2 * hidden_units), "down": (width, hidden_units)}

    def weight_moves(k, first, size, prefix=""):
        moves = []
        sides = (("in", (0, hidden_units)), ("in", (hidden_units, hidden_units)), ("down", None))
        for c, (name, cols) in enumerate(sides):
            base = k * share * part + first
            source = (("send", k, c), (first, size), None)
            landed = (prefix + name, (base, size), cols)
            moves.append((source, landed, k * share, ()))
            for t in range(1, share):
                target = (prefix + name, (base + t * part, size), cols)
                if k:
                    moves.append((landed, target, t, (landed,)))
                else:
                    moves.append((source, target, t, ()))
        return moves

    def many_weight_moves(cuts):
        return [m for cut in cuts for m in weight_moves(*cut)]

    near = [k for k in range(1, experts) if k & (k - 1) == 0]
    far = [k for k in range(1, experts) if k & (k - 1)]
    half_part = part // 2

    far_x, to_send = lax.optimization_barrier((far_x, to_send))
    cut = max(16, part * 3 // 8 // 16 * 16)
    gather_moves = []
    queries, two_planes = attn_experts * head_width, 2 * head_width
    for n, first, size_of, edge in (
        (1, 0, two_planes, queries),
        (0, 0, queries, 0),
        (1, two_planes, queries, queries + two_planes),
    ):
        cols, own_cols = (edge, size_of), (first, size_of)
        moves = []
        held = {0: [(("own", n), 0, part, ())], high: [(("x", n), 0, part, ())], second: [(("y", n), 0, part, ())]}
        corner = []
        for side, mask, low, top in ((("x", n), second, 0, cut), (("y", n), high, cut, part)):
            half = (top - low) // 32 * 16
            for at, size in ((low, half), (low + half, top - low - half)):
                if size:
                    target = (FULL, ((high | second) * part + at, size), cols)
                    corner.append(((side, (at, size), own_cols), target, mask, ()))
        corner = corner[::2] + corner[1::2]
        moves += corner
        held[high | second] = [(FULL, t[1][0] - (high | second) * part, t[1][1], (t,)) for _, t, _, _ in corner]
        for j in (0, high, second):
            source = (held[j][0][0], (0, part), own_cols)
            moves.append((source, (FULL, (j * part, part), cols), None, ()))
        for bit in range(bits_of(group) - 2)[::-1]:
            for j in list(held):
                there = []
                for name, at, size, needs in held[j]:
                    if name == FULL:
                        source = (name, (at + j * part, size), cols)
                    else:
                        source = (name, (at, size), own_cols)
                    target = (FULL, ((j | 1 << bit) * part + at, size), cols)
                    moves.append((source, target, 1 << bit, needs))
                    there.append((FULL, at, size, (target,)))
                held[j | 1 << bit] = there
        gather_moves.append(moves)
    gain_moves = [
        (("gain_own", (0, 16), None), ("gains", (j * 16, 16), None), j, ())
        for j in range(1, group)
    ]
    heads = head_width // HD
    later = weight_moves(0, 0, part) + many_weight_moves([(k, 0, half_part) for k in near])
    gate_ride = jnp.concatenate(split(gate_mlp), axis=1)
    gate_ride = jnp.pad(gate_ride, ((0, 0), (0, HD - 2 * experts)))
    dy_moves = [
        ((name, (k * room, room), None), (target, (k * room, room), None), k * share, ())
        for k in range(1, experts)
        for name, target in (("picked", "slots"), ("picked_ride", "rides"))
    ]
    (gains, hidden_one, qkv, kv, mixed, branch, dy_run, dy_rides), made = front(
        1,
        ctx_count,
        heads,
        part,
        (gain_moves, *gather_moves, dy_moves),
        later,
        {
            **{("own", n): x for n, x in enumerate(attn_own)},
            **{("x", n): x for n, x in enumerate(far_x)},
            **{("y", n): x for n, x in enumerate(far_y)},
            **given_sends([0, *near]),
        },
        weight_shapes,
        (
            tokens_rel,
            gain_own,
            cos,
            sin,
            place_attn,
            about,
            *key_row,
            grad_out,
            gate_ride,
            place_mlp,
        ),
    )
    attn_full, weights = made["kept"], {n: made[n] for n in weight_shapes}
    branch_sum = lax.psum(branch, TP)
    cuts = [(k, half_part, part - half_part) for k in near] + [(k, 0, half_part) for k in far]
    to_send, weights, _ = lax.optimization_barrier((to_send, weights, branch))
    given = {**given_sends([*near, *far]), **weights}
    weights = move("weights_two", 3, ctx_count, many_weight_moves(cuts), given, weight_shapes)
    fetched, far_moves = [], []
    for j in range(group):
        size = half_part if j // share in far else part
        if fetched and sum(fetched[-1]) == j * part:
            fetched[-1] = (fetched[-1][0], fetched[-1][1] + size)
        else:
            fetched.append((j * part, size))
    for k in far:
        far_moves += weight_moves(k, half_part, part - half_part, "w")
    grads_in, grads_down, mlp_slots, back_two_part = run_experts(
        4,
        ctx_count,
        tp_count,
        experts,
        share,
        part,
        fetched,
        far_moves,
        given_sends(far),
        weights,
        tokens_rel,
        branch_sum,
        gains,
        place_mlp,
        dy_run,
        dy_rides,
    )
    back_two = lax.psum(back_two_part, TP)
    got_in, got_down = {0: grads_in}, {0: grads_down}

    def grad_moves(ks, cuts, first=0):
        moves = []
        for at in range(first, part, part // cuts):
            for k in ks:
                for name in ("in", "down"):
                    source = (name, (k * part + at, part // cuts), None)
                    target = ((name, k), (at, part // cuts), None)
                    moves.append((source, target, k * share, ()))
        made_shapes = {("in", k): (part, 2 * hidden_units) for k in ks}
        return moves, {**made_shapes, **{("down", k): (part, hidden_units) for k in ks}}

    def keep_grads(made, ks):
        got_in.update({k: made[("in", k)] for k in ks})
        got_down.update({k: made[("down", k)] for k in ks})

    moves, made_shapes = grad_moves(near, 1)
    early, early_shapes = grad_moves(far, 4)
    moves += early[: len(early) // 4]
    made_shapes.update(early_shapes)
    grads_in, grads_down, _ = lax.optimization_barrier((grads_in, grads_down, back_two_part))
    given = {"in": grads_in, "down": grads_down}
    made = move("grads_near", 5, ctx_count, moves, given, made_shapes)
    keep_grads(made, near)

    moves, made_shapes = grad_moves(far, 4, part // 4)
    back_two, given, made = lax.optimization_barrier((back_two, given, made))
    given.update({name: made[name] for name in made_shapes})
    given["mlp"] = mlp_slots
    (grad_qkv, grad_resid, grad_branch, gain_two_grad, back_one_part, mlp_run), made = attend_back(
        6,
        ctx_count,
        tp_count,
        heads,
        part,
        moves,
        given,
        made_shapes,
        attn_full,
        tokens_rel,
        branch_sum,
        gains,
        back_two,
        grad_out,
        gate_attn,
        qkv,
        kv,
        place_attn,
        about,
        *key_row,
        cos,
        sin,
    )
    keep_grads(made, far)
    upper = list(range(1, bits_of(group)))
    grad_attnw, grad_tokens, gain_grads, mlp_sum = attn_grads(
        7,
        ctx_count,
        tp_count,
        upper,
        part,
        head_width,
        hidden_one,
        grad_branch,
        grad_qkv,
        mixed,
        back_one_part,
        tokens_rel,
        gains,
        grad_resid,
        gain_two_grad,
        mlp_run,
        place_mlp,
    )
    output, grad_tokens = last(me, group, tokens_rel, branch_sum, mlp_sum, grad_tokens)
    grad_query_w, grad_kv_w, grad_out_w = lay_out(
        grad_attnw, (w_query.shape, w_kv.shape, w_out_attn.shape)
    )

    return (
        output[None],
        grad_tokens[None],
        gain_grads[0],
        gain_grads[1],
        grad_kv_w,
        grad_query_w,
        grad_out_w,
        *spread_grads(
            [got_in[k] for k in range(experts)],
            [got_down[k] for k in range(experts)],
            expert_me,
            w_in.shape,
            w_down.shape,
        ),
    )


def solution(mesh):
    rows = P(FSDP, CTX, None)
    weight = P(GROUP, None, TP)
    weight_in = P(GROUP, None, None, TP)
    return jax.shard_map(
        functools.partial(layer, tuple(mesh.shape[a] for a in (FSDP, CTX, TP))),
        mesh=mesh,
        in_specs=(
            rows,
            P(GROUP),
            P(GROUP),
            weight,
            weight,
            weight,
            weight_in,
            weight,
            P(FSDP, None),
            rows,
            rows,
            rows,
            rows,
            rows,
        ),
        out_specs=(rows, rows, P(GROUP), P(GROUP), weight, weight, weight, weight_in, weight),
        check_vma=False,
    )
```

```python
import functools

import jax
import jax.numpy as jnp
from jax import lax
from jax.experimental import pallas as pl
from jax.experimental.pallas import tpu as pltpu
from jax.sharding import PartitionSpec as P

HD = 128
EPSILON = 1e-06
ROPE_BASE = 10000.0
MASKED = -1e30
FSDP, CTX, TP = "fsdp", "ctx", "tp"
GROUP = (FSDP, CTX)
FULL = "full"
BF = jnp.bfloat16
F32 = jnp.float32
VMEM_LIMIT = 56 * 1024 * 1024


def normalize(tensor):
    inverse = lax.rsqrt(jnp.mean(tensor * tensor, axis=-1, keepdims=True) + EPSILON)
    return (tensor * inverse, inverse)


def norm_back(grad_in, normed, inverse, gain_vec):
    scaled = grad_in * gain_vec
    inner_mean = jnp.mean(scaled * normed, axis=-1, keepdims=True)
    return (inverse * (scaled - normed * inner_mean), jnp.sum(grad_in * normed, axis=0))


def dot(a, b, ca, cb):
    return lax.dot_general(a, b, (((ca,), (cb,)), ((), ())), preferred_element_type=F32)


def turn(x, cos, sin):
    return x * cos + pltpu.roll(x, HD // 2, 1) * sin


def swap(x, mask, axes, count):
    return lax.ppermute(x, axes, [(i, i ^ mask) for i in range(count)])


def bits_of(count):
    return count.bit_length() - 1


def flip(value, mask):
    step = 1
    while step <= mask:
        if mask & step:
            value = value + step - 2 * step * ((value // step) % 2)
        step *= 2
    return value


def peer(ctx_count, mask):
    if mask < 0:
        return {TP: flip(lax.axis_index(TP), -mask)}
    return {
        FSDP: flip(lax.axis_index(FSDP), mask // ctx_count),
        CTX: flip(lax.axis_index(CTX), mask % ctx_count),
    }


def greet(ctx_count, masks):
    barrier = pltpu.get_barrier_semaphore()
    for mask in masks:
        pl.semaphore_signal(
            barrier, inc=1, device_id=peer(ctx_count, mask), device_id_type=pl.DeviceIdType.MESH
        )
    pl.semaphore_wait(barrier, len(masks))


def run_cols(size, flips=0):
    return pl.ds(pl.multiple_of(flip(lax.axis_index(TP), flips) * size, size), size)


def window(ref, rows, cols):
    if rows[0] == TP:
        return ref.at[run_cols(rows[1], rows[2])]
    if cols is None:
        return ref.at[pl.ds(rows[0], rows[1])]
    if cols[0] == TP:
        return ref.at[pl.ds(rows[0], rows[1]), run_cols(*cols[1:3])]
    return ref.at[pl.ds(rows[0], rows[1]), pl.ds(cols[0], cols[1])]


def gain_of(gains_ref, which, part):
    rows = gains_ref[...].astype(F32)
    cols = slice(which * part, (which + 1) * part)
    return jnp.concatenate([rows[at : at + 1, cols] for at in range(0, rows.shape[0], 16)], axis=1)


class Moves:
    def __init__(self, ctx_count, moves, arrays, send, recv, bounces=(), base=0):
        self.moves = moves
        self.onward = {}
        bounces = list(bounces)
        self.copies = []
        self.place = {m[1]: i for i, m in enumerate(moves)}
        self.started, self.came, self.sent = set(), set(), set()
        for at, (source, target, mask, _) in enumerate(moves):
            i = base + at
            src = window(arrays[source[0]], *source[1:])
            dst = window(arrays[target[0]], *target[1:])
            if mask:
                copy = pltpu.make_async_remote_copy(
                    src_ref=src,
                    dst_ref=dst,
                    send_sem=send.at[i],
                    recv_sem=recv.at[i],
                    device_id=peer(ctx_count, mask),
                    device_id_type=pl.DeviceIdType.MESH,
                )
            elif mask is None:
                copy = pltpu.make_async_copy(src, dst, recv.at[i])
            else:
                bounce = bounces.pop(0)
                copy = pltpu.make_async_copy(src, bounce, recv.at[i])
                self.onward[at] = pltpu.make_async_copy(bounce, dst, send.at[i])
            self.copies.append(copy)

    def start(self, i):
        if i not in self.started:
            self.started.add(i)
            self.copies[i].start()

    def begin(self, count=None):
        for i, move in enumerate(self.moves[:count]):
            if not move[3]:
                self.start(i)

    def await_one(self, i):
        if i not in self.came:
            self.came.add(i)
            if i in self.onward:
                self.copies[i].wait()
                self.onward[i].start()
            elif self.moves[i][2] is None:
                self.copies[i].wait()
            else:
                self.copies[i].wait_recv()

    def await_sent(self, i):
        if i not in self.sent:
            self.sent.add(i)
            self.copies[i].wait_send()

    def kick(self, first, count):
        for i in range(first, count):
            for target in self.moves[i][3]:
                self.await_one(self.place[target])
            self.start(i)

    def settle(self, count=None, first=0):
        count = len(self.moves) if count is None else count
        for i in range(first, count):
            if i in self.onward:
                self.await_one(i)
        for i in range(first, count):
            for target in self.moves[i][3]:
                self.await_one(self.place[target])
            self.start(i)
        for i in range(first, count):
            self.await_one(i)

    def finish(self):
        self.settle()
        for i in range(len(self.moves)):
            if i in self.onward:
                self.onward[i].wait()
            elif self.moves[i][2] is not None:
                self.await_sent(i)


def masks_of(moves):
    return sorted({move[2] for move in moves if move[2]})


def move_kernel(ctx_count, moves, names_in, names_out, *refs):
    count = len(names_in) + len(names_out)
    refs, (send, recv, *bounces) = refs[:count], refs[count:]
    arrays = dict(zip(names_in, refs))
    arrays.update(zip(names_out, refs[len(names_in) :]))
    greet(ctx_count, masks_of(moves))
    run = Moves(ctx_count, moves, arrays, send, recv, bounces)
    run.begin()
    run.finish()


def move(name, number, ctx_count, moves, given, made):
    names_in = [n for n in given if n not in made] + [n for n in given if n in made]
    plain = [n for n in names_in if n not in made]
    names_out = list(made)
    any_spec = pl.BlockSpec(memory_space=pl.ANY)
    bounces = [
        pltpu.VMEM((source[1][1], (source[2] or (0, given[source[0]].shape[1]))[1]), BF)
        for source, _, mask, _ in moves
        if not mask
    ]
    return dict(
        zip(
            names_out,
            pl.pallas_call(
                functools.partial(
                    move_kernel,
                    ctx_count,
                    moves,
                    plain + ["old_" + n for n in names_in[len(plain) :]],
                    names_out,
                ),
                out_shape=[jax.ShapeDtypeStruct(shape, BF) for shape in made.values()],
                in_specs=[any_spec] * len(names_in),
                out_specs=[any_spec] * len(names_out),
                input_output_aliases={
                    names_in.index(n): names_out.index(n) for n in names_out if n in given
                },
                scratch_shapes=[pltpu.SemaphoreType.DMA((len(moves),))] * 2 + bounces,
                compiler_params=pltpu.CompilerParams(
                    collective_id=number, has_side_effects=True, vmem_limit_bytes=VMEM_LIMIT
                ),
                name=name,
            )(*[given[n] for n in names_in]),
        )
    )


def lanes_of(planes, late, bits):
    lanes = []
    for n, plane in enumerate([*range(late, planes), *range(late)]):
        lanes.append((plane, bits if n % 2 else bits[::-1]))
    last = lanes[-6:]
    return lanes, [p for p, _ in last[::2]] + [p for p, _ in last[1::2]]


def attn_grads_kernel(
    ctx_count,
    groups,
    bits,
    part,
    cols,
    hidden_ref,
    branch_ref,
    qkv_ref,
    mixed_ref,
    back_ref,
    tokens_ref,
    gain_ref,
    resid_ref,
    gain_two_ref,
    mlp_ref,
    place_ref,
    out_ref,
    keep_ref,
    give_ref,
    grad_tokens_ref,
    gain_out_ref,
    mlp_sum_ref,
    mlp_got,
    back_got,
    back_sum,
    gain_send,
    gain_got,
    hidden,
    branch,
    hidden_odd,
    branch_odd,
    right,
    grads,
    got,
    send,
    recv,
    pass_send,
    pass_recv,
):
    rows, width = hidden_ref.shape
    count = width // part // 2
    planes = right.shape[1] // cols
    first = qkv_ref.shape[1]
    group = width // part
    run_rows = groups["spread"][0][0][1][1]
    greet(ctx_count, masks_of([m for moves in groups.values() for m in moves]))
    arrays = dict(
        back=back_ref,
        back_got=back_got,
        back_sum=back_sum,
        mlp=mlp_ref,
        mlp_got=mlp_got,
        mlp_sum=mlp_sum_ref,
        gain_send=gain_send,
        gain_got=gain_got,
        hidden_odd=hidden_odd,
        branch_odd=branch_odd,
        qkv_in=qkv_ref,
        mixed_in=mixed_ref,
        hidden=hidden,
        branch=branch,
        right=right,
    )
    runs, base = {}, 0
    for name, moves in groups.items():
        if name != "sums":
            runs[name] = Moves(ctx_count, moves, arrays, pass_send, pass_recv, (), base)
        base += len(moves)
    run = runs["share"]
    runs["reduce"].begin()
    runs["mlp"].begin()
    for given, even_side, odd_side in (
        (branch_ref, branch, branch_odd),
        (hidden_ref, hidden, hidden_odd),
    ):
        for j in range(count):
            block = slice(j * part, (j + 1) * part)
            even_side[:rows, block] = given[:, 2 * j * part : (2 * j + 1) * part]
            odd_side[:, block] = given[:, (2 * j + 1) * part : (2 * j + 2) * part]
    run.begin()
    right[:rows, :first] = qkv_ref[...]
    right[:rows, first:] = mixed_ref[...]
    number = [0]

    def copy(mask, block, plane):
        i = number[0]
        number[0] += 1
        window_of = (pl.ds(block * part, part), pl.ds(plane * cols, cols))
        return pltpu.make_async_remote_copy(
            src_ref=grads.at[window_of],
            dst_ref=got.at[window_of],
            send_sem=send.at[i],
            recv_sem=recv.at[i],
            device_id=peer(ctx_count, mask),
            device_id_type=pl.DeviceIdType.MESH,
        )

    sent, flying, left = [], {}, {}

    def send_half(plane, order, step):
        at = bits.index(order[step])
        flying[plane] = {
            j: copy(1 << order[step], j, plane) for j in left[plane] if j >> at & 1
        }
        for c in flying[plane].values():
            c.start()
        sent.extend(flying[plane].values())

    late = first // cols
    lanes, last_lanes = lanes_of(planes, late, bits)
    for plane, order in lanes:
        run.settle(2 if plane >= late else 4)
        at = pl.ds(plane * cols, cols)
        left_side = hidden if plane < late else branch
        grads[:, at] = dot(left_side[...], right[:, at], 0, 0).astype(BF)
        left[plane] = list(range(count))
        send_half(plane, order, 0)
    def sum_back():
        runs["reduce"].settle()
        own = run_cols(run_rows)
        total = back_ref[own].astype(F32)
        for r in range(len(groups["reduce"])):
            total = total + back_got[r * run_rows : (r + 1) * run_rows].astype(F32)
        back_sum[own] = total.astype(BF)
        runs["spread"].begin()

    def sum_mlp():
        runs["mlp"].settle()
        room = mlp_ref.shape[0] // place_ref.shape[0]
        total = dot(place_ref[0], mlp_ref[:room], 0, 0)
        for k in range(1, place_ref.shape[0]):
            total = total + dot(place_ref[k], mlp_got[k * room : (k + 1) * room], 0, 0)
        mlp_sum_ref[:, run_cols(mlp_ref.shape[1])] = total.astype(BF)
        runs["mlp_spread"].begin()

    def norm_back():
        runs["spread"].settle()
        x = tokens_ref[...].astype(F32)
        inverse = lax.rsqrt(jnp.mean(x * x, axis=-1, keepdims=True) + EPSILON)
        normed = x * inverse
        back = back_sum[...].astype(F32)
        gain_grad = jnp.sum(back * normed, axis=0, keepdims=True)
        scaled = back * gain_of(gain_ref, 0, part)
        inner = jnp.mean(scaled * normed, axis=-1, keepdims=True)
        grad_tokens_ref[...] = (resid_ref[...] + inverse * (scaled - normed * inner)).astype(BF)
        gain_send[...] = jnp.zeros_like(gain_send)
        for j in range(group):
            block = slice(j * part, (j + 1) * part)
            gain_send[j * 8 : j * 8 + 1] = gain_grad[:, block]
            gain_send[j * 8 + 1 : j * 8 + 2] = gain_two_ref[:, block]
        runs["gains"].begin()

    for step in range(len(bits)):
        for n, (plane, order) in enumerate(lanes):
            if step == len(bits) - 1 and plane in last_lanes:
                continue
            if step == 0 and n == len(lanes) * 2 // 5:
                sum_back()
                sum_mlp()
            if step == 1 and n == min(2, len(lanes) - 1):
                norm_back()
            at = bits.index(order[step])
            left[plane] = [j for j in left[plane] if not j >> at & 1]
            across = pl.ds(plane * cols, cols)
            for j in left[plane]:
                flying[plane][j | 1 << at].wait_recv()
                down, other = pl.ds(j * part, part), pl.ds((j | 1 << at) * part, part)
                total = grads[down, across].astype(F32) + got[other, across].astype(F32)
                if step == len(bits) - 1:
                    at_out = sum(p not in last_lanes for p in range(plane))
                    out_ref[:, at_out * cols : (at_out + 1) * cols] = total
                elif step == len(bits) - 2 and plane in last_lanes:
                    at_last = last_lanes.index(plane)
                    there = slice(at_last * cols, (at_last + 1) * cols)
                    if j:
                        give_ref[:, there] = total.astype(BF)
                    else:
                        keep_ref[:, there] = total
                else:
                    grads[down, across] = total.astype(BF)
            if step < len(bits) - 1 and not (step == len(bits) - 2 and plane in last_lanes):
                send_half(plane, order, step + 1)
    runs["gains"].settle()
    gains = gain_send[:8]
    for j in range(1, group):
        gains = gains + gain_got[j * 8 : (j + 1) * 8]
    gain_out_ref[...] = gains
    for moves in runs.values():
        moves.finish()
    for c in sent:
        c.wait_send()


def attn_grads(number, ctx_count, tp_count, bits, part, cols, hidden, branch, qkv, mixed, *others):
    rows, width = hidden.shape
    group = width // part
    first = qkv.shape[1]
    theirs = (rows, rows)
    run_rows = rows // tp_count
    mlp, place = others[-2:]
    experts, room = place.shape[:2]
    run = mlp.shape[1]
    groups = {
        "mlp": [
            (("mlp", (k * room, room), None), ("mlp_got", (k * room, room), None), k * group // experts, ())
            for k in range(1, experts)
        ],
        "mlp_spread": [
            (("mlp_sum", (0, rows), (TP, run)), ("mlp_sum", (0, rows), (TP, run, 0, r)), -r, ())
            for r in range(1, tp_count)
        ],
        "reduce": [
            (("back", (TP, run_rows, r), None), ("back_got", ((r - 1) * run_rows, run_rows), None), -r, ())
            for r in range(1, tp_count)
        ],
        "spread": [
            (("back_sum", (TP, run_rows, 0), None), ("back_sum", (TP, run_rows, 0), r), -r, ())
            for r in range(1, tp_count)
        ],
        "gains": [
            (("gain_send", (j * 8, 8), None), ("gain_got", (j * 8, 8), None), j, ())
            for j in range(1, group)
        ],
        "share": [
            (("mixed_in", (0, rows), None), ("right", theirs, (first, mixed.shape[1])), 1, ()),
            (("branch_odd", (0, rows), None), ("branch", theirs, None), 1, ()),
            (("qkv_in", (0, rows), None), ("right", theirs, (0, first)), 1, ()),
            (("hidden_odd", (0, rows), None), ("hidden", theirs, None), 1, ()),
        ],
        "sums": [((), (), 1 << b, ()) for b in bits],
    }
    wide = qkv.shape[1] + mixed.shape[1]
    copies = (wide // cols) * (width // part // 2)
    passes = sum(len(moves) for moves in groups.values())
    full = pl.BlockSpec(memory_space=pltpu.VMEM)
    return pl.pallas_call(
        functools.partial(attn_grads_kernel, ctx_count, groups, bits, part, cols),
        out_shape=[
            jax.ShapeDtypeStruct((part, wide - 6 * cols), F32),
            jax.ShapeDtypeStruct((part, 6 * cols), F32),
            jax.ShapeDtypeStruct((part, 6 * cols), BF),
            jax.ShapeDtypeStruct((rows, width), BF),
            jax.ShapeDtypeStruct((8, part), F32),
            jax.ShapeDtypeStruct((rows, width), BF),
        ],
        in_specs=[full] * (4 + len(others)),
        out_specs=[full] * 6,
        scratch_shapes=[
            pltpu.VMEM(mlp.shape, BF),
            pltpu.VMEM(((tp_count - 1) * run_rows, width), BF),
            pltpu.VMEM((rows, width), BF),
            *[pltpu.VMEM((group * 8, part), F32)] * 2,
        ]
        + [pltpu.VMEM((2 * rows, width // 2), BF)] * 2
        + [pltpu.VMEM((rows, width // 2), BF)] * 2
        + [pltpu.VMEM((2 * rows, wide), BF)]
        + [pltpu.VMEM((width // 2, wide), BF)] * 2
        + [pltpu.SemaphoreType.DMA((copies,))] * 2
        + [pltpu.SemaphoreType.DMA((passes,))] * 2,
        compiler_params=pltpu.CompilerParams(
            collective_id=number, has_side_effects=True, vmem_limit_bytes=VMEM_LIMIT
        ),
        name="attn_grads",
    )(hidden, branch, qkv, mixed, *others)


def turn_kernel(me_ref, *refs):
    half = len(refs) // 2
    for given, made in zip(refs[:half], refs[half:]):
        made[...] = given[...]


def in_order(me, arrays, group):
    rows, width = arrays[0].shape
    part = width // group
    if part % HD:
        return [
            jnp.concatenate(
                [lax.dynamic_slice_in_dim(x, (me ^ j) * part, part, 1) for j in range(group)], axis=1
            )
            for x in arrays
        ]
    return pl.pallas_call(
        turn_kernel,
        grid_spec=pltpu.PrefetchScalarGridSpec(
            num_scalar_prefetch=1,
            grid=(group,),
            in_specs=[pl.BlockSpec((rows, part), lambda j, m: (0, m[0] ^ j))] * len(arrays),
            out_specs=[pl.BlockSpec((rows, part), lambda j, m: (0, j))] * len(arrays),
        ),
        out_shape=[jax.ShapeDtypeStruct((rows, width), x.dtype) for x in arrays],
        name="in_order",
    )(me.astype(jnp.int32).reshape(1), *arrays)


def last_kernel(group, me_ref, *refs):
    tokens, branch, mlp, grad, out_ref, grad_out_ref = refs
    width = tokens.shape[1]
    part = width // group
    total = (tokens[...].astype(F32) + branch[...].astype(F32) + mlp[...].astype(F32)).astype(BF)
    for j in range(group):
        cols = slice(j * part, (j + 1) * part)
        at = pl.ds(pl.multiple_of((me_ref[0] ^ j) * part, part), part)
        out_ref[:, at] = total[:, cols]
        grad_out_ref[:, at] = grad[:, cols]


def last(me, group, tokens, branch, mlp, grad):
    rows, width = tokens.shape
    if width // group % HD:
        total = tokens.astype(F32) + branch.astype(F32) + mlp.astype(F32)
        return in_order(me, [total.astype(BF), grad], group)
    whole = pl.BlockSpec((rows, width), lambda i, m: (0, 0))
    return pl.pallas_call(
        functools.partial(last_kernel, group),
        grid_spec=pltpu.PrefetchScalarGridSpec(
            num_scalar_prefetch=1, grid=(1,), in_specs=[whole] * 4, out_specs=[whole] * 2
        ),
        out_shape=[jax.ShapeDtypeStruct((rows, width), BF)] * 2,
        compiler_params=pltpu.CompilerParams(vmem_limit_bytes=VMEM_LIMIT),
        name="last",
    )(me.astype(jnp.int32).reshape(1), tokens, branch, mlp, grad)


def lay_kernel(last, grad_ref, keep_ref, one_ref, two_ref, *out_refs):
    plane = early = 0
    half = len(last) // 2
    for ref in out_refs:
        cols = ref.shape[2]
        for p in range(ref.shape[1]):
            if plane in last:
                at = last.index(plane)
                got_ref = (one_ref, two_ref)[at // half]
                got = got_ref[:, at % half * cols : (at % half + 1) * cols].astype(F32)
                ref[:, p, :] = keep_ref[:, at * cols : (at + 1) * cols] + got
            else:
                ref[:, p, :] = grad_ref[:, early * cols : (early + 1) * cols]
                early += 1
            plane += 1


def lay_out(last, arrays, shapes):
    rows = arrays[0].shape[0]
    step = min(64, rows)
    return pl.pallas_call(
        functools.partial(lay_kernel, last),
        grid=(rows // step,),
        in_specs=[pl.BlockSpec((step, x.shape[1]), lambda i: (i, 0)) for x in arrays],
        out_specs=[pl.BlockSpec((step, *shape[1:]), lambda i: (i, 0, 0)) for shape in shapes],
        out_shape=[jax.ShapeDtypeStruct(shape, F32) for shape in shapes],
        compiler_params=pltpu.CompilerParams(vmem_limit_bytes=VMEM_LIMIT),
        name="lay_out",
    )(*arrays)


def chunks(total, size):
    return [(at, min(size, total - at)) for at in range(0, total, size)]


def experts_kernel(
    ctx_count,
    experts,
    share,
    part,
    groups,
    far_names,
    tokens_ref,
    branch_ref,
    gain_ref,
    place_ref,
    dy_ref,
    rides_ref,
    in_ref,
    down_ref,
    *refs,
):
    far_refs, refs = refs[: len(far_names)], refs[len(far_names) :]
    grads_in, grads_down, mlp_ref, two_part, mlp_first = refs[:5]
    (
        win,
        wdown,
        two,
        slots_out,
        back_out,
        back_got,
        active,
        gu,
        two_out,
        dy_out,
        two_got,
        dy_got,
        gu_got,
        active_got,
        send,
        recv,
    ) = refs[5:]
    slots, width = two.shape
    units = active.shape[1]
    room, run = slots // experts, width // experts
    arrays = dict(
        zip(far_names, far_refs),
        mlp=mlp_ref,
        mlp_first=mlp_first,
        gin=grads_in,
        gdown=grads_down,
        win=win,
        wdown=wdown,
        two=two,
        slots_out=slots_out,
        back_out=back_out,
        back_got=back_got,
        active=active,
        gu=gu,
        two_out=two_out,
        dy_out=dy_out,
        two_got=two_got,
        dy_got=dy_got,
        gu_got=gu_got,
        active_got=active_got,
        down=down_ref,
        **{"in": in_ref},
    )
    runs, base = {}, 0
    for name, moves in groups.items():
        runs[name] = Moves(ctx_count, moves, arrays, send, recv, (), base)
        base += len(moves)
    greet(ctx_count, masks_of([m for moves in groups.values() for m in moves]))
    stages = list_stages(experts)
    runs["load", "in"].begin()
    runs["load", "down"].begin()
    runs["far", "in"].begin()
    runs["far", "down"].begin()
    x = tokens_ref[...].astype(F32) + branch_ref[...].astype(F32)
    inverse = lax.rsqrt(jnp.mean(x * x, axis=-1, keepdims=True) + EPSILON)
    hidden = (x * inverse * gain_of(gain_ref, 1, part)).astype(BF)
    mine = flip(lax.axis_index(FSDP), 0) * ctx_count + lax.axis_index(CTX)
    lane = lax.broadcasted_iota(jnp.int32, (1, HD), 1)
    chosen = (lane % experts == mine // share) & (lane < 2 * experts)
    weights = jnp.sum(jnp.where(chosen, rides_ref[...].astype(F32), 0.0), axis=1, keepdims=True)
    for k in [*range(1, experts), 0]:
        rows = slice(k * room, (k + 1) * room)
        picked = dot(place_ref[k], hidden, 1, 0).astype(BF)
        if k == 0:
            two[rows] = picked
            continue
        for i in range(experts):
            slots_out[rows, i * run : (i + 1) * run] = picked[:, (i ^ k) * run : ((i ^ k) + 1) * run]
        runs["slots"].start(k - 1)
    for move in ("load", "far"):
        for name in ("in", "down"):
            runs[move, name].settle()
    for stage, ks in enumerate(stages):
        rows = slice(ks[0] * room, (ks[-1] + 1) * room)
        for k in ks:
            if k:
                runs["slots"].await_one(k - 1)
        for t in range(1, share):
            out_rows = slice((t - 1) * slots + rows.start, (t - 1) * slots + rows.stop)
            for k in range(experts):
                block = slice(k * part, (k + 1) * part)
                at = slice((k * share + t) * part, (k * share + t + 1) * part)
                two_out[out_rows, block] = two[rows, at]
                dy_out[out_rows, block] = dy_ref[rows, at]
        runs["two", stage, 0].begin()
        runs["dy", stage, 0].begin()
        two_rows, grad_rows = two[rows], dy_ref[rows]
        weight = weights[rows]
        for at, size in chunks(units, 256):
            cols = slice(at, at + size)
            g = dot(two_rows, win[:, cols], 1, 0)
            u = dot(two_rows, win[:, units + at : units + at + size], 1, 0)
            sigmoid = 1.0 / (1.0 + jnp.exp(-g))
            silu = g * sigmoid
            active[rows, cols] = (silu * u * weight).astype(BF)
            grad = dot(grad_rows, wdown[:, cols], 1, 0) * weight
            gu[rows, cols] = (grad * u * (sigmoid * (1.0 + g * (1.0 - sigmoid)))).astype(BF)
            gu[rows, units + at : units + at + size] = (grad * silu).astype(BF)
        runs["active", stage, 0].begin()
        runs["gu", stage, 0].begin()
        for i in range(experts):
            cols = slice(i * run, (i + 1) * run)
            back_out[rows, cols] = dot(gu[rows], win[cols], 1, 1).astype(BF)
        for k in ks:
            if k:
                runs["back"].start(k - 1)
        for i in range(experts):
            cols = slice(i * run, (i + 1) * run)
            out = dot(active[rows], wdown[cols], 1, 1).astype(BF)
            for k in ks:
                at = slice(k * room - rows.start, (k + 1) * room - rows.start)
                turned = slice((i ^ k) * run, ((i ^ k) + 1) * run)
                mlp_ref[k * room : (k + 1) * room, turned] = out[at]
        if stage < 2:
            for r in range(len(groups["mlp"]) // 2):
                runs["mlp"].start(2 * r + stage)
    for name in groups:
        if isinstance(name, tuple) and name[0] != "load":
            runs[name].finish()
    for k in range(experts):
        rows = slice(k * part, (k + 1) * part)
        own = slice(k * share * part, (k * share + 1) * part)
        for out, left, left_got, right, right_got in (
            (win, two, two_got, gu, gu_got),
            (wdown, dy_ref, dy_got, active, active_got),
        ):
            for at, size in chunks(right.shape[1], 512):
                cols = slice(at, at + size)
                total = dot(left[:, own], right[:, cols], 0, 0)
                if share > 1:
                    total = total + dot(left_got[:, rows], right_got[:, cols], 0, 0)
                out[rows, cols] = total.astype(BF)
        runs["out"].start(2 * k)
        runs["out"].start(2 * k + 1)
    runs["back"].settle()
    for i in range(experts):
        cols = slice(i * run, (i + 1) * run)
        total = dot(place_ref[0], back_out[:room, cols], 0, 0)
        for k in range(1, experts):
            at = slice((i ^ k) * run, ((i ^ k) + 1) * run)
            total = total + dot(place_ref[k], back_got[k * room : (k + 1) * room, at], 0, 0)
        two_part[:, cols] = total.astype(BF)
    runs["back"].finish()
    runs["out"].finish()
    runs["mlp"].finish()
    runs["slots"].finish()


def list_stages(experts):
    return [[0], list(range(1, experts - 1)), [experts - 1]]


def run_experts(
    number, ctx_count, tp_count, experts, share, part, fetched, far_moves, far, weights, tokens, *small
):
    place = small[2]
    room, rows = place.shape[1:]
    slots, width = experts * room, tokens.shape[1]
    units = weights["down"].shape[1]
    run = width // experts
    others = max(1, share - 1) * slots
    groups = {
        "slots": [
            (("slots_out", (k * room, room), None), ("two", (k * room, room), None), k * share, ())
            for k in range(1, experts)
        ],
        ("load", "in"): [(("in", r, None), ("win", r, None), None, ()) for r in fetched],
        ("load", "down"): [(("down", r, None), ("wdown", r, None), None, ()) for r in fetched],
        ("far", "in"): [m for m in far_moves if m[1][0] == "win"],
        ("far", "down"): [m for m in far_moves if m[1][0] == "wdown"],
    }
    for stage, ks in enumerate(list_stages(experts)):
        mine = (ks[0] * room, len(ks) * room)
        for name in ("two", "dy", "active", "gu"):
            groups[name, stage, 0] = []
            for t in range(1, share):
                rows_at = ((t - 1) * slots + mine[0], mine[1])
                source = (name + "_out", rows_at, None) if name in ("two", "dy") else (name, mine, None)
                target = (name + "_got", rows_at, None)
                groups[name, stage, 0].append((source, target, t, ()))
    groups["back"] = [
        (("back_out", (k * room, room), None), ("back_got", (k * room, room), None), k * share, ())
        for k in range(1, experts)
    ]
    groups["mlp"] = [
        (("mlp", (k * room, room), (TP, run, r)), ("mlp_first", ((2 * r - 2 + k) * room, room), None), -r, ())
        for r in range(1, tp_count)
        for k in range(2)
    ]
    groups["out"] = []
    for k in range(experts):
        r = (k * part, part)
        groups["out"].append((("win", r, None), ("gin", r, None), None, ()))
        groups["out"].append((("wdown", r, None), ("gdown", r, None), None, ()))
    total = sum(len(moves) for moves in groups.values())
    full = pl.BlockSpec(memory_space=pltpu.VMEM)
    any_spec = pl.BlockSpec(memory_space=pl.ANY)
    return pl.pallas_call(
        functools.partial(experts_kernel, ctx_count, experts, share, part, groups, list(far)),
        out_shape=[
            jax.ShapeDtypeStruct((experts * part, 2 * units), BF),
            jax.ShapeDtypeStruct((experts * part, units), BF),
            jax.ShapeDtypeStruct((slots, width), BF),
            jax.ShapeDtypeStruct((rows, width), BF),
            jax.ShapeDtypeStruct(((tp_count - 1) * 2 * room, run), BF),
        ],
        in_specs=[full] * 6 + [any_spec] * (2 + len(far)),
        out_specs=[any_spec] * 2 + [full] * 3,
        scratch_shapes=[
            pltpu.VMEM((width, 2 * units), BF),
            pltpu.VMEM((width, units), BF),
            *[pltpu.VMEM((slots, width), BF)] * 4,
            pltpu.VMEM((slots, units), BF),
            pltpu.VMEM((slots, 2 * units), BF),
            *[pltpu.VMEM((others, experts * part), BF)] * 4,
            pltpu.VMEM((others, 2 * units), BF),
            pltpu.VMEM((others, units), BF),
        ]
        + [pltpu.SemaphoreType.DMA((total,))] * 2,
        compiler_params=pltpu.CompilerParams(
            collective_id=number, has_side_effects=True, vmem_limit_bytes=VMEM_LIMIT
        ),
        name="experts",
    )(tokens, *small, weights["in"], weights["down"], *far.values())


def head_cols(index):
    return pl.ds(pl.multiple_of(index * HD, HD), HD)


def slot_table(place_ref, about_ref, out):
    experts = place_ref.shape[0]
    for e in range(experts):
        found = dot(place_ref[e], about_ref[...], 1, 0)
        filled = jnp.sum(place_ref[e].astype(F32), axis=1, keepdims=True)
        found = jnp.where(filled > 0, found, about_ref[:1].astype(F32))
        out[e, :, 0:1] = found[:, 0:1]
        out[e, :, 1:2] = found[:, 1:2] * 32.0 + found[:, 2:3]
        gate = found[:, 3 + e : 4 + e] + found[:, 3 + experts + e : 4 + experts + e]
        out[e, :, 2:3] = gate * filled


def scores_of(place, queries, keys, info, segk, idxk):
    segq, idxq = info[:, 0:1], info[:, 1:2]
    slots = dot(place, queries, 1, 0).astype(BF)
    scores = dot(slots, keys, 1, 1) * (HD**-0.5)
    allowed = (segq == segk) & (idxk <= idxq)
    scores = jnp.where(allowed, scores, MASKED)
    top = jnp.max(scores, axis=-1, keepdims=True)
    exps = jnp.exp(scores - top)
    total = jnp.sum(exps, axis=-1, keepdims=True)
    return slots, exps, 1.0 / total


def front_kernel(
    ctx_count,
    moves,
    marks,
    names_in,
    names_out,
    heads,
    part,
    tokens_ref,
    gain_ref,
    cos_ref,
    sin_ref,
    place_ref,
    about_ref,
    segk_ref,
    idxk_ref,
    dy_ref,
    ride_ref,
    place_mlp_ref,
    *refs,
):
    experts, room, rows = place_ref.shape
    width = tokens_ref.shape[1]
    wide = heads * HD
    group = width // part
    given, refs = refs[: len(names_in)], refs[len(names_in) :]
    gains_ref, hidden_ref, qkv_ref, kv_ref, mixed_ref, branch_ref, dy_out, rides_ref = refs[:8]
    refs = refs[8:]
    made, (full, slots_ref, picked, picked_ride, slot_info, send, recv, *bounces) = refs[: len(names_out)], refs[len(names_out) :]
    arrays = dict(
        gain_own=gain_ref,
        gains=gains_ref,
        picked=picked,
        slots=slots_ref,
        picked_ride=picked_ride,
        rides=rides_ref,
        dy=dy_out,
        qkv=qkv_ref,
        kv=kv_ref,
        full=full,
    )
    arrays.update(zip(names_in, given))
    arrays.update(zip(names_out, made))
    greet(ctx_count, masks_of(moves))
    run = Moves(ctx_count, moves, arrays, send, recv, bounces)
    gains_done, first_done, second_done, rest_done, keys_done, dy_done, spread_done = marks
    run_of = dy_ref.shape[1] // experts
    for k in range(experts):
        rows_at = slice(k * room, (k + 1) * room)
        cols = run_cols(run_of, k)
        slots = dot(place_mlp_ref[k], dy_ref[:, cols], 1, 0).astype(BF)
        rides = dot(place_mlp_ref[k], ride_ref[...], 1, 0).astype(BF)
        if k:
            picked[rows_at], picked_ride[rows_at] = slots, rides
        else:
            slots_ref[rows_at], rides_ref[rows_at] = slots, rides
    for i in range(keys_done, dy_done):
        run.start(i)
    run.begin(second_done)
    gains_ref[:16] = gain_ref[...]
    slot_table(place_ref, about_ref, slot_info)
    x = tokens_ref[...].astype(F32)
    normed = x * lax.rsqrt(jnp.mean(x * x, axis=-1, keepdims=True) + EPSILON)
    run.settle(gains_done)
    hidden_ref[...] = (normed * gain_of(gains_ref, 0, part)).astype(BF)
    run.settle(first_done, gains_done)
    run.kick(dy_done, spread_done)
    dy_out[:, run_cols(run_of)] = slots_ref[...]
    cos, sin = cos_ref[:rows], sin_ref[:rows]

    def project(plane):
        y = dot(hidden_ref[...], full[:, plane * wide : (plane + 1) * wide], 1, 0)
        for head in range(heads):
            cols = slice(head * HD, (head + 1) * HD)
            at = slice(plane * wide + head * HD, plane * wide + (head + 1) * HD)
            z = y[:, cols]
            qkv_ref[:, at] = (turn(z, cos, sin) if plane <= experts else z).astype(BF)

    project(experts)
    project(experts + 1)
    for i in range(rest_done, keys_done):
        if not moves[i][3]:
            run.start(i)
    kv_ref[:rows] = qkv_ref[:, experts * wide :]
    run.begin()
    run.settle(second_done, first_done)
    for plane in range(experts):
        project(plane)
    run.settle(keys_done, rest_done)
    run.settle(rest_done, second_done)
    run.start(len(moves) - 1)

    def step(i, carry):
        h, e = i // experts, i % experts
        cols = head_cols(e * heads + h)
        place = place_ref[e]
        _, exps, inv = scores_of(
            place,
            qkv_ref[:, cols],
            kv_ref[:, head_cols(h)],
            slot_info[e],
            segk_ref[...],
            idxk_ref[...],
        )
        attn = dot(exps.astype(BF), kv_ref[:, head_cols(heads + h)], 1, 0) * inv
        mixed = (attn * slot_info[e][:, 2:3]).astype(BF)
        mixed_ref[:, cols] = dot(place, mixed, 0, 0).astype(BF)
        return carry

    lax.fori_loop(0, heads * experts, step, 0)
    for j in range(group):
        rows_at = slice(j * part, (j + 1) * part)
        branch_ref[:, rows_at] = dot(mixed_ref[...], full[rows_at, (experts + 2) * wide :], 1, 1).astype(BF)
    run.finish()


def front(number, ctx_count, heads, part, moves, later, given, made, small):
    tokens, gain_own, place = small[0], small[1], small[4]
    experts, room, rows = place.shape
    width = tokens.shape[1]
    wide = heads * HD
    group = width // part
    full_wide = 2 * (experts + 1) * wide
    kv_moves = []
    order = [0]
    for bit in range(bits_of(ctx_count))[::-1]:
        for at in range(len(order)):
            target = ("kv", ((at + len(order)) * rows, rows), None)
            if at:
                source = ("kv", (at * rows, rows), None)
                kv_moves.append((source, target, 1 << bit, (source,)))
            else:
                source = ("qkv", (0, rows), (experts * wide, 2 * wide))
                kv_moves.append((source, target, 1 << bit, ()))
        order = order + order
    gains_moves, first_moves, second_moves, rest_moves, dy_moves, dy_spread = moves
    marks = [len(gains_moves)]
    for more in (first_moves, second_moves, rest_moves, kv_moves, dy_moves, dy_spread):
        marks.append(marks[-1] + len(more))
    whole = (FULL, (0, width), None)
    gathered = first_moves + second_moves + rest_moves
    landed = tuple(m[1] for m in gathered)
    keep = [(whole, ("kept", (0, width), None), None, landed)]
    moves = gains_moves + gathered + kv_moves + dy_moves + dy_spread + later + keep
    slots_shape = (experts * place.shape[1], width // experts)
    rides_shape = (experts * place.shape[1], HD)
    names_in, names_out = list(given), [*made, "kept"]
    shapes_out = [*made.values(), (width, full_wide)]
    any_spec = pl.BlockSpec(memory_space=pl.ANY)
    full = pl.BlockSpec(memory_space=pltpu.VMEM)
    small_out = [
        ((16 * group, gain_own.shape[1]), BF),
        ((rows, width), BF),
        ((rows, (experts + 2) * wide), BF),
        ((ctx_count * rows, 2 * wide), BF),
        ((rows, experts * wide), BF),
        ((rows, width), BF),
        ((slots_shape[0], width), BF),
        (rides_shape, BF),
    ]
    bounces = [
        pltpu.VMEM((source[1][1], (source[2] or (0, given[source[0]].shape[1]))[1]), BF)
        for source, _, mask, _ in moves
        if mask == 0
    ]
    out = pl.pallas_call(
        functools.partial(
            front_kernel, ctx_count, moves, marks, names_in, names_out, heads, part
        ),
        out_shape=[jax.ShapeDtypeStruct(*x) for x in small_out]
        + [jax.ShapeDtypeStruct(shape, BF) for shape in shapes_out],
        in_specs=[full] * len(small) + [any_spec] * len(names_in),
        out_specs=[full] * len(small_out) + [any_spec] * len(names_out),
        scratch_shapes=[
            pltpu.VMEM((width, full_wide), BF),
            *[pltpu.VMEM(slots_shape, BF)] * 2,
            pltpu.VMEM(rides_shape, BF),
            pltpu.VMEM((experts, room, HD), F32),
        ]
        + [pltpu.SemaphoreType.DMA((len(moves),))] * 2
        + bounces,
        compiler_params=pltpu.CompilerParams(
            collective_id=number, has_side_effects=True, vmem_limit_bytes=VMEM_LIMIT
        ),
        name="front",
    )(*small, *given.values())
    return out[: len(small_out)], dict(zip(names_out, out[len(small_out) :]))


def attend_back_kernel(
    ctx_count,
    moves,
    names_in,
    names_out,
    heads,
    part,
    tokens_ref,
    branch_ref,
    gain_ref,
    back_ref,
    dy_ref,
    gate_ref,
    qkv_ref,
    kv_ref,
    place_ref,
    about_ref,
    segk_ref,
    idxk_ref,
    cos_ref,
    sin_ref,
    mlp_first_ref,
    weight_ref,
    *refs,
):
    experts, _, rows = place_ref.shape
    keys = kv_ref.shape[0]
    wide = heads * HD
    width = tokens_ref.shape[1]
    given, refs = refs[: len(names_in)], refs[len(names_in) :]
    out_ref, resid_ref, grad_branch_ref, gain_out_ref, back_one_ref, mlp_out_ref = refs[:6]
    made, refs = refs[6 : 6 + len(names_out)], refs[6 + len(names_out) :]
    (
        full,
        grad_ref,
        back_acc,
        dk_acc,
        dv_acc,
        total,
        got,
        mlp_mine,
        mlp_got,
        slot_info,
        send,
        recv,
        pass_send,
        pass_recv,
        load,
    ) = refs
    arrays = {**dict(zip(names_in, given)), **dict(zip(names_out, made))}
    arrays.update(mlp_mine=mlp_mine, mlp_got=mlp_got)
    bits = range(bits_of(ctx_count))
    greet(ctx_count, sorted({*masks_of(moves), *[1 << b for b in bits]}))
    run = Moves(ctx_count, moves, arrays, send, recv)
    run.begin()
    slot_table(place_ref, about_ref, slot_info)
    edge = (experts + 2) * wide
    loads = []
    for i, cols in enumerate((pl.ds(edge, experts * wide), pl.ds(0, edge))):
        loads.append(pltpu.make_async_copy(weight_ref.at[:, cols], full.at[:, cols], load.at[i]))
        loads[-1].start()

    x = tokens_ref[...].astype(F32) + branch_ref[...].astype(F32)
    inverse = lax.rsqrt(jnp.mean(x * x, axis=-1, keepdims=True) + EPSILON)
    normed = x * inverse
    back = back_ref[...].astype(F32)
    gain_out_ref[...] = jnp.sum(back * normed, axis=0, keepdims=True)
    scaled = back * gain_of(gain_ref, 1, part)
    inner = jnp.mean(scaled * normed, axis=-1, keepdims=True)
    resid = dy_ref[...].astype(F32) + inverse * (scaled - normed * inner)
    resid_ref[...] = resid
    grad_branch_ref[...] = resid.astype(BF)
    loads[0].wait()
    for e in range(experts):
        cols = slice(edge + e * wide, edge + (e + 1) * wide)
        mixed = dot(grad_branch_ref[...], full[:, cols], 1, 0)
        grad_ref[:, e * wide : (e + 1) * wide] = (mixed * gate_ref[:, e : e + 1]).astype(BF)

    def head_copy(h, bit):
        size = keys >> (bit + 1)
        i = h * len(bits) + bit
        return pltpu.make_async_remote_copy(
            src_ref=total.at[h, pl.ds(size, size)],
            dst_ref=got.at[h, pl.ds(size, size)],
            send_sem=pass_send.at[i],
            recv_sem=pass_recv.at[i],
            device_id=peer(ctx_count, 1 << bit),
            device_id_type=pl.DeviceIdType.MESH,
        )

    def head_sum(h, bit):
        size = keys >> (bit + 1)
        head_copy(h, bit).wait_recv()
        mine = total[h, :size].astype(F32) + got[h, size : 2 * size].astype(F32)
        mine = mine.astype(BF)
        if bit + 1 < len(bits):
            total[h, :size] = mine
            head_copy(h, bit + 1).start()
        else:
            at = experts * wide
            out_ref[:, at + h * HD : at + (h + 1) * HD] = mine[:, :HD]
            at += wide
            out_ref[:, at + h * HD : at + (h + 1) * HD] = mine[:, HD:]

    for h in range(heads):
        dk_acc[...] = jnp.zeros_like(dk_acc)
        dv_acc[...] = jnp.zeros_like(dv_acc)

        def step(e, carry, h=h):
            cols = head_cols(e * heads + h)
            place = place_ref[e]
            k, v = kv_ref[:, h * HD : (h + 1) * HD], kv_ref[:, (heads + h) * HD : (heads + h + 1) * HD]
            slots, exps, inv = scores_of(
                place, qkv_ref[:, cols], k, slot_info[e], segk_ref[...], idxk_ref[...]
            )
            attn = dot(exps.astype(BF), v, 1, 0) * inv
            probs = exps * inv
            grad = dot(place, grad_ref[:, cols], 1, 0)
            delta = jnp.sum(grad * attn, axis=-1, keepdims=True)
            grad = grad.astype(BF)
            dv_acc[...] += dot(probs.astype(BF), grad, 0, 0)
            grad_probs = dot(grad, v, 1, 1)
            grad_scores = (probs * (grad_probs - delta)).astype(BF)
            dq = dot(grad_scores, k, 1, 0) * (HD**-0.5)
            dk_acc[...] += dot(grad_scores, slots, 0, 0) * (HD**-0.5)
            top = dq.astype(BF)
            low = (dq - top.astype(F32)).astype(BF)
            back_q = dot(place, top, 0, 0) + dot(place, low, 0, 0)
            out_ref[:, cols] = turn(back_q, cos_ref[:rows], -sin_ref[:rows]).astype(BF)
            return carry

        lax.fori_loop(0, experts, step, 0)
        total[h, :, :HD] = turn(dk_acc[...], cos_ref[...], -sin_ref[...]).astype(BF)
        total[h, :, HD:] = dv_acc[...].astype(BF)
        head_copy(h, 0).start()
        if h:
            head_sum(h - 1, 0)
    head_sum(heads - 1, 0)
    loads[1].wait()
    queries = experts * wide
    for j in range(width // part):
        rows_at = slice(j * part, (j + 1) * part)
        back_acc[:, rows_at] = dot(out_ref[:, :queries], full[rows_at, :queries], 1, 1)
    for bit in bits[1:]:
        for h in range(heads):
            head_sum(h, bit)
    for j in range(width // part):
        rows_at = slice(j * part, (j + 1) * part)
        keyed = dot(out_ref[:, queries:], full[rows_at, queries:edge], 1, 1)
        back_one_ref[:, rows_at] = (back_acc[:, rows_at] + keyed).astype(BF)
    runs_mlp = [i for i, m in enumerate(moves) if m[0][0] == "mlp"]
    for i in runs_mlp:
        run.await_one(i)
    slots, others = mlp_mine.shape[0], len(runs_mlp) - 1
    first = mlp_first_ref.shape[0] // others
    for low, top, came, size in ((0, first, mlp_first_ref, first), (first, slots, mlp_got, slots)):
        mlp_total = mlp_mine[low:top].astype(F32)
        for r in range(others):
            mlp_total = mlp_total + came[r * size + low : r * size + top].astype(F32)
        mlp_out_ref[low:top] = mlp_total.astype(BF)
    for h in range(heads):
        for bit in bits:
            head_copy(h, bit).wait_send()
    run.finish()


def attend_back(number, ctx_count, tp_count, heads, part, moves, given, made, weight, *small):
    tokens, qkv, kv = small[0], small[6], small[7]
    rows, width = tokens.shape
    keys = kv.shape[0]
    any_spec = pl.BlockSpec(memory_space=pl.ANY)
    full = pl.BlockSpec(memory_space=pltpu.VMEM)
    passes = heads * bits_of(ctx_count)
    slots, run = given["mlp"].shape[0], width // tp_count
    first = small[-1].shape[0] // (tp_count - 1)
    mlp_moves = [(("mlp", (0, slots), (TP, run)), ("mlp_mine", (0, slots), None), None, ())]
    for r in range(1, tp_count):
        source = ("mlp", (first, slots - first), (TP, run, r))
        target = ("mlp_got", ((r - 1) * slots + first, slots - first), None)
        mlp_moves.append((source, target, -r, ()))
    moves = mlp_moves + moves
    small_out = [
        (qkv.shape, BF),
        ((rows, width), F32),
        ((rows, width), BF),
        ((1, width), F32),
        ((rows, width), BF),
        ((slots, run), BF),
    ]
    out = pl.pallas_call(
        functools.partial(
            attend_back_kernel, ctx_count, moves, list(given), list(made), heads, part
        ),
        out_shape=[jax.ShapeDtypeStruct(*x) for x in small_out]
        + [jax.ShapeDtypeStruct(shape, BF) for shape in made.values()],
        in_specs=[full] * len(small) + [any_spec] * (1 + len(given)),
        out_specs=[full] * len(small_out) + [any_spec] * len(made),
        input_output_aliases={
            len(small) + 1 + list(given).index(n): len(small_out) + i for i, n in enumerate(made)
        },
        scratch_shapes=[
            pltpu.VMEM(weight.shape, BF),
            pltpu.VMEM((rows, weight.shape[1] - qkv.shape[1]), BF),
            pltpu.VMEM((rows, width), F32),
        ]
        + [pltpu.VMEM((keys, HD), F32)] * 2
        + [pltpu.VMEM((heads, keys, 2 * HD), BF)] * 2
        + [pltpu.VMEM((slots, run), BF), pltpu.VMEM(((tp_count - 1) * slots, run), BF)]
        + [pltpu.VMEM((*small[8].shape[:2], HD), F32)]
        + [pltpu.SemaphoreType.DMA((len(moves),))] * 2
        + [pltpu.SemaphoreType.DMA((passes,))] * 2
        + [pltpu.SemaphoreType.DMA((2,))],
        compiler_params=pltpu.CompilerParams(
            collective_id=number, has_side_effects=True, vmem_limit_bytes=VMEM_LIMIT
        ),
        name="attend_back",
    )(*small, weight, *given.values())
    return out[: len(small_out)], dict(zip(made, out[len(small_out) :]))


def spread_kernel(experts, me_ref, *refs):
    from_in, from_down = refs[:experts], refs[experts : 2 * experts]
    in_ref, down_ref = refs[2 * experts :]
    units = down_ref.shape[2]
    for m in range(experts):

        @pl.when(me_ref[0] == m)
        def _():
            for e in range(experts):
                for c in range(2):
                    in_ref[:, e, c, :] = from_in[e ^ m][:, c * units : (c + 1) * units].astype(F32)
                down_ref[:, e, :] = from_down[e ^ m][...].astype(F32)


def spread_grads(from_in, from_down, me, in_shape, down_shape):
    experts = len(from_in)
    step = min(64, in_shape[0])

    def rows_of(width):
        return pl.BlockSpec((step, width), lambda i, m: (i, 0))

    return pl.pallas_call(
        functools.partial(spread_kernel, experts),
        grid_spec=pltpu.PrefetchScalarGridSpec(
            num_scalar_prefetch=1,
            grid=(in_shape[0] // step,),
            in_specs=[rows_of(from_in[0].shape[1])] * experts
            + [rows_of(from_down[0].shape[1])] * experts,
            out_specs=[
                pl.BlockSpec((step, *in_shape[1:]), lambda i, m: (i, 0, 0, 0)),
                pl.BlockSpec((step, *down_shape[1:]), lambda i, m: (i, 0, 0)),
            ],
        ),
        out_shape=[
            jax.ShapeDtypeStruct(in_shape, F32),
            jax.ShapeDtypeStruct(down_shape, F32),
        ],
        compiler_params=pltpu.CompilerParams(vmem_limit_bytes=VMEM_LIMIT),
        name="spread_grads",
    )(me.astype(jnp.int32).reshape(1), *from_in, *from_down)


def places(routes, gates, experts, cap, room):
    rows = routes.shape[0]
    named = routes[:, :, None] == jnp.arange(experts, dtype=jnp.int32)[None, None, :]
    member = jnp.any(named, axis=1)
    gate = jnp.sum(jnp.where(named, gates[:, :, None], 0.0), axis=1)
    token = jnp.arange(rows, dtype=jnp.int32)
    earlier = (token[None, :] < token[:, None]).astype(BF)
    rank = dot(earlier, member.astype(BF), 1, 0).astype(jnp.int32)
    slot = jnp.where(member, rank, -1).T
    taken = slot[:, None, :] == jnp.arange(room, dtype=jnp.int32)[None, :, None]
    return taken, gate


def split(x):
    high = x.astype(BF)
    return high, (x - high.astype(F32)).astype(BF)


def layer(
    counts,
    tokens,
    gain_attn,
    gain_mlp,
    w_kv,
    w_query,
    w_out_attn,
    w_in,
    w_down,
    segments,
    attn_routes,
    attn_gates,
    mlp_routes,
    mlp_gates,
    cotangent,
):
    fsdp_count, ctx_count, tp_count = counts
    group = fsdp_count * ctx_count
    me = lax.axis_index(GROUP)
    ctx_me = lax.axis_index(CTX)
    rows, width = tokens.shape[1:]
    cap = 9 * rows // 16
    room = -(-cap // 16) * 16
    part = width // group
    attn_experts = w_query.shape[1]
    experts = w_in.shape[1]
    share = group // experts
    expert_me = me // share
    hidden_units = w_down.shape[2]
    head_width = w_kv.shape[2]

    def piece(x, index, size=part, axis=1):
        return lax.dynamic_slice_in_dim(x, index * size, size, axis)

    def exchange(x, mask):
        return swap(x, mask, GROUP, group)

    def after(x, *events):
        return lax.optimization_barrier((x, *events))[0]

    high, second = group // 2, group // 4

    gain_own = jnp.pad(jnp.concatenate([gain_attn, gain_mlp])[None, :], ((0, 15), (0, 0)))
    kv_out_own = jnp.concatenate([w_kv.reshape(part, -1), w_out_attn.reshape(part, -1)], axis=1)
    attn_own = [w_query.reshape(part, -1), kv_out_own]
    far_x, far_y = [], []
    for own in attn_own:
        far_x.append(exchange(own, high))
        far_y.append(exchange(own, second))

    seg_row = segments[0]
    seq_total = seg_row.shape[0]
    ctx_bits = list(range(bits_of(ctx_count)))[::-1]
    key_order = [0]
    for bit in ctx_bits:
        key_order = key_order + [j | (1 << bit) for j in key_order]
    key_seg = jnp.concatenate([piece(seg_row, ctx_me ^ j, rows, 0) for j in key_order])
    key_idx = jnp.concatenate(
        [(ctx_me ^ j) * rows + jnp.arange(rows, dtype=jnp.int32) for j in key_order]
    )
    place_idx = jnp.arange(seq_total, dtype=jnp.int32)
    pos = jnp.sum(
        (seg_row[None, :] == key_seg[:, None]) & (place_idx[None, :] < key_idx[:, None]),
        axis=1,
        dtype=jnp.int32,
    ).astype(F32)
    frequency = ROPE_BASE ** (-(jnp.arange(HD // 2, dtype=F32) * 2.0) / HD)
    angles = pos[:, None] * frequency[None, :]
    cos_half, sin_half = jnp.cos(angles), jnp.sin(angles)
    cos = jnp.concatenate([cos_half, cos_half], axis=1)
    sin = jnp.concatenate([-sin_half, sin_half], axis=1)
    taken_attn, gate_attn = places(attn_routes[0], attn_gates[0], attn_experts, cap, room)
    place_attn = taken_attn.astype(BF)
    own_seg, own_idx = key_seg[:rows], key_idx[:rows]
    gate_high, gate_low = split(gate_attn)
    about = [own_seg[:, None], (own_idx // 32)[:, None], (own_idx % 32)[:, None], gate_high, gate_low]
    about = jnp.concatenate([x.astype(BF) for x in about], axis=1)
    about = jnp.pad(about, ((0, 0), (0, HD - about.shape[1])))
    key_row = (key_seg.astype(F32)[None, :], key_idx.astype(F32)[None, :])
    taken_mlp, gate_mlp = places(mlp_routes[0], mlp_gates[0], experts, cap, room)
    mine_first = [expert_me ^ k for k in range(experts)]
    place_mlp = jnp.concatenate([piece(taken_mlp, e, 1, 0) for e in mine_first]).astype(BF)
    tokens_rel, grad_out = in_order(me, [tokens[0], cotangent[0]], group)

    def expert_rows(k):
        in_rows = piece(w_in, expert_me ^ k, 1, 1)
        down_rows = piece(w_down, expert_me ^ k, 1, 1)
        return [in_rows[:, 0, 0], in_rows[:, 0, 1], down_rows[:, 0]]

    to_send = [expert_rows(k) for k in range(experts)]

    def given_sends(ks):
        return {("send", k, c): x for k in ks for c, x in enumerate(to_send[k])}

    in_cols, down_cols = (0, 2 * hidden_units), (2 * hidden_units, hidden_units)
    weight_shapes = {"in": (width, 2 * hidden_units), "down": (width, hidden_units)}

    def weight_moves(k, first, size, prefix=""):
        moves = []
        sides = (("in", (0, hidden_units)), ("in", (hidden_units, hidden_units)), ("down", None))
        for c, (name, cols) in enumerate(sides):
            base = k * share * part + first
            source = (("send", k, c), (first, size), None)
            landed = (prefix + name, (base, size), cols)
            moves.append((source, landed, k * share, ()))
            for t in range(1, share):
                target = (prefix + name, (base + t * part, size), cols)
                if k:
                    moves.append((landed, target, t, (landed,)))
                else:
                    moves.append((source, target, t, ()))
        return moves

    def many_weight_moves(cuts):
        return [m for cut in cuts for m in weight_moves(*cut)]

    near = [k for k in range(1, experts) if k & (k - 1) == 0]
    far = [k for k in range(1, experts) if k & (k - 1)]
    half_part = part // 2

    far_x, to_send = lax.optimization_barrier((far_x, to_send))
    cut = max(16, part * 3 // 8 // 16 * 16)
    gather_moves = []
    queries, two_planes = attn_experts * head_width, 2 * head_width
    for n, first, size_of, edge in (
        (1, 0, two_planes, queries),
        (0, 0, queries, 0),
        (1, two_planes, queries, queries + two_planes),
    ):
        cols, own_cols = (edge, size_of), (first, size_of)
        moves = []
        held = {0: [(("own", n), 0, part, ())], high: [(("x", n), 0, part, ())], second: [(("y", n), 0, part, ())]}
        corner = []
        for side, mask, low, top in ((("x", n), second, 0, cut), (("y", n), high, cut, part)):
            half = (top - low) // 32 * 16
            for at, size in ((low, half), (low + half, top - low - half)):
                if size:
                    target = (FULL, ((high | second) * part + at, size), cols)
                    corner.append(((side, (at, size), own_cols), target, mask, ()))
        corner = corner[::2] + corner[1::2]
        moves += corner
        held[high | second] = [(FULL, t[1][0] - (high | second) * part, t[1][1], (t,)) for _, t, _, _ in corner]
        for j in (0, high, second):
            source = (held[j][0][0], (0, part), own_cols)
            moves.append((source, (FULL, (j * part, part), cols), None, ()))
        for bit in range(bits_of(group) - 2)[::-1]:
            for j in list(held):
                there = []
                for name, at, size, needs in held[j]:
                    if name == FULL:
                        source = (name, (at + j * part, size), cols)
                    else:
                        source = (name, (at, size), own_cols)
                    target = (FULL, ((j | 1 << bit) * part + at, size), cols)
                    moves.append((source, target, 1 << bit, needs))
                    there.append((FULL, at, size, (target,)))
                held[j | 1 << bit] = there
        gather_moves.append(moves)
    gain_moves = [
        (("gain_own", (0, 16), None), ("gains", (j * 16, 16), None), j, ())
        for j in range(1, group)
    ]
    heads = head_width // HD
    later = weight_moves(0, 0, part) + many_weight_moves([(k, 0, half_part) for k in near])
    gate_ride = jnp.concatenate(split(gate_mlp), axis=1)
    gate_ride = jnp.pad(gate_ride, ((0, 0), (0, HD - 2 * experts)))
    dy_moves = [
        ((name, (k * room, room), None), (target, (k * room, room), None), k * share, ())
        for k in range(1, experts)
        for name, target in (("picked", "slots"), ("picked_ride", "rides"))
    ]
    dy_spread, run = [], width // tp_count
    for k in range(experts):
        mine = (k * room, room)
        needs = ((("slots", mine, None)),) if k else ()
        for r in range(1, tp_count):
            source, target = ("slots", mine, None), ("dy", mine, (TP, run, 0, r))
            dy_spread.append((source, target, -r, needs))
    (gains, hidden_one, qkv, kv, mixed, branch, dy_slots, dy_rides), made = front(
        1,
        ctx_count,
        heads,
        part,
        (gain_moves, *gather_moves, dy_moves, dy_spread),
        later,
        {
            **{("own", n): x for n, x in enumerate(attn_own)},
            **{("x", n): x for n, x in enumerate(far_x)},
            **{("y", n): x for n, x in enumerate(far_y)},
            **given_sends([0, *near]),
        },
        weight_shapes,
        (
            tokens_rel,
            gain_own,
            cos,
            sin,
            place_attn,
            about,
            *key_row,
            grad_out,
            gate_ride,
            place_mlp,
        ),
    )
    attn_full, weights = made["kept"], {n: made[n] for n in weight_shapes}
    branch_sum = lax.psum(branch, TP)
    cuts = [(k, half_part, part - half_part) for k in near] + [(k, 0, half_part) for k in far]
    to_send, weights, _ = lax.optimization_barrier((to_send, weights, branch))
    given = {**given_sends([*near, *far]), **weights}
    weights = move("weights_two", 3, ctx_count, many_weight_moves(cuts), given, weight_shapes)
    fetched, far_moves = [], []
    for j in range(group):
        size = half_part if j // share in far else part
        if fetched and sum(fetched[-1]) == j * part:
            fetched[-1] = (fetched[-1][0], fetched[-1][1] + size)
        else:
            fetched.append((j * part, size))
    for k in far:
        far_moves += weight_moves(k, half_part, part - half_part, "w")
    grads_in, grads_down, mlp_slots, back_two_part, mlp_first = run_experts(
        4,
        ctx_count,
        tp_count,
        experts,
        share,
        part,
        fetched,
        far_moves,
        given_sends(far),
        weights,
        tokens_rel,
        branch_sum,
        gains,
        place_mlp,
        dy_slots,
        dy_rides,
    )
    back_two = lax.psum(back_two_part, TP)
    got_in, got_down = {0: grads_in}, {0: grads_down}

    def grad_moves(ks, cuts, first=0):
        moves = []
        for at in range(first, part, part // cuts):
            for k in ks:
                for name in ("in", "down"):
                    source = (name, (k * part + at, part // cuts), None)
                    target = ((name, k), (at, part // cuts), None)
                    moves.append((source, target, k * share, ()))
        made_shapes = {("in", k): (part, 2 * hidden_units) for k in ks}
        return moves, {**made_shapes, **{("down", k): (part, hidden_units) for k in ks}}

    def keep_grads(made, ks):
        got_in.update({k: made[("in", k)] for k in ks})
        got_down.update({k: made[("down", k)] for k in ks})

    moves, made_shapes = grad_moves(near, 1)
    early, early_shapes = grad_moves(far, 4)
    moves += early[: len(early) // 4]
    made_shapes.update(early_shapes)
    grads_in, grads_down, _ = lax.optimization_barrier((grads_in, grads_down, back_two_part))
    given = {"in": grads_in, "down": grads_down}
    made = move("grads_near", 5, ctx_count, moves, given, made_shapes)
    keep_grads(made, near)

    moves, made_shapes = grad_moves(far, 4, part // 4)
    back_two, given, made = lax.optimization_barrier((back_two, given, made))
    given.update({name: made[name] for name in made_shapes})
    given["mlp"] = mlp_slots
    (grad_qkv, grad_resid, grad_branch, gain_two_grad, back_one_part, mlp_run), made = attend_back(
        6,
        ctx_count,
        tp_count,
        heads,
        part,
        moves,
        given,
        made_shapes,
        attn_full,
        tokens_rel,
        branch_sum,
        gains,
        back_two,
        grad_out,
        gate_attn,
        qkv,
        kv,
        place_attn,
        about,
        *key_row,
        cos,
        sin,
        mlp_first,
    )
    keep_grads(made, far)
    upper = list(range(1, bits_of(group)))
    grad_attnw, kept, given, grad_tokens, gain_grads, mlp_sum = attn_grads(
        7,
        ctx_count,
        tp_count,
        upper,
        part,
        head_width,
        hidden_one,
        grad_branch,
        grad_qkv,
        mixed,
        back_one_part,
        tokens_rel,
        gains,
        grad_resid,
        gain_two_grad,
        mlp_run,
        place_mlp,
    )
    planes = attn_experts * 2 + 2
    lanes, last_lanes = lanes_of(planes, attn_experts + 2, upper)
    half = given.shape[1] // 2
    came = []
    for i in range(2):
        bit = dict(lanes)[last_lanes[3 * i]][-1]
        came.append(exchange(given[:, i * half : (i + 1) * half], 1 << bit))
    output, grad_tokens = last(me, group, tokens_rel, branch_sum, mlp_sum, grad_tokens)
    grad_in_out, grad_down_out = spread_grads(
        [got_in[k] for k in range(experts)],
        [got_down[k] for k in range(experts)],
        expert_me,
        w_in.shape,
        w_down.shape,
    )
    came, _ = lax.optimization_barrier((came, (output, grad_in_out)))
    grad_query_w, grad_kv_w, grad_out_w = lay_out(
        last_lanes, [grad_attnw, kept, *came], (w_query.shape, w_kv.shape, w_out_attn.shape)
    )
    return (
        output[None],
        grad_tokens[None],
        gain_grads[0],
        gain_grads[1],
        grad_kv_w,
        grad_query_w,
        grad_out_w,
        grad_in_out,
        grad_down_out,
    )


def solution(mesh):
    rows = P(FSDP, CTX, None)
    weight = P(GROUP, None, TP)
    weight_in = P(GROUP, None, None, TP)
    return jax.shard_map(
        functools.partial(layer, tuple(mesh.shape[a] for a in (FSDP, CTX, TP))),
        mesh=mesh,
        in_specs=(
            rows,
            P(GROUP),
            P(GROUP),
            weight,
            weight,
            weight,
            weight_in,
            weight,
            P(FSDP, None),
            rows,
            rows,
            rows,
            rows,
            rows,
        ),
        out_specs=(rows, rows, P(GROUP), P(GROUP), weight, weight, weight, weight_in, weight),
        check_vma=False,
    )
```

```python
import functools

import jax
import jax.numpy as jnp
from jax import lax
from jax.experimental import pallas as pl
from jax.experimental.pallas import tpu as pltpu
from jax.sharding import PartitionSpec as P

HD = 128
EPSILON = 1e-06
ROPE_BASE = 10000.0
MASKED = -1e30
FSDP, CTX, TP = "fsdp", "ctx", "tp"
GROUP = (FSDP, CTX)
FULL = "full"
BF = jnp.bfloat16
F32 = jnp.float32
VMEM_LIMIT = 56 * 1024 * 1024


def normalize(tensor):
    inverse = lax.rsqrt(jnp.mean(tensor * tensor, axis=-1, keepdims=True) + EPSILON)
    return (tensor * inverse, inverse)


def norm_back(grad_in, normed, inverse, gain_vec):
    scaled = grad_in * gain_vec
    inner_mean = jnp.mean(scaled * normed, axis=-1, keepdims=True)
    return (inverse * (scaled - normed * inner_mean), jnp.sum(grad_in * normed, axis=0))


def dot(a, b, ca, cb):
    return lax.dot_general(a, b, (((ca,), (cb,)), ((), ())), preferred_element_type=F32)


def turn(x, cos, sin):
    return x * cos + pltpu.roll(x, HD // 2, 1) * sin


def swap(x, mask, axes, count):
    return lax.ppermute(x, axes, [(i, i ^ mask) for i in range(count)])


def bits_of(count):
    return count.bit_length() - 1


def flip(value, mask):
    step = 1
    while step <= mask:
        if mask & step:
            value = value + step - 2 * step * ((value // step) % 2)
        step *= 2
    return value


def peer(ctx_count, mask):
    if mask < 0:
        return {TP: flip(lax.axis_index(TP), -mask)}
    return {
        FSDP: flip(lax.axis_index(FSDP), mask // ctx_count),
        CTX: flip(lax.axis_index(CTX), mask % ctx_count),
    }


def greet(ctx_count, masks):
    barrier = pltpu.get_barrier_semaphore()
    for mask in masks:
        pl.semaphore_signal(
            barrier, inc=1, device_id=peer(ctx_count, mask), device_id_type=pl.DeviceIdType.MESH
        )
    pl.semaphore_wait(barrier, len(masks))


def run_cols(size, flips=0):
    return pl.ds(pl.multiple_of(flip(lax.axis_index(TP), flips) * size, size), size)


def window(ref, rows, cols):
    if rows[0] == TP:
        return ref.at[run_cols(rows[1], rows[2])]
    if cols is None:
        return ref.at[pl.ds(rows[0], rows[1])]
    if cols[0] == TP:
        return ref.at[pl.ds(rows[0], rows[1]), run_cols(*cols[1:3])]
    return ref.at[pl.ds(rows[0], rows[1]), pl.ds(cols[0], cols[1])]


def gain_of(gains_ref, which, part):
    rows = gains_ref[...].astype(F32)
    cols = slice(which * part, (which + 1) * part)
    return jnp.concatenate([rows[at : at + 1, cols] for at in range(0, rows.shape[0], 16)], axis=1)


class Moves:
    def __init__(self, ctx_count, moves, arrays, send, recv, bounces=(), base=0):
        self.moves = moves
        self.onward = {}
        bounces = list(bounces)
        self.copies = []
        self.place = {m[1]: i for i, m in enumerate(moves)}
        self.started, self.came, self.sent = set(), set(), set()
        for at, (source, target, mask, _) in enumerate(moves):
            i = base + at
            src = window(arrays[source[0]], *source[1:])
            dst = window(arrays[target[0]], *target[1:])
            if mask:
                copy = pltpu.make_async_remote_copy(
                    src_ref=src,
                    dst_ref=dst,
                    send_sem=send.at[i],
                    recv_sem=recv.at[i],
                    device_id=peer(ctx_count, mask),
                    device_id_type=pl.DeviceIdType.MESH,
                )
            elif mask is None:
                copy = pltpu.make_async_copy(src, dst, recv.at[i])
            else:
                bounce = bounces.pop(0)
                copy = pltpu.make_async_copy(src, bounce, recv.at[i])
                self.onward[at] = pltpu.make_async_copy(bounce, dst, send.at[i])
            self.copies.append(copy)

    def start(self, i):
        if i not in self.started:
            self.started.add(i)
            self.copies[i].start()

    def begin(self, count=None):
        for i, move in enumerate(self.moves[:count]):
            if not move[3]:
                self.start(i)

    def await_one(self, i):
        if i not in self.came:
            self.came.add(i)
            if i in self.onward:
                self.copies[i].wait()
                self.onward[i].start()
            elif self.moves[i][2] is None:
                self.copies[i].wait()
            else:
                self.copies[i].wait_recv()

    def await_sent(self, i):
        if i not in self.sent:
            self.sent.add(i)
            self.copies[i].wait_send()

    def kick(self, first, count):
        for i in range(first, count):
            for target in self.moves[i][3]:
                self.await_one(self.place[target])
            self.start(i)

    def settle(self, count=None, first=0):
        count = len(self.moves) if count is None else count
        for i in range(first, count):
            if i in self.onward:
                self.await_one(i)
        for i in range(first, count):
            for target in self.moves[i][3]:
                self.await_one(self.place[target])
            self.start(i)
        for i in range(first, count):
            self.await_one(i)

    def finish(self):
        self.settle()
        for i in range(len(self.moves)):
            if i in self.onward:
                self.onward[i].wait()
            elif self.moves[i][2] is not None:
                self.await_sent(i)


def masks_of(moves):
    return sorted({move[2] for move in moves if move[2]})


def move_kernel(ctx_count, moves, names_in, names_out, *refs):
    count = len(names_in) + len(names_out)
    refs, (send, recv, *bounces) = refs[:count], refs[count:]
    arrays = dict(zip(names_in, refs))
    arrays.update(zip(names_out, refs[len(names_in) :]))
    greet(ctx_count, masks_of(moves))
    run = Moves(ctx_count, moves, arrays, send, recv, bounces)
    run.begin()
    run.finish()


def move(name, number, ctx_count, moves, given, made):
    names_in = [n for n in given if n not in made] + [n for n in given if n in made]
    plain = [n for n in names_in if n not in made]
    names_out = list(made)
    any_spec = pl.BlockSpec(memory_space=pl.ANY)
    bounces = [
        pltpu.VMEM((source[1][1], (source[2] or (0, given[source[0]].shape[1]))[1]), BF)
        for source, _, mask, _ in moves
        if not mask
    ]
    return dict(
        zip(
            names_out,
            pl.pallas_call(
                functools.partial(
                    move_kernel,
                    ctx_count,
                    moves,
                    plain + ["old_" + n for n in names_in[len(plain) :]],
                    names_out,
                ),
                out_shape=[jax.ShapeDtypeStruct(shape, BF) for shape in made.values()],
                in_specs=[any_spec] * len(names_in),
                out_specs=[any_spec] * len(names_out),
                input_output_aliases={
                    names_in.index(n): names_out.index(n) for n in names_out if n in given
                },
                scratch_shapes=[pltpu.SemaphoreType.DMA((len(moves),))] * 2 + bounces,
                compiler_params=pltpu.CompilerParams(
                    collective_id=number, has_side_effects=True, vmem_limit_bytes=VMEM_LIMIT
                ),
                name=name,
            )(*[given[n] for n in names_in]),
        )
    )


def lanes_of(planes, late, bits):
    lanes = []
    for n, plane in enumerate([*range(late, planes), *range(late)]):
        lanes.append((plane, bits if n % 2 else bits[::-1]))
    last = lanes[-6:]
    return lanes, [p for p, _ in last[::2]] + [p for p, _ in last[1::2]]


def attn_grads_kernel(
    ctx_count,
    groups,
    bits,
    part,
    cols,
    hidden_ref,
    branch_ref,
    qkv_ref,
    mixed_ref,
    back_ref,
    tokens_any,
    gain_ref,
    resid_any,
    gain_two_ref,
    mlp_ref,
    place_ref,
    out_ref,
    keep_ref,
    give_one_ref,
    give_two_ref,
    grad_tokens_ref,
    gain_out_ref,
    mlp_sum_ref,
    mlp_got,
    back_got,
    back_sum,
    gain_send,
    gain_got,
    hidden,
    branch,
    hidden_odd,
    branch_odd,
    right,
    grads,
    got,
    tokens_ref,
    resid_ref,
    load,
    send,
    recv,
    pass_send,
    pass_recv,
):
    rows, width = hidden_ref.shape
    count = width // part // 2
    planes = right.shape[1] // cols
    first = qkv_ref.shape[1]
    group = width // part
    run_rows = groups["spread"][0][0][1][1]
    greet(ctx_count, masks_of([m for moves in groups.values() for m in moves]))
    arrays = dict(
        back=back_ref,
        back_got=back_got,
        back_sum=back_sum,
        mlp=mlp_ref,
        mlp_got=mlp_got,
        mlp_sum=mlp_sum_ref,
        gain_send=gain_send,
        gain_got=gain_got,
        hidden_odd=hidden_odd,
        branch_odd=branch_odd,
        qkv_in=qkv_ref,
        mixed_in=mixed_ref,
        hidden=hidden,
        branch=branch,
        right=right,
    )
    runs, base = {}, 0
    for name, moves in groups.items():
        if name != "sums":
            runs[name] = Moves(ctx_count, moves, arrays, pass_send, pass_recv, (), base)
        base += len(moves)
    run = runs["share"]
    late_loads = []
    for i, (far_ref, near_ref) in enumerate(((tokens_any, tokens_ref), (resid_any, resid_ref))):
        late_loads.append(pltpu.make_async_copy(far_ref, near_ref, load.at[i]))
        late_loads[-1].start()
    runs["reduce"].begin()
    runs["mlp"].begin()
    for given, even_side, odd_side in (
        (branch_ref, branch, branch_odd),
        (hidden_ref, hidden, hidden_odd),
    ):
        for j in range(count):
            block = slice(j * part, (j + 1) * part)
            even_side[:rows, block] = given[:, 2 * j * part : (2 * j + 1) * part]
            odd_side[:, block] = given[:, (2 * j + 1) * part : (2 * j + 2) * part]
    run.begin()
    right[:rows, :first] = qkv_ref[...]
    right[:rows, first:] = mixed_ref[...]
    number = [0]

    def copy(mask, block, plane):
        i = number[0]
        number[0] += 1
        window_of = (pl.ds(block * part, part), pl.ds(plane * cols, cols))
        return pltpu.make_async_remote_copy(
            src_ref=grads.at[window_of],
            dst_ref=got.at[window_of],
            send_sem=send.at[i],
            recv_sem=recv.at[i],
            device_id=peer(ctx_count, mask),
            device_id_type=pl.DeviceIdType.MESH,
        )

    sent, flying, left = [], {}, {}

    def send_half(plane, order, step):
        at = bits.index(order[step])
        flying[plane] = {
            j: copy(1 << order[step], j, plane) for j in left[plane] if j >> at & 1
        }
        for c in flying[plane].values():
            c.start()
        sent.extend(flying[plane].values())

    late = first // cols
    lanes, last_lanes = lanes_of(planes, late, bits)
    for plane, order in lanes:
        run.settle(2 if plane >= late else 4)
        at = pl.ds(plane * cols, cols)
        left_side = hidden if plane < late else branch
        grads[:, at] = dot(left_side[...], right[:, at], 0, 0).astype(BF)
        left[plane] = list(range(count))
        send_half(plane, order, 0)
    def sum_back():
        runs["reduce"].settle()
        own = run_cols(run_rows)
        total = back_ref[own].astype(F32)
        for r in range(len(groups["reduce"])):
            total = total + back_got[r * run_rows : (r + 1) * run_rows].astype(F32)
        back_sum[own] = total.astype(BF)
        runs["spread"].begin()

    def sum_mlp():
        runs["mlp"].settle()
        room = mlp_ref.shape[0] // place_ref.shape[0]
        total = dot(place_ref[0], mlp_ref[:room], 0, 0)
        for k in range(1, place_ref.shape[0]):
            total = total + dot(place_ref[k], mlp_got[k * room : (k + 1) * room], 0, 0)
        mlp_sum_ref[:, run_cols(mlp_ref.shape[1])] = total.astype(BF)
        runs["mlp_spread"].begin()

    def norm_back():
        for late_load in late_loads:
            late_load.wait()
        runs["spread"].settle()
        x = tokens_ref[...].astype(F32)
        inverse = lax.rsqrt(jnp.mean(x * x, axis=-1, keepdims=True) + EPSILON)
        normed = x * inverse
        back = back_sum[...].astype(F32)
        gain_grad = jnp.sum(back * normed, axis=0, keepdims=True)
        scaled = back * gain_of(gain_ref, 0, part)
        inner = jnp.mean(scaled * normed, axis=-1, keepdims=True)
        grad_tokens_ref[...] = (resid_ref[...] + inverse * (scaled - normed * inner)).astype(BF)
        gain_send[...] = jnp.zeros_like(gain_send)
        for j in range(group):
            block = slice(j * part, (j + 1) * part)
            gain_send[j * 8 : j * 8 + 1] = gain_grad[:, block]
            gain_send[j * 8 + 1 : j * 8 + 2] = gain_two_ref[:, block]
        runs["gains"].begin()

    for step in range(len(bits)):
        for n, (plane, order) in enumerate(lanes):
            if step == len(bits) - 1 and plane in last_lanes:
                continue
            if step == 0 and n == len(lanes) * 2 // 5:
                sum_back()
                sum_mlp()
            if step == 1 and n == min(2, len(lanes) - 1):
                norm_back()
            at = bits.index(order[step])
            left[plane] = [j for j in left[plane] if not j >> at & 1]
            across = pl.ds(plane * cols, cols)
            for j in left[plane]:
                flying[plane][j | 1 << at].wait_recv()
                down, other = pl.ds(j * part, part), pl.ds((j | 1 << at) * part, part)
                total = grads[down, across].astype(F32) + got[other, across].astype(F32)
                if step == len(bits) - 1:
                    at_out = sum(p not in last_lanes for p in range(plane))
                    out_ref[:, at_out * cols : (at_out + 1) * cols] = total
                elif step == len(bits) - 2 and plane in last_lanes:
                    at_last = last_lanes.index(plane)
                    there = slice(at_last * cols, (at_last + 1) * cols)
                    if j:
                        half = len(last_lanes) // 2
                        give_ref = (give_one_ref, give_two_ref)[at_last // half]
                        at_give = at_last % half * cols
                        give_ref[:, at_give : at_give + cols] = total.astype(BF)
                    else:
                        keep_ref[:, there] = total
                else:
                    grads[down, across] = total.astype(BF)
            if step < len(bits) - 1 and not (step == len(bits) - 2 and plane in last_lanes):
                send_half(plane, order, step + 1)
    runs["gains"].settle()
    gains = gain_send[:8]
    for j in range(1, group):
        gains = gains + gain_got[j * 8 : (j + 1) * 8]
    gain_out_ref[...] = gains
    for moves in runs.values():
        moves.finish()
    for c in sent:
        c.wait_send()


def attn_grads(number, ctx_count, tp_count, bits, part, cols, hidden, branch, qkv, mixed, *others):
    rows, width = hidden.shape
    group = width // part
    first = qkv.shape[1]
    theirs = (rows, rows)
    run_rows = rows // tp_count
    mlp, place = others[-2:]
    experts, room = place.shape[:2]
    run = mlp.shape[1]
    groups = {
        "mlp": [
            (("mlp", (k * room, room), None), ("mlp_got", (k * room, room), None), k * group // experts, ())
            for k in range(1, experts)
        ],
        "mlp_spread": [
            (("mlp_sum", (0, rows), (TP, run)), ("mlp_sum", (0, rows), (TP, run, 0, r)), -r, ())
            for r in range(1, tp_count)
        ],
        "reduce": [
            (("back", (TP, run_rows, r), None), ("back_got", ((r - 1) * run_rows, run_rows), None), -r, ())
            for r in range(1, tp_count)
        ],
        "spread": [
            (("back_sum", (TP, run_rows, 0), None), ("back_sum", (TP, run_rows, 0), r), -r, ())
            for r in range(1, tp_count)
        ],
        "gains": [
            (("gain_send", (j * 8, 8), None), ("gain_got", (j * 8, 8), None), j, ())
            for j in range(1, group)
        ],
        "share": [
            (("mixed_in", (0, rows), None), ("right", theirs, (first, mixed.shape[1])), 1, ()),
            (("branch_odd", (0, rows), None), ("branch", theirs, None), 1, ()),
            (("qkv_in", (0, rows), None), ("right", theirs, (0, first)), 1, ()),
            (("hidden_odd", (0, rows), None), ("hidden", theirs, None), 1, ()),
        ],
        "sums": [((), (), 1 << b, ()) for b in bits],
    }
    wide = qkv.shape[1] + mixed.shape[1]
    copies = (wide // cols) * (width // part // 2)
    passes = sum(len(moves) for moves in groups.values())
    full = pl.BlockSpec(memory_space=pltpu.VMEM)
    return pl.pallas_call(
        functools.partial(attn_grads_kernel, ctx_count, groups, bits, part, cols),
        out_shape=[
            jax.ShapeDtypeStruct((part, wide - 6 * cols), F32),
            jax.ShapeDtypeStruct((part, 6 * cols), F32),
            *[jax.ShapeDtypeStruct((part, 3 * cols), BF)] * 2,
            jax.ShapeDtypeStruct((rows, width), BF),
            jax.ShapeDtypeStruct((8, part), F32),
            jax.ShapeDtypeStruct((rows, width), BF),
        ],
        in_specs=[pl.BlockSpec(memory_space=pl.ANY) if i in (5, 7) else full for i in range(4 + len(others))],
        out_specs=[full] * 7,
        scratch_shapes=[
            pltpu.VMEM(mlp.shape, BF),
            pltpu.VMEM(((tp_count - 1) * run_rows, width), BF),
            pltpu.VMEM((rows, width), BF),
            *[pltpu.VMEM((group * 8, part), F32)] * 2,
        ]
        + [pltpu.VMEM((2 * rows, width // 2), BF)] * 2
        + [pltpu.VMEM((rows, width // 2), BF)] * 2
        + [pltpu.VMEM((2 * rows, wide), BF)]
        + [pltpu.VMEM((width // 2, wide), BF)] * 2
        + [pltpu.VMEM((rows, width), BF), pltpu.VMEM((rows, width), F32), pltpu.SemaphoreType.DMA((2,))]
        + [pltpu.SemaphoreType.DMA((copies,))] * 2
        + [pltpu.SemaphoreType.DMA((passes,))] * 2,
        compiler_params=pltpu.CompilerParams(
            collective_id=number, has_side_effects=True, vmem_limit_bytes=VMEM_LIMIT
        ),
        name="attn_grads",
    )(hidden, branch, qkv, mixed, *others)


def turn_kernel(me_ref, *refs):
    half = len(refs) // 2
    for given, made in zip(refs[:half], refs[half:]):
        made[...] = given[...]


def in_order(me, arrays, group):
    rows, width = arrays[0].shape
    part = width // group
    if part % HD:
        return [
            jnp.concatenate(
                [lax.dynamic_slice_in_dim(x, (me ^ j) * part, part, 1) for j in range(group)], axis=1
            )
            for x in arrays
        ]
    return pl.pallas_call(
        turn_kernel,
        grid_spec=pltpu.PrefetchScalarGridSpec(
            num_scalar_prefetch=1,
            grid=(group,),
            in_specs=[pl.BlockSpec((rows, part), lambda j, m: (0, m[0] ^ j))] * len(arrays),
            out_specs=[pl.BlockSpec((rows, part), lambda j, m: (0, j))] * len(arrays),
        ),
        out_shape=[jax.ShapeDtypeStruct((rows, width), x.dtype) for x in arrays],
        name="in_order",
    )(me.astype(jnp.int32).reshape(1), *arrays)


def last_kernel(group, me_ref, *refs):
    tokens, branch, mlp, grad, out_ref, grad_out_ref = refs
    width = tokens.shape[1]
    part = width // group
    total = (tokens[...].astype(F32) + branch[...].astype(F32) + mlp[...].astype(F32)).astype(BF)
    for j in range(group):
        cols = slice(j * part, (j + 1) * part)
        at = pl.ds(pl.multiple_of((me_ref[0] ^ j) * part, part), part)
        out_ref[:, at] = total[:, cols]
        grad_out_ref[:, at] = grad[:, cols]


def last(me, group, tokens, branch, mlp, grad):
    rows, width = tokens.shape
    if width // group % HD:
        total = tokens.astype(F32) + branch.astype(F32) + mlp.astype(F32)
        return in_order(me, [total.astype(BF), grad], group)
    whole = pl.BlockSpec((rows, width), lambda i, m: (0, 0))
    return pl.pallas_call(
        functools.partial(last_kernel, group),
        grid_spec=pltpu.PrefetchScalarGridSpec(
            num_scalar_prefetch=1, grid=(1,), in_specs=[whole] * 4, out_specs=[whole] * 2
        ),
        out_shape=[jax.ShapeDtypeStruct((rows, width), BF)] * 2,
        compiler_params=pltpu.CompilerParams(vmem_limit_bytes=VMEM_LIMIT),
        name="last",
    )(me.astype(jnp.int32).reshape(1), tokens, branch, mlp, grad)


def lay_kernel(last, grad_ref, keep_ref, one_ref, two_ref, *out_refs):
    plane = early = 0
    half = len(last) // 2
    for ref in out_refs:
        cols = ref.shape[2]
        for p in range(ref.shape[1]):
            if plane in last:
                at = last.index(plane)
                got_ref = (one_ref, two_ref)[at // half]
                got = got_ref[:, at % half * cols : (at % half + 1) * cols].astype(F32)
                ref[:, p, :] = keep_ref[:, at * cols : (at + 1) * cols] + got
            else:
                ref[:, p, :] = grad_ref[:, early * cols : (early + 1) * cols]
                early += 1
            plane += 1


def lay_out(last, arrays, shapes):
    rows = arrays[0].shape[0]
    step = min(64, rows)
    return pl.pallas_call(
        functools.partial(lay_kernel, last),
        grid=(rows // step,),
        in_specs=[pl.BlockSpec((step, x.shape[1]), lambda i: (i, 0)) for x in arrays],
        out_specs=[pl.BlockSpec((step, *shape[1:]), lambda i: (i, 0, 0)) for shape in shapes],
        out_shape=[jax.ShapeDtypeStruct(shape, F32) for shape in shapes],
        compiler_params=pltpu.CompilerParams(vmem_limit_bytes=VMEM_LIMIT),
        name="lay_out",
    )(*arrays)


def chunks(total, size):
    return [(at, min(size, total - at)) for at in range(0, total, size)]


def experts_kernel(
    ctx_count,
    experts,
    share,
    part,
    groups,
    far_names,
    tokens_ref,
    branch_ref,
    gain_ref,
    place_ref,
    dy_ref,
    rides_ref,
    in_ref,
    down_ref,
    *refs,
):
    far_refs, refs = refs[: len(far_names)], refs[len(far_names) :]
    grads_in, grads_down, mlp_ref, two_part, mlp_first = refs[:5]
    (
        win,
        wdown,
        two,
        slots_out,
        back_out,
        back_got,
        active,
        gu,
        two_out,
        dy_out,
        two_got,
        dy_got,
        gu_got,
        active_got,
        send,
        recv,
    ) = refs[5:]
    slots, width = two.shape
    units = active.shape[1]
    room, run = slots // experts, width // experts
    arrays = dict(
        zip(far_names, far_refs),
        mlp=mlp_ref,
        mlp_first=mlp_first,
        gin=grads_in,
        gdown=grads_down,
        win=win,
        wdown=wdown,
        two=two,
        slots_out=slots_out,
        back_out=back_out,
        back_got=back_got,
        active=active,
        gu=gu,
        two_out=two_out,
        dy_out=dy_out,
        two_got=two_got,
        dy_got=dy_got,
        gu_got=gu_got,
        active_got=active_got,
        down=down_ref,
        **{"in": in_ref},
    )
    runs, base = {}, 0
    for name, moves in groups.items():
        runs[name] = Moves(ctx_count, moves, arrays, send, recv, (), base)
        base += len(moves)
    greet(ctx_count, masks_of([m for moves in groups.values() for m in moves]))
    stages = list_stages(experts)
    runs["load", "in"].begin()
    runs["load", "down"].begin()
    runs["far", "in"].begin()
    runs["far", "down"].begin()
    x = tokens_ref[...].astype(F32) + branch_ref[...].astype(F32)
    inverse = lax.rsqrt(jnp.mean(x * x, axis=-1, keepdims=True) + EPSILON)
    hidden = (x * inverse * gain_of(gain_ref, 1, part)).astype(BF)
    mine = flip(lax.axis_index(FSDP), 0) * ctx_count + lax.axis_index(CTX)
    lane = lax.broadcasted_iota(jnp.int32, (1, HD), 1)
    chosen = (lane % experts == mine // share) & (lane < 2 * experts)
    weights = jnp.sum(jnp.where(chosen, rides_ref[...].astype(F32), 0.0), axis=1, keepdims=True)
    for k in [*range(1, experts), 0]:
        rows = slice(k * room, (k + 1) * room)
        picked = dot(place_ref[k], hidden, 1, 0).astype(BF)
        if k == 0:
            two[rows] = picked
            continue
        for i in range(experts):
            slots_out[rows, i * run : (i + 1) * run] = picked[:, (i ^ k) * run : ((i ^ k) + 1) * run]
        runs["slots"].start(k - 1)
    for move in ("load", "far"):
        for name in ("in", "down"):
            runs[move, name].settle()
    for stage, ks in enumerate(stages):
        rows = slice(ks[0] * room, (ks[-1] + 1) * room)
        for k in ks:
            if k:
                runs["slots"].await_one(k - 1)
        for t in range(1, share):
            out_rows = slice((t - 1) * slots + rows.start, (t - 1) * slots + rows.stop)
            for k in range(experts):
                block = slice(k * part, (k + 1) * part)
                at = slice((k * share + t) * part, (k * share + t + 1) * part)
                two_out[out_rows, block] = two[rows, at]
                dy_out[out_rows, block] = dy_ref[rows, at]
        runs["two", stage, 0].begin()
        runs["dy", stage, 0].begin()
        two_rows, grad_rows = two[rows], dy_ref[rows]
        weight = weights[rows]
        for at, size in chunks(units, 256):
            cols = slice(at, at + size)
            g = dot(two_rows, win[:, cols], 1, 0)
            u = dot(two_rows, win[:, units + at : units + at + size], 1, 0)
            sigmoid = 1.0 / (1.0 + jnp.exp(-g))
            silu = g * sigmoid
            active[rows, cols] = (silu * u * weight).astype(BF)
            grad = dot(grad_rows, wdown[:, cols], 1, 0) * weight
            gu[rows, cols] = (grad * u * (sigmoid * (1.0 + g * (1.0 - sigmoid)))).astype(BF)
            gu[rows, units + at : units + at + size] = (grad * silu).astype(BF)
        runs["active", stage, 0].begin()
        runs["gu", stage, 0].begin()
        for i in range(experts):
            cols = slice(i * run, (i + 1) * run)
            back_out[rows, cols] = dot(gu[rows], win[cols], 1, 1).astype(BF)
        for k in ks:
            if k:
                runs["back"].start(k - 1)
        for i in range(experts):
            cols = slice(i * run, (i + 1) * run)
            out = dot(active[rows], wdown[cols], 1, 1).astype(BF)
            for k in ks:
                at = slice(k * room - rows.start, (k + 1) * room - rows.start)
                turned = slice((i ^ k) * run, ((i ^ k) + 1) * run)
                mlp_ref[k * room : (k + 1) * room, turned] = out[at]
        for k in ks:
            if k < 2:
                for r in range(len(groups["mlp"]) // 2):
                    runs["mlp"].start(2 * r + k)
    for name in groups:
        if isinstance(name, tuple) and name[0] != "load":
            runs[name].finish()
    for k in range(experts):
        rows = slice(k * part, (k + 1) * part)
        own = slice(k * share * part, (k * share + 1) * part)
        for out, left, left_got, right, right_got in (
            (win, two, two_got, gu, gu_got),
            (wdown, dy_ref, dy_got, active, active_got),
        ):
            for at, size in chunks(right.shape[1], 512):
                cols = slice(at, at + size)
                total = dot(left[:, own], right[:, cols], 0, 0)
                if share > 1:
                    total = total + dot(left_got[:, rows], right_got[:, cols], 0, 0)
                out[rows, cols] = total.astype(BF)
        runs["out"].start(2 * k)
        runs["out"].start(2 * k + 1)
    runs["back"].settle()
    for i in range(experts):
        cols = slice(i * run, (i + 1) * run)
        total = dot(place_ref[0], back_out[:room, cols], 0, 0)
        for k in range(1, experts):
            at = slice((i ^ k) * run, ((i ^ k) + 1) * run)
            total = total + dot(place_ref[k], back_got[k * room : (k + 1) * room, at], 0, 0)
        two_part[:, cols] = total.astype(BF)
    runs["back"].finish()
    runs["out"].finish()
    runs["mlp"].finish()
    runs["slots"].finish()


def list_stages(experts):
    return [[0], list(range(1, experts - 1)), [experts - 1]]


def run_experts(
    number, ctx_count, tp_count, experts, share, part, fetched, far_moves, far, weights, tokens, *small
):
    place = small[2]
    room, rows = place.shape[1:]
    slots, width = experts * room, tokens.shape[1]
    units = weights["down"].shape[1]
    run = width // experts
    others = max(1, share - 1) * slots
    groups = {
        "slots": [
            (("slots_out", (k * room, room), None), ("two", (k * room, room), None), k * share, ())
            for k in range(1, experts)
        ],
        ("load", "in"): [(("in", r, None), ("win", r, None), None, ()) for r in fetched],
        ("load", "down"): [(("down", r, None), ("wdown", r, None), None, ()) for r in fetched],
        ("far", "in"): [m for m in far_moves if m[1][0] == "win"],
        ("far", "down"): [m for m in far_moves if m[1][0] == "wdown"],
    }
    for stage, ks in enumerate(list_stages(experts)):
        mine = (ks[0] * room, len(ks) * room)
        for name in ("two", "dy", "active", "gu"):
            groups[name, stage, 0] = []
            for t in range(1, share):
                rows_at = ((t - 1) * slots + mine[0], mine[1])
                source = (name + "_out", rows_at, None) if name in ("two", "dy") else (name, mine, None)
                target = (name + "_got", rows_at, None)
                groups[name, stage, 0].append((source, target, t, ()))
    groups["back"] = [
        (("back_out", (k * room, room), None), ("back_got", (k * room, room), None), k * share, ())
        for k in range(1, experts)
    ]
    groups["mlp"] = [
        (("mlp", (k * room, room), (TP, run, r)), ("mlp_first", ((2 * r - 2 + k) * room, room), None), -r, ())
        for r in range(1, tp_count)
        for k in range(2)
    ]
    groups["out"] = []
    for k in range(experts):
        r = (k * part, part)
        groups["out"].append((("win", r, None), ("gin", r, None), None, ()))
        groups["out"].append((("wdown", r, None), ("gdown", r, None), None, ()))
    total = sum(len(moves) for moves in groups.values())
    full = pl.BlockSpec(memory_space=pltpu.VMEM)
    any_spec = pl.BlockSpec(memory_space=pl.ANY)
    return pl.pallas_call(
        functools.partial(experts_kernel, ctx_count, experts, share, part, groups, list(far)),
        out_shape=[
            jax.ShapeDtypeStruct((experts * part, 2 * units), BF),
            jax.ShapeDtypeStruct((experts * part, units), BF),
            jax.ShapeDtypeStruct((slots, width), BF),
            jax.ShapeDtypeStruct((rows, width), BF),
            jax.ShapeDtypeStruct(((tp_count - 1) * 2 * room, run), BF),
        ],
        in_specs=[full] * 6 + [any_spec] * (2 + len(far)),
        out_specs=[any_spec] * 2 + [full] * 3,
        scratch_shapes=[
            pltpu.VMEM((width, 2 * units), BF),
            pltpu.VMEM((width, units), BF),
            *[pltpu.VMEM((slots, width), BF)] * 4,
            pltpu.VMEM((slots, units), BF),
            pltpu.VMEM((slots, 2 * units), BF),
            *[pltpu.VMEM((others, experts * part), BF)] * 4,
            pltpu.VMEM((others, 2 * units), BF),
            pltpu.VMEM((others, units), BF),
        ]
        + [pltpu.SemaphoreType.DMA((total,))] * 2,
        compiler_params=pltpu.CompilerParams(
            collective_id=number, has_side_effects=True, vmem_limit_bytes=VMEM_LIMIT
        ),
        name="experts",
    )(tokens, *small, weights["in"], weights["down"], *far.values())


def head_cols(index):
    return pl.ds(pl.multiple_of(index * HD, HD), HD)


def slot_table(place_ref, about_ref, out):
    experts = place_ref.shape[0]
    for e in range(experts):
        found = dot(place_ref[e], about_ref[...], 1, 0)
        filled = jnp.sum(place_ref[e].astype(F32), axis=1, keepdims=True)
        found = jnp.where(filled > 0, found, about_ref[:1].astype(F32))
        out[e, :, 0:1] = found[:, 0:1]
        out[e, :, 1:2] = found[:, 1:2] * 32.0 + found[:, 2:3]
        gate = found[:, 3 + e : 4 + e] + found[:, 3 + experts + e : 4 + experts + e]
        out[e, :, 2:3] = gate * filled


def scores_of(place, queries, keys, info, segk, idxk):
    segq, idxq = info[:, 0:1], info[:, 1:2]
    slots = dot(place, queries, 1, 0).astype(BF)
    scores = dot(slots, keys, 1, 1) * (HD**-0.5)
    allowed = (segq == segk) & (idxk <= idxq)
    scores = jnp.where(allowed, scores, MASKED)
    top = jnp.max(scores, axis=-1, keepdims=True)
    exps = jnp.exp(scores - top)
    total = jnp.sum(exps, axis=-1, keepdims=True)
    return slots, exps, 1.0 / total


def front_kernel(
    ctx_count,
    moves,
    marks,
    names_in,
    names_out,
    heads,
    part,
    tokens_ref,
    gain_ref,
    cos_ref,
    sin_ref,
    place_ref,
    about_ref,
    segk_ref,
    idxk_ref,
    dy_ref,
    ride_ref,
    place_mlp_ref,
    *refs,
):
    experts, room, rows = place_ref.shape
    width = tokens_ref.shape[1]
    wide = heads * HD
    group = width // part
    given, refs = refs[: len(names_in)], refs[len(names_in) :]
    gains_ref, hidden_out, qkv_out, kv_out, mixed_ref, branch_ref, dy_out, rides_ref = refs[:8]
    refs = refs[8:]
    made, refs = refs[: len(names_out)], refs[len(names_out) :]
    hidden_ref, qkv_ref, kv_ref, early, full, slots_ref, picked, picked_ride, slot_info, send, recv, *bounces = refs
    leaving = []
    for i, pair in enumerate(((hidden_ref, hidden_out), (qkv_ref, qkv_out), (kv_ref, kv_out))):
        leaving.append(pltpu.make_async_copy(*pair, early.at[i]))
    arrays = dict(
        gain_own=gain_ref,
        gains=gains_ref,
        picked=picked,
        slots=slots_ref,
        picked_ride=picked_ride,
        rides=rides_ref,
        dy=dy_out,
        qkv=qkv_ref,
        kv=kv_ref,
        full=full,
    )
    arrays.update(zip(names_in, given))
    arrays.update(zip(names_out, made))
    greet(ctx_count, masks_of(moves))
    run = Moves(ctx_count, moves, arrays, send, recv, bounces)
    gains_done, first_done, second_done, rest_done, keys_done, dy_done, spread_done = marks
    run_of = dy_ref.shape[1] // experts
    for k in range(experts):
        rows_at = slice(k * room, (k + 1) * room)
        cols = run_cols(run_of, k)
        slots = dot(place_mlp_ref[k], dy_ref[:, cols], 1, 0).astype(BF)
        rides = dot(place_mlp_ref[k], ride_ref[...], 1, 0).astype(BF)
        if k:
            picked[rows_at], picked_ride[rows_at] = slots, rides
        else:
            slots_ref[rows_at], rides_ref[rows_at] = slots, rides
    for i in range(keys_done, dy_done):
        run.start(i)
    run.begin(second_done)
    gains_ref[:16] = gain_ref[...]
    slot_table(place_ref, about_ref, slot_info)
    x = tokens_ref[...].astype(F32)
    normed = x * lax.rsqrt(jnp.mean(x * x, axis=-1, keepdims=True) + EPSILON)
    run.settle(gains_done)
    hidden_ref[...] = (normed * gain_of(gains_ref, 0, part)).astype(BF)
    leaving[0].start()
    run.settle(first_done, gains_done)
    run.kick(dy_done, spread_done)
    dy_out[:, run_cols(run_of)] = slots_ref[...]
    cos, sin = cos_ref[:rows], sin_ref[:rows]

    def project(plane):
        y = dot(hidden_ref[...], full[:, plane * wide : (plane + 1) * wide], 1, 0)
        for head in range(heads):
            cols = slice(head * HD, (head + 1) * HD)
            at = slice(plane * wide + head * HD, plane * wide + (head + 1) * HD)
            z = y[:, cols]
            qkv_ref[:, at] = (turn(z, cos, sin) if plane <= experts else z).astype(BF)

    project(experts)
    project(experts + 1)
    for i in range(rest_done, keys_done):
        if not moves[i][3]:
            run.start(i)
    kv_ref[:rows] = qkv_ref[:, experts * wide :]
    run.begin()
    run.settle(second_done, first_done)
    run.start(len(moves) - 2)
    for plane in range(experts):
        project(plane)
    leaving[1].start()
    run.settle(keys_done, rest_done)
    leaving[2].start()

    def step(i, carry):
        h, e = i // experts, i % experts
        cols = head_cols(e * heads + h)
        place = place_ref[e]
        _, exps, inv = scores_of(
            place,
            qkv_ref[:, cols],
            kv_ref[:, head_cols(h)],
            slot_info[e],
            segk_ref[...],
            idxk_ref[...],
        )
        attn = dot(exps.astype(BF), kv_ref[:, head_cols(heads + h)], 1, 0) * inv
        mixed = (attn * slot_info[e][:, 2:3]).astype(BF)
        mixed_ref[:, cols] = dot(place, mixed, 0, 0).astype(BF)
        return carry

    for part_of in range(2):
        half = heads * experts // 2
        lax.fori_loop(part_of * half, (part_of + 1) * half, step, 0, unroll=2)
        if part_of == 0:
            run.settle(rest_done, second_done)
            run.start(len(moves) - 1)
    for j in range(group):
        rows_at = slice(j * part, (j + 1) * part)
        branch_ref[:, rows_at] = dot(mixed_ref[...], full[rows_at, (experts + 2) * wide :], 1, 1).astype(BF)
    run.finish()
    for copy in leaving:
        copy.wait()


def front(number, ctx_count, heads, part, moves, later, given, made, small):
    tokens, gain_own, place = small[0], small[1], small[4]
    experts, room, rows = place.shape
    width = tokens.shape[1]
    wide = heads * HD
    group = width // part
    full_wide = 2 * (experts + 1) * wide
    kv_moves = []
    order = [0]
    for bit in range(bits_of(ctx_count))[::-1]:
        for at in range(len(order)):
            target = ("kv", ((at + len(order)) * rows, rows), None)
            if at:
                source = ("kv", (at * rows, rows), None)
                kv_moves.append((source, target, 1 << bit, (source,)))
            else:
                source = ("qkv", (0, rows), (experts * wide, 2 * wide))
                kv_moves.append((source, target, 1 << bit, ()))
        order = order + order
    gains_moves, first_moves, second_moves, rest_moves, dy_moves, dy_spread = moves
    marks = [len(gains_moves)]
    for more in (first_moves, second_moves, rest_moves, kv_moves, dy_moves, dy_spread):
        marks.append(marks[-1] + len(more))
    gathered = first_moves + second_moves + rest_moves
    edge = (experts + 2) * wide
    keep = []
    for cols, some in (((0, edge), first_moves + second_moves), ((edge, full_wide - edge), rest_moves)):
        rows_at = ((0, width), cols)
        keep.append(((FULL, *rows_at), ("kept", *rows_at), None, tuple(m[1] for m in some)))
    moves = gains_moves + gathered + kv_moves + dy_moves + dy_spread + later + keep
    slots_shape = (experts * place.shape[1], width // experts)
    rides_shape = (experts * place.shape[1], HD)
    names_in, names_out = list(given), [*made, "kept"]
    shapes_out = [*made.values(), (width, full_wide)]
    any_spec = pl.BlockSpec(memory_space=pl.ANY)
    full = pl.BlockSpec(memory_space=pltpu.VMEM)
    small_out = [
        ((16 * group, gain_own.shape[1]), BF),
        ((rows, width), BF),
        ((rows, (experts + 2) * wide), BF),
        ((ctx_count * rows, 2 * wide), BF),
        ((rows, experts * wide), BF),
        ((rows, width), BF),
        ((slots_shape[0], width), BF),
        (rides_shape, BF),
    ]
    bounces = [
        pltpu.VMEM((source[1][1], (source[2] or (0, given[source[0]].shape[1]))[1]), BF)
        for source, _, mask, _ in moves
        if mask == 0
    ]
    out = pl.pallas_call(
        functools.partial(
            front_kernel, ctx_count, moves, marks, names_in, names_out, heads, part
        ),
        out_shape=[jax.ShapeDtypeStruct(*x) for x in small_out]
        + [jax.ShapeDtypeStruct(shape, BF) for shape in shapes_out],
        in_specs=[full] * len(small) + [any_spec] * len(names_in),
        out_specs=[any_spec if i in (1, 2, 3) else full for i in range(len(small_out))]
        + [any_spec] * len(names_out),
        scratch_shapes=[
            *[pltpu.VMEM(*small_out[i]) for i in (1, 2, 3)],
            pltpu.SemaphoreType.DMA((3,)),
            pltpu.VMEM((width, full_wide), BF),
            *[pltpu.VMEM(slots_shape, BF)] * 2,
            pltpu.VMEM(rides_shape, BF),
            pltpu.VMEM((experts, room, HD), F32),
        ]
        + [pltpu.SemaphoreType.DMA((len(moves),))] * 2
        + bounces,
        compiler_params=pltpu.CompilerParams(
            collective_id=number, has_side_effects=True, vmem_limit_bytes=VMEM_LIMIT
        ),
        name="front",
    )(*small, *given.values())
    return out[: len(small_out)], dict(zip(names_out, out[len(small_out) :]))


def attend_back_kernel(
    ctx_count,
    moves,
    names_in,
    names_out,
    heads,
    part,
    tokens_ref,
    branch_ref,
    gain_ref,
    back_ref,
    dy_ref,
    gate_ref,
    place_ref,
    about_ref,
    segk_ref,
    idxk_ref,
    cos_ref,
    sin_ref,
    mlp_first_ref,
    weight_ref,
    qkv_any,
    kv_any,
    *refs,
):
    experts, _, rows = place_ref.shape
    keys = kv_any.shape[0]
    wide = heads * HD
    width = tokens_ref.shape[1]
    given, refs = refs[: len(names_in)], refs[len(names_in) :]
    out_ref, resid_out, grad_branch_out, gain_out_ref, back_one_ref, mlp_out_ref = refs[:6]
    made, refs = refs[6 : 6 + len(names_out)], refs[6 + len(names_out) :]
    (
        full,
        grad_ref,
        back_acc,
        dk_acc,
        dv_acc,
        total,
        got,
        mlp_mine,
        mlp_got,
        slot_info,
        qkv_ref,
        kv_ref,
        resid_ref,
        grad_branch_ref,
        send,
        recv,
        pass_send,
        pass_recv,
        load,
    ) = refs
    arrays = {**dict(zip(names_in, given)), **dict(zip(names_out, made))}
    arrays.update(mlp_mine=mlp_mine, mlp_got=mlp_got)
    bits = range(bits_of(ctx_count))
    greet(ctx_count, sorted({*masks_of(moves), *[1 << b for b in bits]}))
    run = Moves(ctx_count, moves, arrays, send, recv)
    slow = [i for i, m in enumerate(moves) if m[0][0] != "mlp"]
    pace = 2
    paced = [slow[i : i + pace] for i in range(0, len(slow), pace)]
    for i in range(len(moves)):
        if i not in slow:
            run.start(i)

    def send_some(count):
        for _ in range(min(count, len(paced))):
            for i in paced.pop(0):
                run.start(i)

    send_some(2)
    late_loads = []
    for i, (far_ref, near_ref) in enumerate(((qkv_any, qkv_ref), (kv_any, kv_ref))):
        late_loads.append(pltpu.make_async_copy(far_ref, near_ref, load.at[2 + i]))
        late_loads[-1].start()
    slot_table(place_ref, about_ref, slot_info)
    edge = (experts + 2) * wide
    loads = []
    for i, cols in enumerate((pl.ds(edge, experts * wide), pl.ds(0, edge))):
        loads.append(pltpu.make_async_copy(weight_ref.at[:, cols], full.at[:, cols], load.at[i]))
        loads[-1].start()

    x = tokens_ref[...].astype(F32) + branch_ref[...].astype(F32)
    inverse = lax.rsqrt(jnp.mean(x * x, axis=-1, keepdims=True) + EPSILON)
    normed = x * inverse
    back = back_ref[...].astype(F32)
    gain_out_ref[...] = jnp.sum(back * normed, axis=0, keepdims=True)
    scaled = back * gain_of(gain_ref, 1, part)
    inner = jnp.mean(scaled * normed, axis=-1, keepdims=True)
    resid = dy_ref[...].astype(F32) + inverse * (scaled - normed * inner)
    resid_ref[...] = resid
    grad_branch_ref[...] = resid.astype(BF)
    leaving = []
    for i, pair in enumerate(((resid_ref, resid_out), (grad_branch_ref, grad_branch_out))):
        leaving.append(pltpu.make_async_copy(*pair, load.at[4 + i]))
        leaving[-1].start()
    loads[0].wait()
    for e in range(experts):
        cols = slice(edge + e * wide, edge + (e + 1) * wide)
        mixed = dot(grad_branch_ref[...], full[:, cols], 1, 0)
        grad_ref[:, e * wide : (e + 1) * wide] = (mixed * gate_ref[:, e : e + 1]).astype(BF)

    def head_copy(h, bit):
        size = keys >> (bit + 1)
        i = h * len(bits) + bit
        return pltpu.make_async_remote_copy(
            src_ref=total.at[h, pl.ds(size, size)],
            dst_ref=got.at[h, pl.ds(size, size)],
            send_sem=pass_send.at[i],
            recv_sem=pass_recv.at[i],
            device_id=peer(ctx_count, 1 << bit),
            device_id_type=pl.DeviceIdType.MESH,
        )

    def head_sum(h, bit):
        size = keys >> (bit + 1)
        head_copy(h, bit).wait_recv()
        mine = total[h, :size].astype(F32) + got[h, size : 2 * size].astype(F32)
        mine = mine.astype(BF)
        if bit + 1 < len(bits):
            total[h, :size] = mine
            head_copy(h, bit + 1).start()
        else:
            at = experts * wide
            out_ref[:, at + h * HD : at + (h + 1) * HD] = mine[:, :HD]
            at += wide
            out_ref[:, at + h * HD : at + (h + 1) * HD] = mine[:, HD:]

    for late in late_loads:
        late.wait()
    for h in range(heads):
        dk_acc[...] = jnp.zeros_like(dk_acc)
        dv_acc[...] = jnp.zeros_like(dv_acc)

        def step(e, carry, h=h):
            cols = head_cols(e * heads + h)
            place = place_ref[e]
            k, v = kv_ref[:, h * HD : (h + 1) * HD], kv_ref[:, (heads + h) * HD : (heads + h + 1) * HD]
            slots, exps, inv = scores_of(
                place, qkv_ref[:, cols], k, slot_info[e], segk_ref[...], idxk_ref[...]
            )
            attn = dot(exps.astype(BF), v, 1, 0) * inv
            probs = exps * inv
            grad = dot(place, grad_ref[:, cols], 1, 0)
            delta = jnp.sum(grad * attn, axis=-1, keepdims=True)
            grad = grad.astype(BF)
            dv_acc[...] += dot(probs.astype(BF), grad, 0, 0)
            grad_probs = dot(grad, v, 1, 1)
            grad_scores = (probs * (grad_probs - delta)).astype(BF)
            dq = dot(grad_scores, k, 1, 0) * (HD**-0.5)
            dk_acc[...] += dot(grad_scores, slots, 0, 0) * (HD**-0.5)
            top = dq.astype(BF)
            low = (dq - top.astype(F32)).astype(BF)
            back_q = dot(place, top, 0, 0) + dot(place, low, 0, 0)
            out_ref[:, cols] = turn(back_q, cos_ref[:rows], -sin_ref[:rows]).astype(BF)
            return carry

        for low in range(0, experts, 2):
            lax.fori_loop(low, low + 2, step, 0, unroll=2)
            if h < heads // 2:
                send_some(1)
        total[h, :, :HD] = turn(dk_acc[...], cos_ref[...], -sin_ref[...]).astype(BF)
        total[h, :, HD:] = dv_acc[...].astype(BF)
        head_copy(h, 0).start()
        if h:
            head_sum(h - 1, 0)
    head_sum(heads - 1, 0)
    send_some(len(paced))
    loads[1].wait()
    queries = experts * wide
    for j in range(width // part):
        rows_at = slice(j * part, (j + 1) * part)
        back_acc[:, rows_at] = dot(out_ref[:, :queries], full[rows_at, :queries], 1, 1)
    for bit in bits[1:]:
        for h in range(heads):
            head_sum(h, bit)
    for j in range(width // part):
        rows_at = slice(j * part, (j + 1) * part)
        keyed = dot(out_ref[:, queries:], full[rows_at, queries:edge], 1, 1)
        back_one_ref[:, rows_at] = (back_acc[:, rows_at] + keyed).astype(BF)
    runs_mlp = [i for i, m in enumerate(moves) if m[0][0] == "mlp"]
    for i in runs_mlp:
        run.await_one(i)
    slots, others = mlp_mine.shape[0], len(runs_mlp) - 1
    first = mlp_first_ref.shape[0] // others
    for low, top, came, size in ((0, first, mlp_first_ref, first), (first, slots, mlp_got, slots)):
        mlp_total = mlp_mine[low:top].astype(F32)
        for r in range(others):
            mlp_total = mlp_total + came[r * size + low : r * size + top].astype(F32)
        mlp_out_ref[low:top] = mlp_total.astype(BF)
    for h in range(heads):
        for bit in bits:
            head_copy(h, bit).wait_send()
    run.finish()
    for copy in leaving:
        copy.wait()


def attend_back(number, ctx_count, tp_count, heads, part, moves, given, made, weight, qkv, kv, *small):
    tokens = small[0]
    rows, width = tokens.shape
    keys = kv.shape[0]
    any_spec = pl.BlockSpec(memory_space=pl.ANY)
    full = pl.BlockSpec(memory_space=pltpu.VMEM)
    passes = heads * bits_of(ctx_count)
    slots, run = given["mlp"].shape[0], width // tp_count
    first = small[-1].shape[0] // (tp_count - 1)
    mlp_moves = [(("mlp", (0, slots), (TP, run)), ("mlp_mine", (0, slots), None), None, ())]
    for r in range(1, tp_count):
        source = ("mlp", (first, slots - first), (TP, run, r))
        target = ("mlp_got", ((r - 1) * slots + first, slots - first), None)
        mlp_moves.append((source, target, -r, ()))
    moves = mlp_moves + moves
    small_out = [
        (qkv.shape, BF),
        ((rows, width), F32),
        ((rows, width), BF),
        ((1, width), F32),
        ((rows, width), BF),
        ((slots, run), BF),
    ]
    out = pl.pallas_call(
        functools.partial(
            attend_back_kernel, ctx_count, moves, list(given), list(made), heads, part
        ),
        out_shape=[jax.ShapeDtypeStruct(*x) for x in small_out]
        + [jax.ShapeDtypeStruct(shape, BF) for shape in made.values()],
        in_specs=[full] * len(small) + [any_spec] * (3 + len(given)),
        out_specs=[any_spec if i in (1, 2) else full for i in range(len(small_out))]
        + [any_spec] * len(made),
        input_output_aliases={
            len(small) + 3 + list(given).index(n): len(small_out) + i for i, n in enumerate(made)
        },
        scratch_shapes=[
            pltpu.VMEM(weight.shape, BF),
            pltpu.VMEM((rows, weight.shape[1] - qkv.shape[1]), BF),
            pltpu.VMEM((rows, width), F32),
        ]
        + [pltpu.VMEM((keys, HD), F32)] * 2
        + [pltpu.VMEM((heads, keys, 2 * HD), BF)] * 2
        + [pltpu.VMEM((slots, run), BF), pltpu.VMEM(((tp_count - 1) * slots, run), BF)]
        + [pltpu.VMEM((*small[6].shape[:2], HD), F32), pltpu.VMEM(qkv.shape, BF), pltpu.VMEM(kv.shape, BF)]
        + [pltpu.VMEM(*small_out[i]) for i in (1, 2)]
        + [pltpu.SemaphoreType.DMA((len(moves),))] * 2
        + [pltpu.SemaphoreType.DMA((passes,))] * 2
        + [pltpu.SemaphoreType.DMA((6,))],
        compiler_params=pltpu.CompilerParams(
            collective_id=number, has_side_effects=True, vmem_limit_bytes=VMEM_LIMIT
        ),
        name="attend_back",
    )(*small, weight, qkv, kv, *given.values())
    return out[: len(small_out)], dict(zip(made, out[len(small_out) :]))


def spread_kernel(experts, me_ref, *refs):
    from_in, from_down = refs[:experts], refs[experts : 2 * experts]
    in_ref, down_ref = refs[2 * experts :]
    units = down_ref.shape[2]
    for m in range(experts):

        @pl.when(me_ref[0] == m)
        def _():
            for e in range(experts):
                for c in range(2):
                    in_ref[:, e, c, :] = from_in[e ^ m][:, c * units : (c + 1) * units].astype(F32)
                down_ref[:, e, :] = from_down[e ^ m][...].astype(F32)


def spread_grads(from_in, from_down, me, in_shape, down_shape):
    experts = len(from_in)
    step = min(64, in_shape[0])

    def rows_of(width):
        return pl.BlockSpec((step, width), lambda i, m: (i, 0))

    return pl.pallas_call(
        functools.partial(spread_kernel, experts),
        grid_spec=pltpu.PrefetchScalarGridSpec(
            num_scalar_prefetch=1,
            grid=(in_shape[0] // step,),
            in_specs=[rows_of(from_in[0].shape[1])] * experts
            + [rows_of(from_down[0].shape[1])] * experts,
            out_specs=[
                pl.BlockSpec((step, *in_shape[1:]), lambda i, m: (i, 0, 0, 0)),
                pl.BlockSpec((step, *down_shape[1:]), lambda i, m: (i, 0, 0)),
            ],
        ),
        out_shape=[
            jax.ShapeDtypeStruct(in_shape, F32),
            jax.ShapeDtypeStruct(down_shape, F32),
        ],
        compiler_params=pltpu.CompilerParams(vmem_limit_bytes=VMEM_LIMIT),
        name="spread_grads",
    )(me.astype(jnp.int32).reshape(1), *from_in, *from_down)


def places(routes, gates, experts, cap, room):
    rows = routes.shape[0]
    named = routes[:, :, None] == jnp.arange(experts, dtype=jnp.int32)[None, None, :]
    member = jnp.any(named, axis=1)
    gate = jnp.sum(jnp.where(named, gates[:, :, None], 0.0), axis=1)
    token = jnp.arange(rows, dtype=jnp.int32)
    earlier = (token[None, :] < token[:, None]).astype(BF)
    rank = dot(earlier, member.astype(BF), 1, 0).astype(jnp.int32)
    slot = jnp.where(member, rank, -1).T
    taken = slot[:, None, :] == jnp.arange(room, dtype=jnp.int32)[None, :, None]
    return taken, gate


def split(x):
    high = x.astype(BF)
    return high, (x - high.astype(F32)).astype(BF)


def layer(
    counts,
    tokens,
    gain_attn,
    gain_mlp,
    w_kv,
    w_query,
    w_out_attn,
    w_in,
    w_down,
    segments,
    attn_routes,
    attn_gates,
    mlp_routes,
    mlp_gates,
    cotangent,
):
    fsdp_count, ctx_count, tp_count = counts
    group = fsdp_count * ctx_count
    me = lax.axis_index(GROUP)
    ctx_me = lax.axis_index(CTX)
    rows, width = tokens.shape[1:]
    cap = 9 * rows // 16
    room = -(-cap // 16) * 16
    part = width // group
    attn_experts = w_query.shape[1]
    experts = w_in.shape[1]
    share = group // experts
    expert_me = me // share
    hidden_units = w_down.shape[2]
    head_width = w_kv.shape[2]

    def piece(x, index, size=part, axis=1):
        return lax.dynamic_slice_in_dim(x, index * size, size, axis)

    def exchange(x, mask):
        return swap(x, mask, GROUP, group)

    def after(x, *events):
        return lax.optimization_barrier((x, *events))[0]

    high, second = group // 2, group // 4

    gain_own = jnp.pad(jnp.concatenate([gain_attn, gain_mlp])[None, :], ((0, 15), (0, 0)))
    kv_out_own = jnp.concatenate([w_kv.reshape(part, -1), w_out_attn.reshape(part, -1)], axis=1)
    attn_own = [w_query.reshape(part, -1), kv_out_own]
    far_x, far_y = [], []
    for own in attn_own:
        far_x.append(exchange(own, high))
        far_y.append(exchange(own, second))

    seg_row = segments[0]
    seq_total = seg_row.shape[0]
    ctx_bits = list(range(bits_of(ctx_count)))[::-1]
    key_order = [0]
    for bit in ctx_bits:
        key_order = key_order + [j | (1 << bit) for j in key_order]
    key_seg = jnp.concatenate([piece(seg_row, ctx_me ^ j, rows, 0) for j in key_order])
    key_idx = jnp.concatenate(
        [(ctx_me ^ j) * rows + jnp.arange(rows, dtype=jnp.int32) for j in key_order]
    )
    place_idx = jnp.arange(seq_total, dtype=jnp.int32)
    pos = jnp.sum(
        (seg_row[None, :] == key_seg[:, None]) & (place_idx[None, :] < key_idx[:, None]),
        axis=1,
        dtype=jnp.int32,
    ).astype(F32)
    frequency = ROPE_BASE ** (-(jnp.arange(HD // 2, dtype=F32) * 2.0) / HD)
    angles = pos[:, None] * frequency[None, :]
    cos_half, sin_half = jnp.cos(angles), jnp.sin(angles)
    cos = jnp.concatenate([cos_half, cos_half], axis=1)
    sin = jnp.concatenate([-sin_half, sin_half], axis=1)
    taken_attn, gate_attn = places(attn_routes[0], attn_gates[0], attn_experts, cap, room)
    place_attn = taken_attn.astype(BF)
    own_seg, own_idx = key_seg[:rows], key_idx[:rows]
    gate_high, gate_low = split(gate_attn)
    about = [own_seg[:, None], (own_idx // 32)[:, None], (own_idx % 32)[:, None], gate_high, gate_low]
    about = jnp.concatenate([x.astype(BF) for x in about], axis=1)
    about = jnp.pad(about, ((0, 0), (0, HD - about.shape[1])))
    key_row = (key_seg.astype(F32)[None, :], key_idx.astype(F32)[None, :])
    taken_mlp, gate_mlp = places(mlp_routes[0], mlp_gates[0], experts, cap, room)
    mine_first = [expert_me ^ k for k in range(experts)]
    place_mlp = jnp.concatenate([piece(taken_mlp, e, 1, 0) for e in mine_first]).astype(BF)
    tokens_rel, grad_out = in_order(me, [tokens[0], cotangent[0]], group)

    def expert_rows(k):
        in_rows = piece(w_in, expert_me ^ k, 1, 1)
        down_rows = piece(w_down, expert_me ^ k, 1, 1)
        return [in_rows[:, 0, 0], in_rows[:, 0, 1], down_rows[:, 0]]

    to_send = [expert_rows(k) for k in range(experts)]

    def given_sends(ks):
        return {("send", k, c): x for k in ks for c, x in enumerate(to_send[k])}

    in_cols, down_cols = (0, 2 * hidden_units), (2 * hidden_units, hidden_units)
    weight_shapes = {"in": (width, 2 * hidden_units), "down": (width, hidden_units)}

    def weight_moves(k, first, size, prefix=""):
        moves = []
        sides = (("in", (0, hidden_units)), ("in", (hidden_units, hidden_units)), ("down", None))
        for c, (name, cols) in enumerate(sides):
            base = k * share * part + first
            source = (("send", k, c), (first, size), None)
            landed = (prefix + name, (base, size), cols)
            moves.append((source, landed, k * share, ()))
            for t in range(1, share):
                target = (prefix + name, (base + t * part, size), cols)
                if k:
                    moves.append((landed, target, t, (landed,)))
                else:
                    moves.append((source, target, t, ()))
        return moves

    def many_weight_moves(cuts):
        return [m for cut in cuts for m in weight_moves(*cut)]

    near = [k for k in range(1, experts) if k & (k - 1) == 0]
    far = [k for k in range(1, experts) if k & (k - 1)]
    half_part = part // 2

    far_x, to_send = lax.optimization_barrier((far_x, to_send))
    cut = max(16, part * 3 // 8 // 16 * 16)
    gather_moves = []
    queries, two_planes = attn_experts * head_width, 2 * head_width
    for n, first, size_of, edge in (
        (1, 0, two_planes, queries),
        (0, 0, queries, 0),
        (1, two_planes, queries, queries + two_planes),
    ):
        cols, own_cols = (edge, size_of), (first, size_of)
        moves = []
        held = {0: [(("own", n), 0, part, ())], high: [(("x", n), 0, part, ())], second: [(("y", n), 0, part, ())]}
        corner = []
        for side, mask, low, top in ((("x", n), second, 0, cut), (("y", n), high, cut, part)):
            half = (top - low) // 32 * 16
            for at, size in ((low, half), (low + half, top - low - half)):
                if size:
                    target = (FULL, ((high | second) * part + at, size), cols)
                    corner.append(((side, (at, size), own_cols), target, mask, ()))
        corner = corner[::2] + corner[1::2]
        moves += corner
        held[high | second] = [(FULL, t[1][0] - (high | second) * part, t[1][1], (t,)) for _, t, _, _ in corner]
        for j in (0, high, second):
            source = (held[j][0][0], (0, part), own_cols)
            moves.append((source, (FULL, (j * part, part), cols), None, ()))
        for bit in range(bits_of(group) - 2)[::-1]:
            for j in list(held):
                there = []
                for name, at, size, needs in held[j]:
                    if name == FULL:
                        source = (name, (at + j * part, size), cols)
                    else:
                        source = (name, (at, size), own_cols)
                    target = (FULL, ((j | 1 << bit) * part + at, size), cols)
                    moves.append((source, target, 1 << bit, needs))
                    there.append((FULL, at, size, (target,)))
                held[j | 1 << bit] = there
        gather_moves.append(moves)
    gain_moves = [
        (("gain_own", (0, 16), None), ("gains", (j * 16, 16), None), j, ())
        for j in range(1, group)
    ]
    heads = head_width // HD
    later = weight_moves(0, 0, part) + many_weight_moves([(k, 0, half_part) for k in near])
    gate_ride = jnp.concatenate(split(gate_mlp), axis=1)
    gate_ride = jnp.pad(gate_ride, ((0, 0), (0, HD - 2 * experts)))
    dy_moves = [
        ((name, (k * room, room), None), (target, (k * room, room), None), k * share, ())
        for k in range(1, experts)
        for name, target in (("picked", "slots"), ("picked_ride", "rides"))
    ]
    dy_spread, run = [], width // tp_count
    for k in range(experts):
        mine = (k * room, room)
        needs = ((("slots", mine, None)),) if k else ()
        for r in range(1, tp_count):
            source, target = ("slots", mine, None), ("dy", mine, (TP, run, 0, r))
            dy_spread.append((source, target, -r, needs))
    (gains, hidden_one, qkv, kv, mixed, branch, dy_slots, dy_rides), made = front(
        1,
        ctx_count,
        heads,
        part,
        (gain_moves, *gather_moves, dy_moves, dy_spread),
        later,
        {
            **{("own", n): x for n, x in enumerate(attn_own)},
            **{("x", n): x for n, x in enumerate(far_x)},
            **{("y", n): x for n, x in enumerate(far_y)},
            **given_sends([0, *near]),
        },
        weight_shapes,
        (
            tokens_rel,
            gain_own,
            cos,
            sin,
            place_attn,
            about,
            *key_row,
            grad_out,
            gate_ride,
            place_mlp,
        ),
    )
    attn_full, weights = made["kept"], {n: made[n] for n in weight_shapes}
    branch_sum = lax.psum(branch, TP)
    cuts = [(k, half_part, part - half_part) for k in near] + [(k, 0, half_part) for k in far]
    to_send, weights, _ = lax.optimization_barrier((to_send, weights, branch))
    given = {**given_sends([*near, *far]), **weights}
    weights = move("weights_two", 3, ctx_count, many_weight_moves(cuts), given, weight_shapes)
    fetched, far_moves = [], []
    for j in range(group):
        size = half_part if j // share in far else part
        if fetched and sum(fetched[-1]) == j * part:
            fetched[-1] = (fetched[-1][0], fetched[-1][1] + size)
        else:
            fetched.append((j * part, size))
    for k in far:
        far_moves += weight_moves(k, half_part, part - half_part, "w")
    grads_in, grads_down, mlp_slots, back_two_part, mlp_first = run_experts(
        4,
        ctx_count,
        tp_count,
        experts,
        share,
        part,
        fetched,
        far_moves,
        given_sends(far),
        weights,
        tokens_rel,
        branch_sum,
        gains,
        place_mlp,
        dy_slots,
        dy_rides,
    )
    back_two = lax.psum(back_two_part, TP)
    got_in, got_down = {0: grads_in}, {0: grads_down}

    def grad_moves(ks, cuts, first=0):
        moves = []
        for at in range(first, part, part // cuts):
            for k in ks:
                for name in ("in", "down"):
                    source = (name, (k * part + at, part // cuts), None)
                    target = ((name, k), (at, part // cuts), None)
                    moves.append((source, target, k * share, ()))
        made_shapes = {("in", k): (part, 2 * hidden_units) for k in ks}
        return moves, {**made_shapes, **{("down", k): (part, hidden_units) for k in ks}}

    def keep_grads(made, ks):
        got_in.update({k: made[("in", k)] for k in ks})
        got_down.update({k: made[("down", k)] for k in ks})

    cuts = min(8, part // 16)
    moves, made_shapes = grad_moves(near, 1)
    early, early_shapes = grad_moves(far, cuts)
    moves += early[: len(early) // cuts]
    made_shapes.update(early_shapes)
    grads_in, grads_down, _ = lax.optimization_barrier((grads_in, grads_down, back_two_part))
    given = {"in": grads_in, "down": grads_down}
    made = move("grads_near", 5, ctx_count, moves, given, made_shapes)
    keep_grads(made, near)

    moves, made_shapes = grad_moves(far, cuts, part // cuts)
    back_two, given, made = lax.optimization_barrier((back_two, given, made))
    given.update({name: made[name] for name in made_shapes})
    given["mlp"] = mlp_slots
    (grad_qkv, grad_resid, grad_branch, gain_two_grad, back_one_part, mlp_run), made = attend_back(
        6,
        ctx_count,
        tp_count,
        heads,
        part,
        moves,
        given,
        made_shapes,
        attn_full,
        qkv,
        kv,
        tokens_rel,
        branch_sum,
        gains,
        back_two,
        grad_out,
        gate_attn,
        place_attn,
        about,
        *key_row,
        cos,
        sin,
        mlp_first,
    )
    keep_grads(made, far)
    upper = list(range(1, bits_of(group)))
    grad_attnw, kept, *given, grad_tokens, gain_grads, mlp_sum = attn_grads(
        7,
        ctx_count,
        tp_count,
        upper,
        part,
        head_width,
        hidden_one,
        grad_branch,
        grad_qkv,
        mixed,
        back_one_part,
        tokens_rel,
        gains,
        grad_resid,
        gain_two_grad,
        mlp_run,
        place_mlp,
    )
    planes = attn_experts * 2 + 2
    lanes, last_lanes = lanes_of(planes, attn_experts + 2, upper)
    came = []
    for i in range(2):
        bit = dict(lanes)[last_lanes[3 * i]][-1]
        came.append(exchange(given[i], 1 << bit))
    output, grad_tokens = last(me, group, tokens_rel, branch_sum, mlp_sum, grad_tokens)
    grad_in_out, grad_down_out = spread_grads(
        [got_in[k] for k in range(experts)],
        [got_down[k] for k in range(experts)],
        expert_me,
        w_in.shape,
        w_down.shape,
    )
    came, _ = lax.optimization_barrier((came, (output, grad_in_out)))
    grad_query_w, grad_kv_w, grad_out_w = lay_out(
        last_lanes, [grad_attnw, kept, *came], (w_query.shape, w_kv.shape, w_out_attn.shape)
    )
    return (
        output[None],
        grad_tokens[None],
        gain_grads[0],
        gain_grads[1],
        grad_kv_w,
        grad_query_w,
        grad_out_w,
        grad_in_out,
        grad_down_out,
    )


def solution(mesh):
    rows = P(FSDP, CTX, None)
    weight = P(GROUP, None, TP)
    weight_in = P(GROUP, None, None, TP)
    return jax.shard_map(
        functools.partial(layer, tuple(mesh.shape[a] for a in (FSDP, CTX, TP))),
        mesh=mesh,
        in_specs=(
            rows,
            P(GROUP),
            P(GROUP),
            weight,
            weight,
            weight,
            weight_in,
            weight,
            P(FSDP, None),
            rows,
            rows,
            rows,
            rows,
            rows,
        ),
        out_specs=(rows, rows, P(GROUP), P(GROUP), weight, weight, weight, weight_in, weight),
        check_vma=False,
    )
```

```python
import functools

import jax
import jax.numpy as jnp
from jax import lax
from jax.experimental import pallas as pl
from jax.experimental.pallas import tpu as pltpu
from jax.sharding import PartitionSpec as P

HD = 128
EPSILON = 1e-06
ROPE_BASE = 10000.0
MASKED = -1e30
FSDP, CTX, TP = "fsdp", "ctx", "tp"
GROUP = (FSDP, CTX)
FULL = "full"
BF = jnp.bfloat16
F32 = jnp.float32
VMEM_LIMIT = 56 * 1024 * 1024


def normalize(tensor):
    inverse = lax.rsqrt(jnp.mean(tensor * tensor, axis=-1, keepdims=True) + EPSILON)
    return (tensor * inverse, inverse)


def norm_back(grad_in, normed, inverse, gain_vec):
    scaled = grad_in * gain_vec
    inner_mean = jnp.mean(scaled * normed, axis=-1, keepdims=True)
    return (inverse * (scaled - normed * inner_mean), jnp.sum(grad_in * normed, axis=0))


def dot(a, b, ca, cb):
    return lax.dot_general(a, b, (((ca,), (cb,)), ((), ())), preferred_element_type=F32)


def turn(x, cos, sin):
    return x * cos + pltpu.roll(x, HD // 2, 1) * sin


def swap(x, mask, axes, count):
    return lax.ppermute(x, axes, [(i, i ^ mask) for i in range(count)])


def bits_of(count):
    return count.bit_length() - 1


def flip(value, mask):
    step = 1
    while step <= mask:
        if mask & step:
            value = value + step - 2 * step * ((value // step) % 2)
        step *= 2
    return value


def peer(ctx_count, mask):
    if mask < 0:
        return {TP: flip(lax.axis_index(TP), -mask)}
    return {
        FSDP: flip(lax.axis_index(FSDP), mask // ctx_count),
        CTX: flip(lax.axis_index(CTX), mask % ctx_count),
    }


def greet(ctx_count, masks):
    barrier = pltpu.get_barrier_semaphore()
    for mask in masks:
        pl.semaphore_signal(
            barrier, inc=1, device_id=peer(ctx_count, mask), device_id_type=pl.DeviceIdType.MESH
        )
    pl.semaphore_wait(barrier, len(masks))


def run_cols(size, flips=0):
    return pl.ds(pl.multiple_of(flip(lax.axis_index(TP), flips) * size, size), size)


def window(ref, rows, cols):
    if rows[0] == TP:
        return ref.at[run_cols(rows[1], rows[2])]
    if cols is None:
        return ref.at[pl.ds(rows[0], rows[1])]
    if cols[0] == TP:
        return ref.at[pl.ds(rows[0], rows[1]), run_cols(*cols[1:3])]
    return ref.at[pl.ds(rows[0], rows[1]), pl.ds(cols[0], cols[1])]


def gain_of(gains_ref, which, part):
    rows = gains_ref[...].astype(F32)
    cols = slice(which * part, (which + 1) * part)
    return jnp.concatenate([rows[at : at + 1, cols] for at in range(0, rows.shape[0], 16)], axis=1)


class Moves:
    def __init__(self, ctx_count, moves, arrays, send, recv, bounces=(), base=0):
        self.moves = moves
        self.onward = {}
        bounces = list(bounces)
        self.copies = []
        self.place = {m[1]: i for i, m in enumerate(moves)}
        self.started, self.came, self.sent = set(), set(), set()
        for at, (source, target, mask, _) in enumerate(moves):
            i = base + at
            src = window(arrays[source[0]], *source[1:])
            dst = window(arrays[target[0]], *target[1:])
            if mask:
                copy = pltpu.make_async_remote_copy(
                    src_ref=src,
                    dst_ref=dst,
                    send_sem=send.at[i],
                    recv_sem=recv.at[i],
                    device_id=peer(ctx_count, mask),
                    device_id_type=pl.DeviceIdType.MESH,
                )
            elif mask is None:
                copy = pltpu.make_async_copy(src, dst, recv.at[i])
            else:
                bounce = bounces.pop(0)
                copy = pltpu.make_async_copy(src, bounce, recv.at[i])
                self.onward[at] = pltpu.make_async_copy(bounce, dst, send.at[i])
            self.copies.append(copy)

    def start(self, i):
        if i not in self.started:
            self.started.add(i)
            self.copies[i].start()

    def begin(self, count=None):
        for i, move in enumerate(self.moves[:count]):
            if not move[3]:
                self.start(i)

    def await_one(self, i):
        if i not in self.came:
            self.came.add(i)
            if i in self.onward:
                self.copies[i].wait()
                self.onward[i].start()
            elif self.moves[i][2] is None:
                self.copies[i].wait()
            else:
                self.copies[i].wait_recv()

    def await_sent(self, i):
        if i not in self.sent:
            self.sent.add(i)
            self.copies[i].wait_send()

    def kick(self, first, count):
        for i in range(first, count):
            for target in self.moves[i][3]:
                self.await_one(self.place[target])
            self.start(i)

    def settle(self, count=None, first=0):
        count = len(self.moves) if count is None else count
        for i in range(first, count):
            if i in self.onward:
                self.await_one(i)
        for i in range(first, count):
            for target in self.moves[i][3]:
                self.await_one(self.place[target])
            self.start(i)
        for i in range(first, count):
            self.await_one(i)

    def finish(self):
        self.settle()
        for i in range(len(self.moves)):
            if i in self.onward:
                self.onward[i].wait()
            elif self.moves[i][2] is not None:
                self.await_sent(i)


def masks_of(moves):
    return sorted({move[2] for move in moves if move[2]})


def move_kernel(ctx_count, moves, names_in, names_out, *refs):
    count = len(names_in) + len(names_out)
    refs, (send, recv, *bounces) = refs[:count], refs[count:]
    arrays = dict(zip(names_in, refs))
    arrays.update(zip(names_out, refs[len(names_in) :]))
    greet(ctx_count, masks_of(moves))
    run = Moves(ctx_count, moves, arrays, send, recv, bounces)
    run.begin()
    run.finish()


def move(name, number, ctx_count, moves, given, made):
    names_in = [n for n in given if n not in made] + [n for n in given if n in made]
    plain = [n for n in names_in if n not in made]
    names_out = list(made)
    any_spec = pl.BlockSpec(memory_space=pl.ANY)
    bounces = [
        pltpu.VMEM((source[1][1], (source[2] or (0, given[source[0]].shape[1]))[1]), BF)
        for source, _, mask, _ in moves
        if not mask
    ]
    return dict(
        zip(
            names_out,
            pl.pallas_call(
                functools.partial(
                    move_kernel,
                    ctx_count,
                    moves,
                    plain + ["old_" + n for n in names_in[len(plain) :]],
                    names_out,
                ),
                out_shape=[jax.ShapeDtypeStruct(shape, BF) for shape in made.values()],
                in_specs=[any_spec] * len(names_in),
                out_specs=[any_spec] * len(names_out),
                input_output_aliases={
                    names_in.index(n): names_out.index(n) for n in names_out if n in given
                },
                scratch_shapes=[pltpu.SemaphoreType.DMA((len(moves),))] * 2 + bounces,
                compiler_params=pltpu.CompilerParams(
                    collective_id=number, has_side_effects=True, vmem_limit_bytes=VMEM_LIMIT
                ),
                name=name,
            )(*[given[n] for n in names_in]),
        )
    )


def lanes_of(planes, late, bits):
    lanes = []
    for n, plane in enumerate([*range(late, planes), *range(late)]):
        lanes.append((plane, bits if n % 2 else bits[::-1]))
    last = lanes[-6:]
    return lanes, [p for p, _ in last[::2]] + [p for p, _ in last[1::2]]


def attn_grads_kernel(
    ctx_count,
    groups,
    bits,
    part,
    cols,
    hidden_ref,
    branch_ref,
    qkv_ref,
    mixed_ref,
    back_ref,
    tokens_any,
    gain_ref,
    resid_any,
    gain_two_ref,
    mlp_ref,
    place_ref,
    out_ref,
    keep_ref,
    give_one_ref,
    give_two_ref,
    grad_tokens_ref,
    gain_out_ref,
    mlp_sum_ref,
    mlp_got,
    back_got,
    back_sum,
    gain_send,
    gain_got,
    hidden,
    branch,
    hidden_odd,
    branch_odd,
    right,
    grads,
    got,
    tokens_ref,
    resid_ref,
    load,
    send,
    recv,
    pass_send,
    pass_recv,
):
    rows, width = hidden_ref.shape
    count = width // part // 2
    planes = right.shape[1] // cols
    first = qkv_ref.shape[1]
    group = width // part
    run_rows = groups["spread"][0][0][1][1]
    greet(ctx_count, masks_of([m for moves in groups.values() for m in moves]))
    arrays = dict(
        back=back_ref,
        back_got=back_got,
        back_sum=back_sum,
        mlp=mlp_ref,
        mlp_got=mlp_got,
        mlp_sum=mlp_sum_ref,
        gain_send=gain_send,
        gain_got=gain_got,
        hidden_odd=hidden_odd,
        branch_odd=branch_odd,
        qkv_in=qkv_ref,
        mixed_in=mixed_ref,
        hidden=hidden,
        branch=branch,
        right=right,
    )
    runs, base = {}, 0
    for name, moves in groups.items():
        if name != "sums":
            runs[name] = Moves(ctx_count, moves, arrays, pass_send, pass_recv, (), base)
        base += len(moves)
    run = runs["share"]
    late_loads = []
    for i, (far_ref, near_ref) in enumerate(((tokens_any, tokens_ref), (resid_any, resid_ref))):
        late_loads.append(pltpu.make_async_copy(far_ref, near_ref, load.at[i]))
        late_loads[-1].start()
    runs["reduce"].begin()
    runs["mlp"].begin()
    for given, even_side, odd_side in (
        (branch_ref, branch, branch_odd),
        (hidden_ref, hidden, hidden_odd),
    ):
        for j in range(count):
            block = slice(j * part, (j + 1) * part)
            even_side[:rows, block] = given[:, 2 * j * part : (2 * j + 1) * part]
            odd_side[:, block] = given[:, (2 * j + 1) * part : (2 * j + 2) * part]
    run.begin()
    right[:rows, :first] = qkv_ref[...]
    right[:rows, first:] = mixed_ref[...]
    number = [0]

    def copy(mask, block, plane):
        i = number[0]
        number[0] += 1
        window_of = (pl.ds(block * part, part), pl.ds(plane * cols, cols))
        return pltpu.make_async_remote_copy(
            src_ref=grads.at[window_of],
            dst_ref=got.at[window_of],
            send_sem=send.at[i],
            recv_sem=recv.at[i],
            device_id=peer(ctx_count, mask),
            device_id_type=pl.DeviceIdType.MESH,
        )

    sent, flying, left = [], {}, {}

    def send_half(plane, order, step):
        at = bits.index(order[step])
        flying[plane] = {
            j: copy(1 << order[step], j, plane) for j in left[plane] if j >> at & 1
        }
        for c in flying[plane].values():
            c.start()
        sent.extend(flying[plane].values())

    late = first // cols
    lanes, last_lanes = lanes_of(planes, late, bits)
    for plane, order in lanes:
        run.settle(2 if plane >= late else 4)
        at = pl.ds(plane * cols, cols)
        left_side = hidden if plane < late else branch
        grads[:, at] = dot(left_side[...], right[:, at], 0, 0).astype(BF)
        left[plane] = list(range(count))
        send_half(plane, order, 0)
    def sum_back():
        runs["reduce"].settle()
        own = run_cols(run_rows)
        total = back_ref[own].astype(F32)
        for r in range(len(groups["reduce"])):
            total = total + back_got[r * run_rows : (r + 1) * run_rows].astype(F32)
        back_sum[own] = total.astype(BF)
        runs["spread"].begin()

    def sum_mlp():
        runs["mlp"].settle()
        room = mlp_ref.shape[0] // place_ref.shape[0]
        total = dot(place_ref[0], mlp_ref[:room], 0, 0)
        for k in range(1, place_ref.shape[0]):
            total = total + dot(place_ref[k], mlp_got[k * room : (k + 1) * room], 0, 0)
        mlp_sum_ref[:, run_cols(mlp_ref.shape[1])] = total.astype(BF)
        runs["mlp_spread"].begin()

    def norm_back():
        for late_load in late_loads:
            late_load.wait()
        runs["spread"].settle()
        x = tokens_ref[...].astype(F32)
        inverse = lax.rsqrt(jnp.mean(x * x, axis=-1, keepdims=True) + EPSILON)
        normed = x * inverse
        back = back_sum[...].astype(F32)
        gain_grad = jnp.sum(back * normed, axis=0, keepdims=True)
        scaled = back * gain_of(gain_ref, 0, part)
        inner = jnp.mean(scaled * normed, axis=-1, keepdims=True)
        grad_tokens_ref[...] = (resid_ref[...] + inverse * (scaled - normed * inner)).astype(BF)
        gain_send[...] = jnp.zeros_like(gain_send)
        for j in range(group):
            block = slice(j * part, (j + 1) * part)
            gain_send[j * 8 : j * 8 + 1] = gain_grad[:, block]
            gain_send[j * 8 + 1 : j * 8 + 2] = gain_two_ref[:, block]
        runs["gains"].begin()

    for step in range(len(bits)):
        for n, (plane, order) in enumerate(lanes):
            if step == len(bits) - 1 and plane in last_lanes:
                continue
            if step == 0 and n == len(lanes) * 2 // 5:
                sum_back()
                sum_mlp()
            if step == 1 and n == min(2, len(lanes) - 1):
                norm_back()
            at = bits.index(order[step])
            left[plane] = [j for j in left[plane] if not j >> at & 1]
            across = pl.ds(plane * cols, cols)
            for j in left[plane]:
                flying[plane][j | 1 << at].wait_recv()
                down, other = pl.ds(j * part, part), pl.ds((j | 1 << at) * part, part)
                total = grads[down, across].astype(F32) + got[other, across].astype(F32)
                if step == len(bits) - 1:
                    at_out = sum(p not in last_lanes for p in range(plane))
                    out_ref[:, at_out * cols : (at_out + 1) * cols] = total
                elif step == len(bits) - 2 and plane in last_lanes:
                    at_last = last_lanes.index(plane)
                    there = slice(at_last * cols, (at_last + 1) * cols)
                    if j:
                        half = len(last_lanes) // 2
                        give_ref = (give_one_ref, give_two_ref)[at_last // half]
                        at_give = at_last % half * cols
                        give_ref[:, at_give : at_give + cols] = total.astype(BF)
                    else:
                        keep_ref[:, there] = total
                else:
                    grads[down, across] = total.astype(BF)
            if step < len(bits) - 1 and not (step == len(bits) - 2 and plane in last_lanes):
                send_half(plane, order, step + 1)
    runs["gains"].settle()
    gains = gain_send[:8]
    for j in range(1, group):
        gains = gains + gain_got[j * 8 : (j + 1) * 8]
    gain_out_ref[...] = gains
    for moves in runs.values():
        moves.finish()
    for c in sent:
        c.wait_send()


def attn_grads(number, ctx_count, tp_count, bits, part, cols, hidden, branch, qkv, mixed, *others):
    rows, width = hidden.shape
    group = width // part
    first = qkv.shape[1]
    theirs = (rows, rows)
    run_rows = rows // tp_count
    mlp, place = others[-2:]
    experts, room = place.shape[:2]
    run = mlp.shape[1]
    groups = {
        "mlp": [
            (("mlp", (k * room, room), None), ("mlp_got", (k * room, room), None), k * group // experts, ())
            for k in range(1, experts)
        ],
        "mlp_spread": [
            (("mlp_sum", (0, rows), (TP, run)), ("mlp_sum", (0, rows), (TP, run, 0, r)), -r, ())
            for r in range(1, tp_count)
        ],
        "reduce": [
            (("back", (TP, run_rows, r), None), ("back_got", ((r - 1) * run_rows, run_rows), None), -r, ())
            for r in range(1, tp_count)
        ],
        "spread": [
            (("back_sum", (TP, run_rows, 0), None), ("back_sum", (TP, run_rows, 0), r), -r, ())
            for r in range(1, tp_count)
        ],
        "gains": [
            (("gain_send", (j * 8, 8), None), ("gain_got", (j * 8, 8), None), j, ())
            for j in range(1, group)
        ],
        "share": [
            (("mixed_in", (0, rows), None), ("right", theirs, (first, mixed.shape[1])), 1, ()),
            (("branch_odd", (0, rows), None), ("branch", theirs, None), 1, ()),
            (("qkv_in", (0, rows), None), ("right", theirs, (0, first)), 1, ()),
            (("hidden_odd", (0, rows), None), ("hidden", theirs, None), 1, ()),
        ],
        "sums": [((), (), 1 << b, ()) for b in bits],
    }
    wide = qkv.shape[1] + mixed.shape[1]
    copies = (wide // cols) * (width // part // 2)
    passes = sum(len(moves) for moves in groups.values())
    full = pl.BlockSpec(memory_space=pltpu.VMEM)
    return pl.pallas_call(
        functools.partial(attn_grads_kernel, ctx_count, groups, bits, part, cols),
        out_shape=[
            jax.ShapeDtypeStruct((part, wide - 6 * cols), F32),
            jax.ShapeDtypeStruct((part, 6 * cols), F32),
            *[jax.ShapeDtypeStruct((part, 3 * cols), BF)] * 2,
            jax.ShapeDtypeStruct((rows, width), BF),
            jax.ShapeDtypeStruct((8, part), F32),
            jax.ShapeDtypeStruct((rows, width), BF),
        ],
        in_specs=[pl.BlockSpec(memory_space=pl.ANY) if i in (5, 7) else full for i in range(4 + len(others))],
        out_specs=[full] * 7,
        scratch_shapes=[
            pltpu.VMEM(mlp.shape, BF),
            pltpu.VMEM(((tp_count - 1) * run_rows, width), BF),
            pltpu.VMEM((rows, width), BF),
            *[pltpu.VMEM((group * 8, part), F32)] * 2,
        ]
        + [pltpu.VMEM((2 * rows, width // 2), BF)] * 2
        + [pltpu.VMEM((rows, width // 2), BF)] * 2
        + [pltpu.VMEM((2 * rows, wide), BF)]
        + [pltpu.VMEM((width // 2, wide), BF)] * 2
        + [pltpu.VMEM((rows, width), BF), pltpu.VMEM((rows, width), F32), pltpu.SemaphoreType.DMA((2,))]
        + [pltpu.SemaphoreType.DMA((copies,))] * 2
        + [pltpu.SemaphoreType.DMA((passes,))] * 2,
        compiler_params=pltpu.CompilerParams(
            collective_id=number, has_side_effects=True, vmem_limit_bytes=VMEM_LIMIT
        ),
        name="attn_grads",
    )(hidden, branch, qkv, mixed, *others)


def turn_kernel(me_ref, *refs):
    half = len(refs) // 2
    for given, made in zip(refs[:half], refs[half:]):
        made[...] = given[...]


def in_order(me, arrays, group):
    rows, width = arrays[0].shape
    part = width // group
    if part % HD:
        return [
            jnp.concatenate(
                [lax.dynamic_slice_in_dim(x, (me ^ j) * part, part, 1) for j in range(group)], axis=1
            )
            for x in arrays
        ]
    return pl.pallas_call(
        turn_kernel,
        grid_spec=pltpu.PrefetchScalarGridSpec(
            num_scalar_prefetch=1,
            grid=(group,),
            in_specs=[pl.BlockSpec((rows, part), lambda j, m: (0, m[0] ^ j))] * len(arrays),
            out_specs=[pl.BlockSpec((rows, part), lambda j, m: (0, j))] * len(arrays),
        ),
        out_shape=[jax.ShapeDtypeStruct((rows, width), x.dtype) for x in arrays],
        name="in_order",
    )(me.astype(jnp.int32).reshape(1), *arrays)


def last_kernel(group, me_ref, *refs):
    tokens, branch, mlp, grad, out_ref, grad_out_ref = refs
    width = tokens.shape[1]
    part = width // group
    total = (tokens[...].astype(F32) + branch[...].astype(F32) + mlp[...].astype(F32)).astype(BF)
    for j in range(group):
        cols = slice(j * part, (j + 1) * part)
        at = pl.ds(pl.multiple_of((me_ref[0] ^ j) * part, part), part)
        out_ref[:, at] = total[:, cols]
        grad_out_ref[:, at] = grad[:, cols]


def last(me, group, tokens, branch, mlp, grad):
    rows, width = tokens.shape
    if width // group % HD:
        total = tokens.astype(F32) + branch.astype(F32) + mlp.astype(F32)
        return in_order(me, [total.astype(BF), grad], group)
    whole = pl.BlockSpec((rows, width), lambda i, m: (0, 0))
    return pl.pallas_call(
        functools.partial(last_kernel, group),
        grid_spec=pltpu.PrefetchScalarGridSpec(
            num_scalar_prefetch=1, grid=(1,), in_specs=[whole] * 4, out_specs=[whole] * 2
        ),
        out_shape=[jax.ShapeDtypeStruct((rows, width), BF)] * 2,
        compiler_params=pltpu.CompilerParams(vmem_limit_bytes=VMEM_LIMIT),
        name="last",
    )(me.astype(jnp.int32).reshape(1), tokens, branch, mlp, grad)


def lay_kernel(last, grad_ref, keep_ref, one_ref, two_ref, *out_refs):
    plane = early = 0
    half = len(last) // 2
    for ref in out_refs:
        cols = ref.shape[2]
        for p in range(ref.shape[1]):
            if plane in last:
                at = last.index(plane)
                got_ref = (one_ref, two_ref)[at // half]
                got = got_ref[:, at % half * cols : (at % half + 1) * cols].astype(F32)
                ref[:, p, :] = keep_ref[:, at * cols : (at + 1) * cols] + got
            else:
                ref[:, p, :] = grad_ref[:, early * cols : (early + 1) * cols]
                early += 1
            plane += 1


def lay_out(last, arrays, shapes):
    rows = arrays[0].shape[0]
    step = min(64, rows)
    return pl.pallas_call(
        functools.partial(lay_kernel, last),
        grid=(rows // step,),
        in_specs=[pl.BlockSpec((step, x.shape[1]), lambda i: (i, 0)) for x in arrays],
        out_specs=[pl.BlockSpec((step, *shape[1:]), lambda i: (i, 0, 0)) for shape in shapes],
        out_shape=[jax.ShapeDtypeStruct(shape, F32) for shape in shapes],
        compiler_params=pltpu.CompilerParams(vmem_limit_bytes=VMEM_LIMIT),
        name="lay_out",
    )(*arrays)


def chunks(total, size):
    return [(at, min(size, total - at)) for at in range(0, total, size)]


def experts_kernel(
    ctx_count,
    experts,
    share,
    part,
    groups,
    far_names,
    tokens_ref,
    branch_ref,
    gain_ref,
    place_ref,
    dy_ref,
    rides_ref,
    in_ref,
    down_ref,
    *refs,
):
    far_refs, refs = refs[: len(far_names)], refs[len(far_names) :]
    grads_in, grads_down, mlp_out, two_part, mlp_first = refs[:5]
    (
        win,
        wdown,
        two,
        slots_out,
        back_out,
        back_got,
        active,
        gu,
        two_out,
        dy_out,
        two_got,
        dy_got,
        gu_got,
        active_got,
        mlp_ref,
        leave,
        send,
        recv,
    ) = refs[5:]
    slots, width = two.shape
    units = active.shape[1]
    room, run = slots // experts, width // experts
    arrays = dict(
        zip(far_names, far_refs),
        mlp=mlp_ref,
        mlp_first=mlp_first,
        gin=grads_in,
        gdown=grads_down,
        win=win,
        wdown=wdown,
        two=two,
        slots_out=slots_out,
        back_out=back_out,
        back_got=back_got,
        active=active,
        gu=gu,
        two_out=two_out,
        dy_out=dy_out,
        two_got=two_got,
        dy_got=dy_got,
        gu_got=gu_got,
        active_got=active_got,
        down=down_ref,
        **{"in": in_ref},
    )
    runs, base = {}, 0
    for name, moves in groups.items():
        runs[name] = Moves(ctx_count, moves, arrays, send, recv, (), base)
        base += len(moves)
    greet(ctx_count, masks_of([m for moves in groups.values() for m in moves]))
    stages = list_stages(experts)
    runs["load", "in"].begin()
    runs["load", "down"].begin()
    runs["far", "in"].begin()
    runs["far", "down"].begin()
    x = tokens_ref[...].astype(F32) + branch_ref[...].astype(F32)
    inverse = lax.rsqrt(jnp.mean(x * x, axis=-1, keepdims=True) + EPSILON)
    hidden = (x * inverse * gain_of(gain_ref, 1, part)).astype(BF)
    mine = flip(lax.axis_index(FSDP), 0) * ctx_count + lax.axis_index(CTX)
    lane = lax.broadcasted_iota(jnp.int32, (1, HD), 1)
    chosen = (lane % experts == mine // share) & (lane < 2 * experts)
    weights = jnp.sum(jnp.where(chosen, rides_ref[...].astype(F32), 0.0), axis=1, keepdims=True)
    for k in [*range(1, experts), 0]:
        rows = slice(k * room, (k + 1) * room)
        picked = dot(place_ref[k], hidden, 1, 0).astype(BF)
        if k == 0:
            two[rows] = picked
            continue
        for i in range(experts):
            slots_out[rows, i * run : (i + 1) * run] = picked[:, (i ^ k) * run : ((i ^ k) + 1) * run]
        runs["slots"].start(k - 1)
    for move in ("load", "far"):
        for name in ("in", "down"):
            runs[move, name].settle()
    for stage, ks in enumerate(stages):
        rows = slice(ks[0] * room, (ks[-1] + 1) * room)
        for k in ks:
            if k:
                runs["slots"].await_one(k - 1)
        for t in range(1, share):
            out_rows = slice((t - 1) * slots + rows.start, (t - 1) * slots + rows.stop)
            for k in range(experts):
                block = slice(k * part, (k + 1) * part)
                at = slice((k * share + t) * part, (k * share + t + 1) * part)
                two_out[out_rows, block] = two[rows, at]
                dy_out[out_rows, block] = dy_ref[rows, at]
        runs["two", stage, 0].begin()
        runs["dy", stage, 0].begin()
        two_rows, grad_rows = two[rows], dy_ref[rows]
        weight = weights[rows]
        for at, size in chunks(units, 256):
            cols = slice(at, at + size)
            g = dot(two_rows, win[:, cols], 1, 0)
            u = dot(two_rows, win[:, units + at : units + at + size], 1, 0)
            sigmoid = 1.0 / (1.0 + jnp.exp(-g))
            silu = g * sigmoid
            active[rows, cols] = (silu * u * weight).astype(BF)
            grad = dot(grad_rows, wdown[:, cols], 1, 0) * weight
            gu[rows, cols] = (grad * u * (sigmoid * (1.0 + g * (1.0 - sigmoid)))).astype(BF)
            gu[rows, units + at : units + at + size] = (grad * silu).astype(BF)
        runs["active", stage, 0].begin()
        runs["gu", stage, 0].begin()
        for i in range(experts):
            cols = slice(i * run, (i + 1) * run)
            back_out[rows, cols] = dot(gu[rows], win[cols], 1, 1).astype(BF)
        for k in ks:
            if k:
                runs["back"].start(k - 1)
        for i in range(experts):
            cols = slice(i * run, (i + 1) * run)
            out = dot(active[rows], wdown[cols], 1, 1).astype(BF)
            for k in ks:
                at = slice(k * room - rows.start, (k + 1) * room - rows.start)
                turned = slice((i ^ k) * run, ((i ^ k) + 1) * run)
                mlp_ref[k * room : (k + 1) * room, turned] = out[at]
        for k in ks:
            if k < 2:
                for r in range(len(groups["mlp"]) // 2):
                    runs["mlp"].start(2 * r + k)
    leaving = pltpu.make_async_copy(mlp_ref, mlp_out, leave)
    leaving.start()
    for name in groups:
        if isinstance(name, tuple) and name[0] != "load":
            runs[name].finish()
    for k in range(experts):
        rows = slice(k * part, (k + 1) * part)
        own = slice(k * share * part, (k * share + 1) * part)
        for out, left, left_got, right, right_got in (
            (win, two, two_got, gu, gu_got),
            (wdown, dy_ref, dy_got, active, active_got),
        ):
            for at, size in chunks(right.shape[1], 512):
                cols = slice(at, at + size)
                total = dot(left[:, own], right[:, cols], 0, 0)
                if share > 1:
                    total = total + dot(left_got[:, rows], right_got[:, cols], 0, 0)
                out[rows, cols] = total.astype(BF)
        runs["out"].start(2 * k)
        runs["out"].start(2 * k + 1)
    runs["back"].settle()
    for i in range(experts):
        cols = slice(i * run, (i + 1) * run)
        total = dot(place_ref[0], back_out[:room, cols], 0, 0)
        for k in range(1, experts):
            at = slice((i ^ k) * run, ((i ^ k) + 1) * run)
            total = total + dot(place_ref[k], back_got[k * room : (k + 1) * room, at], 0, 0)
        two_part[:, cols] = total.astype(BF)
    runs["back"].finish()
    runs["out"].finish()
    runs["mlp"].finish()
    leaving.wait()
    runs["slots"].finish()


def list_stages(experts):
    return [[0], list(range(1, experts - 1)), [experts - 1]]


def run_experts(
    number, ctx_count, tp_count, experts, share, part, fetched, far_moves, far, weights, tokens, *small
):
    place = small[2]
    room, rows = place.shape[1:]
    slots, width = experts * room, tokens.shape[1]
    units = weights["down"].shape[1]
    run = width // experts
    others = max(1, share - 1) * slots
    groups = {
        "slots": [
            (("slots_out", (k * room, room), None), ("two", (k * room, room), None), k * share, ())
            for k in range(1, experts)
        ],
        ("load", "in"): [(("in", r, None), ("win", r, None), None, ()) for r in fetched],
        ("load", "down"): [(("down", r, None), ("wdown", r, None), None, ()) for r in fetched],
        ("far", "in"): [m for m in far_moves if m[1][0] == "win"],
        ("far", "down"): [m for m in far_moves if m[1][0] == "wdown"],
    }
    for stage, ks in enumerate(list_stages(experts)):
        mine = (ks[0] * room, len(ks) * room)
        for name in ("two", "dy", "active", "gu"):
            groups[name, stage, 0] = []
            for t in range(1, share):
                rows_at = ((t - 1) * slots + mine[0], mine[1])
                source = (name + "_out", rows_at, None) if name in ("two", "dy") else (name, mine, None)
                target = (name + "_got", rows_at, None)
                groups[name, stage, 0].append((source, target, t, ()))
    groups["back"] = [
        (("back_out", (k * room, room), None), ("back_got", (k * room, room), None), k * share, ())
        for k in range(1, experts)
    ]
    groups["mlp"] = [
        (("mlp", (k * room, room), (TP, run, r)), ("mlp_first", ((2 * r - 2 + k) * room, room), None), -r, ())
        for r in range(1, tp_count)
        for k in range(2)
    ]
    groups["out"] = []
    for k in range(experts):
        r = (k * part, part)
        groups["out"].append((("win", r, None), ("gin", r, None), None, ()))
        groups["out"].append((("wdown", r, None), ("gdown", r, None), None, ()))
    total = sum(len(moves) for moves in groups.values())
    full = pl.BlockSpec(memory_space=pltpu.VMEM)
    any_spec = pl.BlockSpec(memory_space=pl.ANY)
    return pl.pallas_call(
        functools.partial(experts_kernel, ctx_count, experts, share, part, groups, list(far)),
        out_shape=[
            jax.ShapeDtypeStruct((experts * part, 2 * units), BF),
            jax.ShapeDtypeStruct((experts * part, units), BF),
            jax.ShapeDtypeStruct((slots, width), BF),
            jax.ShapeDtypeStruct((rows, width), BF),
            jax.ShapeDtypeStruct(((tp_count - 1) * 2 * room, run), BF),
        ],
        in_specs=[full] * 6 + [any_spec] * (2 + len(far)),
        out_specs=[any_spec] * 3 + [full] * 2,
        scratch_shapes=[
            pltpu.VMEM((width, 2 * units), BF),
            pltpu.VMEM((width, units), BF),
            *[pltpu.VMEM((slots, width), BF)] * 4,
            pltpu.VMEM((slots, units), BF),
            pltpu.VMEM((slots, 2 * units), BF),
            *[pltpu.VMEM((others, experts * part), BF)] * 4,
            pltpu.VMEM((others, 2 * units), BF),
            pltpu.VMEM((others, units), BF),
            pltpu.VMEM((slots, width), BF),
            pltpu.SemaphoreType.DMA,
        ]
        + [pltpu.SemaphoreType.DMA((total,))] * 2,
        compiler_params=pltpu.CompilerParams(
            collective_id=number, has_side_effects=True, vmem_limit_bytes=VMEM_LIMIT
        ),
        name="experts",
    )(tokens, *small, weights["in"], weights["down"], *far.values())


def head_cols(index):
    return pl.ds(pl.multiple_of(index * HD, HD), HD)


def slot_table(place_ref, about_ref, out):
    experts = place_ref.shape[0]
    for e in range(experts):
        found = dot(place_ref[e], about_ref[...], 1, 0)
        filled = jnp.sum(place_ref[e].astype(F32), axis=1, keepdims=True)
        found = jnp.where(filled > 0, found, about_ref[:1].astype(F32))
        out[e, :, 0:1] = found[:, 0:1]
        out[e, :, 1:2] = found[:, 1:2] * 32.0 + found[:, 2:3]
        gate = found[:, 3 + e : 4 + e] + found[:, 3 + experts + e : 4 + experts + e]
        out[e, :, 2:3] = gate * filled


def scores_of(place, queries, keys, info, segk, idxk):
    segq, idxq = info[:, 0:1], info[:, 1:2]
    slots = dot(place, queries, 1, 0).astype(BF)
    scores = dot(slots, keys, 1, 1) * (HD**-0.5)
    allowed = (segq == segk) & (idxk <= idxq)
    scores = jnp.where(allowed, scores, MASKED)
    top = jnp.max(scores, axis=-1, keepdims=True)
    exps = jnp.exp(scores - top)
    total = jnp.sum(exps, axis=-1, keepdims=True)
    return slots, exps, 1.0 / total


def front_kernel(
    ctx_count,
    moves,
    marks,
    names_in,
    names_out,
    heads,
    part,
    tokens_ref,
    gain_ref,
    cos_ref,
    sin_ref,
    place_ref,
    about_ref,
    segk_ref,
    idxk_ref,
    dy_ref,
    ride_ref,
    place_mlp_ref,
    *refs,
):
    experts, room, rows = place_ref.shape
    width = tokens_ref.shape[1]
    wide = heads * HD
    group = width // part
    given, refs = refs[: len(names_in)], refs[len(names_in) :]
    gains_ref, hidden_out, qkv_out, kv_out, mixed_ref, branch_ref, dy_out, rides_ref = refs[:8]
    refs = refs[8:]
    made, refs = refs[: len(names_out)], refs[len(names_out) :]
    hidden_ref, qkv_ref, kv_ref, early, full, slots_ref, picked, picked_ride, slot_info, send, recv, *bounces = refs
    leaving = []
    for i, pair in enumerate(((hidden_ref, hidden_out), (qkv_ref, qkv_out), (kv_ref, kv_out))):
        leaving.append(pltpu.make_async_copy(*pair, early.at[i]))
    arrays = dict(
        gain_own=gain_ref,
        gains=gains_ref,
        picked=picked,
        slots=slots_ref,
        picked_ride=picked_ride,
        rides=rides_ref,
        dy=dy_out,
        qkv=qkv_ref,
        kv=kv_ref,
        full=full,
    )
    arrays.update(zip(names_in, given))
    arrays.update(zip(names_out, made))
    greet(ctx_count, masks_of(moves))
    run = Moves(ctx_count, moves, arrays, send, recv, bounces)
    gains_done, first_done, second_done, rest_done, keys_done, dy_done, spread_done = marks
    run_of = dy_ref.shape[1] // experts
    for k in range(experts):
        rows_at = slice(k * room, (k + 1) * room)
        cols = run_cols(run_of, k)
        slots = dot(place_mlp_ref[k], dy_ref[:, cols], 1, 0).astype(BF)
        rides = dot(place_mlp_ref[k], ride_ref[...], 1, 0).astype(BF)
        if k:
            picked[rows_at], picked_ride[rows_at] = slots, rides
        else:
            slots_ref[rows_at], rides_ref[rows_at] = slots, rides
    for i in range(keys_done, dy_done):
        run.start(i)
    run.begin(second_done)
    gains_ref[:16] = gain_ref[...]
    slot_table(place_ref, about_ref, slot_info)
    x = tokens_ref[...].astype(F32)
    normed = x * lax.rsqrt(jnp.mean(x * x, axis=-1, keepdims=True) + EPSILON)
    run.settle(gains_done)
    hidden_ref[...] = (normed * gain_of(gains_ref, 0, part)).astype(BF)
    leaving[0].start()
    run.settle(first_done, gains_done)
    run.kick(dy_done, spread_done)
    dy_out[:, run_cols(run_of)] = slots_ref[...]
    cos, sin = cos_ref[:rows], sin_ref[:rows]

    def project(plane):
        y = dot(hidden_ref[...], full[:, plane * wide : (plane + 1) * wide], 1, 0)
        for head in range(heads):
            cols = slice(head * HD, (head + 1) * HD)
            at = slice(plane * wide + head * HD, plane * wide + (head + 1) * HD)
            z = y[:, cols]
            qkv_ref[:, at] = (turn(z, cos, sin) if plane <= experts else z).astype(BF)

    project(experts)
    project(experts + 1)
    for i in range(rest_done, keys_done):
        if not moves[i][3]:
            run.start(i)
    kv_ref[:rows] = qkv_ref[:, experts * wide :]
    run.begin()
    run.settle(second_done, first_done)
    run.start(len(moves) - 2)
    for plane in range(experts):
        project(plane)
    leaving[1].start()
    run.settle(keys_done, rest_done)
    leaving[2].start()

    def step(i, carry):
        h, e = i // experts, i % experts
        cols = head_cols(e * heads + h)
        place = place_ref[e]
        _, exps, inv = scores_of(
            place,
            qkv_ref[:, cols],
            kv_ref[:, head_cols(h)],
            slot_info[e],
            segk_ref[...],
            idxk_ref[...],
        )
        attn = dot(exps.astype(BF), kv_ref[:, head_cols(heads + h)], 1, 0) * inv
        mixed = (attn * slot_info[e][:, 2:3]).astype(BF)
        mixed_ref[:, cols] = dot(place, mixed, 0, 0).astype(BF)
        return carry

    for part_of in range(2):
        half = heads * experts // 2
        lax.fori_loop(part_of * half, (part_of + 1) * half, step, 0, unroll=2)
        if part_of == 0:
            run.settle(rest_done, second_done)
            run.start(len(moves) - 1)
    for j in range(group):
        rows_at = slice(j * part, (j + 1) * part)
        branch_ref[:, rows_at] = dot(mixed_ref[...], full[rows_at, (experts + 2) * wide :], 1, 1).astype(BF)
    run.finish()
    for copy in leaving:
        copy.wait()


def front(number, ctx_count, heads, part, moves, later, given, made, small):
    tokens, gain_own, place = small[0], small[1], small[4]
    experts, room, rows = place.shape
    width = tokens.shape[1]
    wide = heads * HD
    group = width // part
    full_wide = 2 * (experts + 1) * wide
    kv_moves = []
    order = [0]
    for bit in range(bits_of(ctx_count))[::-1]:
        for at in range(len(order)):
            target = ("kv", ((at + len(order)) * rows, rows), None)
            if at:
                source = ("kv", (at * rows, rows), None)
                kv_moves.append((source, target, 1 << bit, (source,)))
            else:
                source = ("qkv", (0, rows), (experts * wide, 2 * wide))
                kv_moves.append((source, target, 1 << bit, ()))
        order = order + order
    gains_moves, first_moves, second_moves, rest_moves, dy_moves, dy_spread = moves
    marks = [len(gains_moves)]
    for more in (first_moves, second_moves, rest_moves, kv_moves, dy_moves, dy_spread):
        marks.append(marks[-1] + len(more))
    gathered = first_moves + second_moves + rest_moves
    edge = (experts + 2) * wide
    keep = []
    for cols, some in (((0, edge), first_moves + second_moves), ((edge, full_wide - edge), rest_moves)):
        rows_at = ((0, width), cols)
        keep.append(((FULL, *rows_at), ("kept", *rows_at), None, tuple(m[1] for m in some)))
    moves = gains_moves + gathered + kv_moves + dy_moves + dy_spread + later + keep
    slots_shape = (experts * place.shape[1], width // experts)
    rides_shape = (experts * place.shape[1], HD)
    names_in, names_out = list(given), [*made, "kept"]
    shapes_out = [*made.values(), (width, full_wide)]
    any_spec = pl.BlockSpec(memory_space=pl.ANY)
    full = pl.BlockSpec(memory_space=pltpu.VMEM)
    small_out = [
        ((16 * group, gain_own.shape[1]), BF),
        ((rows, width), BF),
        ((rows, (experts + 2) * wide), BF),
        ((ctx_count * rows, 2 * wide), BF),
        ((rows, experts * wide), BF),
        ((rows, width), BF),
        ((slots_shape[0], width), BF),
        (rides_shape, BF),
    ]
    bounces = [
        pltpu.VMEM((source[1][1], (source[2] or (0, given[source[0]].shape[1]))[1]), BF)
        for source, _, mask, _ in moves
        if mask == 0
    ]
    out = pl.pallas_call(
        functools.partial(
            front_kernel, ctx_count, moves, marks, names_in, names_out, heads, part
        ),
        out_shape=[jax.ShapeDtypeStruct(*x) for x in small_out]
        + [jax.ShapeDtypeStruct(shape, BF) for shape in shapes_out],
        in_specs=[full] * len(small) + [any_spec] * len(names_in),
        out_specs=[any_spec if i in (1, 2, 3) else full for i in range(len(small_out))]
        + [any_spec] * len(names_out),
        scratch_shapes=[
            *[pltpu.VMEM(*small_out[i]) for i in (1, 2, 3)],
            pltpu.SemaphoreType.DMA((3,)),
            pltpu.VMEM((width, full_wide), BF),
            *[pltpu.VMEM(slots_shape, BF)] * 2,
            pltpu.VMEM(rides_shape, BF),
            pltpu.VMEM((experts, room, HD), F32),
        ]
        + [pltpu.SemaphoreType.DMA((len(moves),))] * 2
        + bounces,
        compiler_params=pltpu.CompilerParams(
            collective_id=number, has_side_effects=True, vmem_limit_bytes=VMEM_LIMIT
        ),
        name="front",
    )(*small, *given.values())
    return out[: len(small_out)], dict(zip(names_out, out[len(small_out) :]))


def attend_back_kernel(
    ctx_count,
    moves,
    names_in,
    names_out,
    heads,
    part,
    tokens_ref,
    branch_ref,
    gain_ref,
    back_ref,
    dy_ref,
    gate_ref,
    place_ref,
    about_ref,
    segk_ref,
    idxk_ref,
    cos_ref,
    sin_ref,
    mlp_first_ref,
    weight_ref,
    qkv_any,
    kv_any,
    *refs,
):
    experts, _, rows = place_ref.shape
    keys = kv_any.shape[0]
    wide = heads * HD
    width = tokens_ref.shape[1]
    given, refs = refs[: len(names_in)], refs[len(names_in) :]
    out_ref, resid_out, grad_branch_out, gain_out_ref, back_one_ref, mlp_out_ref = refs[:6]
    made, refs = refs[6 : 6 + len(names_out)], refs[6 + len(names_out) :]
    (
        full,
        grad_ref,
        back_acc,
        dk_acc,
        dv_acc,
        total,
        got,
        mlp_mine,
        mlp_got,
        slot_info,
        qkv_ref,
        kv_ref,
        resid_ref,
        grad_branch_ref,
        send,
        recv,
        pass_send,
        pass_recv,
        load,
    ) = refs
    arrays = {**dict(zip(names_in, given)), **dict(zip(names_out, made))}
    arrays.update(mlp_mine=mlp_mine, mlp_got=mlp_got)
    bits = range(bits_of(ctx_count))
    greet(ctx_count, sorted({*masks_of(moves), *[1 << b for b in bits]}))
    run = Moves(ctx_count, moves, arrays, send, recv)
    slow = [i for i, m in enumerate(moves) if m[0][0] != "mlp"]
    pace = 2
    paced = [slow[i : i + pace] for i in range(0, len(slow), pace)]
    for i in range(len(moves)):
        if i not in slow:
            run.start(i)

    def send_some(count):
        for _ in range(min(count, len(paced))):
            for i in paced.pop(0):
                run.start(i)

    send_some(2)
    late_loads = []
    for i, (far_ref, near_ref) in enumerate(((qkv_any, qkv_ref), (kv_any, kv_ref))):
        late_loads.append(pltpu.make_async_copy(far_ref, near_ref, load.at[2 + i]))
        late_loads[-1].start()
    slot_table(place_ref, about_ref, slot_info)
    edge = (experts + 2) * wide
    loads = []
    for i, cols in enumerate((pl.ds(edge, experts * wide), pl.ds(0, edge))):
        loads.append(pltpu.make_async_copy(weight_ref.at[:, cols], full.at[:, cols], load.at[i]))
        loads[-1].start()

    x = tokens_ref[...].astype(F32) + branch_ref[...].astype(F32)
    inverse = lax.rsqrt(jnp.mean(x * x, axis=-1, keepdims=True) + EPSILON)
    normed = x * inverse
    back = back_ref[...].astype(F32)
    gain_out_ref[...] = jnp.sum(back * normed, axis=0, keepdims=True)
    scaled = back * gain_of(gain_ref, 1, part)
    inner = jnp.mean(scaled * normed, axis=-1, keepdims=True)
    resid = dy_ref[...].astype(F32) + inverse * (scaled - normed * inner)
    resid_ref[...] = resid
    grad_branch_ref[...] = resid.astype(BF)
    leaving = []
    for i, pair in enumerate(((resid_ref, resid_out), (grad_branch_ref, grad_branch_out))):
        leaving.append(pltpu.make_async_copy(*pair, load.at[4 + i]))
        leaving[-1].start()
    loads[0].wait()
    for e in range(experts):
        cols = slice(edge + e * wide, edge + (e + 1) * wide)
        mixed = dot(grad_branch_ref[...], full[:, cols], 1, 0)
        grad_ref[:, e * wide : (e + 1) * wide] = (mixed * gate_ref[:, e : e + 1]).astype(BF)

    def head_copy(h, bit):
        size = keys >> (bit + 1)
        i = h * len(bits) + bit
        return pltpu.make_async_remote_copy(
            src_ref=total.at[h, pl.ds(size, size)],
            dst_ref=got.at[h, pl.ds(size, size)],
            send_sem=pass_send.at[i],
            recv_sem=pass_recv.at[i],
            device_id=peer(ctx_count, 1 << bit),
            device_id_type=pl.DeviceIdType.MESH,
        )

    def head_sum(h, bit):
        size = keys >> (bit + 1)
        head_copy(h, bit).wait_recv()
        mine = total[h, :size].astype(F32) + got[h, size : 2 * size].astype(F32)
        mine = mine.astype(BF)
        if bit + 1 < len(bits):
            total[h, :size] = mine
            head_copy(h, bit + 1).start()
        else:
            at = experts * wide
            out_ref[:, at + h * HD : at + (h + 1) * HD] = mine[:, :HD]
            at += wide
            out_ref[:, at + h * HD : at + (h + 1) * HD] = mine[:, HD:]

    for late in late_loads:
        late.wait()
    for h in range(heads):
        dk_acc[...] = jnp.zeros_like(dk_acc)
        dv_acc[...] = jnp.zeros_like(dv_acc)

        def step(e, carry, h=h):
            cols = head_cols(e * heads + h)
            place = place_ref[e]
            k, v = kv_ref[:, h * HD : (h + 1) * HD], kv_ref[:, (heads + h) * HD : (heads + h + 1) * HD]
            slots, exps, inv = scores_of(
                place, qkv_ref[:, cols], k, slot_info[e], segk_ref[...], idxk_ref[...]
            )
            attn = dot(exps.astype(BF), v, 1, 0) * inv
            probs = exps * inv
            grad = dot(place, grad_ref[:, cols], 1, 0)
            delta = jnp.sum(grad * attn, axis=-1, keepdims=True)
            grad = grad.astype(BF)
            dv_acc[...] += dot(probs.astype(BF), grad, 0, 0)
            grad_probs = dot(grad, v, 1, 1)
            grad_scores = (probs * (grad_probs - delta)).astype(BF)
            dq = dot(grad_scores, k, 1, 0) * (HD**-0.5)
            dk_acc[...] += dot(grad_scores, slots, 0, 0) * (HD**-0.5)
            top = dq.astype(BF)
            low = (dq - top.astype(F32)).astype(BF)
            back_q = dot(place, top, 0, 0) + dot(place, low, 0, 0)
            out_ref[:, cols] = turn(back_q, cos_ref[:rows], -sin_ref[:rows]).astype(BF)
            return carry

        for low in range(0, experts, 2):
            lax.fori_loop(low, low + 2, step, 0, unroll=2)
            if h < heads // 2:
                send_some(1)
        total[h, :, :HD] = turn(dk_acc[...], cos_ref[...], -sin_ref[...]).astype(BF)
        total[h, :, HD:] = dv_acc[...].astype(BF)
        head_copy(h, 0).start()
        if h:
            head_sum(h - 1, 0)
    head_sum(heads - 1, 0)
    send_some(len(paced))
    loads[1].wait()
    queries = experts * wide
    for j in range(width // part):
        rows_at = slice(j * part, (j + 1) * part)
        back_acc[:, rows_at] = dot(out_ref[:, :queries], full[rows_at, :queries], 1, 1)
    for bit in bits[1:]:
        for h in range(heads):
            head_sum(h, bit)
    for j in range(width // part):
        rows_at = slice(j * part, (j + 1) * part)
        keyed = dot(out_ref[:, queries:], full[rows_at, queries:edge], 1, 1)
        back_one_ref[:, rows_at] = (back_acc[:, rows_at] + keyed).astype(BF)
    runs_mlp = [i for i, m in enumerate(moves) if m[0][0] == "mlp"]
    for i in runs_mlp:
        run.await_one(i)
    slots, others = mlp_mine.shape[0], len(runs_mlp) - 1
    first = mlp_first_ref.shape[0] // others
    for low, top, came, size in ((0, first, mlp_first_ref, first), (first, slots, mlp_got, slots)):
        mlp_total = mlp_mine[low:top].astype(F32)
        for r in range(others):
            mlp_total = mlp_total + came[r * size + low : r * size + top].astype(F32)
        mlp_out_ref[low:top] = mlp_total.astype(BF)
    for h in range(heads):
        for bit in bits:
            head_copy(h, bit).wait_send()
    run.finish()
    for copy in leaving:
        copy.wait()


def attend_back(number, ctx_count, tp_count, heads, part, moves, given, made, weight, qkv, kv, *small):
    tokens = small[0]
    rows, width = tokens.shape
    keys = kv.shape[0]
    any_spec = pl.BlockSpec(memory_space=pl.ANY)
    full = pl.BlockSpec(memory_space=pltpu.VMEM)
    passes = heads * bits_of(ctx_count)
    slots, run = given["mlp"].shape[0], width // tp_count
    first = small[-1].shape[0] // (tp_count - 1)
    mlp_moves = [(("mlp", (0, slots), (TP, run)), ("mlp_mine", (0, slots), None), None, ())]
    for r in range(1, tp_count):
        source = ("mlp", (first, slots - first), (TP, run, r))
        target = ("mlp_got", ((r - 1) * slots + first, slots - first), None)
        mlp_moves.append((source, target, -r, ()))
    moves = mlp_moves + moves
    small_out = [
        (qkv.shape, BF),
        ((rows, width), F32),
        ((rows, width), BF),
        ((1, width), F32),
        ((rows, width), BF),
        ((slots, run), BF),
    ]
    out = pl.pallas_call(
        functools.partial(
            attend_back_kernel, ctx_count, moves, list(given), list(made), heads, part
        ),
        out_shape=[jax.ShapeDtypeStruct(*x) for x in small_out]
        + [jax.ShapeDtypeStruct(shape, BF) for shape in made.values()],
        in_specs=[full] * len(small) + [any_spec] * (3 + len(given)),
        out_specs=[any_spec if i in (1, 2) else full for i in range(len(small_out))]
        + [any_spec] * len(made),
        input_output_aliases={
            len(small) + 3 + list(given).index(n): len(small_out) + i for i, n in enumerate(made)
        },
        scratch_shapes=[
            pltpu.VMEM(weight.shape, BF),
            pltpu.VMEM((rows, weight.shape[1] - qkv.shape[1]), BF),
            pltpu.VMEM((rows, width), F32),
        ]
        + [pltpu.VMEM((keys, HD), F32)] * 2
        + [pltpu.VMEM((heads, keys, 2 * HD), BF)] * 2
        + [pltpu.VMEM((slots, run), BF), pltpu.VMEM(((tp_count - 1) * slots, run), BF)]
        + [pltpu.VMEM((*small[6].shape[:2], HD), F32), pltpu.VMEM(qkv.shape, BF), pltpu.VMEM(kv.shape, BF)]
        + [pltpu.VMEM(*small_out[i]) for i in (1, 2)]
        + [pltpu.SemaphoreType.DMA((len(moves),))] * 2
        + [pltpu.SemaphoreType.DMA((passes,))] * 2
        + [pltpu.SemaphoreType.DMA((6,))],
        compiler_params=pltpu.CompilerParams(
            collective_id=number, has_side_effects=True, vmem_limit_bytes=VMEM_LIMIT
        ),
        name="attend_back",
    )(*small, weight, qkv, kv, *given.values())
    return out[: len(small_out)], dict(zip(made, out[len(small_out) :]))


def spread_kernel(experts, me_ref, *refs):
    from_in, from_down = refs[:experts], refs[experts : 2 * experts]
    in_ref, down_ref = refs[2 * experts :]
    units = down_ref.shape[2]
    for m in range(experts):

        @pl.when(me_ref[0] == m)
        def _():
            for e in range(experts):
                for c in range(2):
                    in_ref[:, e, c, :] = from_in[e ^ m][:, c * units : (c + 1) * units].astype(F32)
                down_ref[:, e, :] = from_down[e ^ m][...].astype(F32)


def spread_grads(from_in, from_down, me, in_shape, down_shape):
    experts = len(from_in)
    step = min(64, in_shape[0])

    def rows_of(width):
        return pl.BlockSpec((step, width), lambda i, m: (i, 0))

    return pl.pallas_call(
        functools.partial(spread_kernel, experts),
        grid_spec=pltpu.PrefetchScalarGridSpec(
            num_scalar_prefetch=1,
            grid=(in_shape[0] // step,),
            in_specs=[rows_of(from_in[0].shape[1])] * experts
            + [rows_of(from_down[0].shape[1])] * experts,
            out_specs=[
                pl.BlockSpec((step, *in_shape[1:]), lambda i, m: (i, 0, 0, 0)),
                pl.BlockSpec((step, *down_shape[1:]), lambda i, m: (i, 0, 0)),
            ],
        ),
        out_shape=[
            jax.ShapeDtypeStruct(in_shape, F32),
            jax.ShapeDtypeStruct(down_shape, F32),
        ],
        compiler_params=pltpu.CompilerParams(vmem_limit_bytes=VMEM_LIMIT),
        name="spread_grads",
    )(me.astype(jnp.int32).reshape(1), *from_in, *from_down)


def places(routes, gates, experts, cap, room):
    rows = routes.shape[0]
    named = routes[:, :, None] == jnp.arange(experts, dtype=jnp.int32)[None, None, :]
    member = jnp.any(named, axis=1)
    gate = jnp.sum(jnp.where(named, gates[:, :, None], 0.0), axis=1)
    token = jnp.arange(rows, dtype=jnp.int32)
    earlier = (token[None, :] < token[:, None]).astype(BF)
    rank = dot(earlier, member.astype(BF), 1, 0).astype(jnp.int32)
    slot = jnp.where(member, rank, -1).T
    taken = slot[:, None, :] == jnp.arange(room, dtype=jnp.int32)[None, :, None]
    return taken, gate


def split(x):
    high = x.astype(BF)
    return high, (x - high.astype(F32)).astype(BF)


def layer(
    counts,
    tokens,
    gain_attn,
    gain_mlp,
    w_kv,
    w_query,
    w_out_attn,
    w_in,
    w_down,
    segments,
    attn_routes,
    attn_gates,
    mlp_routes,
    mlp_gates,
    cotangent,
):
    fsdp_count, ctx_count, tp_count = counts
    group = fsdp_count * ctx_count
    me = lax.axis_index(GROUP)
    ctx_me = lax.axis_index(CTX)
    rows, width = tokens.shape[1:]
    cap = 9 * rows // 16
    room = -(-cap // 16) * 16
    part = width // group
    attn_experts = w_query.shape[1]
    experts = w_in.shape[1]
    share = group // experts
    expert_me = me // share
    hidden_units = w_down.shape[2]
    head_width = w_kv.shape[2]

    def piece(x, index, size=part, axis=1):
        return lax.dynamic_slice_in_dim(x, index * size, size, axis)

    def exchange(x, mask):
        return swap(x, mask, GROUP, group)

    def after(x, *events):
        return lax.optimization_barrier((x, *events))[0]

    high, second = group // 2, group // 4

    gain_own = jnp.pad(jnp.concatenate([gain_attn, gain_mlp])[None, :], ((0, 15), (0, 0)))
    kv_out_own = jnp.concatenate([w_kv.reshape(part, -1), w_out_attn.reshape(part, -1)], axis=1)
    attn_own = [w_query.reshape(part, -1), kv_out_own]
    far_x, far_y = [], []
    for own in attn_own:
        far_x.append(exchange(own, high))
        far_y.append(exchange(own, second))

    seg_row = segments[0]
    seq_total = seg_row.shape[0]
    ctx_bits = list(range(bits_of(ctx_count)))[::-1]
    key_order = [0]
    for bit in ctx_bits:
        key_order = key_order + [j | (1 << bit) for j in key_order]
    key_seg = jnp.concatenate([piece(seg_row, ctx_me ^ j, rows, 0) for j in key_order])
    key_idx = jnp.concatenate(
        [(ctx_me ^ j) * rows + jnp.arange(rows, dtype=jnp.int32) for j in key_order]
    )
    place_idx = jnp.arange(seq_total, dtype=jnp.int32)
    pos = jnp.sum(
        (seg_row[None, :] == key_seg[:, None]) & (place_idx[None, :] < key_idx[:, None]),
        axis=1,
        dtype=jnp.int32,
    ).astype(F32)
    frequency = ROPE_BASE ** (-(jnp.arange(HD // 2, dtype=F32) * 2.0) / HD)
    angles = pos[:, None] * frequency[None, :]
    cos_half, sin_half = jnp.cos(angles), jnp.sin(angles)
    cos = jnp.concatenate([cos_half, cos_half], axis=1)
    sin = jnp.concatenate([-sin_half, sin_half], axis=1)
    taken_attn, gate_attn = places(attn_routes[0], attn_gates[0], attn_experts, cap, room)
    place_attn = taken_attn.astype(BF)
    own_seg, own_idx = key_seg[:rows], key_idx[:rows]
    gate_high, gate_low = split(gate_attn)
    about = [own_seg[:, None], (own_idx // 32)[:, None], (own_idx % 32)[:, None], gate_high, gate_low]
    about = jnp.concatenate([x.astype(BF) for x in about], axis=1)
    about = jnp.pad(about, ((0, 0), (0, HD - about.shape[1])))
    key_row = (key_seg.astype(F32)[None, :], key_idx.astype(F32)[None, :])
    taken_mlp, gate_mlp = places(mlp_routes[0], mlp_gates[0], experts, cap, room)
    mine_first = [expert_me ^ k for k in range(experts)]
    place_mlp = jnp.concatenate([piece(taken_mlp, e, 1, 0) for e in mine_first]).astype(BF)
    tokens_rel, grad_out = in_order(me, [tokens[0], cotangent[0]], group)

    def expert_rows(k):
        in_rows = piece(w_in, expert_me ^ k, 1, 1)
        down_rows = piece(w_down, expert_me ^ k, 1, 1)
        return [in_rows[:, 0, 0], in_rows[:, 0, 1], down_rows[:, 0]]

    to_send = [expert_rows(k) for k in range(experts)]

    def given_sends(ks):
        return {("send", k, c): x for k in ks for c, x in enumerate(to_send[k])}

    in_cols, down_cols = (0, 2 * hidden_units), (2 * hidden_units, hidden_units)
    weight_shapes = {"in": (width, 2 * hidden_units), "down": (width, hidden_units)}

    def weight_moves(k, first, size, prefix=""):
        moves = []
        sides = (("in", (0, hidden_units)), ("in", (hidden_units, hidden_units)), ("down", None))
        for c, (name, cols) in enumerate(sides):
            base = k * share * part + first
            source = (("send", k, c), (first, size), None)
            landed = (prefix + name, (base, size), cols)
            moves.append((source, landed, k * share, ()))
            for t in range(1, share):
                target = (prefix + name, (base + t * part, size), cols)
                if k:
                    moves.append((landed, target, t, (landed,)))
                else:
                    moves.append((source, target, t, ()))
        return moves

    def many_weight_moves(cuts):
        return [m for cut in cuts for m in weight_moves(*cut)]

    near = [k for k in range(1, experts) if k & (k - 1) == 0]
    far = [k for k in range(1, experts) if k & (k - 1)]
    half_part = part // 2

    far_x, to_send = lax.optimization_barrier((far_x, to_send))
    cut = max(16, part * 3 // 8 // 16 * 16)
    gather_moves = []
    queries, two_planes = attn_experts * head_width, 2 * head_width
    for n, first, size_of, edge in (
        (1, 0, two_planes, queries),
        (0, 0, queries, 0),
        (1, two_planes, queries, queries + two_planes),
    ):
        cols, own_cols = (edge, size_of), (first, size_of)
        moves = []
        held = {0: [(("own", n), 0, part, ())], high: [(("x", n), 0, part, ())], second: [(("y", n), 0, part, ())]}
        corner = []
        for side, mask, low, top in ((("x", n), second, 0, cut), (("y", n), high, cut, part)):
            half = (top - low) // 32 * 16
            for at, size in ((low, half), (low + half, top - low - half)):
                if size:
                    target = (FULL, ((high | second) * part + at, size), cols)
                    corner.append(((side, (at, size), own_cols), target, mask, ()))
        corner = corner[::2] + corner[1::2]
        moves += corner
        held[high | second] = [(FULL, t[1][0] - (high | second) * part, t[1][1], (t,)) for _, t, _, _ in corner]
        for j in (0, high, second):
            source = (held[j][0][0], (0, part), own_cols)
            moves.append((source, (FULL, (j * part, part), cols), None, ()))
        for bit in range(bits_of(group) - 2)[::-1]:
            for j in list(held):
                there = []
                for name, at, size, needs in held[j]:
                    if name == FULL:
                        source = (name, (at + j * part, size), cols)
                    else:
                        source = (name, (at, size), own_cols)
                    target = (FULL, ((j | 1 << bit) * part + at, size), cols)
                    moves.append((source, target, 1 << bit, needs))
                    there.append((FULL, at, size, (target,)))
                held[j | 1 << bit] = there
        gather_moves.append(moves)
    gain_moves = [
        (("gain_own", (0, 16), None), ("gains", (j * 16, 16), None), j, ())
        for j in range(1, group)
    ]
    heads = head_width // HD
    later = weight_moves(0, 0, part) + many_weight_moves([(k, 0, half_part) for k in near])
    gate_ride = jnp.concatenate(split(gate_mlp), axis=1)
    gate_ride = jnp.pad(gate_ride, ((0, 0), (0, HD - 2 * experts)))
    dy_moves = [
        ((name, (k * room, room), None), (target, (k * room, room), None), k * share, ())
        for k in range(1, experts)
        for name, target in (("picked", "slots"), ("picked_ride", "rides"))
    ]
    dy_spread, run = [], width // tp_count
    for k in range(experts):
        mine = (k * room, room)
        needs = ((("slots", mine, None)),) if k else ()
        for r in range(1, tp_count):
            source, target = ("slots", mine, None), ("dy", mine, (TP, run, 0, r))
            dy_spread.append((source, target, -r, needs))
    (gains, hidden_one, qkv, kv, mixed, branch, dy_slots, dy_rides), made = front(
        1,
        ctx_count,
        heads,
        part,
        (gain_moves, *gather_moves, dy_moves, dy_spread),
        later,
        {
            **{("own", n): x for n, x in enumerate(attn_own)},
            **{("x", n): x for n, x in enumerate(far_x)},
            **{("y", n): x for n, x in enumerate(far_y)},
            **given_sends([0, *near]),
        },
        weight_shapes,
        (
            tokens_rel,
            gain_own,
            cos,
            sin,
            place_attn,
            about,
            *key_row,
            grad_out,
            gate_ride,
            place_mlp,
        ),
    )
    attn_full, weights = made["kept"], {n: made[n] for n in weight_shapes}
    branch_sum = lax.psum(branch, TP)
    cuts = [(k, half_part, part - half_part) for k in near] + [(k, 0, half_part) for k in far]
    to_send, weights, _ = lax.optimization_barrier((to_send, weights, branch))
    given = {**given_sends([*near, *far]), **weights}
    weights = move("weights_two", 3, ctx_count, many_weight_moves(cuts), given, weight_shapes)
    fetched, far_moves = [], []
    for j in range(group):
        size = half_part if j // share in far else part
        if fetched and sum(fetched[-1]) == j * part:
            fetched[-1] = (fetched[-1][0], fetched[-1][1] + size)
        else:
            fetched.append((j * part, size))
    for k in far:
        far_moves += weight_moves(k, half_part, part - half_part, "w")
    grads_in, grads_down, mlp_slots, back_two_part, mlp_first = run_experts(
        4,
        ctx_count,
        tp_count,
        experts,
        share,
        part,
        fetched,
        far_moves,
        given_sends(far),
        weights,
        tokens_rel,
        branch_sum,
        gains,
        place_mlp,
        dy_slots,
        dy_rides,
    )
    back_two = lax.psum(back_two_part, TP)
    got_in, got_down = {0: grads_in}, {0: grads_down}

    def grad_moves(ks, cuts, first=0):
        moves = []
        for at in range(first, part, part // cuts):
            for k in ks:
                for name in ("in", "down"):
                    source = (name, (k * part + at, part // cuts), None)
                    target = ((name, k), (at, part // cuts), None)
                    moves.append((source, target, k * share, ()))
        made_shapes = {("in", k): (part, 2 * hidden_units) for k in ks}
        return moves, {**made_shapes, **{("down", k): (part, hidden_units) for k in ks}}

    def keep_grads(made, ks):
        got_in.update({k: made[("in", k)] for k in ks})
        got_down.update({k: made[("down", k)] for k in ks})

    cuts = min(8, part // 16)
    moves, made_shapes = grad_moves(near, 1)
    early, early_shapes = grad_moves(far, cuts)
    moves += early[: len(early) // cuts]
    made_shapes.update(early_shapes)
    grads_in, grads_down, _ = lax.optimization_barrier((grads_in, grads_down, back_two_part))
    given = {"in": grads_in, "down": grads_down}
    made = move("grads_near", 5, ctx_count, moves, given, made_shapes)
    keep_grads(made, near)

    moves, made_shapes = grad_moves(far, cuts, part // cuts)
    back_two, given, made = lax.optimization_barrier((back_two, given, made))
    given.update({name: made[name] for name in made_shapes})
    given["mlp"] = mlp_slots
    (grad_qkv, grad_resid, grad_branch, gain_two_grad, back_one_part, mlp_run), made = attend_back(
        6,
        ctx_count,
        tp_count,
        heads,
        part,
        moves,
        given,
        made_shapes,
        attn_full,
        qkv,
        kv,
        tokens_rel,
        branch_sum,
        gains,
        back_two,
        grad_out,
        gate_attn,
        place_attn,
        about,
        *key_row,
        cos,
        sin,
        mlp_first,
    )
    keep_grads(made, far)
    upper = list(range(1, bits_of(group)))
    grad_attnw, kept, *given, grad_tokens, gain_grads, mlp_sum = attn_grads(
        7,
        ctx_count,
        tp_count,
        upper,
        part,
        head_width,
        hidden_one,
        grad_branch,
        grad_qkv,
        mixed,
        back_one_part,
        tokens_rel,
        gains,
        grad_resid,
        gain_two_grad,
        mlp_run,
        place_mlp,
    )
    planes = attn_experts * 2 + 2
    lanes, last_lanes = lanes_of(planes, attn_experts + 2, upper)
    came = []
    for i in range(2):
        bit = dict(lanes)[last_lanes[3 * i]][-1]
        came.append(exchange(given[i], 1 << bit))
    output, grad_tokens = last(me, group, tokens_rel, branch_sum, mlp_sum, grad_tokens)
    grad_in_out, grad_down_out = spread_grads(
        [got_in[k] for k in range(experts)],
        [got_down[k] for k in range(experts)],
        expert_me,
        w_in.shape,
        w_down.shape,
    )
    came, _ = lax.optimization_barrier((came, (output, grad_in_out)))
    grad_query_w, grad_kv_w, grad_out_w = lay_out(
        last_lanes, [grad_attnw, kept, *came], (w_query.shape, w_kv.shape, w_out_attn.shape)
    )
    return (
        output[None],
        grad_tokens[None],
        gain_grads[0],
        gain_grads[1],
        grad_kv_w,
        grad_query_w,
        grad_out_w,
        grad_in_out,
        grad_down_out,
    )


def solution(mesh):
    rows = P(FSDP, CTX, None)
    weight = P(GROUP, None, TP)
    weight_in = P(GROUP, None, None, TP)
    return jax.shard_map(
        functools.partial(layer, tuple(mesh.shape[a] for a in (FSDP, CTX, TP))),
        mesh=mesh,
        in_specs=(
            rows,
            P(GROUP),
            P(GROUP),
            weight,
            weight,
            weight,
            weight_in,
            weight,
            P(FSDP, None),
            rows,
            rows,
            rows,
            rows,
            rows,
        ),
        out_specs=(rows, rows, P(GROUP), P(GROUP), weight, weight, weight, weight_in, weight),
        check_vma=False,
    )
```
